128 devices in a mesh: section: 2 (over core), ctx: 16 (over x, z), shard: 4 (over y).
Axes of the slice: x: 4, y: 4, z: 4, core: 2. Of those that a mesh axis runs over, the one named last changes fastest.
Arguments:
- hidden_in: bfloat16 [4, 2, 1024, 1088], P('shard', None, 'ctx'), may hold values from -6 to 6
- cotangent: bfloat16 [4, 2, 1024, 1088], P('shard', None, 'ctx'), may hold values from -6 to 6
- block_order: int32 [2, 32], replicated, may hold values from 0 to 31, as said below
- qkv_weight: bfloat16 [2, 1088, 3264], P('section', 'shard'), may hold values from -0.1875 to 0.1875
- out_weight: bfloat16 [2, 1088, 1088], P('section', 'shard'), may hold values from -0.75 to 0.75
- up_weight: bfloat16 [2, 1088, 4352], P('section', 'shard'), may hold values from -0.1875 to 0.1875
- down_weight: bfloat16 [2, 4352, 1088], P('section', 'shard'), may hold values from -0.09375 to 0.09375
- norm_gains: bfloat16 [2, 2, 1088], P('section', None, 'shard'), may hold values from 0.5 to 1.5
- norm_biases: bfloat16 [2, 2, 1088], P('section', None, 'shard'), may hold values from -3 to 3
Outputs:
- activations: bfloat16 [2, 4, 2, 1024, 1088], P('section', 'shard', None, 'ctx')
- input_grads: bfloat16 [2, 4, 2, 1024, 1088], P('section', 'shard', None, 'ctx')
- qkv_grad: float32 [2, 1088, 3264], P('section', 'shard')
- out_grad: float32 [2, 1088, 1088], P('section', 'shard')
- up_grad: float32 [2, 1088, 4352], P('section', 'shard')
- down_grad: float32 [2, 4352, 1088], P('section', 'shard')
- gain_grad: float32 [2, 2, 1088], P('section', None, 'shard')
- bias_grad: float32 [2, 2, 1088], P('section', None, 'shard')
The draws below stay inside these ranges and needn't reach their ends.
Inputs may be any that keep to these rules, and one draw needn't show every extreme that they name: `block_order`: each row holds every block number once, and entries 2 c and 2 c + 1 sum to 31.
All inputs are finite; a program needn't handle non-finite values.
Results may differ from the reference program's by a relative error of at most 0.018.
Values may be sent and summed in bfloat16 or wider, within the bound.
A program may use at most 320 MiB of HBM per device.

```python
import math
import jax
import jax.numpy as jnp
from jax import lax

D = 1088
HEADS = 17
HEAD_DIM = 64
FF = 4352
MB = 2
SEQ_LEN = 2048
BLK = 32
GROUP = 1024
BLOCKS = 32
SEQS = 4
N_SECTION = 2


def draw_block_order(key, part):
    key = jax.random.fold_in(key, 7)

    def one_row(row_key):
        pair_key, flip_key = jax.random.split(row_key)
        lower = jax.random.permutation(pair_key, BLOCKS // 2).astype(jnp.int32)
        flipped = jax.random.randint(flip_key, (BLOCKS // 2,), 0, 2)
        upper = BLOCKS - 1 - lower
        first_slot = jnp.where(flipped == 1, upper, lower)
        second_slot = jnp.where(flipped == 1, lower, upper)
        return jnp.stack([first_slot, second_slot], axis=1).reshape(BLOCKS)
    return jax.vmap(one_row)(jax.random.split(key, MB)).astype(jnp.int32)


def steps_of(key, shape, pieces, low, high):
    gain = 1.0
    for position, blocks in pieces:
        heights = jax.random.uniform(jax.random.fold_in(jax.random.fold_in(key, 6), position), (blocks,), jnp.float32, low / len(pieces), high / len(pieces))
        gain = gain * jnp.repeat(jnp.exp(heights), shape[position] // blocks).reshape((-1,) + (1,) * (len(shape) - 1 - position))
    return gain


def noise(own_key, dims, scale, reach, shards=(), kind=jnp.bfloat16):
    gain = steps_of(own_key, dims, shards, -0.22, 0.18) if shards else 1.0
    array = jax.random.normal(own_key, dims, jnp.float32) * scale * gain
    return jnp.minimum(jnp.maximum(array, -reach), reach).astype(kind)


def setup_inputs(seed: int = 0) -> dict:
    seeds = jax.random.split(jax.random.key(seed), 10)
    hidden_in = noise(seeds[0], (SEQS, MB, GROUP, D), 1.0, 6.0, ((0, 4), (2, 16)))
    cotangent = noise(seeds[1], (SEQS, MB, GROUP, D), 1.0, 6.0, ((0, 4), (2, 16)))
    block_order = draw_block_order(jax.random.fold_in(seeds[9], 71), 0)
    qkv_weight = noise(seeds[3], (N_SECTION, D, 3 * D), D ** -0.5, 0.1875, ((0, 2), (1, 4)))
    out_weight = noise(seeds[4], (N_SECTION, D, D), (D // 16) ** -0.5, 0.75, ((0, 2), (1, 4)))
    up_weight = noise(seeds[5], (N_SECTION, D, FF), D ** -0.5, 0.1875, ((0, 2), (1, 4)))
    down_weight = noise(seeds[6], (N_SECTION, FF, D), FF ** -0.5, 0.09375, ((0, 2), (1, 4)))
    norm_gains = jnp.clip(1.0 + 0.1 * jax.random.normal(seeds[7], (N_SECTION, 2, D), jnp.float32), 0.5, 1.5).astype(jnp.bfloat16)
    norm_biases = noise(seeds[8], (N_SECTION, 2, D), 0.5, 3.0, ((0, 2), (2, 4)))
    return dict(hidden_in=hidden_in, cotangent=cotangent, block_order=block_order, qkv_weight=qkv_weight, out_weight=out_weight, up_weight=up_weight, down_weight=down_weight, norm_gains=norm_gains, norm_biases=norm_biases)


EPSILON = 1e-05
NEG_LARGE = -1e+30

@jax.custom_vjp
def low(v):
    return lax.optimization_barrier(v.astype(jnp.bfloat16)).astype(jnp.float32)

@jax.custom_vjp
def low_back(v):
    return v

def low_keep(v):
    return (low(v), None)

def low_pass(kept, grad):
    return (grad,)

def back_keep(v):
    return (v, None)

def back_low(kept, grad):
    return (low(grad),)
low.defvjp(low_keep, low_pass)
low_back.defvjp(back_keep, back_low)

def layer_norm(values, gain_row, shift_row):
    center = values - lax.optimization_barrier(jnp.mean(values, axis=-1, keepdims=True))
    spread = lax.optimization_barrier(jnp.mean(center * center, axis=-1, keepdims=True))
    return center * lax.rsqrt(spread + EPSILON) * gain_row + shift_row

def key_positions(block_order):
    offsets = lax.broadcasted_iota(jnp.int32, (1, 1, BLK), 2)
    group_ids = lax.broadcasted_iota(jnp.int32, (MB, 1, 1), 0)
    return (group_ids * GROUP + block_order.astype(jnp.int32)[:, :, None] * BLK + offsets).reshape(-1)

def attend(query_block, query_pos, key_heads, value_heads, key_pos):
    scores = jnp.einsum('qhd,khd->hqk', query_block, key_heads, precision=lax.Precision.HIGHEST) * HEAD_DIM ** (-0.5)
    scores = low_back(scores)
    scores = jnp.where(query_pos[None, :, None] >= key_pos[None, None, :], scores, NEG_LARGE)
    row_max = lax.optimization_barrier(jnp.max(scores, axis=-1, keepdims=True))
    exponent = jnp.exp(scores - row_max)
    probs = low(exponent / lax.optimization_barrier(jnp.sum(exponent, axis=-1, keepdims=True)))
    return jnp.einsum('hqk,khd->qhd', probs, value_heads, precision=lax.Precision.HIGHEST)

def layer(sequence, positions, w_qkv, w_out, w_up, w_down, gain_rows, shift_rows):
    highest = lax.Precision.HIGHEST
    normed = low(layer_norm(sequence, gain_rows[0], shift_rows[0]))
    projected = low(low_back(jnp.dot(normed, w_qkv, precision=highest)))
    queries = projected[:, :D]
    key_heads = projected[:, D:2 * D].reshape(SEQ_LEN, HEADS, HEAD_DIM)
    value_heads = projected[:, 2 * D:].reshape(SEQ_LEN, HEADS, HEAD_DIM)
    block_len = math.gcd(SEQ_LEN, 512)
    block_count = SEQ_LEN // block_len
    query_blocks = queries.reshape(block_count, block_len, HEADS, HEAD_DIM)
    pos_blocks = positions.reshape(block_count, block_len)
    checked = jax.checkpoint(attend)
    context = lax.map(lambda block_item: checked(block_item[0], block_item[1], key_heads, value_heads, positions), (query_blocks, pos_blocks))
    context = low(low_back(context.reshape(SEQ_LEN, D)))
    residual = sequence + low_back(jnp.dot(context, w_out, precision=highest))
    normed2 = low(layer_norm(residual, gain_rows[1], shift_rows[1]))
    pre_act = low_back(jnp.dot(normed2, w_up, precision=highest))
    hidden = low(jax.nn.gelu(pre_act, approximate=True))
    return residual + low_back(jnp.dot(hidden, w_down, precision=highest))

def reference(hidden_in, cotangent, block_order, qkv_weight, out_weight, up_weight, down_weight, norm_gains, norm_biases):
    positions = key_positions(block_order)
    inputs = hidden_in.astype(jnp.float32).reshape(SEQS, SEQ_LEN, D)
    seed_grad = cotangent.astype(jnp.float32).reshape(SEQS, SEQ_LEN, D)

    def forward(inputs, extra, w_qkv, w_out, w_up, w_down, gain_all, shift_all):

        def one(carried, block_item):
            sequence, added = block_item
            first_out = layer(sequence, positions, w_qkv[0], w_out[0], w_up[0], w_down[0], gain_all[0], shift_all[0])
            second = layer(low(low_back(first_out)) + added, positions, w_qkv[1], w_out[1], w_up[1], w_down[1], gain_all[1], shift_all[1])
            return (carried, (first_out, second))
        _, results = lax.scan(one, jnp.zeros((), jnp.float32), (inputs, extra))
        return results
    primals = (inputs, jnp.zeros_like(inputs), qkv_weight.astype(jnp.float32), out_weight.astype(jnp.float32), up_weight.astype(jnp.float32), down_weight.astype(jnp.float32), norm_gains.astype(jnp.float32), norm_biases.astype(jnp.float32))
    (first_out, second), pullback = jax.vjp(forward, *primals)
    grads = pullback((jnp.zeros_like(first_out), seed_grad))
    activations = jnp.stack([first_out, second]).reshape(N_SECTION, SEQS, MB, GROUP, D).astype(jnp.bfloat16)
    input_grads = jnp.stack([grads[0], grads[1]]).reshape(N_SECTION, SEQS, MB, GROUP, D).astype(jnp.bfloat16)
    return (activations, input_grads, grads[2], grads[3], grads[4], grads[5], grads[6], grads[7])
```

```python
import types

import jax
import jax.numpy as jnp
from jax import lax
from jax.experimental import pallas as pl
from jax.experimental.pallas import tpu as pltpu
from jax.sharding import PartitionSpec as P

D = 1088
HEADS = 17
HEAD_DIM = 64
FF = 4352
SHARD = 4
CTX = 16
ROWS = 64
GROUP = 1024
SEQ = 2048
WINDOW = 640
SLICE = D // SHARD
EPSILON = 1e-05
NEG_LARGE = -1e30
BF16 = jnp.bfloat16
F32 = jnp.float32
MESH = pl.DeviceIdType.MESH
VMEM = pltpu.VMEM
ANY = pl.ANY
VMEM_BYTES = 56 * 2**20


def spec(shape, dtype=BF16):
    return jax.ShapeDtypeStruct(shape, dtype)


def call(name, body, ins, outs, scratch, collective_id=None, prefetch=None):
    in_names, out_names, scratch_names = list(ins), list(outs), list(scratch)
    names = in_names + out_names + scratch_names

    def kernel(*refs):
        body(types.SimpleNamespace(**dict(zip(names, refs))))

    extra = {} if collective_id is None else dict(collective_id=collective_id, has_side_effects=True)
    results = pl.pallas_call(
        kernel,
        out_shape=tuple(outs[n][0] for n in out_names),
        in_specs=[pl.BlockSpec(memory_space=ins[n][1]) for n in in_names],
        out_specs=tuple(pl.BlockSpec(memory_space=outs[n][1]) for n in out_names),
        scratch_shapes=[scratch[n] for n in scratch_names],
        compiler_params=pltpu.CompilerParams(vmem_limit_bytes=VMEM_BYTES, **extra),
        name=name,
    )(*(ins[n][0] for n in in_names))
    return dict(zip(out_names, results))


def dot(a, b):
    return jnp.dot(a, b, preferred_element_type=F32)


def dot_nt(a, b):
    return lax.dot_general(a, b, (((1,), (1,)), ((), ())), preferred_element_type=F32)


def dot_tn(a, b):
    return lax.dot_general(a, b, (((0,), (0,)), ((), ())), preferred_element_type=F32)


def norm_parts(values):
    center = values - jnp.mean(values, axis=-1, keepdims=True)
    rate = lax.rsqrt(jnp.mean(center * center, axis=-1, keepdims=True) + EPSILON)
    return center * rate, rate


def layer_norm(values, gain, bias):
    return norm_parts(values)[0] * gain + bias


def gelu(u):
    return 0.5 * u * (1.0 + jnp.tanh(0.7978845608028654 * (u + 0.044715 * u * u * u)))


class Here:
    def __init__(self, sems):
        self.s = lax.axis_index("section")
        self.c = lax.axis_index("ctx")
        self.y = lax.axis_index("shard")
        self.sems, self.used, self.sent = sems, 0, []

    def sem(self):
        self.used += 1
        return self.sems.at[self.used - 1]

    def shard(self, step):
        return lax.rem(self.y + step, SHARD)

    def rows(self, shard, core):
        return pl.ds(pl.multiple_of((shard * 2 + core) * ROWS, ROWS), ROWS)

    def barrier(self):
        sem = pltpu.get_barrier_semaphore()
        count = 0
        for step in range(SHARD):
            for core in range(2):
                if step or core:
                    to = (lax.rem(self.s + core, 2), self.c, self.shard(step))
                    pl.semaphore_signal(sem, inc=1, device_id=to, device_id_type=MESH)
                    count += 1
        for step in range(1, CTX):
            for core in range(2):
                to = (core, lax.rem(self.c + step, CTX), self.y)
                pl.semaphore_signal(sem, inc=1, device_id=to, device_id_type=MESH)
                count += 1
        pl.semaphore_wait(sem, count)

    def send(self, src, dst, to, arrive, leave=None):
        copy = pltpu.make_async_remote_copy(
            src_ref=src, dst_ref=dst, send_sem=self.sem() if leave is None else leave,
            recv_sem=arrive, device_id=to, device_id_type=MESH)
        copy.start()
        if leave is None:
            self.sent.append(copy)
        return copy

    def send_or_keep(self, src, dst, to, is_self, arrive):
        leave = self.sem()
        copy = pltpu.make_async_remote_copy(
            src_ref=src, dst_ref=dst, send_sem=leave, recv_sem=arrive, device_id=to, device_id_type=MESH)
        kept = pltpu.make_async_copy(src, dst, arrive)
        pl.when(jnp.logical_not(is_self))(copy.start)
        pl.when(is_self)(kept.start)

        def wait_send():
            pl.when(jnp.logical_not(is_self))(copy.wait_send)

        self.sent.append(types.SimpleNamespace(wait_send=wait_send))

    def sibling(self):
        return (1 - self.s, self.c, self.y)

    def finish(self):
        for copy in self.sent:
            copy.wait_send()
        self.sent = []


def wait_bytes(ref, sem):
    pltpu.make_async_copy(ref, ref, sem).wait()


class Gather8:
    def __init__(self, here, full):
        self.here, self.full = here, full
        self.own = [here.sem() for _ in range(SHARD)]
        self.other = [here.sem() for _ in range(SHARD)]

    def start(self, value):
        h = self.here
        mine = self.full.at[h.rows(h.y, h.s)]
        mine[...] = value
        h.send(mine, mine, h.sibling(), self.other[0])
        for step in (1, 3, 2):
            h.send(mine, mine, (h.s, h.c, h.shard(step)), self.own[SHARD - step])

    def relay(self, step):
        h = self.here
        part = self.full.at[h.rows(h.shard(step), h.s)]
        wait_bytes(part, self.own[step])
        h.send(part, part, h.sibling(), self.other[step])

    def wait(self, step):
        h = self.here
        wait_bytes(self.full.at[h.rows(h.shard(step), 1 - h.s)], self.other[step])


class Scatter8:
    def __init__(self, here, bufs):
        self.here = here
        self.to_core, self.mine, self.from_core, self.to_shard, self.from_shard = bufs
        self.core = [here.sem() for _ in range(SHARD)]
        self.shard = [here.sem() for _ in range(SHARD)]

    def put(self, step, block):
        h = self.here
        low, high = block[:ROWS], block[ROWS:]
        self.to_core[step] = jnp.where(h.s == 0, high, low).astype(BF16)
        self.mine[step] = jnp.where(h.s == 0, low, high)
        h.send(self.to_core.at[step], self.from_core.at[step], h.sibling(), self.core[step])

    def relay(self, step):
        h = self.here
        wait_bytes(self.from_core.at[step], self.core[step])
        self.to_shard[step] = (self.mine[step] + self.from_core[step].astype(F32)).astype(BF16)
        h.send(self.to_shard.at[step], self.from_shard.at[step], (h.s, h.c, h.shard(step)), self.shard[step])

    def result(self):
        wait_bytes(self.from_core.at[0], self.core[0])
        total = self.mine[0] + self.from_core[0].astype(F32)
        for step in (1, 3, 2):
            wait_bytes(self.from_shard.at[step], self.shard[step])
            total = total + self.from_shard[step].astype(F32)
        return total


def scatter_scratch(name):
    quarter = (SHARD, ROWS, D)
    return {
        name + "_to_core": VMEM(quarter, BF16),
        name + "_mine": VMEM(quarter, F32),
        name + "_from_core": VMEM(quarter, BF16),
        name + "_to_shard": VMEM(quarter, BF16),
        name + "_from_shard": VMEM(quarter, BF16),
    }


def scatter(here, r, name):
    parts = ("_to_core", "_mine", "_from_core", "_to_shard", "_from_shard")
    return Scatter8(here, [getattr(r, name + p) for p in parts])


ORDER = (0, 1, 3, 2)


def window_offset(group):
    return 32 * lax.rem(group, 4)


class Weights:
    def __init__(self, here, r, layer):
        self.h, self.r, self.layer = here, r, layer
        self.holds = here.s == layer
        self.arrive = {n: here.sem() for n in ("qkv", "h16", "up", "down", "out")}
        self.zero = [here.sem() for _ in range(3)]
        self.kept = []

    def everyone(self):
        for step in (1, 3, 2, 0):
            for core in range(2):
                yield step, core, (core, self.h.c, self.h.shard(step))

    def copies(self, name, pairs):
        h = self.h
        started = []
        for step, core, src, dst in pairs:
            if step == 0 and core == self.layer:
                started.append(pltpu.make_async_copy(src, dst, self.arrive[name]))
            else:
                copy = pltpu.make_async_remote_copy(
                    src_ref=src, dst_ref=dst, send_sem=h.sem(), recv_sem=self.arrive[name],
                    device_id=(core, h.c, h.shard(step)), device_id_type=MESH)
                started.append(copy)
                self.kept.append(copy)

        @pl.when(self.holds)
        def _():
            for copy in started:
                copy.start()

    def rows_of(self, ref):
        return ref.at[pl.ds(pl.multiple_of(self.h.y * SLICE, 16), SLICE)]

    def send_qkv(self):
        h, r = self.h, self.r
        load = pltpu.make_async_copy(r.w_qkv, r.qkv_rows, h.sem())

        @pl.when(self.holds)
        def _():
            load.start()
            load.wait()
            rows = r.qkv_rows
            for g in range(8):
                first = rows[:, 128 * g : 128 * g + 128]
                keys = rows[:, D + 128 * g : D + 128 * g + 128]
                values = rows[:, 2 * D + 128 * g : 2 * D + 128 * g + 128]
                r.qkv_packed[g] = jnp.concatenate(
                    [first, keys[:, :64], values[:, :64], keys[:, 64:], values[:, 64:]], axis=1)
            r.h16_packed[...] = jnp.concatenate(
                [rows[:, D - 64 : D], rows[:, 2 * D - 64 : 2 * D], rows[:, 3 * D - 64 : 3 * D]], axis=1)

        self.copies("qkv", [
            (step, core, r.qkv_packed.at[h.shard(step) * 2 + core], self.rows_of(r.qkv_w))
            for step, core, _ in self.everyone()])
        self.copies("h16", [
            (step, core, r.h16_packed, self.rows_of(r.h16_w)) for step, core, _ in self.everyone()])

    def send_rest(self):
        h, r = self.h, self.r
        pairs = []
        for step, core, _ in self.everyone():
            start = pl.multiple_of(128 * ((17 * (h.shard(step) * 2 + core)) // 4), 128)
            pairs.append((step, core, r.w_up.at[:, pl.ds(start, WINDOW)], self.rows_of(r.up_w)))
        self.copies("up", pairs)
        r.zeros[...] = jnp.zeros_like(r.zeros)
        offset = window_offset(h.y * 2 + h.s)
        for i in range(3):
            row = jnp.where(32 * i < offset, 32 * i, 544 + 32 * i)
            pltpu.make_async_copy(
                r.zeros, r.down_w.at[pl.ds(pl.multiple_of(row, 32), 32)], self.zero[i]).start()
        pairs = []
        for core in range(2):
            at = pl.multiple_of(window_offset(h.y * 2 + core), 32)
            pairs.append((0, core, r.w_down.at[pl.ds(544 * core, 544)], r.down_w.at[pl.ds(at, 544)]))
        self.copies("down", pairs)
        self.out_tiles = []
        for i in range(17):
            tile = h.y * 17 + i
            group = jnp.minimum(tile // 8, 7)
            core, shard = lax.rem(group, 2), group // 2
            src = r.w_out.at[pl.ds(16 * i, 16)]
            row = pl.multiple_of(lax.rem(tile, 8) * 16, 16)
            dst = r.out_w.at[pl.ds(row, 16)]
            copy = pltpu.make_async_remote_copy(
                src_ref=src, dst_ref=dst, send_sem=h.sem(), recv_sem=self.arrive["out"],
                device_id=(core, h.c, shard), device_id_type=MESH)
            same = pltpu.make_async_copy(src, dst, self.arrive["out"])
            mine = self.holds & (tile < 64)
            is_self = (core == self.layer) & (shard == h.y)
            pl.when(mine & is_self)(same.start)
            pl.when(mine & jnp.logical_not(is_self))(copy.start)
            self.out_tiles.append((mine & jnp.logical_not(is_self), copy))
        self.last = []
        for step, core, to in self.everyone():
            src, dst = r.w_out.at[pl.ds(SLICE - 64, 64)], r.out_w.at[pl.ds(128, 64)]
            if step == 0 and core == self.layer:
                self.last.append(pltpu.make_async_copy(src, dst, self.arrive["out"]))
            else:
                copy = pltpu.make_async_remote_copy(
                    src_ref=src, dst_ref=dst, send_sem=h.sem(), recv_sem=self.arrive["out"],
                    device_id=to, device_id_type=MESH)
                self.last.append(copy)

        @pl.when(self.holds & (h.y == SHARD - 1))
        def _():
            for copy in self.last:
                copy.start()

    def wait_qkv(self):
        r = self.r
        wait_bytes(r.qkv_w, self.arrive["qkv"])
        wait_bytes(r.h16_w, self.arrive["h16"])

    def wait_rest(self):
        r, h = self.r, self.h
        wait_bytes(r.up_w, self.arrive["up"])
        wait_bytes(r.out_w, self.arrive["out"])
        wait_bytes(r.down_w.at[pl.ds(0, 544)], self.arrive["down"])
        for i in range(3):
            wait_bytes(r.zeros, self.zero[i])

        @pl.when(self.holds)
        def _():
            for copy in self.kept:
                copy.wait_send()

        for cond, copy in self.out_tiles:
            pl.when(cond)(copy.wait_send)

        @pl.when(self.holds & (h.y == SHARD - 1))
        def _():
            for copy in self.last[:-2] + self.last[-1:] if self.layer == 0 else self.last[:-1]:
                copy.wait_send()


def weight_outs():
    return {
        "qkv_w": (spec((D, 384)), ANY),
        "h16_w": (spec((D, 192)), ANY),
        "up_w": (spec((D, WINDOW)), ANY),
        "down_w": (spec((WINDOW, D)), ANY),
        "out_w": (spec((192, D)), ANY),
    }


def weight_scratch():
    return {
        "qkv_rows": VMEM((SLICE, 3 * D), BF16),
        "qkv_packed": VMEM((8, SLICE, 384), BF16),
        "h16_packed": VMEM((SLICE, 192), BF16),
        "zeros": VMEM((32, D), BF16),
    }


def head_outs():
    return {
        "a_full": (spec((512, D)), VMEM),
        "message_in": (spec((CTX, 160, 128)), VMEM),
        "kv16_in": (spec((2, CTX, ROWS, 128)), VMEM),
        "q16": (spec((ROWS, HEAD_DIM)), VMEM),
    }


def head_scratch():
    return {
        "message": VMEM((2, 4, 2, 160, 128), BF16),
        "qkv_vm": VMEM((D, 384), BF16),
        "h16_vm": VMEM((D, 192), BF16),
    }


def start_head(h, r, a_value):
    gather = Gather8(h, r.a_full)
    gather.start(a_value)
    return gather


def run_head(h, r, gather, weights, a_value):
    load = [pltpu.make_async_copy(r.qkv_w, r.qkv_vm, h.sem()), pltpu.make_async_copy(r.h16_w, r.h16_vm, h.sem())]
    weights.wait_qkv()
    for copy in load:
        copy.start()
    arrive = h.sem()
    for copy in load:
        copy.wait()
    own16 = dot(a_value, r.h16_vm[...]).astype(BF16)
    r.q16[...] = own16[:, :64]
    r.kv16_in[h.s, h.c] = own16[:, 64:]
    own_kv = r.kv16_in.at[h.s, h.c]
    leave16, arrive16, cross16 = h.sem(), h.sem(), h.sem()
    for step in range(1, CTX):
        h.send(own_kv, own_kv, (h.s, lax.rem(h.c + step, CTX), h.y), arrive16, leave16)
    for step in ORDER:
        if step:
            gather.relay(step)
        gather.wait(step)
        shard = h.shard(step)
        block = r.a_full[pl.ds(pl.multiple_of(shard * 128, 128), 128)]
        out = dot(block, r.qkv_vm[...]).astype(BF16)
        for e in range(2):
            for core in range(2):
                r.message[e, shard, core, :128] = out[:, 128 + 128 * e : 256 + 128 * e]
                for b in range(2):
                    at = 32 * b + 16 * core
                    lanes = slice(64 * e, 64 * e + 64)
                    packed = jnp.concatenate([out[at : at + 16, lanes], out[64 + at : 80 + at, lanes]], axis=1)
                    r.message[e, shard, core, 128 + 16 * b : 144 + 16 * b] = packed
                chip = 8 * h.s + 4 * e + shard
                h.send_or_keep(
                    r.message.at[e, shard, core], r.message_in.at[h.c], (core, chip, h.y),
                    (chip == h.c) & (h.s == core), arrive)
    wait_bytes(r.kv16_in.at[h.s, pl.ds(0, CTX - 1)], arrive16)
    cross = r.kv16_in.at[h.s]
    h.send(cross, cross, h.sibling(), cross16)
    wait_bytes(r.kv16_in.at[h.s, pl.ds(0, CTX - 1)], leave16)
    wait_bytes(r.kv16_in.at[1 - h.s], cross16)
    wait_bytes(r.message_in, arrive)


def first_kernel(hidden, params, w_qkv, w_out, w_up, w_down):
    def body(r):
        h = Here(r.sems)
        weights = Weights(h, r, 0)
        h.barrier()
        arrive = h.sem()
        own = r.params_in.at[h.s * SHARD + h.y]
        own[...] = r.params[...]
        for step, core, to in weights.everyone():
            if step:
                h.send(own, own, to, arrive)
        h.send(own, own, h.sibling(), arrive)
        weights.send_qkv()
        wait_bytes(r.params_in.at[pl.ds(0, 7)], arrive)
        for layer in range(2):
            r.norms[layer] = jnp.concatenate([r.params_in[layer * SHARD + i] for i in range(SHARD)], axis=1)
        x = r.hidden[h.s].astype(F32)
        a_value = layer_norm(x, r.norms[0, 0:1], r.norms[0, 2:3]).astype(BF16)
        gather = start_head(h, r, a_value)
        weights.send_rest()
        run_head(h, r, gather, weights, a_value)
        weights.wait_rest()
        h.finish()

    outs = {"norms": (spec((2, 8, D), F32), VMEM), **head_outs(), **weight_outs()}
    ins = {
        "hidden": (hidden, VMEM), "params": (params, VMEM), "w_qkv": (w_qkv, ANY), "w_out": (w_out, ANY),
        "w_up": (w_up, ANY), "w_down": (w_down, ANY),
    }
    scratch = {
        "params_in": VMEM((8, 8, SLICE), F32), **head_scratch(), **weight_scratch(),
        "sems": pltpu.SemaphoreType.DMA((200,)),
    }
    return call("first", body, ins, outs, scratch, collective_id=0)


def attend(block_order, positions, own_positions, message_in, kv16_in, q16):
    def body(r):
        half = lax.axis_index("section")
        for c in range(CTX):
            for m in range(2):
                for b in range(2):
                    block = 32 * m + r.order[m, 2 * c + b]
                    rows = r.message_in[c, 64 * m + 32 * b : 64 * m + 32 * b + 32, :]
                    at = pl.ds(pl.multiple_of(block * 32, 32), 32)
                    r.keys[at] = rows[:, :64]
                    r.values[at] = rows[:, 64:]
                    at = pl.ds(pl.multiple_of(block * 16, 16), 16)
                    r.queries[at] = r.message_in[c, 128 + 16 * b : 144 + 16 * b, 64 * m : 64 * m + 64] * 0.125
        row = lax.broadcasted_iota(jnp.int32, (256, 512), 0)
        row = 32 * (row // 16) + 16 * half + row % 16
        visible = row >= lax.broadcasted_iota(jnp.int32, (256, 512), 1)
        for t in range(4):
            query = r.queries[256 * t : 256 * t + 256]
            parts = [dot_nt(query, r.keys[512 * u : 512 * u + 512]) for u in range(t + 1)]
            parts[t] = jnp.where(visible, parts[t], NEG_LARGE)
            top = parts[0]
            for p in parts[1:]:
                top = jnp.maximum(top, p)
            top = jnp.max(top, axis=-1, keepdims=True)
            parts = [jnp.exp(p - top) for p in parts]
            total = parts[0]
            for p in parts[1:]:
                total = total + p
            total = jnp.sum(total, axis=-1, keepdims=True)
            out = dot(parts[0].astype(BF16), r.values[:512])
            for u in range(1, t + 1):
                out = out + dot(parts[u].astype(BF16), r.values[512 * u : 512 * u + 512])
            r.sorted_out[256 * t : 256 * t + 256] = (out / total).astype(BF16)
            r.logs[256 * t : 256 * t + 256] = jnp.broadcast_to(top + jnp.log(total), (256, 128))
        for c in range(CTX):
            for m in range(2):
                for b in range(2):
                    at = pl.multiple_of((32 * m + r.order[m, 2 * c + b]) * 16, 16)
                    r.out[c, 16 * b : 16 * b + 16, 64 * m : 64 * m + 64] = r.sorted_out[pl.ds(at, 16)]
        kv = r.kv16_in[...].reshape(SEQ, 128)
        scores = dot_nt(r.q16[...] * 0.125, kv[:, :64])
        scores = jnp.where(r.own_positions[...] >= r.positions[...], scores, NEG_LARGE)
        top = jnp.max(scores, axis=-1, keepdims=True)
        scores = jnp.exp(scores - top)
        total = jnp.sum(scores, axis=-1, keepdims=True)
        out = dot(scores.astype(BF16), kv[:, 64:])
        r.out16[...] = (out / total).astype(BF16)
        r.logs16[...] = jnp.broadcast_to(top + jnp.log(total), (ROWS, 128))

    ins = {
        "order": (block_order, pltpu.SMEM), "positions": (positions, VMEM), "own_positions": (own_positions, VMEM),
        "message_in": (message_in, VMEM), "kv16_in": (kv16_in, VMEM), "q16": (q16, VMEM),
    }
    outs = {
        "out": (spec((CTX, 32, 128)), VMEM), "out16": (spec((ROWS, 64)), VMEM),
        "sorted_out": (spec((1024, 64)), VMEM), "logs": (spec((1024, 128), F32), VMEM),
        "logs16": (spec((ROWS, 128), F32), VMEM),
    }
    scratch = {
        "keys": VMEM((SEQ, 64), BF16), "values": VMEM((SEQ, 64), BF16), "queries": VMEM((1024, 64), BF16),
    }
    return call("attend", body, ins, outs, scratch)


def middle_scratch():
    return {
        "context_in": VMEM((2, 4, 2, 32, 128), BF16),
        "out_vm": VMEM((192, D), BF16), "up_vm": VMEM((D, WINDOW), BF16), "down_vm": VMEM((WINDOW, D), BF16),
        **scatter_scratch("o"), **scatter_scratch("f"),
    }


def load_weights(h, r, layer_weights):
    loads = []
    for name in ("out", "up", "down"):
        copy = pltpu.make_async_copy(layer_weights[name], getattr(r, name + "_vm"), h.sem())
        copy.start()
        loads.append(copy)
    return loads


def gather_context(h, r):
    arrive = h.sem()
    to_core = h.c // 8
    e, j = lax.rem(h.c // 4, 2), lax.rem(h.c, 4)
    for c in range(CTX):
        h.send_or_keep(
            r.attended.at[c], r.context_in.at[e, j, h.s], (to_core, c, h.y), (h.c == c) & (h.s == to_core), arrive)
    return arrive


def unpack_context(r, store):
    for j in range(4):
        for m in range(2):
            for b in range(2):
                for core in range(2):
                    lanes = slice(64 * m, 64 * m + 64)
                    piece = jnp.concatenate(
                        [r.context_in[e, j, core, 16 * b : 16 * b + 16, lanes] for e in range(2)], axis=1)
                    at = 128 * j + 64 * m + 32 * b + 16 * core
                    store[at : at + 16] = piece


def block_rows(h, step):
    return pl.ds(pl.multiple_of(h.shard(step) * 128, 128), 128)


def run_out(h, r, x):
    sums = scatter(h, r, "o")
    for step in (2, 1, 3, 0):
        sums.put(step, dot(r.context[block_rows(h, step)], r.out_vm[:128]))
    for step in (2, 1, 3):
        sums.relay(step)
    own = x + dot(r.attended16[...], r.out_vm[128:])
    return own + sums.result()


def middle_kernel(layer, attended, attended16, x, norms, layer_weights, next_weights):
    w_qkv, w_out, w_up, w_down = next_weights

    def body(r):
        h = Here(r.sems)
        weights = Weights(h, r, layer + 1)
        h.barrier()
        loads = load_weights(h, r, {"out": r.out_l, "up": r.up_l, "down": r.down_l})
        arrive = gather_context(h, r)
        weights.send_qkv()
        for copy in loads:
            copy.wait()
        wait_bytes(r.context_in, arrive)
        unpack_context(r, r.context)
        residual = run_out(h, r, r.x[h.s].astype(F32) if layer == 0 else r.x[...].astype(F32))
        r.residual[...] = residual
        b_value = layer_norm(residual, r.norms[layer, 1:2], r.norms[layer, 3:4]).astype(BF16)
        gather = Gather8(h, r.b_full)
        gather.start(b_value)
        weights.send_rest()
        sums = scatter(h, r, "f")
        for step in ORDER:
            if step:
                gather.relay(step)
            gather.wait(step)
            rows = block_rows(h, step)
            u = dot(r.b_full[rows], r.up_vm[...])
            r.pre[rows] = u
            sums.put(step, dot(gelu(u).astype(BF16), r.down_vm[...]))
        for step in (1, 3, 2):
            sums.relay(step)
        y = (residual + sums.result()).astype(BF16)
        r.y[...] = y
        a_value = layer_norm(y.astype(F32), r.norms[layer + 1, 0:1], r.norms[layer + 1, 2:3]).astype(BF16)
        gather = start_head(h, r, a_value)
        run_head(h, r, gather, weights, a_value)
        weights.wait_rest()
        h.finish()

    ins = {
        "attended": (attended, VMEM), "attended16": (attended16, VMEM), "x": (x, VMEM), "norms": (norms, VMEM),
        "out_l": (layer_weights["out_w"], ANY), "up_l": (layer_weights["up_w"], ANY),
        "down_l": (layer_weights["down_w"], ANY),
        "w_qkv": (w_qkv, ANY), "w_out": (w_out, ANY), "w_up": (w_up, ANY), "w_down": (w_down, ANY),
    }
    outs = {
        "context": (spec((512, 128)), VMEM), "residual": (spec((ROWS, D), F32), VMEM), "b_full": (spec((512, D)), VMEM),
        "pre": (spec((512, WINDOW), F32), VMEM), "y": (spec((ROWS, D)), VMEM), **head_outs(), **weight_outs(),
    }
    scratch = {
        **middle_scratch(), **head_scratch(), **weight_scratch(), "sems": pltpu.SemaphoreType.DMA((280,)),
    }
    return call("middle", body, ins, outs, scratch, collective_id=1)


def token_positions(block_order):
    offsets = jnp.arange(32, dtype=jnp.int32)
    groups = jnp.arange(2, dtype=jnp.int32)[:, None, None] * GROUP
    return (groups + block_order[:, :, None] * 32 + offsets).reshape(2, GROUP)


def forward(hidden_in, cotangent, block_order, qkv_weight, out_weight, up_weight, down_weight, norm_gains, norm_biases):
    section, ctx = lax.axis_index("section"), lax.axis_index("ctx")
    own_weights = (qkv_weight[0], out_weight[0], up_weight[0], down_weight[0])
    params = jnp.concatenate([norm_gains[0], norm_biases[0]], axis=0).astype(F32)
    params = jnp.pad(params, ((0, 4), (0, 0)))
    grid = token_positions(block_order)
    own_positions = lax.dynamic_slice(grid, (section, ctx * ROWS), (1, ROWS)).reshape(ROWS, 1)
    positions = grid.reshape(1, SEQ)
    hidden = hidden_in[0]
    first = first_kernel(hidden, params, *own_weights)
    attended = attend(block_order, positions, own_positions, first["message_in"], first["kv16_in"], first["q16"])
    middle = middle_kernel(0, attended["out"], attended["out16"], hidden, first["norms"], first, own_weights)
    return middle["y"]
CTX_AXES = ("ctx",)


def in_one_piece(arrays, axis, dim, along):
    both = jnp.concatenate(arrays, axis=along)
    out, at, outs = (lax.all_gather(both, axis, axis=dim, tiled=True), 0, [])
    for a in arrays:
        outs.append(lax.slice_in_dim(out, at, at + a.shape[along], axis=along))
        at += a.shape[along]
    return tuple(outs)


def shifted(value, axis, steps):
    count = lax.axis_size(axis)
    first, last = (max(0, -steps), min(count, count - steps))
    return lax.ppermute(value, axis, [(source, source + steps) for source in range(first, last)])


def summed_rows(x, axes, dim):
    for axis in axes:
        x = lax.psum_scatter(x, axis, scatter_dimension=dim, tiled=True)
    return x


def in_one_piece_2(arrays, axis, dim, along):
    ends, at = ([], 0)
    for a in arrays[:-1]:
        at += a.shape[along]
        ends.append(at)
    both = jnp.concatenate(arrays, axis=along)
    return tuple(
        jnp.split(lax.psum_scatter(both, axis, scatter_dimension=dim, tiled=True), ends, axis=along)
    )


def for_sending(x):

    def short(part):
        return part.astype(jnp.bfloat16) if part.dtype == jnp.float32 else part

    return jax.tree.map(short, x)


def layer_norm_rows(values, gain_row, shift_row):
    center = values - jnp.mean(values, axis=-1, keepdims=True)
    spread = jnp.mean(center * center, axis=-1, keepdims=True)
    return center * lax.rsqrt(spread + EPSILON) * gain_row + shift_row


def gelu_tanh(values):
    return jax.nn.gelu(values, approximate=True)


def matmul(left_side, right_side):
    return jnp.dot(left_side, right_side, preferred_element_type=jnp.float32)


def matmul_tn(left_side, right_side):
    return lax.dot_general(
        left_side, right_side, (((0,), (0,)), ((), ())), preferred_element_type=jnp.float32
    )


def matmul_nt(left_side, right_side):
    return lax.dot_general(
        left_side, right_side, (((1,), (1,)), ((), ())), preferred_element_type=jnp.float32
    )


def key_positions(block_order, group_len, block_len):
    offsets = lax.broadcasted_iota(jnp.int32, (1, 1, block_len), 2)
    group_ids = lax.broadcasted_iota(jnp.int32, (block_order.shape[0], 1, 1), 0)
    return (group_ids * group_len + block_order[:, :, None] * block_len + offsets).reshape(-1)


def split_heads(matrix):
    return matrix.reshape(matrix.shape[0], HEADS, HEAD_DIM)


def attention_probs(queries, key_rows, query_pos, key_pos):
    scores = jnp.einsum(
        "qhd,khd->hqk",
        split_heads(queries),
        split_heads(key_rows),
        preferred_element_type=jnp.float32,
    ) * HEAD_DIM ** (-0.5)
    scores = jnp.where(query_pos[None, :, None] >= key_pos[None, None, :], scores, NEG_LARGE)
    row_max = jnp.max(scores, axis=-1, keepdims=True)
    exponent = jnp.exp(scores - row_max)
    return exponent / jnp.sum(exponent, axis=-1, keepdims=True)


def layer_tail(
    layer_in, queries, kv_cache, query_pos, key_pos, w_out, w_up, w_down, gain_row, shift_row
):
    model_width = layer_in.shape[1]
    attn_probs = attention_probs(queries, kv_cache[:, :model_width], query_pos, key_pos)
    probs_low = attn_probs.astype(jnp.bfloat16)
    mixed = jnp.einsum(
        "hqk,khd->qhd",
        probs_low,
        split_heads(kv_cache[:, model_width:]),
        preferred_element_type=jnp.float32,
    )
    context_low = mixed.reshape(mixed.shape[0], model_width).astype(jnp.bfloat16)
    residual = layer_in.astype(jnp.float32) + matmul(context_low, w_out)
    normed2 = layer_norm_rows(residual, gain_row, shift_row).astype(jnp.bfloat16)
    pre_act = matmul(normed2, w_up)
    hidden_low = gelu_tanh(pre_act).astype(jnp.bfloat16)
    result = residual + matmul(hidden_low, w_down)
    return (attn_probs, probs_low, context_low, residual, normed2, pre_act, hidden_low, result)


def attention_back(grad_context, attn_probs, probs_low, queries, key_rows, value_rows):
    scale = HEAD_DIM ** (-0.5)
    grad_heads = split_heads(grad_context)
    grad_probs = jnp.einsum(
        "qhd,khd->hqk", grad_heads, split_heads(value_rows), preferred_element_type=jnp.float32
    )
    grad_values = jnp.einsum(
        "hqk,qhd->khd", probs_low, grad_heads, preferred_element_type=jnp.float32
    )
    grad_scores = (
        attn_probs * (grad_probs - jnp.sum(attn_probs * grad_probs, axis=-1, keepdims=True))
    ).astype(jnp.bfloat16)
    grad_queries = (
        jnp.einsum(
            "hqk,khd->qhd", grad_scores, split_heads(key_rows), preferred_element_type=jnp.float32
        )
        * scale
    )
    grad_keys = (
        jnp.einsum(
            "hqk,qhd->khd", grad_scores, split_heads(queries), preferred_element_type=jnp.float32
        )
        * scale
    )
    query_count = grad_queries.shape[0]
    key_count = grad_keys.shape[0]
    grad_queries = grad_queries.reshape(query_count, -1).astype(jnp.bfloat16)
    return (grad_queries, grad_keys.reshape(key_count, -1), grad_values.reshape(key_count, -1))


def gather_weights(qkv_weight, out_weight, up_weight, down_weight, norm_gains, norm_biases):
    return (
        *in_one_piece((qkv_weight[0], out_weight[0], up_weight[0]), "shard", 0, 1),
        lax.all_gather(down_weight[0], "shard", axis=0, tiled=True),
        *in_one_piece((norm_gains[0], norm_biases[0]), "shard", 1, 0),
    )


def shards(
    hidden_in,
    cotangent,
    block_order,
    qkv_weight,
    out_weight,
    up_weight,
    down_weight,
    norm_gains,
    norm_biases,
):
    section_index = lax.axis_index("section")
    ctx_index = lax.axis_index(CTX_AXES)
    row_count = hidden_in.shape[2]
    micro_count = hidden_in.shape[1]
    model_width = hidden_in.shape[3]
    group_len = row_count * lax.axis_size(CTX_AXES)
    key_pos = key_positions(block_order, group_len, row_count // 2)
    pos_grid = key_pos.reshape(micro_count, group_len)
    is_first = section_index == 0
    is_last = section_index == lax.axis_size("section") - 1
    gathered_weights = gather_weights(
        qkv_weight, out_weight, up_weight, down_weight, norm_gains, norm_biases
    )
    w_qkv, w_out, w_up, w_down, gains, shifts = gathered_weights
    gains32 = gains.astype(jnp.float32)
    shifts32 = shifts.astype(jnp.float32)
    inputs_kept = jnp.zeros((micro_count, row_count, model_width), jnp.bfloat16)
    outputs_kept = jnp.zeros_like(inputs_kept)
    kv_cache = jnp.zeros((micro_count * group_len, 2 * model_width), jnp.bfloat16)
    incoming = jnp.zeros((row_count, model_width), jnp.bfloat16)
    for period in range(micro_count + 1):
        slot_raw = period - section_index
        is_valid = (slot_raw >= 0) & (slot_raw < micro_count)
        slot_index = jnp.clip(slot_raw, 0, micro_count - 1)
        layer_in = jnp.where(is_first, hidden_in[0, min(period, micro_count - 1)], incoming)
        query_pos = lax.dynamic_slice(
            pos_grid, (slot_index, ctx_index * row_count), (1, row_count)
        )[0]
        normed = layer_norm_rows(layer_in.astype(jnp.float32), gains32[0], shifts32[0]).astype(
            jnp.bfloat16
        )
        projected = matmul(normed, w_qkv).astype(jnp.bfloat16)
        gathered = lax.all_gather(projected[:, model_width:], CTX_AXES, axis=0, tiled=True)
        old_slot = lax.dynamic_slice_in_dim(kv_cache, slot_index * group_len, group_len, 0)
        kv_cache = lax.dynamic_update_slice_in_dim(
            kv_cache, jnp.where(is_valid, gathered, old_slot), slot_index * group_len, 0
        )
        tail = layer_tail(
            layer_in,
            projected[:, :model_width],
            kv_cache,
            query_pos,
            key_pos,
            w_out,
            w_up,
            w_down,
            gains32[1],
            shifts32[1],
        )
        sent = tail[7].astype(jnp.bfloat16)
        old_in = lax.dynamic_index_in_dim(inputs_kept, slot_index, 0, keepdims=False)
        inputs_kept = lax.dynamic_update_index_in_dim(
            inputs_kept, jnp.where(is_valid, layer_in, old_in), slot_index, 0
        )
        old_out = lax.dynamic_index_in_dim(outputs_kept, slot_index, 0, keepdims=False)
        outputs_kept = lax.dynamic_update_index_in_dim(
            outputs_kept, jnp.where(is_valid, sent, old_out), slot_index, 0
        )
        incoming = shifted(sent, "section", 1)
    gathered_weights = gather_weights(
        qkv_weight, out_weight, up_weight, down_weight, norm_gains, norm_biases
    )
    w_qkv, w_out, w_up, w_down, gains, shifts = gathered_weights
    gains32 = gains.astype(jnp.float32)
    shifts32 = shifts.astype(jnp.float32)
    grad_sum = tuple((jnp.zeros(member.shape, jnp.float32) for member in gathered_weights))
    w_query = w_qkv[:, :model_width]
    key_grads = jnp.zeros((micro_count * group_len, 2 * model_width), jnp.float32)
    grads_kept = jnp.zeros((micro_count, row_count, model_width), jnp.bfloat16)
    incoming = jnp.zeros((row_count, model_width), jnp.bfloat16)
    for period in range(micro_count + 1):
        slot_raw = micro_count - period - section_index
        is_valid = (slot_raw >= 0) & (slot_raw < micro_count)
        live_scale = is_valid.astype(jnp.float32)
        slot_index = jnp.clip(slot_raw, 0, micro_count - 1)
        layer_in = lax.dynamic_index_in_dim(inputs_kept, slot_index, 0, keepdims=False)
        seed_rows = lax.dynamic_index_in_dim(cotangent[0], slot_index, 0, keepdims=False)
        grad_out = jnp.where(is_last, seed_rows, incoming).astype(jnp.float32) * live_scale
        query_pos = lax.dynamic_slice(
            pos_grid, (slot_index, ctx_index * row_count), (1, row_count)
        )[0]
        layer_in32 = layer_in.astype(jnp.float32)
        normed = layer_norm_rows(layer_in32, gains32[0], shifts32[0]).astype(jnp.bfloat16)
        queries = matmul(normed, w_query).astype(jnp.bfloat16)
        attn_probs, probs_low, context_low, residual, normed2, pre_act, hidden_low, result = (
            layer_tail(
                layer_in,
                queries,
                kv_cache,
                query_pos,
                key_pos,
                w_out,
                w_up,
                w_down,
                gains32[1],
                shifts32[1],
            )
        )
        grad_branch = grad_out.astype(jnp.bfloat16)
        grad_down = matmul_tn(hidden_low, grad_branch)
        grad_hidden = matmul_nt(grad_branch, w_down)
        _, gelu_pull = jax.vjp(gelu_tanh, pre_act)
        grad_pre = gelu_pull(grad_hidden)[0].astype(jnp.bfloat16)
        grad_up = matmul_tn(normed2, grad_pre)
        grad_normed2 = matmul_nt(grad_pre, w_up)
        _, norm_pull2 = jax.vjp(layer_norm_rows, residual, gains32[1], shifts32[1])
        grad_mid_part, grad_gain2, grad_shift2 = norm_pull2(grad_normed2)
        grad_mid = grad_out + grad_mid_part
        grad_attn = grad_mid.astype(jnp.bfloat16)
        grad_outw = matmul_tn(context_low, grad_attn)
        grad_context = matmul_nt(grad_attn, w_out).astype(jnp.bfloat16)
        grad_queries, grad_keys, grad_values = attention_back(
            grad_context,
            attn_probs,
            probs_low,
            queries,
            kv_cache[:, :model_width],
            kv_cache[:, model_width:],
        )
        key_grads = key_grads + jnp.concatenate([grad_keys, grad_values], axis=1)
        grad_group = lax.dynamic_slice_in_dim(key_grads, slot_index * group_len, group_len, 0)
        grad_kv = (
            summed_rows(grad_group.astype(jnp.bfloat16), CTX_AXES, 0).astype(jnp.float32) * live_scale
        )
        grad_proj = jnp.concatenate([grad_queries, grad_kv.astype(jnp.bfloat16)], axis=1)
        grad_qkvw = matmul_tn(normed, grad_proj)
        grad_normed = matmul_nt(grad_proj, w_qkv)
        _, norm_pull1 = jax.vjp(layer_norm_rows, layer_in32, gains32[0], shifts32[0])
        grad_in_part, grad_gain1, grad_shift1 = norm_pull1(grad_normed)
        grad_in_low = (grad_mid + grad_in_part).astype(jnp.bfloat16)
        old_grad = lax.dynamic_index_in_dim(grads_kept, slot_index, 0, keepdims=False)
        grads_kept = lax.dynamic_update_index_in_dim(
            grads_kept, jnp.where(is_valid, grad_in_low, old_grad), slot_index, 0
        )
        period_grads = (
            grad_qkvw,
            grad_outw,
            grad_up,
            grad_down,
            jnp.stack([grad_gain1, grad_gain2]),
            jnp.stack([grad_shift1, grad_shift2]),
        )
        grad_sum = jax.tree.map(jnp.add, grad_sum, period_grads)
        incoming = shifted(grad_in_low, "section", -1)
    grad_sum = (
        *tuple(
            (
                part.astype(jnp.float32)
                for part in in_one_piece_2(
                    (
                        grad_sum[0].astype(jnp.bfloat16),
                        grad_sum[1].astype(jnp.bfloat16),
                        grad_sum[2].astype(jnp.bfloat16),
                    ),
                    "shard",
                    0,
                    1,
                )
            )
        ),
        lax.psum_scatter(
            grad_sum[3].astype(jnp.bfloat16), "shard", scatter_dimension=0, tiled=True
        ).astype(jnp.float32),
        *tuple(
            (
                part.astype(jnp.float32)
                for part in in_one_piece_2(
                    (grad_sum[4].astype(jnp.bfloat16), grad_sum[5].astype(jnp.bfloat16)),
                    "shard",
                    1,
                    0,
                )
            )
        ),
    )
    grad_sum = jax.tree.map(
        lambda part: part.astype(jnp.float32), lax.psum(for_sending(grad_sum), CTX_AXES)
    )
    qkv_grad, out_grad, up_grad, down_grad, gain_grad, bias_grad = grad_sum
    y = forward(hidden_in, cotangent, block_order, qkv_weight, out_weight, up_weight, down_weight, norm_gains, norm_biases)
    other = lax.ppermute(y, "section", [(0, 1), (1, 0)])
    outputs_kept = jnp.where(is_first, jnp.stack([y, other]), outputs_kept)
    return (
        outputs_kept[None, None],
        grads_kept[None, None],
        qkv_grad[None],
        out_grad[None],
        up_grad[None],
        down_grad[None],
        gain_grad[None],
        bias_grad[None],
    )


def solution(mesh):
    placed = (
        P("shard", None, CTX_AXES, None),
        P("shard", None, CTX_AXES, None),
        P(),
        P("section", "shard", None),
        P("section", "shard", None),
        P("section", "shard", None),
        P("section", "shard", None),
        P("section", None, "shard"),
        P("section", None, "shard"),
    )
    return jax.shard_map(
        shards,
        mesh=mesh,
        in_specs=placed,
        out_specs=(
            P("section", "shard", None, CTX_AXES, None),
            P("section", "shard", None, CTX_AXES, None),
            P("section", "shard", None),
            P("section", "shard", None),
            P("section", "shard", None),
            P("section", "shard", None),
            P("section", None, "shard"),
            P("section", None, "shard"),
        ),
        check_vma=False,
    )
```

```python
import types

import jax
import jax.numpy as jnp
from jax import lax
from jax.experimental import pallas as pl
from jax.experimental.pallas import tpu as pltpu
from jax.sharding import PartitionSpec as P

D = 1088
HEADS = 17
HEAD_DIM = 64
FF = 4352
SHARD = 4
CTX = 16
ROWS = 64
GROUP = 1024
SEQ = 2048
WINDOW = 640
SLICE = D // SHARD
EPSILON = 1e-05
NEG_LARGE = -1e30
BF16 = jnp.bfloat16
F32 = jnp.float32
MESH = pl.DeviceIdType.MESH
VMEM = pltpu.VMEM
ANY = pl.ANY
VMEM_BYTES = 56 * 2**20
SECTION, CONTEXT, LINE = "section", "ctx", "shard"
TILES = (68, 16, WINDOW)


def spec(shape, dtype=BF16):
    return jax.ShapeDtypeStruct(shape, dtype)


def call(name, body, ins, outs, scratch, collective_id=None):
    def kernel(*refs):
        refs, found = list(refs), {}
        for key, value in [*ins.items(), *outs.items(), *scratch.items()]:
            if isinstance(value, list):
                found[key], refs = refs[: len(value)], refs[len(value) :]
            else:
                found[key] = refs.pop(0)
        body(types.SimpleNamespace(**found))

    extra = {} if collective_id is None else dict(collective_id=collective_id, has_side_effects=True)
    shapes, given = [], []
    for value in scratch.values():
        shapes += value if isinstance(value, list) else [value]
    for value in ins.values():
        given += value if isinstance(value, list) else [value]
    results = pl.pallas_call(
        kernel,
        out_shape=tuple(value[0] for value in outs.values()),
        in_specs=[pl.BlockSpec(memory_space=space) for _, space in given],
        out_specs=tuple(pl.BlockSpec(memory_space=value[1]) for value in outs.values()),
        scratch_shapes=shapes,
        compiler_params=pltpu.CompilerParams(vmem_limit_bytes=VMEM_BYTES, **extra),
        name=name,
    )(*(array for array, _ in given))
    return types.SimpleNamespace(**dict(zip(outs, results)))


def dot(a, b):
    return jnp.dot(a, b, preferred_element_type=F32)


def dot_nt(a, b):
    return lax.dot_general(a, b, (((1,), (1,)), ((), ())), preferred_element_type=F32)


def dot_tn(a, b):
    return lax.dot_general(a, b, (((0,), (0,)), ((), ())), preferred_element_type=F32)


def norm_parts(values):
    center = values - jnp.mean(values, axis=-1, keepdims=True)
    rate = lax.rsqrt(jnp.mean(center * center, axis=-1, keepdims=True) + EPSILON)
    return center * rate, rate


def layer_norm(values, gain, bias):
    return norm_parts(values)[0] * gain + bias


def gelu(u):
    return 0.5 * u * (1.0 + jnp.tanh(0.7978845608028654 * (u + 0.044715 * u * u * u)))


class Here:
    def __init__(self, sems):
        self.s = lax.axis_index(SECTION)
        self.c = lax.axis_index(CONTEXT)
        self.y = lax.axis_index(LINE)
        self.sems, self.used, self.sent = sems, 0, []

    def sem(self):
        self.used += 1
        return self.sems.at[self.used - 1]

    def shard(self, step):
        return lax.rem(self.y + step, SHARD)

    def rows(self, shard, core):
        return pl.ds(pl.multiple_of((shard * 2 + core) * ROWS, ROWS), ROWS)

    def barrier(self, whole=True):
        sem = pltpu.get_barrier_semaphore()
        peers = []
        for step in range(SHARD):
            for core in range(2):
                if step or core:
                    peers.append((lax.rem(self.s + core, 2), self.c, self.shard(step)))
        for step in range(1, CTX if whole else 1):
            for core in range(2):
                peers.append((core, lax.rem(self.c + step, CTX), self.y))
        for to in peers:
            pl.semaphore_signal(sem, inc=1, device_id=to, device_id_type=MESH)
        pl.semaphore_wait(sem, len(peers))

    def local(self, src, dst):
        copy = pltpu.make_async_copy(src, dst, self.sem())
        copy.start()
        return copy

    def save(self, src, dst):
        copy = self.local(src, dst)
        self.sent.append(types.SimpleNamespace(wait_send=copy.wait))

    def send(self, src, dst, to, arrive, leave=None):
        copy = pltpu.make_async_remote_copy(
            src_ref=src, dst_ref=dst, send_sem=self.sem() if leave is None else leave,
            recv_sem=arrive, device_id=to, device_id_type=MESH)
        copy.start()
        if leave is None:
            self.sent.append(copy)
        return copy

    def send_or_keep(self, src, dst, to, is_self, arrive):
        leave = self.sem()
        copy = pltpu.make_async_remote_copy(
            src_ref=src, dst_ref=dst, send_sem=leave, recv_sem=arrive, device_id=to, device_id_type=MESH)
        kept = pltpu.make_async_copy(src, dst, arrive)
        pl.when(jnp.logical_not(is_self))(copy.start)
        pl.when(is_self)(kept.start)

        def wait_send():
            pl.when(jnp.logical_not(is_self))(copy.wait_send)

        self.sent.append(types.SimpleNamespace(wait_send=wait_send))

    def sibling(self):
        return (1 - self.s, self.c, self.y)

    def finish(self):
        for copy in self.sent:
            copy.wait_send()
        self.sent = []


def wait_bytes(ref, sem):
    pltpu.make_async_copy(ref, ref, sem).wait()


class Gather8:
    def __init__(self, here, full):
        self.here, self.full = here, full
        self.own = [here.sem() for _ in range(SHARD)]
        self.other = [here.sem() for _ in range(SHARD)]

    def start(self, value):
        h = self.here
        mine = self.full.at[h.rows(h.y, h.s)]
        mine[...] = value
        h.send(mine, mine, h.sibling(), self.other[0])
        for step in (1, 3, 2):
            h.send(mine, mine, (h.s, h.c, h.shard(step)), self.own[SHARD - step])

    def relay(self, step):
        h = self.here
        part = self.full.at[h.rows(h.shard(step), h.s)]
        wait_bytes(part, self.own[step])
        h.send(part, part, h.sibling(), self.other[step])

    def wait(self, step):
        h = self.here
        wait_bytes(self.full.at[h.rows(h.shard(step), 1 - h.s)], self.other[step])


class Scatter8:
    def __init__(self, here, bufs):
        self.here = here
        self.to_core, self.mine, self.from_core, self.to_shard, self.from_shard = bufs
        self.core = [here.sem() for _ in range(SHARD)]
        self.shard = [here.sem() for _ in range(SHARD)]

    def put(self, step, block):
        h = self.here
        low, high = block[:ROWS], block[ROWS:]
        self.to_core[step] = jnp.where(h.s == 0, high, low).astype(BF16)
        self.mine[step] = jnp.where(h.s == 0, low, high)
        h.send(self.to_core.at[step], self.from_core.at[step], h.sibling(), self.core[step])

    def relay(self, step):
        h = self.here
        wait_bytes(self.from_core.at[step], self.core[step])
        self.to_shard[step] = (self.mine[step] + self.from_core[step].astype(F32)).astype(BF16)
        h.send(self.to_shard.at[step], self.from_shard.at[step], (h.s, h.c, h.shard(step)), self.shard[step])

    def result(self):
        wait_bytes(self.from_core.at[0], self.core[0])
        total = self.mine[0] + self.from_core[0].astype(F32)
        for step in (1, 3, 2):
            wait_bytes(self.from_shard.at[step], self.shard[step])
            total = total + self.from_shard[step].astype(F32)
        return total


def scatter_scratch():
    quarter = (SHARD, ROWS, D)
    return [VMEM(quarter, BF16), VMEM(quarter, F32), VMEM(quarter, BF16), VMEM(quarter, BF16), VMEM(quarter, BF16)]


ORDER = (0, 1, 3, 2)


def window_offset(group):
    return 32 * lax.rem(group, 4)


def everyone(h):
    for step in (1, 3, 2, 0):
        for other in range(2):
            yield step, other, (lax.rem(h.s + other, 2), h.c, h.shard(step))


def packed_qkv(rows, g):
    keys = rows[:, D + 128 * g : D + 128 * g + 128]
    values = rows[:, 2 * D + 128 * g : 2 * D + 128 * g + 128]
    return jnp.concatenate([
        rows[:, 128 * g : 128 * g + 128], keys[:, :64], values[:, :64], keys[:, 64:], values[:, 64:],
        rows[:, D - 64 : D], rows[:, 2 * D - 64 : 2 * D], rows[:, 3 * D - 64 : 3 * D], jnp.zeros_like(keys[:, :64])],
        axis=1)


def window(g):
    return slice(128 * (17 * g // 4), 128 * (17 * g // 4) + WINDOW)


def spread_kernel(params, w_qkv, w_up):
    def body(r):
        h = Here(r.sems)
        own = pl.ds(pl.multiple_of(h.c * 16, 16), 16)
        loads = [
            h.local(ref.at[0, rows], dst.at[pl.ds(16 * i, 16)])
            for ref, dst in ((r.w_up, r.up_rows), (r.w_qkv, r.qkv_rows)) for i, rows in enumerate((own, pl.ds(256, 16)))]
        h.barrier(whole=False)
        arrive, arrive_mid, arrive_up = h.sem(), h.sem(), h.sem()
        mine = r.params_in.at[h.s * SHARD + h.y]
        mine[...] = r.params[...]
        for step, other, to in everyone(h):
            if step or other:
                h.send(mine, mine, to, arrive)
        for copy in loads:
            copy.wait()

        @pl.when(h.s == 0)
        def _():
            for g in range(8):
                r.mid[g] = r.up_rows[:, window(g)].reshape(2, 16, WINDOW)

        @pl.when(h.s == 1)
        def _():
            for g in range(8):
                r.mid[g] = packed_qkv(r.qkv_rows[...], g).reshape(2, 16, WINDOW)
                r.up[g] = r.up_rows[:, window(g)].reshape(2, 16, WINDOW)

        up_copies = []
        for step, other, to in everyone(h):
            g = 2 * to[2] + to[0]
            for half, dst, dst_up in ((0, r.mid_piece, r.up_piece), (1, r.mid_last, r.up_last)):
                src, dst = r.mid.at[g, half], dst.at[h.s * SHARD + h.y]
                src_up, dst_up = r.up.at[g, half], dst_up.at[h.y]
                if step or other:
                    h.send(src, dst, to, arrive_mid)
                    up_copies.append(pltpu.make_async_remote_copy(
                        src_ref=src_up, dst_ref=dst_up, send_sem=h.sem(), recv_sem=arrive_up, device_id=to,
                        device_id_type=MESH))
                else:
                    pltpu.make_async_copy(src, dst, arrive_mid).start()
                    up_copies.append(pltpu.make_async_copy(src_up, dst_up, arrive_up))

        @pl.when(h.s == 1)
        def _():
            for copy in up_copies:
                copy.start()

        wait_bytes(r.params_in.at[pl.ds(0, 7)], arrive)
        for layer in range(2):
            r.norms[layer] = jnp.concatenate([r.params_in[layer * SHARD + i] for i in range(SHARD)], axis=1)
        wait_bytes(r.mid, arrive_mid)
        wait_bytes(r.up.at[pl.ds(0, SHARD)], arrive_up)

        @pl.when(h.s == 1)
        def _():
            for copy in up_copies[:-4] + up_copies[-2:]:
                copy.wait_send()

        h.finish()

    ins = dict(params=(params, VMEM), w_qkv=(w_qkv, ANY), w_up=(w_up, ANY))
    outs = dict(
        norms=(spec((2, 8, D), F32), VMEM), mid_piece=(spec((8, 16, WINDOW)), VMEM),
        mid_last=(spec((8, 16, WINDOW)), VMEM), up_piece=(spec((SHARD, 16, WINDOW)), VMEM),
        up_last=(spec((SHARD, 16, WINDOW)), VMEM))
    scratch = dict(
        params_in=VMEM((8, 8, SLICE), F32), up_rows=VMEM((32, FF), BF16), qkv_rows=VMEM((32, 3 * D), BF16),
        mid=VMEM((8, 2, 16, WINDOW), BF16), up=VMEM((8, 2, 16, WINDOW), BF16), sems=pltpu.SemaphoreType.DMA((64,)))
    return call("spread", body, ins, outs, scratch, collective_id=0)


def load_tiles(h, gathered, last, dst, first=0):
    copies = []
    for i in range(SHARD):
        copies.append(h.local(gathered.at[:, first + i], dst.at[pl.ds(17 * i, 16)]))
        copies.append(h.local(last.at[first + i], dst.at[17 * i + 16]))
    return copies


def save_tiles(h, src, sixteenths, last):
    for i in range(SHARD):
        for x in range(4):
            h.save(src.at[pl.ds(17 * i + 4 * x, 4)], sixteenths.at[x, :, i])
        h.save(src.at[17 * i + 16], last.at[i])


def whole(ref):
    return ref[...].reshape(D, WINDOW)


class FirstWeights:
    def __init__(self, h, r):
        self.h, self.r = h, r
        self.arrive = [h.sem() for _ in range(3)]

    def load(self):
        h, r = self.h, self.r
        self.rows = pltpu.make_async_copy(r.w_qkv.at[0], r.qkv_rows, h.sem())
        pl.when(h.s == 0)(self.rows.start)
        self.loads = [h.local(r.w_down.at[0], r.down_rows), h.local(r.w_out.at[0], r.out_rows)]

    def send_qkv(self):
        h, r = self.h, self.r
        self.copies = []
        for step in (1, 3, 2, 0):
            for core in range(2):
                src = r.qkv_packed.at[h.shard(step) * 2 + core]
                dst = r.qkv_vm.at[pl.ds(h.y * 17, 17)]
                if step or core:
                    self.copies.append(pltpu.make_async_remote_copy(
                        src_ref=src, dst_ref=dst, send_sem=h.sem(), recv_sem=self.arrive[0],
                        device_id=(core, h.c, h.shard(step)), device_id_type=MESH))
                else:
                    kept = pltpu.make_async_copy(src, dst, self.arrive[0])

        @pl.when(h.s == 0)
        def _():
            self.rows.wait()
            for g in range(8):
                r.qkv_packed[g] = packed_qkv(r.qkv_rows[...], g).reshape(17, 16, WINDOW)
            for copy in self.copies:
                copy.start()
            kept.start()

    def send_rest(self):
        h, r = self.h, self.r
        for copy in self.loads:
            copy.wait()
        for other in range(2):
            core = lax.rem(h.s + other, 2)
            at = pl.multiple_of(window_offset(h.y * 2 + core), 32)
            src = r.down_rows.at[pl.ds(pl.multiple_of(544 * core, 16), 544)]
            dst = r.down_vm.at[h.s, pl.ds(at, 544)]
            if other:
                h.send(src, dst, h.sibling(), self.arrive[1])
            else:
                pltpu.make_async_copy(src, dst, self.arrive[1]).start()
        self.tiles = []
        for i in range(17):
            tile = h.y * 17 + i
            group = jnp.minimum(tile // 8, 7)
            core, shard = lax.rem(group, 2), group // 2
            src = r.out_rows.at[pl.ds(16 * i, 16)]
            dst = r.out_vm.at[h.s, pl.ds(pl.multiple_of(lax.rem(tile, 8) * 16, 16), 16)]
            copy = pltpu.make_async_remote_copy(
                src_ref=src, dst_ref=dst, send_sem=h.sem(), recv_sem=self.arrive[2],
                device_id=(core, h.c, shard), device_id_type=MESH)
            same = pltpu.make_async_copy(src, dst, self.arrive[2])
            is_self = (core == h.s) & (shard == h.y)
            pl.when((tile < 64) & is_self)(same.start)
            away = (tile < 64) & jnp.logical_not(is_self)
            pl.when(away)(copy.start)
            self.tiles.append((away, copy))
        src, dst = r.out_rows.at[pl.ds(SLICE - 64, 64)], r.out_vm.at[h.s, pl.ds(128, 64)]
        same = pltpu.make_async_copy(src, dst, self.arrive[2])
        self.last = []
        for step, other, to in everyone(h):
            if step or other:
                self.last.append(pltpu.make_async_remote_copy(
                    src_ref=src, dst_ref=dst, send_sem=h.sem(), recv_sem=self.arrive[2], device_id=to,
                    device_id_type=MESH))

        @pl.when(h.y == SHARD - 1)
        def _():
            same.start()
            for copy in self.last:
                copy.start()

    def wait_qkv(self):
        wait_bytes(self.r.qkv_vm, self.arrive[0])

    def finish(self):
        r, h = self.r, self.h
        wait_bytes(r.down_vm.at[:, pl.ds(0, 544)], self.arrive[1])
        h.save(r.down_vm, r.down_w)
        wait_bytes(r.out_vm, self.arrive[2])
        h.save(r.out_vm, r.out_w)

        @pl.when(h.s == 0)
        def _():
            for copy in self.copies:
                copy.wait_send()

        for away, copy in self.tiles:
            pl.when(away)(copy.wait_send)

        @pl.when(h.y == SHARD - 1)
        def _():
            for copy in self.last:
                copy.wait_send()


def head_outs():
    return dict(
        a_full=(spec((512, D)), ANY), message_in=(spec((CTX, 160, 128)), VMEM),
        kv16_in=(spec((2, CTX, ROWS, 128)), VMEM), q16=(spec((ROWS, HEAD_DIM)), VMEM))


def head_scratch():
    return dict(message=VMEM((2, 4, 2, 160, 128), BF16), qkv_vm=VMEM(TILES, BF16), a_vm=VMEM((512, D), BF16))


def run_head(h, r, gather, a_value, after=None):
    arrive = h.sem()
    own16 = dot(a_value, r.qkv_vm[:, :, 384:].reshape(D, 256)).astype(BF16)
    r.q16[...] = own16[:, :64]
    r.kv16_in[h.s, h.c] = own16[:, 64:192]
    own_kv = r.kv16_in.at[h.s, h.c]
    leave16, arrive16, cross16 = h.sem(), h.sem(), h.sem()
    for step in range(1, CTX):
        h.send(own_kv, own_kv, (h.s, lax.rem(h.c + step, CTX), h.y), arrive16, leave16)
    for step in ORDER:
        if step:
            gather.relay(step)
        gather.wait(step)
        shard = h.shard(step)
        block = r.a_vm[pl.ds(pl.multiple_of(shard * 128, 128), 128)]
        out = dot(block, r.qkv_vm[:, :, :384].reshape(D, 384)).astype(BF16)
        for e in range(2):
            for core in range(2):
                r.message[e, shard, core, :128] = out[:, 128 + 128 * e : 256 + 128 * e]
                for b in range(2):
                    at = 32 * b + 16 * core
                    lanes = slice(64 * e, 64 * e + 64)
                    packed = jnp.concatenate([out[at : at + 16, lanes], out[64 + at : 80 + at, lanes]], axis=1)
                    r.message[e, shard, core, 128 + 16 * b : 144 + 16 * b] = packed
                chip = 8 * h.s + 4 * e + shard
                h.send_or_keep(
                    r.message.at[e, shard, core], r.message_in.at[h.c], (core, chip, h.y),
                    (chip == h.c) & (h.s == core), arrive)
    h.save(r.a_vm, r.a_full)
    if after is not None:
        after()
    wait_bytes(r.kv16_in.at[h.s, pl.ds(0, CTX - 1)], arrive16)
    cross = r.kv16_in.at[h.s]
    h.send(cross, cross, h.sibling(), cross16)
    wait_bytes(r.kv16_in.at[h.s, pl.ds(0, CTX - 1)], leave16)
    wait_bytes(r.kv16_in.at[1 - h.s], cross16)
    wait_bytes(r.message_in, arrive)


def first_kernel(hidden, norms, w_qkv, w_out, w_down):
    def body(r):
        h = Here(r.sems)
        weights = FirstWeights(h, r)
        weights.load()
        r.down_vm[...] = jnp.zeros_like(r.down_vm)
        h.barrier()
        weights.send_qkv()
        x = r.hidden[h.s].astype(F32)
        a_value = layer_norm(x, r.norms[0, 0:1], r.norms[0, 2:3]).astype(BF16)
        gather = Gather8(h, r.a_vm)
        gather.start(a_value)
        weights.wait_qkv()
        h.save(r.qkv_vm, r.qkv_w)
        run_head(h, r, gather, a_value, weights.send_rest)
        weights.finish()
        h.finish()

    ins = dict(hidden=(hidden, VMEM), norms=(norms, VMEM), w_qkv=(w_qkv, ANY), w_out=(w_out, ANY), w_down=(w_down, ANY))
    outs = dict(
        **head_outs(), qkv_w=(spec(TILES), ANY), out_w=(spec((2, 192, D)), ANY), down_w=(spec((2, WINDOW, D)), ANY))
    scratch = dict(
        **head_scratch(), qkv_rows=VMEM((SLICE, 3 * D), BF16), qkv_packed=VMEM((8, 17, 16, WINDOW), BF16),
        down_rows=VMEM((D, D), BF16), out_rows=VMEM((SLICE, D), BF16), down_vm=VMEM((2, WINDOW, D), BF16),
        out_vm=VMEM((2, 192, D), BF16), sems=pltpu.SemaphoreType.DMA((200,)))
    return call("first", body, ins, outs, scratch, collective_id=1)


def attend(block_order, positions, own_positions, message_in, kv16_in, q16):
    def body(r):
        half = lax.axis_index(SECTION)
        for c in range(CTX):
            for m in range(2):
                for b in range(2):
                    block = 32 * m + r.order[m, 2 * c + b]
                    rows = r.message_in[c, 64 * m + 32 * b : 64 * m + 32 * b + 32, :]
                    at = pl.ds(pl.multiple_of(block * 32, 32), 32)
                    r.keys[at] = rows[:, :64]
                    r.values[at] = rows[:, 64:]
                    at = pl.ds(pl.multiple_of(block * 16, 16), 16)
                    r.queries[at] = r.message_in[c, 128 + 16 * b : 144 + 16 * b, 64 * m : 64 * m + 64] * 0.125
        row = lax.broadcasted_iota(jnp.int32, (256, 512), 0)
        row = 32 * (row // 16) + 16 * half + row % 16
        visible = row >= lax.broadcasted_iota(jnp.int32, (256, 512), 1)
        for t in range(4):
            query = r.queries[256 * t : 256 * t + 256]
            parts = [dot_nt(query, r.keys[512 * u : 512 * u + 512]) for u in range(t + 1)]
            parts[t] = jnp.where(visible, parts[t], NEG_LARGE)
            top = parts[0]
            for p in parts[1:]:
                top = jnp.maximum(top, p)
            top = jnp.max(top, axis=-1, keepdims=True)
            parts = [jnp.exp(p - top) for p in parts]
            total = parts[0]
            for p in parts[1:]:
                total = total + p
            total = jnp.sum(total, axis=-1, keepdims=True)
            out = dot(parts[0].astype(BF16), r.values[:512])
            for u in range(1, t + 1):
                out = out + dot(parts[u].astype(BF16), r.values[512 * u : 512 * u + 512])
            r.sorted_out[256 * t : 256 * t + 256] = (out / total).astype(BF16)
            r.logs[256 * t : 256 * t + 256] = jnp.broadcast_to(top + jnp.log(total), (256, 128))
        for c in range(CTX):
            for m in range(2):
                for b in range(2):
                    at = pl.multiple_of((32 * m + r.order[m, 2 * c + b]) * 16, 16)
                    r.out[c, 16 * b : 16 * b + 16, 64 * m : 64 * m + 64] = r.sorted_out[pl.ds(at, 16)]
        kv = r.kv16_in[...].reshape(SEQ, 128)
        scores = dot_nt(r.q16[...] * 0.125, kv[:, :64])
        scores = jnp.where(r.own_positions[...] >= r.positions[...], scores, NEG_LARGE)
        top = jnp.max(scores, axis=-1, keepdims=True)
        scores = jnp.exp(scores - top)
        total = jnp.sum(scores, axis=-1, keepdims=True)
        out = dot(scores.astype(BF16), kv[:, 64:])
        r.out16[...] = (out / total).astype(BF16)
        r.logs16[...] = jnp.broadcast_to(top + jnp.log(total), (ROWS, 128))

    ins = dict(
        order=(block_order, pltpu.SMEM), positions=(positions, VMEM), own_positions=(own_positions, VMEM),
        message_in=(message_in, VMEM), kv16_in=(kv16_in, VMEM), q16=(q16, VMEM),)
    outs = dict(
        out=(spec((CTX, 32, 128)), VMEM), out16=(spec((ROWS, 64)), VMEM),
        sorted_out=(spec((1024, 64)), VMEM), logs=(spec((1024, 128), F32), VMEM),
        logs16=(spec((ROWS, 128), F32), VMEM),)
    scratch = dict(
        keys=VMEM((SEQ, 64), BF16), values=VMEM((SEQ, 64), BF16), queries=VMEM((1024, 64), BF16),)
    return call("attend", body, ins, outs, scratch)


def middle_scratch():
    return dict(
        context_in=VMEM((2, 4, 2, 32, 128), BF16), out_vm=VMEM((192, D), BF16), up_vm=VMEM(TILES, BF16),
        down_vm=VMEM((WINDOW, D), BF16), to_out=scatter_scratch(), to_down=scatter_scratch())


def load_layer(h, r, layer, first):
    loads = [h.local(r.out_w.at[layer], r.out_vm), h.local(r.down_w.at[layer], r.down_vm)]
    return loads + load_tiles(h, r.up_all, r.up_last, r.up_vm, first)


def gather_context(h, r):
    arrive = h.sem()
    to_core = h.c // 8
    e, j = lax.rem(h.c // 4, 2), lax.rem(h.c, 4)
    for c in range(CTX):
        h.send_or_keep(
            r.attended.at[c], r.context_in.at[e, j, h.s], (to_core, c, h.y), (h.c == c) & (h.s == to_core), arrive)
    return arrive


def unpack_context(r, store):
    for j in range(4):
        for m in range(2):
            for b in range(2):
                for core in range(2):
                    lanes = slice(64 * m, 64 * m + 64)
                    piece = jnp.concatenate(
                        [r.context_in[e, j, core, 16 * b : 16 * b + 16, lanes] for e in range(2)], axis=1)
                    at = 128 * j + 64 * m + 32 * b + 16 * core
                    store[at : at + 16] = piece


def block_rows(h, step):
    return pl.ds(pl.multiple_of(h.shard(step) * 128, 128), 128)


def run_out(h, r, x):
    sums = Scatter8(h, r.to_out)
    for step in (2, 1, 3, 0):
        sums.put(step, dot(r.context[block_rows(h, step)], r.out_vm[:128]))
    for step in (2, 1, 3):
        sums.relay(step)
    own = x + dot(r.attended16[...], r.out_vm[128:])
    return own + sums.result()


def middle_kernel(attended, attended16, x, norms, first, mid_all, mid_last):
    def body(r):
        h = Here(r.sems)
        loads = load_layer(h, r, 0, 0)
        head_loads = load_tiles(h, r.up_all, r.up_last, r.qkv_vm, SHARD)
        h.barrier()
        arrive = gather_context(h, r)
        for copy in loads:
            copy.wait()
        wait_bytes(r.context_in, arrive)
        unpack_context(r, r.context)
        residual = run_out(h, r, r.x[h.s].astype(F32))
        r.residual[...] = residual
        b_value = layer_norm(residual, r.norms[0, 1:2], r.norms[0, 3:4]).astype(BF16)
        gather = Gather8(h, r.b_vm)
        gather.start(b_value)
        sums = Scatter8(h, r.to_down)
        for step in ORDER:
            if step:
                gather.relay(step)
            gather.wait(step)
            rows = block_rows(h, step)
            u = dot(r.b_vm[rows], whole(r.up_vm))
            r.pre_vm[rows] = u
            sums.put(step, dot(gelu(u).astype(BF16), r.down_vm[...]))
        for step in (1, 3, 2):
            sums.relay(step)
        h.save(r.b_vm, r.b_full)
        h.save(r.pre_vm, r.pre)
        for copy in head_loads:
            copy.wait()
        y = (residual + sums.result()).astype(BF16)
        r.y[...] = y
        a_value = layer_norm(y.astype(F32), r.norms[1, 0:1], r.norms[1, 2:3]).astype(BF16)
        gather = Gather8(h, r.a_vm)
        gather.start(a_value)
        run_head(h, r, gather, a_value)
        h.finish()

    ins = dict(
        attended=(attended, VMEM), attended16=(attended16, VMEM), x=(x, VMEM), norms=(norms, VMEM),
        out_w=(first.out_w, ANY), down_w=(first.down_w, ANY), up_all=(mid_all, ANY), up_last=(mid_last, ANY))
    outs = dict(
        context=(spec((512, 128)), VMEM), residual=(spec((ROWS, D), F32), VMEM), b_full=(spec((512, D)), ANY),
        pre=(spec((512, WINDOW), F32), ANY), y=(spec((ROWS, D)), VMEM), **head_outs())
    scratch = dict(
        **middle_scratch(), **head_scratch(), b_vm=VMEM((512, D), BF16), pre_vm=VMEM((512, WINDOW), F32),
        sems=pltpu.SemaphoreType.DMA((200,)))
    return call("middle", body, ins, outs, scratch, collective_id=2)


def gelu_slope(u):
    t = jnp.tanh(0.7978845608028654 * (u + 0.044715 * u * u * u))
    return 0.5 * (1.0 + t) + 0.5 * u * (1.0 - t * t) * 0.7978845608028654 * (1.0 + 0.134145 * u * u)


def norm_back(grad, values, gain):
    normed, rate = norm_parts(values)
    scaled = grad * gain
    mean = jnp.mean(scaled, axis=-1, keepdims=True)
    along = jnp.mean(scaled * normed, axis=-1, keepdims=True)
    back = rate * (scaled - mean - normed * along)
    return back, grad * normed


def columns(at, gain_rows, bias_rows):
    lane = lax.broadcasted_iota(jnp.int32, (ROWS, 64), 1)

    def into(rows, column):
        return lax.dot_general(
            rows, (lane == column).astype(F32), (((0,), (0,)), ((), ())), precision=lax.Precision.HIGHEST,
            preferred_element_type=F32)

    return into(gain_rows, at) + into(bias_rows, at + 1)


def back_outs():
    return dict(
        mid_grad=(spec((ROWS, D), F32), VMEM), context_grad_in=(spec((CTX, 32, 128)), VMEM),
        context16_grad=(spec((ROWS, HEAD_DIM)), VMEM), up_g=(spec((4, 4, SHARD, 16, WINDOW)), ANY),
        up_g_last=(spec((SHARD, 16, WINDOW)), ANY), down_g=(spec((544, D)), ANY), out_g=(spec((192, D)), VMEM),
        norm2_g=(spec((68, 16, 64)), VMEM))


def back_scratch():
    return dict(
        m_full=VMEM((512, D), BF16), z_full=VMEM((512, D), BF16), hidden_low=VMEM((512, WINDOW), BF16),
        pre_grad=VMEM((512, WINDOW), BF16), context_message=VMEM((2, 4, 2, 32, 128), BF16), up_grad=VMEM(TILES, BF16),
        down_grad=VMEM((WINDOW, D), BF16), b_vm=VMEM((512, D), BF16), to_norm2=scatter_scratch())


def back_block(h, r, rows, sums, step, u, g):
    r.hidden_low[rows] = g
    hidden_grad = dot_nt(r.m_full[rows], r.down_vm[...])
    pre_grad = (hidden_grad * gelu_slope(u)).astype(BF16)
    r.pre_grad[rows] = pre_grad
    sums.put(step, dot_nt(pre_grad, whole(r.up_vm)))


def finish_back(h, r, sums, layer, residual, out_grad, context, beside=None):
    r.down_grad[...] = dot_tn(r.hidden_low[...], r.m_full[...]).astype(BF16)
    offset = pl.multiple_of(window_offset(h.y * 2 + h.s), 32)
    h.save(r.down_grad.at[pl.ds(offset, 544)], r.down_g)
    r.up_grad[...] = dot_tn(r.b_vm[...], r.pre_grad[...]).astype(BF16).reshape(TILES)
    save_tiles(h, r.up_grad, r.up_g, r.up_g_last)
    normed_grad = sums.result()
    back, gain_rows = norm_back(normed_grad, residual, r.norms[layer, 1:2])
    mid_grad = out_grad + back
    r.mid_grad[...] = mid_grad
    z = mid_grad.astype(BF16)
    gather = Gather8(h, r.z_full)
    gather.start(z)
    r.norm2_g[...] = columns(2, gain_rows, normed_grad).astype(BF16).reshape(68, 16, 64)
    if beside is not None:
        beside()
    arrive = h.sem()
    r.context16_grad[...] = dot_nt(z, r.out_vm[128:]).astype(BF16)
    for step in ORDER:
        if step:
            gather.relay(step)
        gather.wait(step)
        shard = h.shard(step)
        out = dot_nt(r.z_full[block_rows(h, step)], r.out_vm[:128]).astype(BF16)
        for e in range(2):
            for core in range(2):
                lanes = slice(64 * e, 64 * e + 64)
                for b in range(2):
                    at = 32 * b + 16 * core
                    r.context_message[e, shard, core, 16 * b : 16 * b + 16] = jnp.concatenate(
                        [out[at : at + 16, lanes], out[64 + at : 80 + at, lanes]], axis=1)
                chip = 8 * h.s + 4 * e + shard
                h.send_or_keep(
                    r.context_message.at[e, shard, core], r.context_grad_in.at[h.c], (core, chip, h.y),
                    (chip == h.c) & (h.s == core), arrive)
    r.out_g[:128] = dot_tn(context[...], r.z_full[...]).astype(BF16)
    r.out_g[128:] = dot_tn(r.attended16[...], z).astype(BF16)
    wait_bytes(r.context_grad_in, arrive)


def turn_kernel(attended, attended16, x, norms, first, up_all, up_last, cotangent):
    def body(r):
        h = Here(r.sems)
        loads = load_layer(h, r, 1, 0)
        h.barrier()
        arrive = gather_context(h, r)
        out_grad = r.cotangent[h.s]
        gather_m = Gather8(h, r.m_full)
        gather_m.start(out_grad)
        for copy in loads:
            copy.wait()
        wait_bytes(r.context_in, arrive)
        unpack_context(r, r.context)
        residual = run_out(h, r, r.x[...].astype(F32))
        b_value = layer_norm(residual, r.norms[1, 1:2], r.norms[1, 3:4]).astype(BF16)
        gather = Gather8(h, r.b_vm)
        gather.start(b_value)
        back_sums, sums = Scatter8(h, r.to_norm2), Scatter8(h, r.to_down)
        for step in ORDER:
            if step:
                gather_m.relay(step)
                gather.relay(step)
            gather_m.wait(step)
            gather.wait(step)
            rows = block_rows(h, step)
            u = dot(r.b_vm[rows], whole(r.up_vm))
            g = gelu(u).astype(BF16)
            back_block(h, r, rows, back_sums, step, u, g)
            sums.put(step, dot(g, r.down_vm[...]))
        for step in (1, 3, 2):
            back_sums.relay(step)
        for step in (1, 3, 2):
            sums.relay(step)

        def beside():
            r.out[...] = (residual + sums.result()).astype(BF16)

        finish_back(h, r, back_sums, 1, residual, out_grad.astype(F32), r.context, beside)
        h.finish()

    ins = dict(
        attended=(attended, VMEM), attended16=(attended16, VMEM), x=(x, VMEM), norms=(norms, VMEM),
        out_w=(first.out_w, ANY), down_w=(first.down_w, ANY), up_all=(up_all, ANY), up_last=(up_last, ANY),
        cotangent=(cotangent, VMEM))
    outs = dict(out=(spec((ROWS, D)), VMEM), **back_outs())
    scratch = dict(
        context=VMEM((512, 128), BF16), **middle_scratch(), **back_scratch(), sems=pltpu.SemaphoreType.DMA((200,)))
    return call("turn", body, ins, outs, scratch, collective_id=3)


def attend_back(block_order, positions, own_positions, message_in, kv16_in, q16, saved, grad_in, grad16):
    def body(r):
        half = lax.axis_index(SECTION)
        for c in range(CTX):
            for m in range(2):
                for b in range(2):
                    block = 32 * m + r.order[m, 2 * c + b]
                    rows = r.message_in[c, 64 * m + 32 * b : 64 * m + 32 * b + 32, :]
                    at = pl.ds(pl.multiple_of(block * 32, 32), 32)
                    r.keys[at] = rows[:, :64]
                    r.values[at] = rows[:, 64:]
                    at = pl.ds(pl.multiple_of(block * 16, 16), 16)
                    r.queries[at] = r.message_in[c, 128 + 16 * b : 144 + 16 * b, 64 * m : 64 * m + 64] * 0.125
                    r.grads[at] = r.grad_in[c, 16 * b : 16 * b + 16, 64 * m : 64 * m + 64]
        r.key_grads[...] = jnp.zeros_like(r.key_grads)
        r.value_grads[...] = jnp.zeros_like(r.value_grads)
        column = lax.broadcasted_iota(jnp.int32, (512, 256), 1)
        column = 32 * (column // 16) + 16 * half + column % 16
        visible = column >= lax.broadcasted_iota(jnp.int32, (512, 256), 0)
        ones = jnp.ones((8, 64), F32)

        def row_of(grads, outs):
            product = grads.astype(F32) * outs.astype(F32)
            return lax.dot_general(
                ones, product, (((1,), (1,)), ((), ())), precision=lax.Precision.HIGHEST,
                preferred_element_type=F32)[0:1]

        for t in range(4):
            part = slice(256 * t, 256 * t + 256)
            query, grad = r.queries[part], r.grads[part]
            logs = jnp.transpose(r.logs[part])[0:1]
            delta = row_of(grad, r.sorted_out[part])
            query_grad = jnp.zeros((256, 64), F32)
            for u in range(t + 1):
                chunk = slice(512 * u, 512 * u + 512)
                keys = r.keys[chunk]
                scores = dot_nt(keys, query)
                if u == t:
                    scores = jnp.where(visible, scores, NEG_LARGE)
                probs = jnp.exp(scores - logs)
                probs_grad = dot_nt(r.values[chunk], grad)
                scores_grad = (probs * (probs_grad - delta)).astype(BF16)
                r.value_grads[chunk] += dot(probs.astype(BF16), grad)
                r.key_grads[chunk] += dot(scores_grad, query)
                query_grad = query_grad + dot_tn(scores_grad, keys)
            r.query_grads[part] = (query_grad * 0.125).astype(BF16)
        for c in range(CTX):
            for m in range(2):
                for b in range(2):
                    block = 32 * m + r.order[m, 2 * c + b]
                    at = pl.ds(pl.multiple_of(block * 32, 32), 32)
                    r.message[c, 64 * m + 32 * b : 64 * m + 32 * b + 32, :] = jnp.concatenate(
                        [r.key_grads[at], r.value_grads[at]], axis=1).astype(BF16)
                    at = pl.ds(pl.multiple_of(block * 16, 16), 16)
                    r.message[c, 128 + 16 * b : 144 + 16 * b, 64 * m : 64 * m + 64] = r.query_grads[at]
        kv = r.kv16_in[...].reshape(SEQ, 128)
        query, grad = r.q16[...] * 0.125, r.grad16[...]
        scores = dot_nt(kv[:, :64], query)
        scores = jnp.where(r.own_positions[...] >= r.positions[...], scores, NEG_LARGE)
        probs = jnp.exp(scores - jnp.transpose(r.logs16[...])[0:1])
        probs_grad = dot_nt(kv[:, 64:], grad)
        scores_grad = (probs * (probs_grad - row_of(grad, r.out16[...]))).astype(BF16)
        both = jnp.concatenate([dot(scores_grad, query), dot(probs.astype(BF16), grad)], axis=1)
        r.kv16_grad[...] = both.astype(BF16).reshape(2, CTX, ROWS, 128)
        r.q16_grad[...] = (dot_tn(scores_grad, kv[:, :64]) * 0.125).astype(BF16)

    ins = dict(
        order=(block_order, pltpu.SMEM), positions=(positions, VMEM), own_positions=(own_positions, VMEM),
        message_in=(message_in, VMEM), kv16_in=(kv16_in, VMEM), q16=(q16, VMEM),
        sorted_out=(saved.sorted_out, VMEM), logs=(saved.logs, VMEM), logs16=(saved.logs16, VMEM),
        out16=(saved.out16, VMEM), grad_in=(grad_in, VMEM), grad16=(grad16, VMEM),)
    outs = dict(
        message=(spec((CTX, 160, 128)), VMEM), kv16_grad=(spec((2, CTX, ROWS, 128)), VMEM),
        q16_grad=(spec((ROWS, 64)), VMEM),)
    scratch = dict(
        keys=VMEM((SEQ, 64), BF16), values=VMEM((SEQ, 64), BF16), queries=VMEM((1024, 64), BF16),
        grads=VMEM((1024, 64), BF16), query_grads=VMEM((1024, 64), BF16),
        key_grads=VMEM((SEQ, 64), F32), value_grads=VMEM((SEQ, 64), F32),)
    return call("attend_back", body, ins, outs, scratch)


def tail_ins(back, a_full, x, above, norms):
    return dict(
        message=(back.message, VMEM), kv16_grad=(back.kv16_grad, VMEM), q16_grad=(back.q16_grad, VMEM),
        a_full=(a_full, ANY), x=(x, VMEM), mid_in=(above.mid_grad, VMEM), norms=(norms, VMEM),
        norm2_in=(above.norm2_g, VMEM))


def tail_outs():
    return dict(
        in_grad=(spec((ROWS, D)), VMEM), qkv_g=(spec((4, 4, SHARD, 16, WINDOW)), ANY),
        qkv_g_last=(spec((SHARD, 16, WINDOW)), ANY))


def tail_scratch():
    return dict(
        message_in=VMEM((2, 4, 2, 160, 128), BF16), core16=VMEM((CTX, ROWS, 128), BF16),
        sum16=VMEM((CTX, ROWS, 128), BF16), own16=VMEM((CTX, ROWS, 128), BF16), qkv_grads=VMEM((512, 384), BF16),
        qkv_vm=VMEM(TILES, BF16), qkv_grad=VMEM(TILES, BF16), a_vm=VMEM((512, D), BF16), to_norm1=scatter_scratch())


def start_tail(h, r):
    cross = h.sem()
    h.send(r.kv16_grad.at[1 - h.s], r.core16, h.sibling(), cross)
    arrive = h.sem()
    to_core = h.c // 8
    e, j = lax.rem(h.c // 4, 2), lax.rem(h.c, 4)
    for c in range(CTX):
        h.send_or_keep(
            r.message.at[c], r.message_in.at[e, j, h.s], (to_core, c, h.y), (h.c == c) & (h.s == to_core), arrive)
    wait_bytes(r.core16, cross)
    r.sum16[...] = (r.kv16_grad[h.s].astype(F32) + r.core16[...].astype(F32)).astype(BF16)
    leave16, arrive16 = h.sem(), h.sem()
    for step in range(1, CTX):
        to = lax.rem(h.c + step, CTX)
        h.send(r.sum16.at[to], r.own16.at[step], (h.s, to, h.y), arrive16, leave16)
    return arrive, leave16, arrive16


def run_tail(h, r, layer, x, waits, loads, beside=()):
    arrive, leave16, arrive16 = waits
    for copy in loads:
        copy.wait()
    weights = whole(r.qkv_vm)
    wait_bytes(r.message_in, arrive)
    for j in range(4):
        for e in range(2):
            both = r.message_in[e, j, 0, :128].astype(F32) + r.message_in[e, j, 1, :128].astype(F32)
            r.qkv_grads[128 * j : 128 * j + 128, 128 + 128 * e : 256 + 128 * e] = both.astype(BF16)
        for m in range(2):
            for b in range(2):
                for core in range(2):
                    lanes = slice(64 * m, 64 * m + 64)
                    piece = jnp.concatenate(
                        [r.message_in[e, j, core, 128 + 16 * b : 144 + 16 * b, lanes] for e in range(2)], axis=1)
                    at = 128 * j + 64 * m + 32 * b + 16 * core
                    r.qkv_grads[at : at + 16, :128] = piece
    sums = Scatter8(h, r.to_norm1)
    for step in (2, 1, 3, 0):
        sums.put(step, dot_nt(r.qkv_grads[block_rows(h, step)], weights[:, :384]))
    for step in (2, 1, 3):
        sums.relay(step)
    for each in beside:
        each()
    wait_bytes(r.own16.at[pl.ds(1, CTX - 1)], arrive16)
    wait_bytes(r.own16.at[pl.ds(1, CTX - 1)], leave16)
    kv16 = r.sum16[h.c].astype(F32)
    for step in range(1, CTX):
        kv16 = kv16 + r.own16[step].astype(F32)
    grads16 = jnp.concatenate([r.q16_grad[...], kv16.astype(BF16)], axis=1)
    own = dot_nt(grads16, weights[:, 384:576])
    r.qkv_grad[:, :, :384] = dot_tn(r.a_vm[...], r.qkv_grads[...]).astype(BF16).reshape(68, 16, 384)
    own_grad = dot_tn(r.a_vm[h.rows(h.y, h.s)], grads16)
    normed_grad = own + sums.result()
    back, gain_rows = norm_back(normed_grad, x, r.norms[layer, 0:1])
    in_grad = (r.mid_in[...] + back).astype(BF16)
    r.in_grad[...] = in_grad

    def finish():
        sums_of_rows = columns(0, gain_rows, normed_grad) + r.norm2_in[...].reshape(D, 64).astype(F32)
        r.qkv_grad[:, :, 384:] = jnp.concatenate([own_grad, sums_of_rows], axis=1).astype(BF16).reshape(68, 16, 256)
        save_tiles(h, r.qkv_grad, r.qkv_g, r.qkv_g_last)

    return in_grad, finish


def back_kernel(back, a_full, x, above, norms, first, middle, attended16, mid_all, mid_last):
    def body(r):
        h = Here(r.sems)
        tail_loads = load_tiles(h, r.up_all, r.up_last, r.qkv_vm, SHARD)
        tail_loads.append(h.local(r.a_full, r.a_vm))
        loads = load_layer(h, r, 0, 0)
        loads += [h.local(r.b_full, r.b_vm), h.local(r.pre, r.pre_vm), h.local(r.context, r.context_vm)]
        h.barrier()
        waits = start_tail(h, r)
        out_grad, finish = run_tail(h, r, 1, r.x[...].astype(F32), waits, tail_loads)
        gather = Gather8(h, r.m_full)
        gather.start(out_grad)
        finish()
        for copy in loads:
            copy.wait()
        sums = Scatter8(h, r.to_norm2)
        for step in ORDER:
            if step:
                gather.relay(step)
            gather.wait(step)
            rows = block_rows(h, step)
            u = r.pre_vm[rows]
            back_block(h, r, rows, sums, step, u, gelu(u).astype(BF16))
        for step in (1, 3, 2):
            sums.relay(step)
        finish_back(h, r, sums, 0, r.residual[...], out_grad.astype(F32), r.context_vm)
        h.finish()

    ins = dict(
        **tail_ins(back, a_full, x, above, norms), pre=(middle.pre, ANY), b_full=(middle.b_full, ANY),
        context=(middle.context, ANY), residual=(middle.residual, VMEM), attended16=(attended16, VMEM),
        out_w=(first.out_w, ANY), down_w=(first.down_w, ANY), up_all=(mid_all, ANY), up_last=(mid_last, ANY))
    outs = dict(**tail_outs(), **back_outs())
    scratch = dict(
        out_vm=VMEM((192, D), BF16), up_vm=VMEM(TILES, BF16), down_vm=VMEM((WINDOW, D), BF16),
        pre_vm=VMEM((512, WINDOW), F32), context_vm=VMEM((512, 128), BF16), **tail_scratch(), **back_scratch(),
        sems=pltpu.SemaphoreType.DMA((240,)))
    return call("back", body, ins, outs, scratch, collective_id=4)


class Reduce16:
    def __init__(self, h, part, bufs, x_first):
        self.h, self.part, self.x_first = h, part, x_first
        self.first_in, self.mine, self.second_in = bufs
        self.x, self.z = h.c // 4, lax.rem(h.c, 4)
        self.first = [h.sem() for _ in range(3)]
        self.second = [h.sem() for _ in range(3)]

    def chip(self, x, z):
        return (self.h.s, 4 * lax.rem(x, 4) + lax.rem(z, 4), self.h.y)

    def start(self):
        for j in (1, 3, 2):
            if self.x_first:
                src, to = self.part.at[lax.rem(self.x + j, 4)], self.chip(self.x + j, self.z)
            else:
                src, to = self.part.at[:, lax.rem(self.z + j, 4)], self.chip(self.x, self.z + j)
            self.h.send(src, self.first_in.at[j - 1], to, self.first[j - 1])

    def middle(self):
        for j in range(3):
            wait_bytes(self.first_in.at[j], self.first[j])
        for k in range(4):
            own = self.part[self.x, k] if self.x_first else self.part[k, self.z]
            total = own.astype(F32)
            for j in range(3):
                total = total + self.first_in[j, k].astype(F32)
            self.mine[k] = total.astype(BF16)
        for j in (1, 3, 2):
            if self.x_first:
                src, to = self.mine.at[lax.rem(self.z + j, 4)], self.chip(self.x, self.z + j)
            else:
                src, to = self.mine.at[lax.rem(self.x + j, 4)], self.chip(self.x + j, self.z)
            self.h.send(src, self.second_in.at[j - 1], to, self.second[j - 1])

    def result(self):
        total = self.mine[self.z if self.x_first else self.x].astype(F32)
        for j in range(3):
            wait_bytes(self.second_in.at[j], self.second[j])
            total = total + self.second_in[j].astype(F32)
        return total.astype(BF16)


def reduce_scratch(units):
    return [VMEM((3, 4, units, 16, WINDOW), BF16), VMEM((4, units, 16, WINDOW), BF16), VMEM((3, units, 16, WINDOW), BF16)]


class Spread16:
    def __init__(self, h, parts, x_first):
        self.h, self.parts, self.x_first = h, parts, x_first
        self.x, self.z = h.c // 4, lax.rem(h.c, 4)
        self.first = [h.sem() for _ in range(3)]
        self.second = [h.sem() for _ in range(3)]

    def chip(self, x, z):
        return (self.h.s, 4 * lax.rem(x, 4) + lax.rem(z, 4), self.h.y)

    def start(self):
        own = self.parts.at[self.x, self.z]
        for j in (1, 3, 2):
            to = self.chip(self.x + j, self.z) if self.x_first else self.chip(self.x, self.z + j)
            self.h.send(own, own, to, self.first[j - 1])

    def middle(self):
        for j in range(3):
            wait_bytes(self.parts.at[0, 0], self.first[j])
        for j in (1, 3, 2):
            if self.x_first:
                line, to = self.parts.at[:, self.z], self.chip(self.x, self.z + j)
            else:
                line, to = self.parts.at[self.x], self.chip(self.x + j, self.z)
            self.h.send(line, line, to, self.second[j - 1])

    def finish(self):
        for j in range(3):
            wait_bytes(self.parts.at[0], self.second[j])


def last_kernel(back, a_full, hidden, above, norms, qkv_w):
    def body(r):
        h = Here(r.sems)
        part_loads = [h.local(r.up_g, r.up_part), h.local(r.qkv_g_above, r.qkv_part)]
        loads = [h.local(r.qkv_w, r.qkv_vm), h.local(r.a_full, r.a_vm)]
        h.barrier()
        waits = start_tail(h, r)
        for copy in part_loads:
            copy.wait()
        up = Reduce16(h, r.up_part, r.up_sums, True)
        qkv = Reduce16(h, r.qkv_part, r.qkv_sums, False)
        up.start()
        qkv.start()
        in_grad, finish = run_tail(h, r, 0, r.x[h.s].astype(F32), waits, loads, (up.middle, qkv.middle))
        finish()
        r.up_piece[...] = up.result()
        r.qkv_piece[...] = qkv.result()
        h.finish()

    parts = VMEM((4, 4, SHARD, 16, WINDOW), BF16)
    scratch = dict(
        **tail_scratch(), up_part=parts, qkv_part=parts, up_sums=reduce_scratch(SHARD),
        qkv_sums=reduce_scratch(SHARD), sems=pltpu.SemaphoreType.DMA((200,)))
    ins = dict(
        **tail_ins(back, a_full, hidden, above, norms), qkv_w=(qkv_w, ANY), up_g=(above.up_g, ANY),
        qkv_g_above=(above.qkv_g, ANY))
    piece = (spec((SHARD, 16, WINDOW)), VMEM)
    outs = dict(**tail_outs(), up_piece=piece, qkv_piece=piece)
    return call("last", body, ins, outs, scratch, collective_id=5)


def share_kernel(qkv0, qkv0_last, up0_piece, up0_last, up1, up1_last, qkv1_piece, qkv1_last):
    def body(r):
        h = Here(r.sems)
        x, z = h.c // 4, lax.rem(h.c, 4)
        group = 2 * h.y + h.s
        loads = [h.local(r.qkv0.at[:, :, pl.ds(2 * i, 2)], r.part.at[i]) for i in range(2)]
        up1_load = h.local(r.up1.at[x, z], r.up1_vm)
        h.barrier()
        for copy in loads:
            copy.wait()
        sums = [Reduce16(h, r.part.at[i], (r.sums_a, r.sums_b)[i], i == 0) for i in range(2)]
        for each in sums:
            each.start()
        arrive_last = h.sem()
        for i in range(SHARD):
            r.last_message[i, 0] = r.up0_last[i]
            r.last_message[i, 1] = r.qkv0_last[i]
            r.last_message[i, 2] = r.qkv1_last[i]
            chip = 4 * i + h.y
            h.send_or_keep(r.last_message.at[i], r.last_in.at[h.c], (h.s, chip, h.y), chip == h.c, arrive_last)
        up1_load.wait()
        arrive_up = h.sem()
        for layer, piece in ((0, r.up0_piece), (1, r.up1_vm)):
            for step in (1, 3, 2, 0):
                shard = h.shard(step)
                h.send_or_keep(
                    piece.at[shard], r.up_in.at[group], (layer, h.c, shard), (h.s == layer) & (step == 0), arrive_up)
        wait_bytes(r.up_in, arrive_up)
        spreads = []
        for i, parts in enumerate((r.up_low, r.up_high)):
            parts[x, z] = r.up_in[4 * i : 4 * i + 4]
            spreads.append(Spread16(h, parts, i == 0))
            spreads[i].start()
        for each in sums:
            each.middle()
        for i in range(2):
            r.qkv0_piece[2 * i : 2 * i + 2] = sums[i].result()
        arrive_qkv = h.sem()
        for layer, piece in ((0, r.qkv0_piece), (1, r.qkv1_piece)):
            for step in (1, 3, 2, 0):
                shard = h.shard(step)
                h.send_or_keep(
                    piece.at[shard], r.qkv_in.at[group], (layer, h.c, shard), (h.s == layer) & (step == 0), arrive_qkv)
        for each in spreads:
            each.middle()
        arrive_rest = h.sem()
        reduces = z == h.y

        @pl.when(reduces)
        def _():
            wait_bytes(r.last_in, arrive_last)
            total = r.last_in[0].astype(F32)
            for c in range(1, CTX):
                total = total + r.last_in[c].astype(F32)
            total = total.astype(BF16)
            r.rest_message[0] = total[:2]
            r.rest_message[1, 0] = r.up1_last[x]
            r.rest_message[1, 1] = total[2]

        rest = []
        for layer in range(2):
            leave = h.sem()
            src, dst = r.rest_message.at[layer], r.rest.at[z, h.s]
            copy = pltpu.make_async_remote_copy(
                src_ref=src, dst_ref=dst, send_sem=leave, recv_sem=arrive_rest, device_id=(layer, h.c, x),
                device_id_type=MESH)
            kept = pltpu.make_async_copy(src, dst, arrive_rest)
            is_self = (h.s == layer) & (x == h.y)
            pl.when(reduces & is_self)(kept.start)
            away = reduces & jnp.logical_not(is_self)
            pl.when(away)(copy.start)
            rest.append((away, copy))
        wait_bytes(r.qkv_in, arrive_qkv)
        for i, parts in enumerate((r.qkv_low, r.qkv_high)):
            parts[x, z] = r.qkv_in[4 * i : 4 * i + 4, :, :384]
            spreads.append(Spread16(h, parts, i == 0))
            spreads[2 + i].start()
        own = r.qkv_in[0, :, 384:].astype(F32)
        for g in range(1, 8):
            own = own + r.qkv_in[g, :, 384:].astype(F32)
        r.own_sums[x, z] = own.astype(BF16)
        spreads.append(Spread16(h, r.own_sums, True))
        spreads[4].start()
        owner = x == h.y
        across = [h.sem() for _ in range(4)]
        along = [h.sem() for _ in range(3)]
        line = r.rest.at[z]

        @pl.when(owner)
        def _():
            wait_bytes(line, arrive_rest)

        wide = []
        for j in range(1, 4):
            wide.append(pltpu.make_async_remote_copy(
                src_ref=line, dst_ref=line, send_sem=across[j], recv_sem=across[0],
                device_id=(h.s, 4 * lax.rem(x + j, 4) + z, h.y), device_id_type=MESH))

        @pl.when(owner)
        def _():
            for copy in wide:
                copy.start()

        @pl.when(jnp.logical_not(owner))
        def _():
            wait_bytes(line, across[0])

        for j in range(1, 4):
            h.send(line, line, (h.s, 4 * x + lax.rem(z + j, 4), h.y), along[j - 1])
        for each in spreads[2:]:
            each.middle()
        for each in spreads:
            each.finish()
        for sem in along:
            wait_bytes(line, sem)

        @pl.when(owner)
        def _():
            for copy in wide:
                copy.wait_send()

        for away, copy in rest:
            pl.when(away)(copy.wait_send)
        h.finish()

    ins = dict(
        qkv0=(qkv0, ANY), qkv0_last=(qkv0_last, VMEM), up0_piece=(up0_piece, VMEM), up0_last=(up0_last, VMEM),
        up1=(up1, ANY), up1_last=(up1_last, VMEM), qkv1_piece=(qkv1_piece, VMEM), qkv1_last=(qkv1_last, VMEM))
    up_half, qkv_half = (spec((4, 4, 4, 16, WINDOW)), VMEM), (spec((4, 4, 4, 16, 384)), VMEM)
    outs = dict(
        up_low=up_half, up_high=up_half, qkv_low=qkv_half, qkv_high=qkv_half,
        own_sums=(spec((4, 4, 16, 256)), VMEM), rest=(spec((4, 2, 2, 16, WINDOW)), VMEM))
    scratch = dict(
        part=VMEM((2, 4, 4, 2, 16, WINDOW), BF16), sums_a=reduce_scratch(2), sums_b=reduce_scratch(2),
        up1_vm=VMEM((SHARD, 16, WINDOW), BF16), qkv0_piece=VMEM((SHARD, 16, WINDOW), BF16),
        last_message=VMEM((SHARD, 3, 16, WINDOW), BF16), last_in=VMEM((CTX, 3, 16, WINDOW), BF16),
        up_in=VMEM((8, 16, WINDOW), BF16), qkv_in=VMEM((8, 16, WINDOW), BF16),
        rest_message=VMEM((2, 2, 16, WINDOW), BF16), sems=pltpu.SemaphoreType.DMA((160,)))
    return call("share", body, ins, outs, scratch, collective_id=6)


def settle_kernel(layers):
    def body(r):
        h = Here(r.sems)
        parts = [r.layer0, r.layer1]
        group = 2 * h.y + h.s
        loads = [h.local(parts[layer][0], r.down_vm.at[layer]) for layer in range(2)]
        h.barrier(whole=False)
        arrive_out, arrive_last, arrive_down = (h.sem() for _ in range(3))
        for copy in loads:
            copy.wait()
        for layer in range(2):
            out = parts[layer][1]
            h.send_or_keep(r.down_vm.at[layer], r.down.at[h.s], (layer, h.c, h.y), h.s == layer, arrive_down)
            for i in range(8):
                tile = 8 * group + i
                to = tile // 17
                row = pl.multiple_of(lax.rem(tile, 17) * 16, 16)
                h.send_or_keep(
                    out.at[pl.ds(16 * i, 16)], r.out_in.at[pl.ds(row, 16)], (layer, h.c, to),
                    (h.s == layer) & (to == h.y), arrive_out)
            h.send_or_keep(
                out.at[pl.ds(128, 64)], r.last_in.at[group], (layer, h.c, SHARD - 1),
                (h.s == layer) & (h.y == SHARD - 1), arrive_last)

        @pl.when(h.y < SHARD - 1)
        def _():
            wait_bytes(r.out_in, arrive_out)
            r.out[...] = r.out_in[...].astype(F32)

        @pl.when(h.y == SHARD - 1)
        def _():
            wait_bytes(r.out_in.at[pl.ds(0, SLICE - 64)], arrive_out)
            wait_bytes(r.last_in, arrive_last)
            r.out[: SLICE - 64] = r.out_in[: SLICE - 64].astype(F32)
            total = r.last_in[0].astype(F32)
            for g in range(1, 8):
                total = total + r.last_in[g].astype(F32)
            r.out[SLICE - 64 :] = total

        wait_bytes(r.down, arrive_down)
        h.finish()

    spaces = [ANY, VMEM]
    ins = dict(layer0=list(zip(layers[0], spaces)), layer1=list(zip(layers[1], spaces)))
    outs = dict(out=(spec((SLICE, D), F32), VMEM), down=(spec((2, 544, D)), VMEM))
    scratch = dict(
        down_vm=VMEM((2, 544, D), BF16), out_in=VMEM((SLICE, D), BF16), last_in=VMEM((8, 64, D), BF16),
        sems=pltpu.SemaphoreType.DMA((64,)))
    return call("settle", body, ins, outs, scratch, collective_id=7)


def join_kernel(share):
    def body(up_low, up_high, qkv_low, qkv_high, own_sums, rest, up_ref, qkv_ref, norm_ref):
        def join(windows, blocks, own):
            for g in range(8):
                main = windows[g][:, :512]
                if g % 4:
                    main = jnp.concatenate([main[:, :128] + windows[g - 1][:, 512:], main[:, 128:]], axis=1)
                at = 128 * (17 * g // 4)
                up_ref[:, at : at + 512] = main
                if g % 4 == 3:
                    up_ref[:, at + 512 : at + 640] = windows[g][:, 512:]
            queries = [blocks[g][:, :128] for g in range(8)] + [own[:, :64]]
            keys = [blocks[g][:, a : a + 64] for g in range(8) for a in (128, 256)] + [own[:, 64:128]]
            values = [blocks[g][:, a : a + 64] for g in range(8) for a in (192, 320)] + [own[:, 128:192]]
            qkv_ref[...] = jnp.concatenate(queries + keys + values, axis=1)
            norm_ref[...] = jnp.concatenate([own[:, 192:], jnp.zeros((16, 64), F32)], axis=1)

        @pl.when(pl.program_id(0) < CTX)
        def _():
            windows = [ref[0, 0, g].astype(F32) for ref in (up_low, up_high) for g in range(4)]
            blocks = [ref[0, 0, g].astype(F32) for ref in (qkv_low, qkv_high) for g in range(4)]
            join(windows, blocks, own_sums[0, 0].astype(F32))

        @pl.when(pl.program_id(0) == CTX)
        def _():
            windows = [rest[g // 2, g % 2, 0].astype(F32) for g in range(8)]
            blocks = [rest[g // 2, g % 2, 1].astype(F32) for g in range(8)]
            own = blocks[0][:, 384:]
            for g in range(1, 8):
                own = own + blocks[g][:, 384:]
            join(windows, blocks, own)

    def chip(*block):
        zeros = (0,) * len(block)
        return pl.BlockSpec((1, 1, *block), lambda i: (jnp.minimum(i, 15) // 4, jnp.minimum(i, 15) % 4, *zeros))

    def rows(width):
        return pl.BlockSpec((16, width), lambda i: (i, 0))

    return pl.pallas_call(
        body,
        grid=(17,),
        out_shape=(spec((SLICE, FF), F32), spec((SLICE, 3 * D), F32), spec((SLICE, 128), F32)),
        in_specs=[
            chip(4, 16, WINDOW), chip(4, 16, WINDOW), chip(4, 16, 384), chip(4, 16, 384), chip(16, 256),
            pl.BlockSpec((4, 2, 2, 16, WINDOW), lambda i: (0,) * 5)],
        out_specs=(rows(FF), rows(3 * D), rows(128)),
        name="join",
    )(share.up_low, share.up_high, share.qkv_low, share.qkv_high, share.own_sums, share.rest)


def token_positions(block_order):
    offsets = jnp.arange(32, dtype=jnp.int32)
    groups = jnp.arange(2, dtype=jnp.int32)[:, None, None] * GROUP
    return (groups + block_order[:, :, None] * 32 + offsets).reshape(2, GROUP)


def swapped(section, first, second):
    own = jnp.where(section == 0, first, second)
    other = lax.ppermute(jnp.where(section == 0, second, first), SECTION, [(0, 1), (1, 0)])
    return jnp.where(section == 0, own, other), jnp.where(section == 0, other, own)


def gathered(x):
    return lax.all_gather(x, CONTEXT)


def shards(hidden_in, cotangent, block_order, qkv_weight, out_weight, up_weight, down_weight, norm_gains, norm_biases):
    section, ctx = lax.axis_index(SECTION), lax.axis_index(CONTEXT)
    params = jnp.concatenate([norm_gains[0], norm_biases[0]], axis=0).astype(F32)
    params = jnp.pad(params, ((0, 4), (0, 0)))
    grid = token_positions(block_order)
    own_positions = lax.dynamic_slice(grid, (section, ctx * ROWS), (1, ROWS))
    positions = grid.reshape(1, SEQ)
    hidden = hidden_in[0]
    spread = spread_kernel(params, qkv_weight, up_weight)
    norms = spread.norms
    mid_all = gathered(spread.mid_piece)
    first = first_kernel(hidden, norms, qkv_weight, out_weight, down_weight)
    up_piece, q16 = lax.optimization_barrier((spread.up_piece, first.q16))
    up_all = gathered(up_piece)
    at = (block_order, positions, own_positions.reshape(ROWS, 1))
    attended0 = attend(*at, first.message_in, first.kv16_in, q16)
    middle = middle_kernel(attended0.out, attended0.out16, hidden, norms, first, mid_all, spread.mid_last)
    attended1 = attend(*at, middle.message_in, middle.kv16_in, middle.q16)
    turn = turn_kernel(
        attended1.out, attended1.out16, middle.y, norms, first, up_all, spread.up_last, cotangent[0])
    up1, up1_last, down1, out1 = lax.psum((turn.up_g, turn.up_g_last, turn.down_g, turn.out_g), CONTEXT)
    at = (block_order, positions.reshape(SEQ, 1), own_positions)
    back1 = attend_back(
        *at, middle.message_in, middle.kv16_in, middle.q16, attended1, turn.context_grad_in, turn.context16_grad)
    back = back_kernel(
        back1, middle.a_full, middle.y, turn, norms, first, middle, attended0.out16, mid_all, spread.mid_last)
    (down_g, out_g), (up1, up1_last, down1, out1) = lax.optimization_barrier(
        ((back.down_g, back.out_g), (up1, up1_last, down1, out1)))
    down0, out0 = lax.psum((down_g, out_g), CONTEXT)
    back0 = attend_back(
        *at, first.message_in, first.kv16_in, first.q16, attended0, back.context_grad_in, back.context16_grad)
    last = last_kernel(back0, first.a_full, hidden, back, norms, first.qkv_w)
    share = share_kernel(
        last.qkv_g, last.qkv_g_last, last.up_piece, back.up_g_last, up1, up1_last, last.qkv_piece, back.qkv_g_last)
    up, qkv, norm_sums = join_kernel(share)
    settle = settle_kernel(((down0, out0), (down1, out1)))
    norm_sums = norm_sums[:, :4].T
    activations = jnp.stack(swapped(section, middle.y, turn.out))
    input_grads = jnp.stack(swapped(section, last.in_grad, back.in_grad))
    return (
        activations[None, None],
        input_grads[None, None],
        qkv[None],
        settle.out[None],
        up[None],
        settle.down.reshape(D, D).astype(F32)[None],
        norm_sums[None, 0::2],
        norm_sums[None, 1::2],
    )


def solution(mesh):
    tokens = P(LINE, None, CONTEXT, None)
    rows = P(SECTION, LINE, None)
    norms = P(SECTION, None, LINE)
    layers = P(SECTION, LINE, None, CONTEXT, None)
    return jax.shard_map(
        shards,
        mesh=mesh,
        in_specs=(tokens, tokens, P(), rows, rows, rows, rows, norms, norms),
        out_specs=(layers, layers, rows, rows, rows, rows, norms, norms),
        check_vma=False,
    )
```

```python
import functools
import types

import jax
import jax.numpy as jnp
from jax import lax
from jax.experimental import pallas as pl
from jax.experimental.pallas import tpu as pltpu
from jax.sharding import PartitionSpec as P

D = 1088
HEADS = 17
HEAD_DIM = 64
FF = 4352
SHARD = 4
CTX = 16
ROWS = 64
GROUP = 1024
SEQ = 2048
WINDOW = 640
SLICE = D // SHARD
EPSILON = 1e-05
NEG_LARGE = -1e30
BF16 = jnp.bfloat16
F32 = jnp.float32
MESH = pl.DeviceIdType.MESH
VMEM = pltpu.VMEM
ANY = pl.ANY
VMEM_BYTES = 56 * 2**20
SECTION, CONTEXT, LINE = "section", "ctx", "shard"
TILES = (68, 16, WINDOW)


def spec(shape, dtype=BF16):
    return jax.ShapeDtypeStruct(shape, dtype)


def call(name, body, ins, outs, scratch, collective_id=None):
    def kernel(*refs):
        refs, found = list(refs), {}
        for key, value in [*ins.items(), *outs.items(), *scratch.items()]:
            if isinstance(value, list):
                found[key], refs = refs[: len(value)], refs[len(value) :]
            else:
                found[key] = refs.pop(0)
        body(types.SimpleNamespace(**found))

    extra = {} if collective_id is None else dict(collective_id=collective_id, has_side_effects=True)
    shapes, given = [], []
    for value in scratch.values():
        shapes += value if isinstance(value, list) else [value]
    for value in ins.values():
        given += value if isinstance(value, list) else [value]
    results = pl.pallas_call(
        kernel,
        out_shape=tuple(value[0] for value in outs.values()),
        in_specs=[pl.BlockSpec(memory_space=space) for _, space in given],
        out_specs=tuple(pl.BlockSpec(memory_space=value[1]) for value in outs.values()),
        scratch_shapes=shapes,
        compiler_params=pltpu.CompilerParams(vmem_limit_bytes=VMEM_BYTES, **extra),
        name=name,
    )(*(array for array, _ in given))
    return types.SimpleNamespace(**dict(zip(outs, results)))


def dot(a, b):
    return jnp.dot(a, b, preferred_element_type=F32)


def dot_nt(a, b):
    return lax.dot_general(a, b, (((1,), (1,)), ((), ())), preferred_element_type=F32)


def dot_tn(a, b):
    return lax.dot_general(a, b, (((0,), (0,)), ((), ())), preferred_element_type=F32)


def norm_parts(values):
    center = values - jnp.mean(values, axis=-1, keepdims=True)
    rate = lax.rsqrt(jnp.mean(center * center, axis=-1, keepdims=True) + EPSILON)
    return center * rate, rate


def layer_norm(values, gain, bias):
    return norm_parts(values)[0] * gain + bias


def gelu(u):
    return 0.5 * u * (1.0 + jnp.tanh(0.7978845608028654 * (u + 0.044715 * u * u * u)))


class Here:
    def __init__(self, sems):
        self.s = lax.axis_index(SECTION)
        self.c = lax.axis_index(CONTEXT)
        self.y = lax.axis_index(LINE)
        self.sems, self.used, self.sent = sems, 0, []

    def sem(self):
        self.used += 1
        return self.sems.at[self.used - 1]

    def shard(self, step):
        return lax.rem(self.y + step, SHARD)

    def rows(self, shard, core):
        return pl.ds(pl.multiple_of((shard * 2 + core) * ROWS, ROWS), ROWS)

    def barrier(self, whole=True):
        sem = pltpu.get_barrier_semaphore()
        peers = []
        for step in range(SHARD):
            for core in range(2):
                if step or core:
                    peers.append((lax.rem(self.s + core, 2), self.c, self.shard(step)))
        for step in range(1, CTX if whole else 1):
            for core in range(2):
                peers.append((core, lax.rem(self.c + step, CTX), self.y))
        for to in peers:
            pl.semaphore_signal(sem, inc=1, device_id=to, device_id_type=MESH)
        self.awaited = len(peers)

    def ready(self):
        pl.semaphore_wait(pltpu.get_barrier_semaphore(), self.awaited)

    def save_on(self, core, src, dst):
        copy = pltpu.make_async_copy(src, dst, self.sem())
        pl.when(self.s == core)(copy.start)
        self.sent.append(types.SimpleNamespace(wait_send=lambda: pl.when(self.s == core)(copy.wait)))

    def local(self, src, dst):
        copy = pltpu.make_async_copy(src, dst, self.sem())
        copy.start()
        return copy

    def save(self, src, dst):
        copy = self.local(src, dst)
        self.sent.append(types.SimpleNamespace(wait_send=copy.wait))

    def send(self, src, dst, to, arrive, leave=None):
        copy = pltpu.make_async_remote_copy(
            src_ref=src, dst_ref=dst, send_sem=self.sem() if leave is None else leave,
            recv_sem=arrive, device_id=to, device_id_type=MESH)
        copy.start()
        if leave is None:
            self.sent.append(copy)
        return copy

    def send_or_keep(self, src, dst, to, is_self, arrive):
        leave = self.sem()
        copy = pltpu.make_async_remote_copy(
            src_ref=src, dst_ref=dst, send_sem=leave, recv_sem=arrive, device_id=to, device_id_type=MESH)
        kept = pltpu.make_async_copy(src, dst, arrive)
        pl.when(jnp.logical_not(is_self))(copy.start)
        pl.when(is_self)(kept.start)

        def wait_send():
            pl.when(jnp.logical_not(is_self))(copy.wait_send)

        self.sent.append(types.SimpleNamespace(wait_send=wait_send))

    def sibling(self):
        return (1 - self.s, self.c, self.y)

    def finish(self):
        for copy in self.sent:
            copy.wait_send()
        self.sent = []


def wait_bytes(ref, sem):
    pltpu.make_async_copy(ref, ref, sem).wait()


HALF = ROWS // 2


def half_rows(half):
    return slice(HALF * half, HALF * half + HALF)


class Gather8:
    def __init__(self, here, full):
        self.here, self.full = here, full
        self.own = [[here.sem() for _ in range(2)] for _ in range(SHARD)]
        self.other = [[here.sem() for _ in range(2)] for _ in range(SHARD)]

    def rows(self, shard, core, half):
        return self.full.at[pl.ds(pl.multiple_of((shard * 2 + core) * ROWS + half * HALF, HALF), HALF)]

    def start(self, value, half):
        h = self.here
        mine = self.rows(h.y, h.s, half)
        mine[...] = value
        h.send(mine, mine, h.sibling(), self.other[0][half])
        for step in (1, 3, 2):
            h.send(mine, mine, (h.s, h.c, h.shard(step)), self.own[SHARD - step][half])

    def relay(self, step):
        h = self.here
        for half in range(2):
            part = self.rows(h.shard(step), h.s, half)
            wait_bytes(part, self.own[step][half])
            h.send(part, part, h.sibling(), self.other[step][half])

    def wait(self, step):
        h = self.here
        for half in range(2):
            wait_bytes(self.rows(h.shard(step), 1 - h.s, half), self.other[step][half])


class Scatter8:
    def __init__(self, here, bufs):
        self.here = here
        self.to_core, self.mine, self.from_core, self.to_shard, self.from_shard = bufs
        self.core = [[here.sem() for _ in range(2)] for _ in range(SHARD)]
        self.shard = [[here.sem() for _ in range(2)] for _ in range(SHARD)]

    def part(self, ref, step, half):
        return ref.at[step, pl.ds(half * HALF, HALF)]

    def put(self, step, block):
        h = self.here
        low, high = block[:ROWS], block[ROWS:]
        self.to_core[step] = jnp.where(h.s == 0, high, low).astype(BF16)
        self.mine[step] = jnp.where(h.s == 0, low, high)
        for half in range(2):
            h.send(
                self.part(self.to_core, step, half), self.part(self.from_core, step, half), h.sibling(),
                self.core[step][half])

    def relay(self, steps):
        h = self.here
        for half in range(2):
            for step in steps:
                part = self.part(self.from_core, step, half)
                wait_bytes(part, self.core[step][half])
                total = self.mine[step, half_rows(half)] + part[...].astype(F32)
                out = self.part(self.to_shard, step, half)
                out[...] = total.astype(BF16)
                h.send(
                    out, self.part(self.from_shard, step, half), (h.s, h.c, h.shard(step)), self.shard[step][half])

    def result(self, half):
        part = self.part(self.from_core, 0, half)
        wait_bytes(part, self.core[0][half])
        total = self.mine[0, half_rows(half)] + part[...].astype(F32)
        for step in (1, 3, 2):
            part = self.part(self.from_shard, step, half)
            wait_bytes(part, self.shard[step][half])
            total = total + part[...].astype(F32)
        return total


def scatter_scratch():
    quarter = (SHARD, ROWS, D)
    return [VMEM(quarter, BF16), VMEM(quarter, F32), VMEM(quarter, BF16), VMEM(quarter, BF16), VMEM(quarter, BF16)]


ORDER = (0, 1, 3, 2)


def window_offset(group):
    return 32 * lax.rem(group, 4)


def everyone(h):
    for step in (1, 3, 2, 0):
        for other in range(2):
            yield step, other, (lax.rem(h.s + other, 2), h.c, h.shard(step))


def packed_qkv(rows, g):
    keys = rows[:, D + 128 * g : D + 128 * g + 128]
    values = rows[:, 2 * D + 128 * g : 2 * D + 128 * g + 128]
    return jnp.concatenate([
        rows[:, 128 * g : 128 * g + 128], keys[:, :64], values[:, :64], keys[:, 64:], values[:, 64:],
        rows[:, D - 64 : D], rows[:, 2 * D - 64 : 2 * D], rows[:, 3 * D - 64 : 3 * D], jnp.zeros_like(keys[:, :64])],
        axis=1)


def window(g):
    return slice(128 * (17 * g // 4), 128 * (17 * g // 4) + WINDOW)


def spread_kernel(params, w_qkv, w_up):
    def body(r):
        h = Here(r.sems)
        own = pl.ds(pl.multiple_of(h.c * 16, 16), 16)
        loads = [
            h.local(ref.at[0, rows], dst.at[pl.ds(16 * i, 16)])
            for ref, dst in ((r.w_up, r.up_rows), (r.w_qkv, r.qkv_rows)) for i, rows in enumerate((own, pl.ds(256, 16)))]
        h.barrier(whole=False)
        h.ready()
        arrive, arrive_mid, arrive_up = h.sem(), h.sem(), h.sem()
        mine = r.params_in.at[h.s * SHARD + h.y]
        mine[...] = r.params[...]
        for step, other, to in everyone(h):
            if step or other:
                h.send(mine, mine, to, arrive)
        for copy in loads:
            copy.wait()

        @pl.when(h.s == 0)
        def _():
            for g in range(8):
                r.mid[g] = r.up_rows[:, window(g)].reshape(2, 16, WINDOW)
                r.up[g] = packed_qkv(r.qkv_rows[...], g).reshape(2, 16, WINDOW)

        @pl.when(h.s == 1)
        def _():
            for g in range(8):
                r.mid[g] = packed_qkv(r.qkv_rows[...], g).reshape(2, 16, WINDOW)
                r.up[g] = r.up_rows[:, window(g)].reshape(2, 16, WINDOW)

        for step, other, to in everyone(h):
            g = 2 * to[2] + to[0]
            slot = h.s * SHARD + h.y
            for sem, source, targets in (
                    (arrive_up, r.up, (r.side_piece, r.side_last)), (arrive_mid, r.mid, (r.mid_piece, r.mid_last))):
                for half in range(2):
                    src, dst = source.at[g, half], targets[half].at[slot]
                    if step or other:
                        h.send(src, dst, to, sem)
                    else:
                        pltpu.make_async_copy(src, dst, sem).start()
        wait_bytes(r.params_in.at[pl.ds(0, 7)], arrive)
        for layer in range(2):
            r.norms[layer] = jnp.concatenate([r.params_in[layer * SHARD + i] for i in range(SHARD)], axis=1)
        wait_bytes(r.mid, arrive_mid)
        wait_bytes(r.up, arrive_up)
        h.finish()

    ins = dict(params=(params, VMEM), w_qkv=(w_qkv, ANY), w_up=(w_up, ANY))
    outs = dict(
        norms=(spec((2, 8, D), F32), VMEM), mid_piece=(spec((8, 16, WINDOW)), VMEM),
        mid_last=(spec((8, 16, WINDOW)), VMEM), side_piece=(spec((8, 16, WINDOW)), VMEM),
        side_last=(spec((8, 16, WINDOW)), VMEM))
    scratch = dict(
        params_in=VMEM((8, 8, SLICE), F32), up_rows=VMEM((32, FF), BF16), qkv_rows=VMEM((32, 3 * D), BF16),
        mid=VMEM((8, 2, 16, WINDOW), BF16), up=VMEM((8, 2, 16, WINDOW), BF16), sems=pltpu.SemaphoreType.DMA((64,)))
    return call("spread", body, ins, outs, scratch, collective_id=0)


def load_tiles(h, gathered, last, dst, first=0):
    copies = []
    for i in range(SHARD):
        copies.append(h.local(gathered.at[:, first + i], dst.at[pl.ds(17 * i, 16)]))
        copies.append(h.local(last.at[first + i], dst.at[17 * i + 16]))
    return copies


def place(value, parts, last):
    tiles = value.astype(BF16).reshape(68, 16, value.shape[1])
    for i in range(SHARD):
        for c in range(CTX):
            parts[c // 4, c % 4, i] = tiles[17 * i + c]
        last[i] = tiles[17 * i + 16]


def whole(ref):
    return ref[...].reshape(D, WINDOW)


class FirstWeights:
    def __init__(self, h, r):
        self.h, self.r = h, r
        self.arrive = [h.sem() for _ in range(3)]
        self.spreads = [Spread16(h, parts, i == 0) for i, parts in enumerate((r.qkv_low, r.qkv_high))]

    def load(self):
        h, r = self.h, self.r
        self.loads = [h.local(r.w_down.at[0], r.down_rows), h.local(r.w_out.at[0], r.out_rows)]

    def send_qkv(self):
        r = self.r
        for i, (each, parts) in enumerate(zip(self.spreads, (r.qkv_low, r.qkv_high))):
            parts[each.x, each.z] = r.side_piece[2 * i : 2 * i + 2]
            each.start()

    def send_qkv_on(self):
        for each in self.spreads:
            each.middle()

    def send_rest(self):
        h, r = self.h, self.r
        for copy in self.loads:
            copy.wait()
        for other in range(2):
            core = lax.rem(h.s + other, 2)
            at = pl.multiple_of(window_offset(h.y * 2 + core), 32)
            src = r.down_rows.at[pl.ds(pl.multiple_of(544 * core, 16), 544)]
            dst = r.down_vm.at[h.s, pl.ds(at, 544)]
            if other:
                h.send(src, dst, h.sibling(), self.arrive[1])
            else:
                pltpu.make_async_copy(src, dst, self.arrive[1]).start()
        self.tiles = []
        for i in range(17):
            tile = h.y * 17 + i
            group = jnp.minimum(tile // 8, 7)
            core, shard = lax.rem(group, 2), group // 2
            src = r.out_rows.at[pl.ds(16 * i, 16)]
            dst = r.out_vm.at[h.s, pl.ds(pl.multiple_of(lax.rem(tile, 8) * 16, 16), 16)]
            copy = pltpu.make_async_remote_copy(
                src_ref=src, dst_ref=dst, send_sem=h.sem(), recv_sem=self.arrive[2],
                device_id=(core, h.c, shard), device_id_type=MESH)
            same = pltpu.make_async_copy(src, dst, self.arrive[2])
            is_self = (core == h.s) & (shard == h.y)
            pl.when((tile < 64) & is_self)(same.start)
            away = (tile < 64) & jnp.logical_not(is_self)
            pl.when(away)(copy.start)
            self.tiles.append((away, copy))
        src, dst = r.out_rows.at[pl.ds(SLICE - 64, 64)], r.out_vm.at[h.s, pl.ds(128, 64)]
        same = pltpu.make_async_copy(src, dst, self.arrive[2])
        self.last = []
        for step, other, to in everyone(h):
            if step or other:
                self.last.append(pltpu.make_async_remote_copy(
                    src_ref=src, dst_ref=dst, send_sem=h.sem(), recv_sem=self.arrive[2], device_id=to,
                    device_id_type=MESH))

        @pl.when(h.y == SHARD - 1)
        def _():
            same.start()
            for copy in self.last:
                copy.start()

    def wait_qkv(self):
        r = self.r
        for each in self.spreads:
            each.finish()
        for i in range(SHARD):
            for c in range(CTX):
                parts = (r.qkv_low, r.qkv_high)[i // 2]
                r.qkv_vm[17 * i + c] = parts[c // 4, c % 4, i % 2]
            r.qkv_vm[17 * i + 16] = r.side_last[i]

    def finish(self):
        r, h = self.r, self.h
        wait_bytes(r.down_vm.at[:, pl.ds(0, 544)], self.arrive[1])
        h.save(r.down_vm, r.down_w)
        wait_bytes(r.out_vm, self.arrive[2])
        h.save(r.out_vm, r.out_w)

        for away, copy in self.tiles:
            pl.when(away)(copy.wait_send)

        @pl.when(h.y == SHARD - 1)
        def _():
            for copy in self.last:
                copy.wait_send()


def head_outs():
    return dict(
        a_full=(spec((512, D)), ANY), message_in=(spec((CTX, 160, 128)), VMEM),
        kv16_in=(spec((2, CTX, ROWS, 128)), VMEM), q16=(spec((ROWS, HEAD_DIM)), VMEM))


def head_scratch():
    return dict(message=VMEM((2, 4, 2, 160, 128), BF16), qkv_vm=VMEM(TILES, BF16), a_vm=VMEM((512, D), BF16))


def run_head(h, r, gather, after=None):
    arrive = h.sem()
    own16 = dot(r.a_vm[h.rows(h.y, h.s)], r.qkv_vm[:, :, 384:].reshape(D, 256)).astype(BF16)
    r.q16[...] = own16[:, :64]
    r.kv16_in[h.s, h.c] = own16[:, 64:192]
    own_kv = r.kv16_in.at[h.s, h.c]
    leave16, arrive16, cross16 = h.sem(), h.sem(), h.sem()
    for step in range(1, CTX):
        h.send(own_kv, own_kv, (h.s, lax.rem(h.c + step, CTX), h.y), arrive16, leave16)
    for step in ORDER:
        if step:
            gather.relay(step)
        gather.wait(step)
        shard = h.shard(step)
        block = r.a_vm[pl.ds(pl.multiple_of(shard * 128, 128), 128)]
        out = dot(block, r.qkv_vm[:, :, :384].reshape(D, 384)).astype(BF16)
        for e in range(2):
            for core in range(2):
                r.message[e, shard, core, :128] = out[:, 128 + 128 * e : 256 + 128 * e]
                for b in range(2):
                    at = 32 * b + 16 * core
                    lanes = slice(64 * e, 64 * e + 64)
                    packed = jnp.concatenate([out[at : at + 16, lanes], out[64 + at : 80 + at, lanes]], axis=1)
                    r.message[e, shard, core, 128 + 16 * b : 144 + 16 * b] = packed
                chip = 8 * h.s + 4 * e + shard
                h.send_or_keep(
                    r.message.at[e, shard, core], r.message_in.at[h.c], (core, chip, h.y),
                    (chip == h.c) & (h.s == core), arrive)
    h.save(r.a_vm, r.a_full)
    if after is not None:
        after()
    wait_bytes(r.kv16_in.at[h.s, pl.ds(0, CTX - 1)], arrive16)
    cross = r.kv16_in.at[h.s]
    h.send(cross, cross, h.sibling(), cross16)
    wait_bytes(r.kv16_in.at[h.s, pl.ds(0, CTX - 1)], leave16)
    wait_bytes(r.kv16_in.at[1 - h.s], cross16)
    wait_bytes(r.message_in, arrive)


def first_kernel(hidden, norms, side_piece, side_last, w_out, w_down):
    def body(r):
        h = Here(r.sems)
        weights = FirstWeights(h, r)
        weights.load()
        r.down_vm[...] = jnp.zeros_like(r.down_vm)
        h.barrier()
        h.ready()
        weights.send_qkv()
        x = r.hidden[h.s].astype(F32)
        a_value = layer_norm(x, r.norms[0, 0:1], r.norms[0, 2:3]).astype(BF16)
        gather = Gather8(h, r.a_vm)
        for half in range(2):
            gather.start(a_value[half_rows(half)], half)
        weights.send_qkv_on()
        weights.wait_qkv()
        h.save(r.qkv_vm, r.qkv_w)
        run_head(h, r, gather, weights.send_rest)
        weights.finish()
        h.finish()

    ins = dict(hidden=(hidden, VMEM), norms=(norms, VMEM), side_piece=(side_piece, VMEM), side_last=(side_last, VMEM),
        w_out=(w_out, ANY), w_down=(w_down, ANY))
    outs = dict(
        **head_outs(), qkv_w=(spec(TILES), ANY), out_w=(spec((2, 192, D)), ANY), down_w=(spec((2, WINDOW, D)), ANY))
    scratch = dict(
        **head_scratch(), qkv_low=VMEM((4, 4, 2, 16, WINDOW), BF16), qkv_high=VMEM((4, 4, 2, 16, WINDOW), BF16),
        down_rows=VMEM((D, D), BF16), out_rows=VMEM((SLICE, D), BF16), down_vm=VMEM((2, WINDOW, D), BF16),
        out_vm=VMEM((2, 192, D), BF16), sems=pltpu.SemaphoreType.DMA((240,)))
    return call("first", body, ins, outs, scratch, collective_id=1)


def sort_rows(r):
    for m in range(2):
        for p in range(32):
            at = 32 * m + p
            tile = r.places[0, m, p]
            for i in range(2):
                rows = r.kept[tile + i]
                r.keys[32 * at + 16 * i : 32 * at + 16 * i + 16] = rows[:, :64]
                r.values[32 * at + 16 * i : 32 * at + 16 * i + 16] = rows[:, 64:]
            query = r.kept[r.places[1, m, p]]
            r.queries[16 * at : 16 * at + 16] = query[:, 64 * m : 64 * m + 64] * 0.125


def attend(h, r):
    row = lax.broadcasted_iota(jnp.int32, (256, 512), 0)
    row = 32 * (row // 16) + 16 * h.s + row % 16
    visible = row >= lax.broadcasted_iota(jnp.int32, (256, 512), 1)
    for t in range(4):
        query = r.queries[256 * t : 256 * t + 256]
        parts = [dot_nt(query, r.keys[512 * u : 512 * u + 512]) for u in range(t + 1)]
        parts[t] = jnp.where(visible, parts[t], NEG_LARGE)
        top = parts[0]
        for p in parts[1:]:
            top = jnp.maximum(top, p)
        top = jnp.max(top, axis=-1, keepdims=True)
        parts = [jnp.exp(p - top) for p in parts]
        total = parts[0]
        for p in parts[1:]:
            total = total + p
        total = jnp.sum(total, axis=-1, keepdims=True)
        out = dot(parts[0].astype(BF16), r.values[:512])
        for u in range(1, t + 1):
            out = out + dot(parts[u].astype(BF16), r.values[512 * u : 512 * u + 512])
        r.sorted_out[16 * t : 16 * t + 16] = (out / total).astype(BF16).reshape(16, 16, 64)
        r.logs[256 * t : 256 * t + 256] = jnp.broadcast_to(top + jnp.log(total), (256, 128))
    for c in range(CTX):
        for m in range(2):
            for b in range(2):
                rows = r.sorted_out[32 * m + r.order[m, 2 * c + b]]
                r.attended[c, 16 * b : 16 * b + 16, 64 * m : 64 * m + 64] = rows


def attend_last(r):
    kv = r.kept16[...].reshape(SEQ, 128)
    scores = dot_nt(r.kept_q16[...] * 0.125, kv[:, :64])
    scores = jnp.where(r.own_positions[...] >= r.positions[...], scores, NEG_LARGE)
    top = jnp.max(scores, axis=-1, keepdims=True)
    scores = jnp.exp(scores - top)
    total = jnp.sum(scores, axis=-1, keepdims=True)
    out = dot(scores.astype(BF16), kv[:, 64:])
    r.attended16[...] = (out / total).astype(BF16)
    r.logs16[...] = jnp.broadcast_to(top + jnp.log(total), (ROWS, 128))


def attend_ins(kept, at):
    order, places, positions, own_positions = at
    return dict(
        order=(order, pltpu.SMEM), places=(places, pltpu.SMEM), positions=(positions, VMEM),
        own_positions=(own_positions, VMEM), kept=(kept.message_in.reshape(160, 16, 128), VMEM), kept16=(kept.kv16_in, VMEM),
        kept_q16=(kept.q16, VMEM))


def attend_outs():
    return dict(
        attended16=(spec((ROWS, 64)), VMEM), sorted_out=(spec((64, 16, 64)), VMEM), logs=(spec((1024, 128), F32), VMEM),
        logs16=(spec((ROWS, 128), F32), VMEM))


def attend_scratch():
    return dict(
        keys=VMEM((SEQ, 64), BF16), values=VMEM((SEQ, 64), BF16), queries=VMEM((1024, 64), BF16),
        attended=VMEM((CTX, 32, 128), BF16))


def middle_scratch():
    return dict(
        context_in=VMEM((2, 4, 2, 32, 128), BF16), out_vm=VMEM((192, D), BF16), up_vm=VMEM(TILES, BF16),
        down_vm=VMEM((WINDOW, D), BF16), to_out=scatter_scratch(), to_down=scatter_scratch())


def load_layer(h, r, layer, first):
    loads = [h.local(r.out_w.at[layer], r.out_vm), h.local(r.down_w.at[layer], r.down_vm)]
    return loads + load_tiles(h, r.up_all, r.up_last, r.up_vm, first)


def gather_context(h, r):
    arrive = h.sem()
    to_core = h.c // 8
    e, j = lax.rem(h.c // 4, 2), lax.rem(h.c, 4)
    for c in range(CTX):
        h.send_or_keep(
            r.attended.at[c], r.context_in.at[e, j, h.s], (to_core, c, h.y), (h.c == c) & (h.s == to_core), arrive)
    return arrive


def unpack_context(r, store):
    for j in range(4):
        for m in range(2):
            for b in range(2):
                for core in range(2):
                    lanes = slice(64 * m, 64 * m + 64)
                    piece = jnp.concatenate(
                        [r.context_in[e, j, core, 16 * b : 16 * b + 16, lanes] for e in range(2)], axis=1)
                    at = 128 * j + 64 * m + 32 * b + 16 * core
                    store[at : at + 16] = piece


def block_rows(h, step):
    return pl.ds(pl.multiple_of(h.shard(step) * 128, 128), 128)


def run_out(h, r, x, ready):
    sums = Scatter8(h, r.to_out)
    for step in (2, 1, 3, 0):
        sums.put(step, dot(r.context[block_rows(h, step)], r.out_vm[:128]))
    sums.relay((2, 1, 3))
    own = x + dot(r.attended16[...], r.out_vm[128:])
    for half in range(2):
        residual = own[half_rows(half)] + sums.result(half)
        r.residual[half_rows(half)] = residual
        ready(half, residual)


def middle_kernel(at, x, norms, first, mid_all, mid_last):
    def body(r):
        h = Here(r.sems)
        loads = load_layer(h, r, 0, 0)
        head_loads = load_tiles(h, r.up_all, r.up_last, r.qkv_vm, SHARD)
        h.barrier()
        sort_rows(r)
        attend(h, r)
        h.ready()
        arrive = gather_context(h, r)
        attend_last(r)
        for copy in loads:
            copy.wait()
        wait_bytes(r.context_in, arrive)
        unpack_context(r, r.context)
        gather = Gather8(h, r.b_vm)

        def ready(half, residual):
            gather.start(layer_norm(residual, r.norms[0, 1:2], r.norms[0, 3:4]).astype(BF16), half)

        run_out(h, r, r.x[h.s].astype(F32), ready)
        sums = Scatter8(h, r.to_down)
        for step in ORDER:
            if step:
                gather.relay(step)
            gather.wait(step)
            rows = block_rows(h, step)
            u = dot(r.b_vm[rows], whole(r.up_vm))
            r.pre_vm[rows] = u
            sums.put(step, dot(gelu(u).astype(BF16), r.down_vm[...]))
        sums.relay((1, 3, 2))
        h.save(r.b_vm, r.b_full)
        h.save(r.pre_vm, r.pre)
        for copy in head_loads:
            copy.wait()
        gather = Gather8(h, r.a_vm)
        for half in range(2):
            y = (r.residual[half_rows(half)] + sums.result(half)).astype(BF16)
            r.y[half_rows(half)] = y
            gather.start(layer_norm(y.astype(F32), r.norms[1, 0:1], r.norms[1, 2:3]).astype(BF16), half)
        run_head(h, r, gather)
        h.finish()

    ins = dict(
        **attend_ins(first, at), x=(x, VMEM), norms=(norms, VMEM), out_w=(first.out_w, ANY),
        down_w=(first.down_w, ANY), up_all=(mid_all, ANY), up_last=(mid_last, ANY))
    outs = dict(
        **attend_outs(), context=(spec((512, 128)), VMEM), residual=(spec((ROWS, D), F32), VMEM), b_full=(spec((512, D)), ANY),
        pre=(spec((512, WINDOW), F32), ANY), y=(spec((ROWS, D)), VMEM), **head_outs())
    scratch = dict(
        **attend_scratch(), **middle_scratch(), **head_scratch(), b_vm=VMEM((512, D), BF16), pre_vm=VMEM((512, WINDOW), F32),
        sems=pltpu.SemaphoreType.DMA((300,)))
    return call("middle", body, ins, outs, scratch, collective_id=2)


def gelu_slope(u):
    t = jnp.tanh(0.7978845608028654 * (u + 0.044715 * u * u * u))
    return 0.5 * (1.0 + t) + 0.5 * u * (1.0 - t * t) * 0.7978845608028654 * (1.0 + 0.134145 * u * u)


def norm_back(grad, values, gain):
    normed, rate = norm_parts(values)
    scaled = grad * gain
    mean = jnp.mean(scaled, axis=-1, keepdims=True)
    along = jnp.mean(scaled * normed, axis=-1, keepdims=True)
    back = rate * (scaled - mean - normed * along)
    return back, grad * normed


def columns(at, gain_rows, bias_rows):
    lane = lax.broadcasted_iota(jnp.int32, (ROWS, 64), 1)

    def into(rows, column):
        return dot_tn(rows.astype(BF16), (lane == column).astype(BF16))

    return into(gain_rows, at) + into(bias_rows, at + 1)


def back_outs():
    return dict(
        mid_grad=(spec((ROWS, D), F32), VMEM), context_grad_in=(spec((CTX, 32, 128)), VMEM),
        context16_grad=(spec((ROWS, HEAD_DIM)), VMEM),
        up_g_last=(spec((SHARD, 16, WINDOW)), VMEM), norm2_g=(spec((68, 16, 64)), VMEM))


def back_scratch():
    return dict(
        m_full=VMEM((512, D), BF16), z_full=VMEM((512, D), BF16), hidden_low=VMEM((512, WINDOW), BF16),
        pre_grad=VMEM((512, WINDOW), BF16), context_message=VMEM((2, 4, 2, 32, 128), BF16), up_grad=VMEM((4, 4, SHARD, 16, WINDOW), BF16),
        down_grad=VMEM((40, 16, D), BF16), b_vm=VMEM((512, D), BF16), to_norm2=scatter_scratch())


def back_block(h, r, rows, sums, step, u, g):
    r.hidden_low[rows] = g
    hidden_grad = dot_nt(r.m_full[rows], r.down_vm[...])
    pre_grad = (hidden_grad * gelu_slope(u)).astype(BF16)
    r.pre_grad[rows] = pre_grad
    sums.put(step, dot_nt(pre_grad, whole(r.up_vm)))


def finish_back(h, r, sums, layer, residual, out_grad, context, down_ready, up_ready, beside, near_end=None):
    r.down_grad[...] = dot_tn(r.hidden_low[...], r.m_full[...]).astype(BF16).reshape(40, 16, D)
    down_ready(r.down_grad.at[pl.ds(2 * lax.rem(h.y * 2 + h.s, 4), 34)])
    place(dot_tn(r.b_vm[...], r.pre_grad[...]), r.up_grad, r.up_g_last)
    up_ready()
    gather = Gather8(h, r.z_full)
    gain_rows, normed_grad = [], []
    for half in range(2):
        rows = half_rows(half)
        normed_grad.append(sums.result(half))
        back, gains = norm_back(normed_grad[half], residual[rows], r.norms[layer, 1:2])
        gain_rows.append(gains)
        mid_grad = out_grad[rows] + back
        r.mid_grad[rows] = mid_grad
        gather.start(mid_grad.astype(BF16), half)
    gain_rows, normed_grad = jnp.concatenate(gain_rows, axis=0), jnp.concatenate(normed_grad, axis=0)
    z = r.z_full[h.rows(h.y, h.s)]
    r.norm2_g[...] = columns(2, gain_rows, normed_grad).astype(BF16).reshape(68, 16, 64)
    beside()
    arrive = h.sem()
    r.context16_grad[...] = dot_nt(z, r.out_vm[128:]).astype(BF16)
    for step in ORDER:
        if step:
            gather.relay(step)
        gather.wait(step)
        shard = h.shard(step)
        out = dot_nt(r.z_full[block_rows(h, step)], r.out_vm[:128]).astype(BF16)
        for e in range(2):
            for core in range(2):
                lanes = slice(64 * e, 64 * e + 64)
                for b in range(2):
                    at = 32 * b + 16 * core
                    r.context_message[e, shard, core, 16 * b : 16 * b + 16] = jnp.concatenate(
                        [out[at : at + 16, lanes], out[64 + at : 80 + at, lanes]], axis=1)
                chip = 8 * h.s + 4 * e + shard
                h.send_or_keep(
                    r.context_message.at[e, shard, core], r.context_grad_in.at[h.c], (core, chip, h.y),
                    (chip == h.c) & (h.s == core), arrive)
    r.out_g[:8] = dot_tn(context[...], r.z_full[...]).astype(BF16).reshape(8, 16, D)
    r.out_g[8:] = dot_tn(r.attended16[...], z).astype(BF16).reshape(4, 16, D)
    if near_end is not None:
        near_end()
    wait_bytes(r.context_grad_in, arrive)


def turn_kernel(at, kept, x, norms, first, up_all, up_last, cotangent):
    def body(r):
        h = Here(r.sems)
        loads = load_layer(h, r, 1, 0)
        h.barrier()
        sort_rows(r)
        h.ready()
        out_grad = r.cotangent[h.s]
        gather_m = Gather8(h, r.m_full)
        for half in range(2):
            gather_m.start(out_grad[half_rows(half)], half)
        attend(h, r)
        arrive = gather_context(h, r)
        attend_last(r)
        for step in (1, 3, 2):
            gather_m.relay(step)
        for copy in loads:
            copy.wait()
        wait_bytes(r.context_in, arrive)
        unpack_context(r, r.context)
        gather = Gather8(h, r.b_vm)

        def ready(half, residual):
            gather.start(layer_norm(residual, r.norms[1, 1:2], r.norms[1, 3:4]).astype(BF16), half)

        run_out(h, r, r.x[...].astype(F32), ready)
        back_sums, sums = Scatter8(h, r.to_norm2), Scatter8(h, r.to_down)
        for step in ORDER:
            if step:
                gather.relay(step)
            gather_m.wait(step)
            gather.wait(step)
            rows = block_rows(h, step)
            u = dot(r.b_vm[rows], whole(r.up_vm))
            g = gelu(u).astype(BF16)
            back_block(h, r, rows, back_sums, step, u, g)
            sums.put(step, dot(g, r.down_vm[...]))
        back_sums.relay((1, 3, 2))
        sums.relay((1, 3, 2))

        ups = [
            Reduce16(h, r.up_grad.at[:, :, pl.ds(2 * i, 2)], (r.ups_in.at[i], (r.up_mine_a, r.up_mine_b)[i], None), i == 0)
            for i in range(2)]
        first_rows = FirstRows(h, r)

        def up_ready():
            for each in ups:
                each.start()
            first_rows.start()

        def near_end():
            for each in ups:
                each.add()
            first_rows.add()

        def beside():
            for half in range(2):
                rows = half_rows(half)
                r.out[rows] = (r.residual[rows] + sums.result(half)).astype(BF16)

        finish_back(
            h, r, back_sums, 1, r.residual[...], out_grad.astype(F32), r.context, first_rows.load,
            up_ready, beside, near_end)
        h.finish()

    ins = dict(
        **attend_ins(kept, at), x=(x, VMEM), norms=(norms, VMEM), out_w=(first.out_w, ANY),
        down_w=(first.down_w, ANY), up_all=(up_all, ANY), up_last=(up_last, ANY),
        cotangent=(cotangent, VMEM))
    outs = dict(
        **attend_outs(), out=(spec((ROWS, D)), VMEM), **first_rows_outs(),
        up_mine_a=(spec((4, 2, 16, WINDOW)), VMEM), up_mine_b=(spec((4, 2, 16, WINDOW)), VMEM), out_g=(spec((12, 16, D)), VMEM), **back_outs())
    scratch = dict(
        **attend_scratch(), context=VMEM((512, 128), BF16), residual=VMEM((ROWS, D), F32), **middle_scratch(),
        **first_rows_scratch(), ups_in=VMEM((2, 3, 4, 2, 16, WINDOW), BF16), **back_scratch(), sems=pltpu.SemaphoreType.DMA((400,)))
    return call("turn", body, ins, outs, scratch, collective_id=3)


def row_of(grads, outs):
    product = grads.astype(F32) * outs.astype(F32)
    return lax.dot_general(
        jnp.ones((8, 64), F32), product, (((1,), (1,)), ((), ())), precision=lax.Precision.HIGHEST,
        preferred_element_type=F32)[0:1]


def sort_grads(r):
    sort_rows(r)
    for m in range(2):
        for p in range(32):
            at = 32 * m + p
            r.grads[16 * at : 16 * at + 16] = r.grad_in[r.places[2, m, p]][:, 64 * m : 64 * m + 64]
    r.key_grads[...] = jnp.zeros_like(r.key_grads)
    r.value_grads[...] = jnp.zeros_like(r.value_grads)


def attend_back(h, r):
    column = lax.broadcasted_iota(jnp.int32, (512, 256), 1)
    column = 32 * (column // 16) + 16 * h.s + column % 16
    visible = column >= lax.broadcasted_iota(jnp.int32, (512, 256), 0)
    for t in range(4):
        part = slice(256 * t, 256 * t + 256)
        query, grad = r.queries[part], r.grads[part]
        logs = jnp.transpose(r.logs[part])[0:1]
        delta = row_of(grad, r.sorted_out[16 * t : 16 * t + 16].reshape(256, 64))
        query_grad = jnp.zeros((256, 64), F32)
        for u in range(t + 1):
            chunk = slice(512 * u, 512 * u + 512)
            keys = r.keys[chunk]
            scores = dot_nt(keys, query)
            if u == t:
                scores = jnp.where(visible, scores, NEG_LARGE)
            probs = jnp.exp(scores - logs)
            probs_grad = dot_nt(r.values[chunk], grad)
            scores_grad = (probs * (probs_grad - delta)).astype(BF16)
            blocks = slice(16 * u, 16 * u + 16)
            r.value_grads[blocks] += dot(probs.astype(BF16), grad).reshape(16, 32, 64)
            r.key_grads[blocks] += dot(scores_grad, query).reshape(16, 32, 64)
            query_grad = query_grad + dot_tn(scores_grad, keys)
        r.query_grads[16 * t : 16 * t + 16] = (query_grad * 0.125).astype(BF16).reshape(16, 16, 64)
    for c in range(CTX):
        for m in range(2):
            for b in range(2):
                block = 32 * m + r.order[m, 2 * c + b]
                r.message[c, 64 * m + 32 * b : 64 * m + 32 * b + 32, :] = jnp.concatenate(
                    [r.key_grads[block], r.value_grads[block]], axis=1).astype(BF16)
                r.message[c, 128 + 16 * b : 144 + 16 * b, 64 * m : 64 * m + 64] = r.query_grads[block]


def attend_back_last(r):
    kv = r.kept16[...].reshape(SEQ, 128)
    query, grad = r.kept_q16[...] * 0.125, r.grad16[...]
    scores = dot_nt(kv[:, :64], query)
    scores = jnp.where(r.own_positions[...] >= r.positions[...], scores, NEG_LARGE)
    probs = jnp.exp(scores - jnp.transpose(r.logs16[...])[0:1])
    probs_grad = dot_nt(kv[:, 64:], grad)
    scores_grad = (probs * (probs_grad - row_of(grad, r.out16[...]))).astype(BF16)
    both = jnp.concatenate([dot(scores_grad, query), dot(probs.astype(BF16), grad)], axis=1)
    r.kv16_grad[...] = both.astype(BF16).reshape(2, CTX, ROWS, 128)
    r.q16_grad[...] = (dot_tn(scores_grad, kv[:, :64]) * 0.125).astype(BF16)


def tail_ins(at, kept, saved, a_full, x, above, norms):
    return dict(
        **attend_ins(kept, at), sorted_out=(saved.sorted_out, VMEM), logs=(saved.logs, VMEM), logs16=(saved.logs16, VMEM),
        out16=(saved.attended16, VMEM), grad_in=(above.context_grad_in.reshape(32, 16, 128), VMEM), grad16=(above.context16_grad, VMEM),
        a_full=(a_full, ANY), x=(x, VMEM), mid_in=(above.mid_grad, VMEM), norms=(norms, VMEM),
        norm2_in=(above.norm2_g, VMEM))


def tail_outs():
    return dict(in_grad=(spec((ROWS, D)), VMEM))


def tail_scratch():
    return dict(
        keys=VMEM((SEQ, 64), BF16), values=VMEM((SEQ, 64), BF16), queries=VMEM((1024, 64), BF16),
        grads=VMEM((1024, 64), BF16), query_grads=VMEM((64, 16, 64), BF16), key_grads=VMEM((64, 32, 64), F32),
        value_grads=VMEM((64, 32, 64), F32), message=VMEM((CTX, 160, 128), BF16),
        kv16_grad=VMEM((2, CTX, ROWS, 128), BF16), q16_grad=VMEM((ROWS, 64), BF16),
        message_in=VMEM((2, 4, 2, 160, 128), BF16), core16=VMEM((CTX, ROWS, 128), BF16),
        sum16=VMEM((CTX, ROWS, 128), BF16), own16=VMEM((CTX, ROWS, 128), BF16), qkv_grads=VMEM((512, 384), BF16),
        qkv_vm=VMEM(TILES, BF16), a_vm=VMEM((512, D), BF16), main_part=VMEM((4, 4, SHARD, 16, 384), BF16),
        side_part=VMEM((4, 4, SHARD, 16, 256), BF16), to_norm1=scatter_scratch())


def start_tail(h, r):
    attend_back_last(r)
    cross = h.sem()
    h.send(r.kv16_grad.at[1 - h.s], r.core16, h.sibling(), cross)
    attend_back(h, r)
    arrive = h.sem()
    to_core = h.c // 8
    e, j = lax.rem(h.c // 4, 2), lax.rem(h.c, 4)
    for c in range(CTX):
        h.send_or_keep(
            r.message.at[c], r.message_in.at[e, j, h.s], (to_core, c, h.y), (h.c == c) & (h.s == to_core), arrive)
    wait_bytes(r.core16, cross)
    r.sum16[...] = (r.kv16_grad[h.s].astype(F32) + r.core16[...].astype(F32)).astype(BF16)
    leave16, arrive16 = h.sem(), h.sem()
    for step in range(1, CTX):
        to = lax.rem(h.c + step, CTX)
        h.send(r.sum16.at[to], r.own16.at[step], (h.s, to, h.y), arrive16, leave16)
    return arrive, leave16, arrive16


def run_tail(h, r, layer, x, waits, loads, last, main_ready, side_ready, arrived, beside, in_ready):
    arrive, leave16, arrive16 = waits
    for copy in loads:
        copy.wait()
    weights = whole(r.qkv_vm)
    wait_bytes(r.message_in, arrive)
    arrived()
    for j in range(4):
        for e in range(2):
            both = r.message_in[e, j, 0, :128].astype(F32) + r.message_in[e, j, 1, :128].astype(F32)
            r.qkv_grads[128 * j : 128 * j + 128, 128 + 128 * e : 256 + 128 * e] = both.astype(BF16)
        for m in range(2):
            for b in range(2):
                for core in range(2):
                    lanes = slice(64 * m, 64 * m + 64)
                    piece = jnp.concatenate(
                        [r.message_in[e, j, core, 128 + 16 * b : 144 + 16 * b, lanes] for e in range(2)], axis=1)
                    at = 128 * j + 64 * m + 32 * b + 16 * core
                    r.qkv_grads[at : at + 16, :128] = piece
    sums = Scatter8(h, r.to_norm1)
    for step in (2, 1, 3, 0):
        sums.put(step, dot_nt(r.qkv_grads[block_rows(h, step)], weights[:, :384]))
    sums.relay((2, 1, 3))
    wait_bytes(r.own16.at[pl.ds(1, CTX - 1)], arrive16)
    wait_bytes(r.own16.at[pl.ds(1, CTX - 1)], leave16)
    kv16 = r.sum16[h.c].astype(F32)
    for step in range(1, CTX):
        kv16 = kv16 + r.own16[step].astype(F32)
    grads16 = jnp.concatenate([r.q16_grad[...], kv16.astype(BF16)], axis=1)
    own = dot_nt(grads16, weights[:, 384:576])
    place(dot_tn(r.a_vm[...], r.qkv_grads[...]), r.main_part, last.at[:, :, pl.ds(0, 384)])
    main_ready()
    own_grad = dot_tn(r.a_vm[h.rows(h.y, h.s)], grads16)
    beside()
    gain_rows, normed_grad = [], []
    for half in range(2):
        rows = half_rows(half)
        normed_grad.append(own[rows] + sums.result(half))
        back, gains = norm_back(normed_grad[half], x[rows], r.norms[layer, 0:1])
        gain_rows.append(gains)
        in_grad = (r.mid_in[rows] + back).astype(BF16)
        r.in_grad[rows] = in_grad
        in_ready(half, in_grad)
    gain_rows, normed_grad = jnp.concatenate(gain_rows, axis=0), jnp.concatenate(normed_grad, axis=0)

    def finish():
        sums_of_rows = columns(0, gain_rows, normed_grad) + r.norm2_in[...].reshape(D, 64).astype(F32)
        side = jnp.concatenate([own_grad, sums_of_rows], axis=1)
        place(side, r.side_part, last.at[:, :, pl.ds(384, 256)])
        side_ready()

    return finish


def send_out(h, r, out, layer, arrive, arrive_last):
    group = 2 * h.y + h.s
    for i in range(8):
        tile = 8 * group + i
        to = tile // 17
        h.send_or_keep(
            out.at[i], r.out_sum.at[lax.rem(tile, 17)], (layer, h.c, to), (h.s == layer) & (to == h.y), arrive)
    h.send_or_keep(
        out.at[pl.ds(8, 4)], r.last_in.at[group], (layer, h.c, SHARD - 1), (h.s == layer) & (h.y == SHARD - 1),
        arrive_last)


def back_kernel(at, kept, saved, x, above, norms, first, attended16, mid_all, mid_last):
    def body(r):
        h = Here(r.sems)
        tail_loads = load_tiles(h, r.up_all, r.up_last, r.qkv_vm, SHARD)
        tail_loads.append(h.local(r.a_full, r.a_vm))
        loads = load_layer(h, r, 0, 0)
        loads += [h.local(r.b_full, r.b_vm), h.local(r.pre, r.pre_vm), h.local(r.context, r.context_vm)]
        h.barrier()
        sort_grads(r)
        arrive_out, arrive_last = h.sem(), h.sem()
        x, z = h.c // 4, lax.rem(h.c, 4)
        ups = [
            Reduce16(h, None, (None, (r.up_mine_a, r.up_mine_b)[i], r.ups_second.at[i]), i == 0) for i in range(2)]
        main = Reduce16(h, r.main_part, r.main_sums, False)
        side = Reduce16(h, r.side_part, r.side_sums, True)
        up0 = Reduce16(h, r.up_grad, (r.up0_in, r.up0_mine, None), True)
        rows16 = Rows16(h, r, 1)
        first_rows = FirstRows(h, r)
        h.ready()
        for each in ups:
            each.send_on()
        rows16.start()
        send_out(h, r, r.out1_g, 1, arrive_out, arrive_last)
        waits = start_tail(h, r)

        def settle(core):
            @pl.when(h.s == core)
            def _():
                @pl.when(h.y < SHARD - 1)
                def _():
                    wait_bytes(r.out_sum, arrive_out)

                @pl.when(h.y == SHARD - 1)
                def _():
                    wait_bytes(r.out_sum.at[pl.ds(0, 13)], arrive_out)
                    wait_bytes(r.last_in, arrive_last)
                    r.out_sum[13:] = added([r.last_in[g] for g in range(8)])

        arrive_up = h.sem()
        spreads = [Spread16(h, parts, i == 0, 1) for i, parts in enumerate((r.up_low, r.up_high))]

        def arrived():
            for i in range(2):
                r.up1_piece[2 * i : 2 * i + 2] = ups[i].result()
            send_piece(h, r.up1_piece, r.up_in, 1, arrive_up)
            settle(1)
            rows16.start_out()

        def beside_sums():
            rows16.middle()

            @pl.when(h.s == 1)
            def _():
                wait_bytes(r.up_in, arrive_up)
                rows = joined_up([r.up_in[g] for g in range(8)])
                for i, parts in enumerate((r.up_low, r.up_high)):
                    parts[x, z] = rows[:, 2176 * i : 2176 * i + 2176]

            for each in spreads:
                each.start()

        gather = Gather8(h, r.m_full)
        finish = run_tail(
            h, r, 1, r.x[...].astype(F32), waits, tail_loads, r.qkv_g_last, main.start, side.start,
            arrived, beside_sums, lambda half, value: gather.start(value, half))
        finish()
        rows16.spread()
        for copy in loads:
            copy.wait()
        sums = Scatter8(h, r.to_norm2)
        for step in ORDER:
            if step:
                gather.relay(step)
            gather.wait(step)
            rows = block_rows(h, step)
            u = r.pre_vm[rows]
            back_block(h, r, rows, sums, step, u, gelu(u).astype(BF16))
            if step == 0:
                for each in spreads:
                    each.middle()
            if step == 1:
                rows16.spread_on()
        sums.relay((1, 3, 2))
        def down_ready(rows):
            first_rows.load(rows)
            main.middle()
            side.middle()

        def up_ready():
            up0.start()
            first_rows.start()

        def beside():
            r.qkv1_piece[:, :, :384] = main.result()
            r.qkv1_piece[:, :, 384:] = side.result()

        def near_end():
            send_out(h, r, r.out_g, 0, arrive_out, arrive_last)
            up0.add()
            first_rows.add()
            for each in spreads:
                each.finish()
            h.save_on(1, r.up_low, r.up_low_all)
            h.save_on(1, r.up_high, r.up_high_all)

        finish_back(
            h, r, sums, 0, r.residual[...], r.in_grad[...].astype(F32), r.context_vm, down_ready, up_ready, beside, near_end)
        rows16.finish()

        settle(0)
        h.finish()

    ins = dict(
        **tail_ins(at, kept, saved, kept.a_full, x, above, norms), pre=(kept.pre, ANY), b_full=(kept.b_full, ANY),
        context=(kept.context, ANY), residual=(kept.residual, VMEM), attended16=(attended16, VMEM),
        out_w=(first.out_w, ANY), down_w=(first.down_w, ANY), up_all=(mid_all, ANY), up_last=(mid_last, ANY),
        up_mine_a=(above.up_mine_a, VMEM), up_mine_b=(above.up_mine_b, VMEM), out1_g=(above.out_g, VMEM),
        mine_a=(above.next_a, VMEM), mine_b=(above.next_b, VMEM), mine_beside=(above.next_beside, VMEM))
    piece, half = (spec((SHARD, 16, WINDOW)), VMEM), (spec((4, 4, 16, 2176)), ANY)
    outs = dict(
        **tail_outs(), **back_outs(), qkv_g_last=piece, qkv1_piece=piece, up0_mine=(spec((4, SHARD, 16, WINDOW)), VMEM),
        up_low_all=half, up_high_all=half, **rows_outs(), **rows_results(),
        **first_rows_outs(), out_sum=(spec((17, 16, D)), VMEM))
    scratch = dict(
        out_vm=VMEM((192, D), BF16), up_vm=VMEM(TILES, BF16), down_vm=VMEM((WINDOW, D), BF16),
        pre_vm=VMEM((512, WINDOW), F32), context_vm=VMEM((512, 128), BF16), out_g=VMEM((12, 16, D), BF16),
        ups_second=VMEM((2, 3, 2, 16, WINDOW), BF16), **first_rows_scratch(),
        up0_in=VMEM((3, 4, SHARD, 16, WINDOW), BF16), up_low=VMEM((4, 4, 16, 2176), BF16),
        up_high=VMEM((4, 4, 16, 2176), BF16), main_sums=reduce_scratch(SHARD, 384), side_sums=reduce_scratch(SHARD, 256),
        up1_piece=VMEM((SHARD, 16, WINDOW), BF16), up_in=VMEM((8, 16, WINDOW), BF16), last_in=VMEM((8, 4, 16, D), BF16), **tail_scratch(), **back_scratch(),
        **rows_scratch(), sems=pltpu.SemaphoreType.DMA((520,)))
    return call("back", body, ins, outs, scratch, collective_id=4)


class Plane16:
    def __init__(self, h, x_first, core=None):
        self.h, self.x_first = h, x_first
        self.on = None if core is None else h.s == core
        self.x, self.z = h.c // 4, lax.rem(h.c, 4)
        self.first = [h.sem() for _ in range(3)]
        self.second = [h.sem() for _ in range(3)]

    def when(self, act):
        act() if self.on is None else pl.when(self.on)(act)

    def chip(self, x, z):
        return (self.h.s, 4 * lax.rem(x, 4) + lax.rem(z, 4), self.h.y)

    def along(self, axis_x):
        return [self.chip(self.x + j, self.z) if axis_x else self.chip(self.x, self.z + j) for j in (1, 2, 3)]

    def send(self, pairs, targets, sems):
        copies = [
            pltpu.make_async_remote_copy(
                src_ref=src, dst_ref=dst, send_sem=self.h.sem(), recv_sem=sem, device_id=to, device_id_type=MESH)
            for (src, dst), to, sem in zip(pairs, targets, sems)]

        def start():
            for i in (0, 2, 1):
                copies[i].start()

        def wait_send():
            for copy in copies:
                copy.wait_send()

        self.when(start)
        self.h.sent.append(types.SimpleNamespace(wait_send=lambda: self.when(wait_send)))


class Reduce16(Plane16):
    def __init__(self, h, part, bufs, x_first, core=None):
        super().__init__(h, x_first, core)
        self.part = part
        self.first_in, self.mine, self.second_in = bufs

    def start(self):
        pairs = []
        for j in (1, 2, 3):
            src = self.part.at[lax.rem(self.x + j, 4)] if self.x_first else self.part.at[:, lax.rem(self.z + j, 4)]
            pairs.append((src, self.first_in.at[j - 1]))
        self.send(pairs, self.along(self.x_first), self.first)

    def add(self):
        def add():
            for j in range(3):
                wait_bytes(self.first_in.at[j], self.first[j])
            for k in range(4):
                own = self.part[self.x, k] if self.x_first else self.part[k, self.z]
                self.mine[k] = added([own] + [self.first_in[j, k] for j in range(3)])

        self.when(add)

    def send_on(self):
        at = self.z if self.x_first else self.x
        pairs = [(self.mine.at[lax.rem(at + j, 4)], self.second_in.at[j - 1]) for j in (1, 2, 3)]
        self.send(pairs, self.along(not self.x_first), self.second)

    def middle(self):
        self.add()
        self.send_on()

    def result(self):
        for j in range(3):
            wait_bytes(self.second_in.at[j], self.second[j])
        return added([self.mine[self.z if self.x_first else self.x]] + [self.second_in[j] for j in range(3)])


def reduce_scratch(units, width):
    return [VMEM((3, 4, units, 16, width), BF16), VMEM((4, units, 16, width), BF16), VMEM((3, units, 16, width), BF16)]


class Spread16(Plane16):
    def __init__(self, h, parts, x_first, core=None):
        super().__init__(h, x_first, core)
        self.parts = parts

    def start(self):
        own = self.parts.at[self.x, self.z]
        self.send([(own, own)] * 3, self.along(self.x_first), self.first)

    def middle(self):
        def wait():
            for sem in self.first:
                wait_bytes(self.parts.at[0, 0], sem)

        self.when(wait)
        line = self.parts.at[:, self.z] if self.x_first else self.parts.at[self.x]
        self.send([(line, line)] * 3, self.along(not self.x_first), self.second)

    def finish(self):
        def wait():
            for sem in self.second:
                wait_bytes(self.parts.at[0], sem)

        self.when(wait)


class FirstRows:
    def __init__(self, h, r):
        self.h, self.r = h, r
        self.sums = [
            Reduce16(h, r.rows_a, (r.rows_in.at[0], r.next_a, None), True),
            Reduce16(h, r.rows_b, (r.rows_in.at[1], r.next_b, None), False)]

    def load(self, down):
        h, r = self.h, self.r
        self.loads = [h.local(down.at[pl.ds(32, 2)], r.next_beside)]
        for x in range(4):
            for i, parts in enumerate((r.rows_a, r.rows_b)):
                self.loads += [h.local(down.at[8 * x + 2 * z + i], parts.at[x, z, 0]) for z in range(4)]

    def start(self):
        for copy in self.loads:
            copy.wait()
        for each in self.sums:
            each.start()

    def add(self):
        for each in self.sums:
            each.add()


def first_rows_outs():
    mine = (spec((4, 1, 16, D)), VMEM)
    return dict(next_a=mine, next_b=mine, next_beside=(spec((2, 16, D)), VMEM))


def first_rows_scratch():
    part = VMEM((4, 4, 1, 16, D), BF16)
    return dict(rows_a=part, rows_b=part, rows_in=VMEM((2, 3, 4, 1, 16, D), BF16))


class Rows16:
    def __init__(self, h, r, core):
        self.h, self.r, self.core = h, r, core
        self.sums = [
            Reduce16(h, None, (None, r.mine_a, r.rows_second.at[0]), True),
            Reduce16(h, None, (None, r.mine_b, r.rows_second.at[1]), False),
            Reduce16(h, r.rows_c, r.rows_sums_c, True, core)]
        self.spreads = [
            Spread16(h, r.rows_all.at[0], True), Spread16(h, r.rows_all.at[1], False), Spread16(h, r.rows_out, False, core)]
        self.arrive = h.sem()
        self.arrive_each = [h.sem() for _ in range(3)]
        self.cross = [h.sem() for _ in range(2)]

    def on(self, i):
        return self.h.s == self.core if i == 2 else None

    def when(self, i, act, also=None):
        conditions = [c for c in (self.on(i), also) if c is not None]
        if not conditions:
            return act()
        return pl.when(functools.reduce(jnp.logical_and, conditions))(act)

    def start(self):
        for i in range(2):
            self.sums[i].send_on()
            self.send_tile(self.r.mine_beside.at[i], i)

    def start_out(self):
        h, r = self.h, self.r

        @pl.when(h.s == self.core)
        def _():
            for c in range(CTX):
                r.rows_c[c // 4, c % 4, 0] = r.out_sum[c]

        self.sums[2].start()
        self.send_tile(r.out_sum.at[16], 2)

    def send_tile(self, src, i):
        h = self.h
        dst, leave = self.r.tile_in.at[h.c], h.sem()
        copy = pltpu.make_async_remote_copy(
            src_ref=src, dst_ref=dst, send_sem=leave, recv_sem=self.arrive, device_id=(h.s, 5 * i, h.y),
            device_id_type=MESH)
        kept = pltpu.make_async_copy(src, dst, self.arrive)
        self.when(i, copy.start, h.c != 5 * i)
        self.when(i, kept.start, h.c == 5 * i)
        h.sent.append(types.SimpleNamespace(
            wait_send=functools.partial(self.when, i, copy.wait_send, h.c != 5 * i)))

    def middle(self):
        self.sums[2].middle()

    def spread(self):
        h, r = self.h, self.r
        x, z = h.c // 4, lax.rem(h.c, 4)
        r.rows_all[0, x, z] = self.sums[0].result()
        r.rows_all[1, x, z] = self.sums[1].result()

        def out():
            r.rows_out[x, z] = self.sums[2].result()

        self.when(2, out)
        for each in self.spreads:
            each.start()
        for i in range(3):
            copies = [
                pltpu.make_async_remote_copy(
                    src_ref=r.tiles.at[i], dst_ref=r.tiles.at[i], send_sem=h.sem(), recv_sem=self.arrive_each[i],
                    device_id=(h.s, lax.rem(h.c + step, CTX), h.y), device_id_type=MESH)
                for step in range(1, CTX)]

            def start(i=i, copies=copies):
                wait_bytes(r.tile_in, self.arrive)
                r.tiles[i] = added([r.tile_in[c] for c in range(CTX)])
                for copy in copies:
                    copy.start()

            def wait_send(copies=copies):
                for copy in copies:
                    copy.wait_send()

            self.when(i, start, h.c == 5 * i)
            h.sent.append(types.SimpleNamespace(
                wait_send=functools.partial(self.when, i, wait_send, h.c == 5 * i)))

    def spread_on(self):
        for each in self.spreads:
            each.middle()

    def finish(self):
        h, r = self.h, self.r
        for each in self.spreads:
            each.finish()
        for i in range(3):
            self.when(i, functools.partial(wait_bytes, r.tiles.at[i], self.arrive_each[i]), h.c != 5 * i)
        copies = [
            pltpu.make_async_remote_copy(
                src_ref=src, dst_ref=dst, send_sem=h.sem(), recv_sem=sem, device_id=h.sibling(), device_id_type=MESH)
            for src, dst, sem in (
                (r.rows_all, r.rows_other, self.cross[0]),
                (r.tiles.at[pl.ds(0, 2)], r.tiles_other, self.cross[1]))]

        @pl.when(h.s != self.core)
        def _():
            for copy in copies:
                copy.start()

        h.save_on(self.core, r.rows_all, r.rows_own)
        h.save_on(self.core, r.rows_out, r.rows_out_all)

        @pl.when(h.s != self.core)
        def _():
            for copy in copies:
                copy.wait_send()

        @pl.when(h.s == self.core)
        def _():
            wait_bytes(r.rows_other, self.cross[0])
            wait_bytes(r.tiles_other, self.cross[1])

        h.save_on(self.core, r.rows_other, r.rows_cross)


def rows_outs():
    return dict(tiles=(spec((3, 16, D)), VMEM), tiles_other=(spec((2, 16, D)), VMEM))


def rows_scratch():
    part = VMEM((4, 4, 1, 16, D), BF16)
    return dict(
        rows_c=part, rows_sums_c=reduce_scratch(1, D), rows_second=VMEM((2, 3, 1, 16, D), BF16),
        tile_in=VMEM((CTX, 16, D), BF16), rows_all=VMEM((2, 4, 4, 1, 16, D), BF16), rows_out=part,
        rows_other=VMEM((2, 4, 4, 1, 16, D), BF16))


def rows_results():
    whole_rows = (spec((2, 4, 4, 1, 16, D)), ANY)
    return dict(rows_own=whole_rows, rows_cross=whole_rows, rows_out_all=(spec((4, 4, 1, 16, D)), ANY))


def send_piece(h, piece, dst, layer, arrive):
    for step in (1, 3, 2, 0):
        shard = h.shard(step)
        h.send_or_keep(
            piece.at[shard], dst.at[2 * h.y + h.s], (layer, h.c, shard), (h.s == layer) & (step == 0), arrive)


def joined_up(windows):
    parts = []
    for g in range(8):
        main = windows[g][:, :512]
        if g % 4:
            main = jnp.concatenate([main[:, :128] + windows[g - 1][:, 512:], main[:, 128:]], axis=1)
        parts.append(main)
        if g % 4 == 3:
            parts.append(windows[g][:, 512:])
    return jnp.concatenate(parts, axis=1)


def joined_qkv(blocks, own):
    queries = [blocks[g][:, :128] for g in range(8)] + [own[:, :64]]
    keys = [blocks[g][:, a : a + 64] for g in range(8) for a in (128, 256)] + [own[:, 64:128]]
    values = [blocks[g][:, a : a + 64] for g in range(8) for a in (192, 320)] + [own[:, 128:192]]
    return jnp.concatenate(queries + keys + values + [own[:, 192:]], axis=1)


def added(blocks):
    total = blocks[0].astype(F32)
    for block in blocks[1:]:
        total = total + block.astype(F32)
    return total.astype(BF16)


def last_kernel(at, kept, saved, hidden, above, turn_up_last, norms):
    def body(r):
        h = Here(r.sems)
        x, z = h.c // 4, lax.rem(h.c, 4)
        group = 2 * h.y + h.s
        loads = [h.local(r.qkv_w, r.qkv_vm), h.local(r.a_full, r.a_vm)]
        h.barrier()
        sort_grads(r)
        h.ready()
        up0 = Reduce16(h, None, (None, r.up0_mine, r.up0_in), True)
        up0.send_on()
        main = Reduce16(h, r.main_part, r.main_sums, True)
        side = Reduce16(h, r.side_part, r.side_sums, False)
        arrive_wide = h.sem()
        send_piece(h, r.qkv1_piece, r.wide_in, 1, arrive_wide)
        rows16 = Rows16(h, r, 0)
        rows16.start()
        rows16.start_out()
        arrive_last, arrive_late = h.sem(), h.sem()
        for i in range(SHARD):
            chip = 4 * i + h.y
            r.last_message[i, 0] = r.up_last[i]
            r.last_message[i, 1] = r.up1_last[i]
            r.last_message[i, 2] = r.qkv1_last[i]
            h.send_or_keep(r.last_message.at[i], r.last_in.at[h.c], (h.s, chip, h.y), chip == h.c, arrive_last)
        waits = start_tail(h, r)
        wide = [Spread16(h, parts, i == 0) for i, parts in enumerate((r.wide_low, r.wide_high))]

        def spread_wide():
            wait_bytes(r.wide_in, arrive_wide)
            blocks = [r.wide_in[g] for g in range(8)]

            @pl.when(h.s == 0)
            def _():
                rows = joined_up(blocks)
                r.wide_low[x, z] = rows[:, :2176]
                r.wide_high[x, z] = rows[:, 2176:]

            @pl.when(h.s == 1)
            def _():
                rows = joined_qkv(blocks, added([block[:, 384:] for block in blocks]))
                r.wide_low[x, z] = rows[:, :2176]
                r.wide_high[x, z] = jnp.concatenate([rows[:, 2176:], jnp.zeros((16, 1024), BF16)], axis=1)

            for each in wide:
                each.start()

        def arrived():
            rows16.middle()
            r.up0_piece[...] = up0.result()
            send_piece(h, r.up0_piece, r.wide_in, 0, arrive_wide)

        def beside():
            rows16.spread()
            spread_wide()

        finish = run_tail(
            h, r, 0, r.x[h.s].astype(F32), waits, loads, r.qkv_last, main.start, side.start, arrived, beside,
            lambda half, value: None)
        finish()
        for i in range(SHARD):
            chip = 4 * i + h.y
            h.send_or_keep(r.qkv_last.at[i], r.late_in.at[h.c], (h.s, chip, h.y), chip == h.c, arrive_late)
        main.middle()
        side.middle()
        for each in wide:
            each.middle()
        rows16.spread_on()
        arrive_rest = h.sem()
        reduces = z == h.y

        @pl.when(reduces)
        def _():
            wait_bytes(r.last_in, arrive_last)
            wait_bytes(r.late_in, arrive_late)
            early = added([r.last_in[c] for c in range(CTX)])
            r.rest_message[0, 0] = early[0]
            r.rest_message[0, 1] = added([r.late_in[c] for c in range(CTX)])
            r.rest_message[1] = early[1:]

        rest = []
        for layer in range(2):
            leave = h.sem()
            src, dst = r.rest_message.at[layer], r.rest.at[z, h.s]
            copy = pltpu.make_async_remote_copy(
                src_ref=src, dst_ref=dst, send_sem=leave, recv_sem=arrive_rest, device_id=(layer, h.c, x),
                device_id_type=MESH)
            kept = pltpu.make_async_copy(src, dst, arrive_rest)
            is_self = (h.s == layer) & (x == h.y)
            pl.when(reduces & is_self)(kept.start)
            away = reduces & jnp.logical_not(is_self)
            pl.when(away)(copy.start)
            rest.append((away, copy))
        r.qkv_piece[:, :, :384] = main.result()
        r.qkv_piece[:, :, 384:] = side.result()
        arrive_qkv = h.sem()
        send_piece(h, r.qkv_piece, r.qkv_in, 0, arrive_qkv)
        owner = x == h.y
        across = [h.sem() for _ in range(4)]
        along = [h.sem() for _ in range(3)]
        line = r.rest.at[z]
        lines = []
        for j in range(1, 4):
            lines.append(pltpu.make_async_remote_copy(
                src_ref=line, dst_ref=line, send_sem=across[j], recv_sem=across[0],
                device_id=(h.s, 4 * lax.rem(x + j, 4) + z, h.y), device_id_type=MESH))

        @pl.when(owner)
        def _():
            wait_bytes(line, arrive_rest)
            for copy in lines:
                copy.start()

        spreads = [Spread16(h, parts, i == 0, 0) for i, parts in enumerate((r.qkv_low, r.qkv_high))]

        @pl.when(h.s == 0)
        def _():
            wait_bytes(r.qkv_in, arrive_qkv)
            blocks = [r.qkv_in[g] for g in range(8)]
            rows = joined_qkv(blocks, added([block[:, 384:] for block in blocks]))
            r.qkv_low[x, z] = rows[:, :1664]
            r.qkv_high[x, z] = rows[:, 1664:]

        for each in spreads:
            each.start()
        for each in wide:
            each.finish()
        h.save(r.wide_low, r.wide_low_all)
        h.save(r.wide_high, r.wide_high_all)

        @pl.when(jnp.logical_not(owner))
        def _():
            wait_bytes(line, across[0])

        for j in range(1, 4):
            h.send(line, line, (h.s, 4 * x + lax.rem(z + j, 4), h.y), along[j - 1])
        for each in spreads:
            each.middle()
        rows16.finish()
        for sem in along:
            wait_bytes(line, sem)
        r.up_rest[...] = joined_up([r.rest[g // 2, g % 2, 0] for g in range(8)])
        blocks = [r.rest[g // 2, g % 2, 1] for g in range(8)]
        r.qkv_rest[...] = joined_qkv(blocks, added([block[:, 384:] for block in blocks]))
        for each in spreads:
            each.finish()
        h.save_on(0, r.qkv_low, r.qkv_low_all)
        h.save_on(0, r.qkv_high, r.qkv_high_all)

        @pl.when(owner)
        def _():
            for copy in lines:
                copy.wait_send()

        for away, copy in rest:
            pl.when(away)(copy.wait_send)
        h.finish()

    ins = dict(
        **tail_ins(at, kept, saved, kept.a_full, hidden, above, norms), qkv_w=(kept.qkv_w, ANY), up0_mine=(above.up0_mine, VMEM),
        qkv1_piece=(above.qkv1_piece, VMEM), up_last=(above.up_g_last, VMEM), qkv1_last=(above.qkv_g_last, VMEM),
        up1_last=(turn_up_last, VMEM), mine_a=(above.next_a, VMEM), mine_b=(above.next_b, VMEM), mine_beside=(above.next_beside, VMEM),
        out_sum=(above.out_sum, VMEM))
    up_half, qkv_half = (spec((4, 4, 16, 2176)), ANY), (spec((4, 4, 16, 1664)), ANY)
    outs = dict(
        **tail_outs(), wide_low_all=up_half, wide_high_all=up_half, qkv_low_all=qkv_half, qkv_high_all=qkv_half,
        up_rest=(spec((16, FF)), VMEM), qkv_rest=(spec((16, 3328)), VMEM), **rows_outs(), **rows_results())
    piece, eight = VMEM((SHARD, 16, WINDOW), BF16), VMEM((8, 16, WINDOW), BF16)
    scratch = dict(
        **tail_scratch(),
        main_sums=reduce_scratch(SHARD, 384), side_sums=reduce_scratch(SHARD, 256), **rows_scratch(), wide_low=VMEM((4, 4, 16, 2176), BF16), wide_high=VMEM((4, 4, 16, 2176), BF16),
        qkv_low=VMEM((4, 4, 16, 1664), BF16), qkv_high=VMEM((4, 4, 16, 1664), BF16), qkv_piece=piece, qkv_last=piece, last_message=VMEM((SHARD, 3, 16, WINDOW), BF16),
        last_in=VMEM((CTX, 3, 16, WINDOW), BF16), late_in=VMEM((CTX, 16, WINDOW), BF16), wide_in=eight, qkv_in=eight, up0_piece=piece,
        up0_in=VMEM((3, SHARD, 16, WINDOW), BF16),
        rest_message=VMEM((2, 2, 16, WINDOW), BF16), rest=VMEM((4, 2, 2, 16, WINDOW), BF16),
        sems=pltpu.SemaphoreType.DMA((440,)))
    return call("last", body, ins, outs, scratch, collective_id=5)


def join_kernel(back, last):
    def body(
        _, up_low, up_high, wide_low, wide_high, qkv_low, qkv_high, own0, cross0, out0, own1, cross1, out1, up_rest, qkv_rest,
        tiles0, tiles_other0, tiles1, tiles_other1, up_ref, qkv_ref, norm_ref, down_ref, out_ref):
        def store(rows, up_parts, qkv_parts):
            for at, block in up_parts:
                up_ref[:rows, at : at + block.shape[1]] = block.astype(F32)
            for at, block in qkv_parts:
                block = block.astype(F32)
                if at + block.shape[1] == 3328:
                    norm_ref[:rows] = block[:, -128:]
                    block = block[:, :-64]
                qkv_ref[:rows, at : at + block.shape[1]] = block

        def rows_from(halves, out, tiles):
            @pl.when(pl.program_id(0) < 4)
            def _():
                for c in range(4):
                    for i in range(2):
                        for half in range(2):
                            at = 32 * c + 16 * i
                            down_ref[half, at : at + 16] = halves[half][i, 0, c, 0].astype(F32)
                    out_ref[16 * c : 16 * c + 16] = out[0, c, 0].astype(F32)

            @pl.when(pl.program_id(0) == 4)
            def _():
                for half in range(2):
                    down_ref[half, :32] = tiles[half][:2].reshape(32, D).astype(F32)
                out_ref[:16] = tiles[2].astype(F32)

        first = lax.axis_index(SECTION) == 0
        pl.when(first)(lambda: rows_from((own0, cross0), out0, (tiles0, tiles_other0, tiles0[2])))
        pl.when(jnp.logical_not(first))(
            lambda: rows_from((cross1, own1), out1, (tiles_other1, tiles1, tiles1[2])))
        low, high = (ref[0].reshape(64, 2176) for ref in (wide_low, wide_high))

        @pl.when((pl.program_id(0) < 4) & first)
        def _():
            parts = [ref[0].reshape(64, 1664) for ref in (qkv_low, qkv_high)]
            store(64, ((0, low), (2176, high)), ((0, parts[0]), (1664, parts[1])))

        @pl.when((pl.program_id(0) < 4) & jnp.logical_not(first))
        def _():
            parts = [ref[0].reshape(64, 2176) for ref in (up_low, up_high)]
            store(64, ((0, parts[0]), (2176, parts[1])), ((0, low), (2176, high[:, :1152])))

        @pl.when(pl.program_id(0) == 4)
        def _():
            store(16, ((0, up_rest[...]),), ((0, qkv_rest[...]),))

    def place(i, section, core):
        return jnp.where((core < 0) | (section[0] == core), jnp.minimum(i, 3), 0)

    def line(width, core):
        return pl.BlockSpec((1, 4, 16, width), lambda i, section: (place(i, section, core), 0, 0, 0))

    def tile_line(core, *lead):
        zeros = (0,) * len(lead)
        return pl.BlockSpec(
            (*lead, 1, 4, 1, 16, D), lambda i, section: (*zeros, place(i, section, core), 0, 0, 0, 0))

    def tiles_of(count):
        return pl.BlockSpec((count, 16, D), lambda i, section: (0, 0, 0))

    def rows(width, count=64):
        return pl.BlockSpec((count, width), lambda i, section: (i, 0))

    def all_of(width):
        return pl.BlockSpec((16, width), lambda i, section: (0, 0))

    return pl.pallas_call(
        body,
        out_shape=(
            spec((SLICE, FF), F32), spec((SLICE, 3 * D), F32), spec((SLICE, 128), F32), spec((2, 544, D), F32),
            spec((SLICE, D), F32)),
        grid_spec=pltpu.PrefetchScalarGridSpec(
            num_scalar_prefetch=1,
            grid=(5,),
            in_specs=[
                line(2176, 1), line(2176, 1), line(2176, -1), line(2176, -1), line(1664, 0), line(1664, 0),
                tile_line(0, 2), tile_line(0, 2), tile_line(0), tile_line(1, 2), tile_line(1, 2), tile_line(1),
                all_of(FF), all_of(3328), *[tiles_of(3), tiles_of(2)] * 2],
            out_specs=(
                rows(FF), rows(3 * D), rows(128), pl.BlockSpec((2, 128, D), lambda i, section: (0, i, 0)), rows(D))),
        name="join",
    )(lax.axis_index(SECTION).astype(jnp.int32).reshape(1), back.up_low_all, back.up_high_all, last.wide_low_all, last.wide_high_all, last.qkv_low_all, last.qkv_high_all, last.rows_own,
      last.rows_cross, last.rows_out_all, back.rows_own, back.rows_cross, back.rows_out_all, last.up_rest, last.qkv_rest,
      last.tiles, last.tiles_other, back.tiles, back.tiles_other)


def token_positions(block_order):
    offsets = jnp.arange(32, dtype=jnp.int32)
    groups = jnp.arange(2, dtype=jnp.int32)[:, None, None] * GROUP
    return (groups + block_order[:, :, None] * 32 + offsets).reshape(2, GROUP)


def swapped(section, first, second):
    own = jnp.where(section == 0, first, second)
    other = lax.ppermute(jnp.where(section == 0, second, first), SECTION, [(0, 1), (1, 0)])
    return jnp.where(section == 0, own, other), jnp.where(section == 0, other, own)


def gathered(x):
    return lax.all_gather(x, CONTEXT)


def shards(hidden_in, cotangent, block_order, qkv_weight, out_weight, up_weight, down_weight, norm_gains, norm_biases):
    section, ctx = lax.axis_index(SECTION), lax.axis_index(CONTEXT)
    params = jnp.concatenate([norm_gains[0], norm_biases[0]], axis=0).astype(F32)
    params = jnp.pad(params, ((0, 4), (0, 0)))
    grid = token_positions(block_order)
    own_positions = lax.dynamic_slice(grid, (section, ctx * ROWS), (1, ROWS))
    positions = grid.reshape(1, SEQ)
    slots = jnp.arange(32, dtype=jnp.int32)
    slot = jnp.sum(jnp.where(block_order[:, None, :] == slots[None, :, None], slots[None, None, :], 0), axis=2)
    group, odd = jnp.arange(2, dtype=jnp.int32)[:, None], slot % 2
    chip = slot // 2
    places = jnp.stack([10 * chip + 4 * group + 2 * odd, 10 * chip + 8 + odd, 2 * chip + odd])
    at = (block_order, places, positions, own_positions.reshape(ROWS, 1))
    at_back = (block_order, places, positions.reshape(SEQ, 1), own_positions)
    hidden = hidden_in[0]
    spread = spread_kernel(params, qkv_weight, up_weight)
    norms = spread.norms
    mid_all = gathered(spread.mid_piece)
    first = first_kernel(hidden, norms, spread.side_piece, spread.side_last, out_weight, down_weight)
    up_piece, first.q16 = lax.optimization_barrier((spread.side_piece[SHARD:], first.q16))
    up_all = gathered(up_piece)
    middle = middle_kernel(at, hidden, norms, first, mid_all, spread.mid_last)
    turn = turn_kernel(at, middle, middle.y, norms, first, up_all, spread.side_last[SHARD:], cotangent[0])
    back = back_kernel(
        at_back, middle, turn, middle.y, turn, norms, first, middle.attended16, mid_all, spread.mid_last)
    last = last_kernel(at_back, first, middle, hidden, back, turn.up_g_last, norms)
    up, qkv, norm_sums, down, out = join_kernel(back, last)
    norm_sums = norm_sums[:, 64:68].T
    activations = jnp.stack(swapped(section, middle.y, turn.out))
    input_grads = jnp.stack(swapped(section, last.in_grad, back.in_grad))
    return (
        activations[None, None],
        input_grads[None, None],
        qkv[None],
        out[None],
        up[None],
        down.reshape(D, D)[None],
        norm_sums[None, 0::2],
        norm_sums[None, 1::2],
    )


def solution(mesh):
    tokens = P(LINE, None, CONTEXT, None)
    rows = P(SECTION, LINE, None)
    norms = P(SECTION, None, LINE)
    layers = P(SECTION, LINE, None, CONTEXT, None)
    return jax.shard_map(
        shards,
        mesh=mesh,
        in_specs=(tokens, tokens, P(), rows, rows, rows, rows, norms, norms),
        out_specs=(layers, layers, rows, rows, rows, rows, norms, norms),
        check_vma=False,
    )
```

```python
import functools
import types

import jax
import jax.numpy as jnp
from jax import lax
from jax.experimental import pallas as pl
from jax.experimental.pallas import tpu as pltpu
from jax.sharding import PartitionSpec as P

D = 1088
HEADS = 17
HEAD_DIM = 64
FF = 4352
SHARD = 4
CTX = 16
ROWS = 64
GROUP = 1024
SEQ = 2048
WINDOW = 640
SLICE = D // SHARD
EPSILON = 1e-05
NEG_LARGE = -1e30
BF16 = jnp.bfloat16
F32 = jnp.float32
MESH = pl.DeviceIdType.MESH
VMEM = pltpu.VMEM
ANY = pl.ANY
VMEM_BYTES = 58 * 2**20
SECTION, CONTEXT, LINE = "section", "ctx", "shard"
TILES = (68, 16, WINDOW)


def spec(shape, dtype=BF16):
    return jax.ShapeDtypeStruct(shape, dtype)


def call(name, body, ins, outs, scratch, collective_id=None):
    def kernel(*refs):
        refs, found = list(refs), {}
        for key, value in [*ins.items(), *outs.items(), *scratch.items()]:
            if isinstance(value, list):
                found[key], refs = refs[: len(value)], refs[len(value) :]
            else:
                found[key] = refs.pop(0)
        body(types.SimpleNamespace(**found))

    extra = {} if collective_id is None else dict(collective_id=collective_id, has_side_effects=True)
    shapes, given = [], []
    for value in scratch.values():
        shapes += value if isinstance(value, list) else [value]
    for value in ins.values():
        given += value if isinstance(value, list) else [value]
    results = pl.pallas_call(
        kernel,
        out_shape=tuple(value[0] for value in outs.values()),
        in_specs=[pl.BlockSpec(memory_space=space) for _, space in given],
        out_specs=tuple(pl.BlockSpec(memory_space=value[1]) for value in outs.values()),
        scratch_shapes=shapes,
        compiler_params=pltpu.CompilerParams(vmem_limit_bytes=VMEM_BYTES, **extra),
        name=name,
    )(*(array for array, _ in given))
    return types.SimpleNamespace(**dict(zip(outs, results)))


def dot(a, b):
    return jnp.dot(a, b, preferred_element_type=F32)


def dot_nt(a, b):
    return lax.dot_general(a, b, (((1,), (1,)), ((), ())), preferred_element_type=F32)


def dot_tn(a, b):
    return lax.dot_general(a, b, (((0,), (0,)), ((), ())), preferred_element_type=F32)


def norm_parts(values):
    center = values - jnp.mean(values, axis=-1, keepdims=True)
    rate = lax.rsqrt(jnp.mean(center * center, axis=-1, keepdims=True) + EPSILON)
    return center * rate, rate


def layer_norm(values, gain, bias):
    return norm_parts(values)[0] * gain + bias


def gelu(u):
    return 0.5 * u * (1.0 + jnp.tanh(0.7978845608028654 * (u + 0.044715 * u * u * u)))


class Here:
    def __init__(self, sems):
        self.s = lax.axis_index(SECTION)
        self.c = lax.axis_index(CONTEXT)
        self.y = lax.axis_index(LINE)
        self.sems, self.used, self.sent = sems, 0, []

    def sem(self):
        self.used += 1
        return self.sems.at[self.used - 1]

    def shard(self, step):
        return lax.rem(self.y + step, SHARD)

    def rows(self, shard, core):
        return pl.ds(pl.multiple_of((shard * 2 + core) * ROWS, ROWS), ROWS)

    def barrier(self, whole=True):
        sem = pltpu.get_barrier_semaphore()
        peers = []
        for step in range(SHARD):
            for core in range(2):
                if step or core:
                    peers.append((lax.rem(self.s + core, 2), self.c, self.shard(step)))
        for step in range(1, CTX if whole else 1):
            for core in range(2):
                peers.append((core, lax.rem(self.c + step, CTX), self.y))
        for to in peers:
            pl.semaphore_signal(sem, inc=1, device_id=to, device_id_type=MESH)
        self.awaited = len(peers)

    def ready(self):
        pl.semaphore_wait(pltpu.get_barrier_semaphore(), self.awaited)

    def save_on(self, core, src, dst):
        copy = pltpu.make_async_copy(src, dst, self.sem())
        pl.when(self.s == core)(copy.start)
        self.sent.append(types.SimpleNamespace(wait_send=lambda: pl.when(self.s == core)(copy.wait)))

    def local(self, src, dst):
        copy = pltpu.make_async_copy(src, dst, self.sem())
        copy.start()
        return copy

    def save(self, src, dst):
        copy = self.local(src, dst)
        self.sent.append(types.SimpleNamespace(wait_send=copy.wait))

    def wait_later(self, ref, sem):
        self.sent.append(types.SimpleNamespace(wait_send=lambda: wait_bytes(ref, sem)))

    def send(self, src, dst, to, arrive, leave=None):
        copy = pltpu.make_async_remote_copy(
            src_ref=src, dst_ref=dst, send_sem=self.sem() if leave is None else leave,
            recv_sem=arrive, device_id=to, device_id_type=MESH)
        copy.start()
        if leave is None:
            self.sent.append(copy)
        return copy

    def send_or_keep(self, src, dst, to, is_self, arrive):
        leave = self.sem()
        copy = pltpu.make_async_remote_copy(
            src_ref=src, dst_ref=dst, send_sem=leave, recv_sem=arrive, device_id=to, device_id_type=MESH)
        kept = pltpu.make_async_copy(src, dst, arrive)
        pl.when(jnp.logical_not(is_self))(copy.start)
        pl.when(is_self)(kept.start)

        def wait_send():
            pl.when(jnp.logical_not(is_self))(copy.wait_send)

        self.sent.append(types.SimpleNamespace(wait_send=wait_send))

    def sibling(self):
        return (1 - self.s, self.c, self.y)

    def finish(self):
        for copy in self.sent:
            copy.wait_send()
        self.sent = []


def wait_bytes(ref, sem):
    pltpu.make_async_copy(ref, ref, sem).wait()


PARTS = 2
HALF = ROWS // PARTS


def half_rows(half):
    return slice(HALF * half, HALF * half + HALF)


class Messages:
    def __init__(self, h, arrived):
        self.h, self.arrived, self.leave = h, arrived, h.sem()

    def add(self, sends):
        for src, dst, to, here, arrive in sends:
            copy = pltpu.make_async_remote_copy(
                src_ref=src, dst_ref=dst, send_sem=self.leave, recv_sem=arrive, device_id=to, device_id_type=MESH)
            pl.when(jnp.logical_not(here))(copy.start)
            pl.when(here)(pltpu.make_async_copy(src, dst, arrive).start)

    def done(self):
        h = self.h

        def wait_send():
            pl.when(h.c // 8 != h.s)(lambda: wait_bytes(self.arrived, self.leave))
            pl.when(h.c // 8 == h.s)(lambda: wait_bytes(self.arrived.at[pl.ds(0, 15)], self.leave))

        h.sent.append(types.SimpleNamespace(wait_send=wait_send))


class Gather8:
    def __init__(self, here, full):
        self.here, self.full = here, full
        self.own = [[here.sem() for _ in range(PARTS)] for _ in range(SHARD)]
        self.other = [[here.sem() for _ in range(PARTS)] for _ in range(SHARD)]
        self.leave = here.sem()
        here.wait_later(full.at[pl.ds(0, 7 * ROWS)], self.leave)

    def rows(self, shard, core, half):
        return self.full.at[pl.ds(pl.multiple_of((shard * 2 + core) * ROWS + half * HALF, HALF), HALF)]

    def start(self, value, half):
        h = self.here
        mine = self.rows(h.y, h.s, half)
        mine[...] = value
        h.send(mine, mine, h.sibling(), self.other[0][half], self.leave)
        for step in (1, 3, 2):
            h.send(mine, mine, (h.s, h.c, h.shard(step)), self.own[SHARD - step][half], self.leave)

    def relay(self, step):
        h = self.here
        for half in range(PARTS):
            part = self.rows(h.shard(step), h.s, half)
            wait_bytes(part, self.own[step][half])
            h.send(part, part, h.sibling(), self.other[step][half], self.leave)

    def wait(self, step):
        h = self.here
        for half in range(PARTS):
            wait_bytes(self.rows(h.shard(step), 1 - h.s, half), self.other[step][half])


class Scatter8:
    def __init__(self, here, bufs):
        self.here = here
        self.to_core, self.mine, self.from_core, self.to_shard, self.from_shard = bufs
        self.core = [[here.sem() for _ in range(PARTS)] for _ in range(SHARD)]
        self.shard = [[here.sem() for _ in range(PARTS)] for _ in range(SHARD)]
        self.leave = [here.sem(), here.sem()]
        here.wait_later(self.from_core, self.leave[0])
        here.wait_later(self.from_shard.at[pl.ds(0, 3)], self.leave[1])

    def part(self, ref, step, half):
        return ref.at[step, pl.ds(half * HALF, HALF)]

    def put(self, step, block):
        h = self.here
        low, high = block[:ROWS], block[ROWS:]
        self.to_core[step] = jnp.where(h.s == 0, high, low).astype(BF16)
        self.mine[step] = jnp.where(h.s == 0, low, high)
        for half in range(PARTS):
            h.send(
                self.part(self.to_core, step, half), self.part(self.from_core, step, half), h.sibling(),
                self.core[step][half], self.leave[0])

    def relay(self, steps):
        h = self.here
        for half in range(PARTS):
            for step in steps:
                part = self.part(self.from_core, step, half)
                wait_bytes(part, self.core[step][half])
                total = self.mine[step, half_rows(half)] + part[...].astype(F32)
                out = self.part(self.to_shard, step, half)
                out[...] = total.astype(BF16)
                h.send(
                    out, self.part(self.from_shard, step, half), (h.s, h.c, h.shard(step)), self.shard[step][half],
                    self.leave[1])

    def result(self, half):
        part = self.part(self.from_core, 0, half)
        wait_bytes(part, self.core[0][half])
        total = self.mine[0, half_rows(half)] + part[...].astype(F32)
        for step in (1, 3, 2):
            part = self.part(self.from_shard, step, half)
            wait_bytes(part, self.shard[step][half])
            total = total + part[...].astype(F32)
        return total


def scatter_scratch():
    quarter = (SHARD, ROWS, D)
    return [VMEM(quarter, BF16), VMEM(quarter, F32), VMEM(quarter, BF16), VMEM(quarter, BF16), VMEM(quarter, BF16)]


ORDER = (0, 1, 3, 2)


def window_offset(group):
    return 32 * lax.rem(group, 4)


def everyone(h):
    for step in (1, 3, 2, 0):
        for other in range(2):
            yield step, other, (lax.rem(h.s + other, 2), h.c, h.shard(step))


def packed_qkv(rows, g):
    keys = rows[:, D + 128 * g : D + 128 * g + 128]
    values = rows[:, 2 * D + 128 * g : 2 * D + 128 * g + 128]
    return jnp.concatenate([
        rows[:, 128 * g : 128 * g + 128], keys[:, :64], values[:, :64], keys[:, 64:], values[:, 64:],
        rows[:, D - 64 : D], rows[:, 2 * D - 64 : 2 * D], rows[:, 3 * D - 64 : 3 * D], jnp.zeros_like(keys[:, :64])],
        axis=1)


def window(g):
    return slice(128 * (17 * g // 4), 128 * (17 * g // 4) + WINDOW)


def spread_kernel(params, w_qkv, w_up):
    def body(r):
        h = Here(r.sems)
        own = pl.ds(pl.multiple_of(h.c * 16, 16), 16)
        loads = [
            h.local(ref.at[0, rows], dst.at[pl.ds(16 * i, 16)])
            for ref, dst in ((r.w_up, r.up_rows), (r.w_qkv, r.qkv_rows)) for i, rows in enumerate((own, pl.ds(256, 16)))]
        h.barrier(whole=False)
        h.ready()
        arrive, arrive_mid, arrive_up = h.sem(), h.sem(), h.sem()
        mine = r.params_in.at[h.s * SHARD + h.y]
        mine[...] = r.params[...]
        for step, other, to in everyone(h):
            if step or other:
                h.send(mine, mine, to, arrive)
        for copy in loads:
            copy.wait()

        @pl.when(h.s == 0)
        def _():
            for g in range(8):
                r.mid[g] = r.up_rows[:, window(g)].reshape(2, 16, WINDOW)
                r.up[g] = packed_qkv(r.qkv_rows[...], g).reshape(2, 16, WINDOW)

        @pl.when(h.s == 1)
        def _():
            for g in range(8):
                r.mid[g] = packed_qkv(r.qkv_rows[...], g).reshape(2, 16, WINDOW)
                r.up[g] = r.up_rows[:, window(g)].reshape(2, 16, WINDOW)

        for step, other, to in everyone(h):
            g = 2 * to[2] + to[0]
            slot = h.s * SHARD + h.y
            for sem, source, targets in (
                    (arrive_up, r.up, (r.side_piece, r.side_last)), (arrive_mid, r.mid, (r.mid_piece, r.mid_last))):
                for half in range(2):
                    src, dst = source.at[g, half], targets[half].at[slot]
                    if step or other:
                        h.send(src, dst, to, sem)
                    else:
                        pltpu.make_async_copy(src, dst, sem).start()
        wait_bytes(r.params_in.at[pl.ds(0, 7)], arrive)
        for layer in range(2):
            r.norms[layer] = jnp.concatenate([r.params_in[layer * SHARD + i] for i in range(SHARD)], axis=1)
        wait_bytes(r.mid, arrive_mid)
        wait_bytes(r.up, arrive_up)
        h.finish()

    ins = dict(params=(params, VMEM), w_qkv=(w_qkv, ANY), w_up=(w_up, ANY))
    outs = dict(
        norms=(spec((2, 8, D), F32), VMEM), mid_piece=(spec((8, 16, WINDOW)), VMEM),
        mid_last=(spec((8, 16, WINDOW)), VMEM), side_piece=(spec((8, 16, WINDOW)), VMEM),
        side_last=(spec((8, 16, WINDOW)), VMEM))
    scratch = dict(
        params_in=VMEM((8, 8, SLICE), F32), up_rows=VMEM((32, FF), BF16), qkv_rows=VMEM((32, 3 * D), BF16),
        mid=VMEM((8, 2, 16, WINDOW), BF16), up=VMEM((8, 2, 16, WINDOW), BF16), sems=pltpu.SemaphoreType.DMA((42,)))
    return call("spread", body, ins, outs, scratch, collective_id=0)


def load_tiles(h, gathered, last, dst, first=0):
    sem = h.sem()
    for i in range(SHARD):
        pltpu.make_async_copy(gathered.at[:, first + i], dst.at[pl.ds(17 * i, 16)], sem).start()
        pltpu.make_async_copy(last.at[first + i], dst.at[17 * i + 16], sem).start()
    return [types.SimpleNamespace(wait=lambda: wait_bytes(dst, sem))]


def place(value, parts, last):
    tiles = value.astype(BF16).reshape(68, 16, value.shape[1])
    for i in range(SHARD):
        for c in range(CTX):
            parts[c // 4, c % 4, i] = tiles[17 * i + c]
        last[i] = tiles[17 * i + 16]


def whole(ref):
    return ref[...].reshape(D, WINDOW)


class FirstWeights:
    def __init__(self, h, r):
        self.h, self.r = h, r
        self.arrive = [h.sem() for _ in range(3)]
        self.spreads = [Spread16(h, parts, i == 0) for i, parts in enumerate((r.qkv_low, r.qkv_high))]

    def load(self):
        h, r = self.h, self.r
        self.loads = [h.local(r.w_down.at[0], r.down_rows), h.local(r.w_out.at[0], r.out_rows)]

    def send_qkv(self):
        r = self.r
        for i, (each, parts) in enumerate(zip(self.spreads, (r.qkv_low, r.qkv_high))):
            parts[each.x, each.z] = r.side_piece[2 * i : 2 * i + 2]
            each.start()

    def send_qkv_on(self):
        for each in self.spreads:
            each.middle()

    def send_rest(self):
        h, r = self.h, self.r
        for copy in self.loads:
            copy.wait()
        for other in range(2):
            core = lax.rem(h.s + other, 2)
            at = pl.multiple_of(window_offset(h.y * 2 + core), 32)
            src = r.down_rows.at[pl.ds(pl.multiple_of(544 * core, 16), 544)]
            dst = r.down_vm.at[h.s, pl.ds(at, 544)]
            if other:
                h.send(src, dst, h.sibling(), self.arrive[1])
            else:
                pltpu.make_async_copy(src, dst, self.arrive[1]).start()
        self.tiles = []
        for i in range(17):
            tile = h.y * 17 + i
            group = jnp.minimum(tile // 8, 7)
            core, shard = lax.rem(group, 2), group // 2
            src = r.out_rows.at[pl.ds(16 * i, 16)]
            dst = r.out_vm.at[h.s, pl.ds(pl.multiple_of(lax.rem(tile, 8) * 16, 16), 16)]
            copy = pltpu.make_async_remote_copy(
                src_ref=src, dst_ref=dst, send_sem=h.sem(), recv_sem=self.arrive[2],
                device_id=(core, h.c, shard), device_id_type=MESH)
            same = pltpu.make_async_copy(src, dst, self.arrive[2])
            is_self = (core == h.s) & (shard == h.y)
            pl.when((tile < 64) & is_self)(same.start)
            away = (tile < 64) & jnp.logical_not(is_self)
            pl.when(away)(copy.start)
            self.tiles.append((away, copy))
        src, dst = r.out_rows.at[pl.ds(SLICE - 64, 64)], r.out_vm.at[h.s, pl.ds(128, 64)]
        same = pltpu.make_async_copy(src, dst, self.arrive[2])
        self.last = []
        for step, other, to in everyone(h):
            if step or other:
                self.last.append(pltpu.make_async_remote_copy(
                    src_ref=src, dst_ref=dst, send_sem=h.sem(), recv_sem=self.arrive[2], device_id=to,
                    device_id_type=MESH))

        @pl.when(h.y == SHARD - 1)
        def _():
            same.start()
            for copy in self.last:
                copy.start()

    def wait_qkv(self):
        r = self.r
        for each in self.spreads:
            each.finish()
        for i in range(SHARD):
            for c in range(CTX):
                parts = (r.qkv_low, r.qkv_high)[i // 2]
                r.qkv_vm[17 * i + c] = parts[c // 4, c % 4, i % 2]
            r.qkv_vm[17 * i + 16] = r.side_last[i]

    def finish(self):
        r, h = self.r, self.h
        wait_bytes(r.down_vm.at[:, pl.ds(0, 544)], self.arrive[1])
        h.save(r.down_vm, r.down_w)
        wait_bytes(r.out_vm, self.arrive[2])
        h.save(r.out_vm, r.out_w)

        for away, copy in self.tiles:
            pl.when(away)(copy.wait_send)

        @pl.when(h.y == SHARD - 1)
        def _():
            for copy in self.last:
                copy.wait_send()


def head_outs():
    return dict(
        a_full=(spec((512, D)), ANY), message_in=(spec((CTX, 160, 128)), VMEM),
        kv16_in=(spec((2, CTX, ROWS, 128)), VMEM), q16=(spec((ROWS, HEAD_DIM)), VMEM))


def head_scratch():
    return dict(message=VMEM((2, 4, 2, 160, 128), BF16), qkv_vm=VMEM(TILES, BF16), a_vm=VMEM((512, D), BF16))


def run_head(h, r, gather, after=None):
    arrive = h.sem()
    own16 = dot(r.a_vm[h.rows(h.y, h.s)], r.qkv_vm[:, :, 384:].reshape(D, 256)).astype(BF16)
    r.q16[...] = own16[:, :64]
    r.kv16_in[h.s, h.c] = own16[:, 64:192]
    own_kv = r.kv16_in.at[h.s, h.c]
    leave16, arrive16, cross16 = h.sem(), h.sem(), h.sem()
    for step in range(1, CTX):
        h.send(own_kv, own_kv, (h.s, lax.rem(h.c + step, CTX), h.y), arrive16, leave16)
    messages = Messages(h, r.message_in)
    for step in ORDER:
        if step:
            gather.relay(step)
        gather.wait(step)
        sends = []
        shard = h.shard(step)
        block = r.a_vm[pl.ds(pl.multiple_of(shard * 128, 128), 128)]
        out = dot(block, r.qkv_vm[:, :, :384].reshape(D, 384)).astype(BF16)
        for e in range(2):
            for core in range(2):
                r.message[e, shard, core, :128] = out[:, 128 + 128 * e : 256 + 128 * e]
                for b in range(2):
                    at = 32 * b + 16 * core
                    lanes = slice(64 * e, 64 * e + 64)
                    packed = jnp.concatenate([out[at : at + 16, lanes], out[64 + at : 80 + at, lanes]], axis=1)
                    r.message[e, shard, core, 128 + 16 * b : 144 + 16 * b] = packed
                chip = 8 * h.s + 4 * e + shard
                sends.append((
                    r.message.at[e, shard, core], r.message_in.at[h.c], (core, chip, h.y),
                    (chip == h.c) & (h.s == core), arrive))
        messages.add(sends)
    messages.done()
    h.save(r.a_vm, r.a_full)
    if after is not None:
        after()
    wait_bytes(r.kv16_in.at[h.s, pl.ds(0, CTX - 1)], arrive16)
    cross = r.kv16_in.at[h.s]
    h.send(cross, cross, h.sibling(), cross16)
    wait_bytes(r.kv16_in.at[h.s, pl.ds(0, CTX - 1)], leave16)
    wait_bytes(r.kv16_in.at[1 - h.s], cross16)
    wait_bytes(r.message_in, arrive)


def first_kernel(hidden, norms, side_piece, side_last, w_out, w_down):
    def body(r):
        h = Here(r.sems)
        weights = FirstWeights(h, r)
        weights.load()
        r.down_vm[...] = jnp.zeros_like(r.down_vm)
        h.barrier()
        h.ready()
        weights.send_qkv()
        x = r.hidden[h.s].astype(F32)
        a_value = layer_norm(x, r.norms[0, 0:1], r.norms[0, 2:3]).astype(BF16)
        gather = Gather8(h, r.a_vm)
        for half in range(PARTS):
            gather.start(a_value[half_rows(half)], half)
        weights.send_qkv_on()
        weights.wait_qkv()
        h.save(r.qkv_vm, r.qkv_w)
        run_head(h, r, gather, weights.send_rest)
        weights.finish()
        h.finish()

    ins = dict(hidden=(hidden, VMEM), norms=(norms, VMEM), side_piece=(side_piece, VMEM), side_last=(side_last, VMEM),
        w_out=(w_out, ANY), w_down=(w_down, ANY))
    outs = dict(
        **head_outs(), qkv_w=(spec(TILES), ANY), out_w=(spec((2, 192, D)), ANY), down_w=(spec((2, WINDOW, D)), ANY))
    scratch = dict(
        **head_scratch(), qkv_low=VMEM((4, 4, 2, 16, WINDOW), BF16), qkv_high=VMEM((4, 4, 2, 16, WINDOW), BF16),
        down_rows=VMEM((D, D), BF16), out_rows=VMEM((SLICE, D), BF16), down_vm=VMEM((2, WINDOW, D), BF16),
        out_vm=VMEM((2, 192, D), BF16), sems=pltpu.SemaphoreType.DMA((65,)))
    return call("first", body, ins, outs, scratch, collective_id=1)


def sort_rows(r):
    for m in range(2):
        for p in range(32):
            at = 32 * m + p
            tile = r.places[0, m, p]
            for i in range(2):
                rows = r.kept[tile + i]
                r.keys[32 * at + 16 * i : 32 * at + 16 * i + 16] = rows[:, :64]
                r.values[32 * at + 16 * i : 32 * at + 16 * i + 16] = rows[:, 64:]
            query = r.kept[r.places[1, m, p]]
            r.queries[16 * at : 16 * at + 16] = query[:, 64 * m : 64 * m + 64] * 0.125


def attend(h, r):
    row = lax.broadcasted_iota(jnp.int32, (256, 512), 0)
    row = 32 * (row // 16) + 16 * h.s + row % 16
    visible = row >= lax.broadcasted_iota(jnp.int32, (256, 512), 1)
    for t in range(4):
        query = r.queries[256 * t : 256 * t + 256]
        parts = [dot_nt(query, r.keys[512 * u : 512 * u + 512]) for u in range(t + 1)]
        parts[t] = jnp.where(visible, parts[t], NEG_LARGE)
        top = parts[0]
        for p in parts[1:]:
            top = jnp.maximum(top, p)
        top = jnp.max(top, axis=-1, keepdims=True)
        parts = [jnp.exp(p - top) for p in parts]
        total = parts[0]
        for p in parts[1:]:
            total = total + p
        total = jnp.sum(total, axis=-1, keepdims=True)
        out = dot(parts[0].astype(BF16), r.values[:512])
        for u in range(1, t + 1):
            out = out + dot(parts[u].astype(BF16), r.values[512 * u : 512 * u + 512])
        r.sorted_out[16 * t : 16 * t + 16] = (out / total).astype(BF16).reshape(16, 16, 64)
        r.logs[256 * t : 256 * t + 256] = jnp.broadcast_to(top + jnp.log(total), (256, 128))
    for c in range(CTX):
        for m in range(2):
            for b in range(2):
                rows = r.sorted_out[32 * m + r.order[m, 2 * c + b]]
                r.attended[c, 16 * b : 16 * b + 16, 64 * m : 64 * m + 64] = rows


def attend_last(r):
    kv = r.kept16[...].reshape(SEQ, 128)
    scores = dot_nt(r.kept_q16[...] * 0.125, kv[:, :64])
    scores = jnp.where(r.own_positions[...] >= r.positions[...], scores, NEG_LARGE)
    top = jnp.max(scores, axis=-1, keepdims=True)
    scores = jnp.exp(scores - top)
    total = jnp.sum(scores, axis=-1, keepdims=True)
    out = dot(scores.astype(BF16), kv[:, 64:])
    r.attended16[...] = (out / total).astype(BF16)
    r.logs16[...] = jnp.broadcast_to(top + jnp.log(total), (ROWS, 128))


def attend_ins(kept, at):
    order, places, positions, own_positions = at
    return dict(
        order=(order, pltpu.SMEM), places=(places, pltpu.SMEM), positions=(positions, VMEM),
        own_positions=(own_positions, VMEM), kept=(kept.message_in.reshape(160, 16, 128), VMEM), kept16=(kept.kv16_in, VMEM),
        kept_q16=(kept.q16, VMEM))


def attend_outs():
    return dict(
        attended16=(spec((ROWS, 64)), VMEM), sorted_out=(spec((64, 16, 64)), VMEM), logs=(spec((1024, 128), F32), VMEM),
        logs16=(spec((ROWS, 128), F32), VMEM))


def attend_scratch():
    return dict(
        keys=VMEM((SEQ, 64), BF16), values=VMEM((SEQ, 64), BF16), queries=VMEM((1024, 64), BF16),
        attended=VMEM((CTX, 32, 128), BF16))


def middle_scratch():
    return dict(
        context_in=VMEM((2, 4, 2, 32, 128), BF16), out_vm=VMEM((192, D), BF16), up_vm=VMEM(TILES, BF16),
        down_vm=VMEM((WINDOW, D), BF16), to_out=scatter_scratch(), to_down=scatter_scratch())


def load_layer(h, r, layer, first):
    loads = [h.local(r.out_w.at[layer], r.out_vm), h.local(r.down_w.at[layer], r.down_vm)]
    return loads + load_tiles(h, r.up_all, r.up_last, r.up_vm, first)


def gather_context(h, r):
    arrive = h.sem()
    to_core = h.c // 8
    e, j = lax.rem(h.c // 4, 2), lax.rem(h.c, 4)
    messages = Messages(h, r.attended)
    messages.add([
        (r.attended.at[c], r.context_in.at[e, j, h.s], (to_core, c, h.y), (h.c == c) & (h.s == to_core), arrive)
        for c in range(CTX)])
    messages.done()
    return arrive


def unpack_context(r, store):
    for j in range(4):
        for m in range(2):
            for b in range(2):
                for core in range(2):
                    lanes = slice(64 * m, 64 * m + 64)
                    piece = jnp.concatenate(
                        [r.context_in[e, j, core, 16 * b : 16 * b + 16, lanes] for e in range(2)], axis=1)
                    at = 128 * j + 64 * m + 32 * b + 16 * core
                    store[at : at + 16] = piece


def block_rows(h, step):
    return pl.ds(pl.multiple_of(h.shard(step) * 128, 128), 128)


def run_out(h, r, x, ready):
    sums = Scatter8(h, r.to_out)
    for step in (2, 1, 3, 0):
        sums.put(step, dot(r.context[block_rows(h, step)], r.out_vm[:128]))
    sums.relay((2, 1, 3))
    own = x + dot(r.attended16[...], r.out_vm[128:])
    for half in range(PARTS):
        residual = own[half_rows(half)] + sums.result(half)
        r.residual[half_rows(half)] = residual
        ready(half, residual)


def middle_kernel(at, x, norms, first, mid_all, mid_last):
    def body(r):
        h = Here(r.sems)
        loads = load_layer(h, r, 0, 0)
        head_loads = load_tiles(h, r.up_all, r.up_last, r.qkv_vm, SHARD)
        h.barrier()
        sort_rows(r)
        attend(h, r)
        h.ready()
        arrive = gather_context(h, r)
        attend_last(r)
        for copy in loads:
            copy.wait()
        wait_bytes(r.context_in, arrive)
        unpack_context(r, r.context)
        gather = Gather8(h, r.b_vm)

        def ready(half, residual):
            gather.start(layer_norm(residual, r.norms[0, 1:2], r.norms[0, 3:4]).astype(BF16), half)

        run_out(h, r, r.x[h.s].astype(F32), ready)
        sums = Scatter8(h, r.to_down)
        for step in ORDER:
            if step:
                gather.relay(step)
            gather.wait(step)
            rows = block_rows(h, step)
            u = dot(r.b_vm[rows], whole(r.up_vm))
            r.pre_vm[rows] = u
            sums.put(step, dot(gelu(u).astype(BF16), r.down_vm[...]))
        sums.relay((1, 3, 2))
        h.save(r.b_vm, r.b_full)
        h.save(r.pre_vm, r.pre)
        for copy in head_loads:
            copy.wait()
        gather = Gather8(h, r.a_vm)
        for half in range(PARTS):
            y = (r.residual[half_rows(half)] + sums.result(half)).astype(BF16)
            r.y[half_rows(half)] = y
            gather.start(layer_norm(y.astype(F32), r.norms[1, 0:1], r.norms[1, 2:3]).astype(BF16), half)
        run_head(h, r, gather)
        h.finish()

    ins = dict(
        **attend_ins(first, at), x=(x, VMEM), norms=(norms, VMEM), out_w=(first.out_w, ANY),
        down_w=(first.down_w, ANY), up_all=(mid_all, ANY), up_last=(mid_last, ANY))
    outs = dict(
        **attend_outs(), context=(spec((512, 128)), VMEM), residual=(spec((ROWS, D), F32), VMEM), b_full=(spec((512, D)), ANY),
        pre=(spec((512, WINDOW), F32), ANY), y=(spec((ROWS, D)), VMEM), **head_outs())
    scratch = dict(
        **attend_scratch(), **middle_scratch(), **head_scratch(), b_vm=VMEM((512, D), BF16), pre_vm=VMEM((512, WINDOW), F32),
        sems=pltpu.SemaphoreType.DMA((85,)))
    return call("middle", body, ins, outs, scratch, collective_id=2)


def gelu_slope(u):
    t = jnp.tanh(0.7978845608028654 * (u + 0.044715 * u * u * u))
    return 0.5 * (1.0 + t) + 0.5 * u * (1.0 - t * t) * 0.7978845608028654 * (1.0 + 0.134145 * u * u)


def norm_back(grad, values, gain):
    normed, rate = norm_parts(values)
    scaled = grad * gain
    mean = jnp.mean(scaled, axis=-1, keepdims=True)
    along = jnp.mean(scaled * normed, axis=-1, keepdims=True)
    back = rate * (scaled - mean - normed * along)
    return back, grad * normed


def columns(at, gain_rows, bias_rows):
    lane = lax.broadcasted_iota(jnp.int32, (ROWS, 64), 1)

    def into(rows, column):
        return dot_tn(rows.astype(BF16), (lane == column).astype(BF16))

    return into(gain_rows, at) + into(bias_rows, at + 1)


def back_outs():
    return dict(
        mid_grad=(spec((ROWS, D), F32), VMEM), context_grad_in=(spec((CTX, 32, 128)), VMEM),
        context16_grad=(spec((ROWS, HEAD_DIM)), VMEM),
        up_g_last=(spec((SHARD, 16, WINDOW)), VMEM), norm2_g=(spec((68, 16, 64)), VMEM))


def back_scratch():
    return dict(
        m_full=VMEM((512, D), BF16), z_full=VMEM((512, D), BF16), hidden_low=VMEM((512, WINDOW), BF16),
        pre_grad=VMEM((512, WINDOW), BF16), context_message=VMEM((2, 4, 2, 32, 128), BF16), up_grad=VMEM((4, 4, SHARD, 16, WINDOW), BF16),
        down_grad=VMEM((40, 16, D), BF16), b_vm=VMEM((512, D), BF16), to_norm2=scatter_scratch())


def back_block(h, r, rows, sums, step, u, g):
    r.hidden_low[rows] = g
    hidden_grad = dot_nt(r.m_full[rows], r.down_vm[...])
    pre_grad = (hidden_grad * gelu_slope(u)).astype(BF16)
    r.pre_grad[rows] = pre_grad
    sums.put(step, dot_nt(pre_grad, whole(r.up_vm)))


def finish_back(h, r, sums, layer, residual, out_grad, context, down_ready, up_ready, beside, near_end=None):
    r.down_grad[...] = dot_tn(r.hidden_low[...], r.m_full[...]).astype(BF16).reshape(40, 16, D)
    down_ready(r.down_grad, 2 * lax.rem(h.y * 2 + h.s, 4))
    place(dot_tn(r.b_vm[...], r.pre_grad[...]), r.up_grad, r.up_g_last)
    up_ready()
    gather = Gather8(h, r.z_full)
    gain_rows, normed_grad = [], []
    for half in range(PARTS):
        rows = half_rows(half)
        normed_grad.append(sums.result(half))
        back, gains = norm_back(normed_grad[half], residual[rows], r.norms[layer, 1:2])
        gain_rows.append(gains)
        mid_grad = out_grad[rows] + back
        r.mid_grad[rows] = mid_grad
        gather.start(mid_grad.astype(BF16), half)
    gain_rows, normed_grad = jnp.concatenate(gain_rows, axis=0), jnp.concatenate(normed_grad, axis=0)
    z = r.z_full[h.rows(h.y, h.s)]
    r.norm2_g[...] = columns(2, gain_rows, normed_grad).astype(BF16).reshape(68, 16, 64)
    beside()
    arrive = h.sem()
    r.context16_grad[...] = dot_nt(z, r.out_vm[128:]).astype(BF16)
    messages = Messages(h, r.context_grad_in)
    for step in ORDER:
        if step:
            gather.relay(step)
        gather.wait(step)
        sends = []
        shard = h.shard(step)
        out = dot_nt(r.z_full[block_rows(h, step)], r.out_vm[:128]).astype(BF16)
        for e in range(2):
            for core in range(2):
                lanes = slice(64 * e, 64 * e + 64)
                for b in range(2):
                    at = 32 * b + 16 * core
                    r.context_message[e, shard, core, 16 * b : 16 * b + 16] = jnp.concatenate(
                        [out[at : at + 16, lanes], out[64 + at : 80 + at, lanes]], axis=1)
                chip = 8 * h.s + 4 * e + shard
                sends.append((
                    r.context_message.at[e, shard, core], r.context_grad_in.at[h.c], (core, chip, h.y),
                    (chip == h.c) & (h.s == core), arrive))
        messages.add(sends)
    messages.done()
    r.out_g[:8] = dot_tn(context[...], r.z_full[...]).astype(BF16).reshape(8, 16, D)
    r.out_g[8:] = dot_tn(r.attended16[...], z).astype(BF16).reshape(4, 16, D)
    if near_end is not None:
        near_end()
    wait_bytes(r.context_grad_in, arrive)


def turn_kernel(at, kept, x, norms, first, up_all, up_last, cotangent):
    def body(r):
        h = Here(r.sems)
        loads = load_layer(h, r, 1, 0)
        h.barrier()
        sort_rows(r)
        h.ready()
        out_grad = r.cotangent[h.s]
        gather_m = Gather8(h, r.m_full)
        for half in range(PARTS):
            gather_m.start(out_grad[half_rows(half)], half)
        attend(h, r)
        arrive = gather_context(h, r)
        attend_last(r)
        for step in (1, 3, 2):
            gather_m.relay(step)
        for copy in loads:
            copy.wait()
        wait_bytes(r.context_in, arrive)
        unpack_context(r, r.context)
        gather = Gather8(h, r.b_vm)

        def ready(half, residual):
            gather.start(layer_norm(residual, r.norms[1, 1:2], r.norms[1, 3:4]).astype(BF16), half)

        run_out(h, r, r.x[...].astype(F32), ready)
        back_sums = Scatter8(h, r.to_norm2)
        for step in ORDER:
            if step:
                gather.relay(step)
            gather_m.wait(step)
            gather.wait(step)
            rows = block_rows(h, step)
            u = dot(r.b_vm[rows], whole(r.up_vm))
            g = gelu(u).astype(BF16)
            back_block(h, r, rows, back_sums, step, u, g)
        back_sums.relay((1, 3, 2))
        h.save(r.hidden_low, r.hidden_out)

        ups = [
            Reduce16(h, r.up_grad.at[:, :, pl.ds(2 * i, 2)], (r.ups_in.at[i], (r.up_mine_a, r.up_mine_b)[i], None), i == 0)
            for i in range(2)]
        first_rows = FirstRows(h, r)

        def up_ready():
            for each in ups:
                each.start()
            first_rows.start()

        def near_end():
            for each in ups:
                each.add()
            first_rows.add()

        finish_back(
            h, r, back_sums, 1, r.residual[...], out_grad.astype(F32), r.context, first_rows.load,
            up_ready, lambda: None, near_end)
        h.finish()

    ins = dict(
        **attend_ins(kept, at), x=(x, VMEM), norms=(norms, VMEM), out_w=(first.out_w, ANY),
        down_w=(first.down_w, ANY), up_all=(up_all, ANY), up_last=(up_last, ANY),
        cotangent=(cotangent, VMEM))
    outs = dict(
        **attend_outs(), hidden_out=(spec((512, WINDOW)), ANY), residual=(spec((ROWS, D), F32), VMEM), **first_rows_outs(),
        up_mine_a=(spec((4, 2, 16, WINDOW)), VMEM), up_mine_b=(spec((4, 2, 16, WINDOW)), VMEM), out_g=(spec((12, 16, D)), VMEM), **back_outs())
    scratch = dict(
        **attend_scratch(), context=VMEM((512, 128), BF16), **middle_scratch(),
        **first_rows_scratch(), ups_in=VMEM((2, 3, 4, 2, 16, WINDOW), BF16), **back_scratch(), sems=pltpu.SemaphoreType.DMA((107,)))
    return call("turn", body, ins, outs, scratch, collective_id=3)


def row_of(grads, outs):
    product = grads.astype(F32) * outs.astype(F32)
    return lax.dot_general(
        jnp.ones((8, 64), F32), product, (((1,), (1,)), ((), ())), precision=lax.Precision.HIGHEST,
        preferred_element_type=F32)[0:1]


def sort_grads(r):
    sort_rows(r)
    for m in range(2):
        for p in range(32):
            at = 32 * m + p
            r.grads[16 * at : 16 * at + 16] = r.grad_in[r.places[2, m, p]][:, 64 * m : 64 * m + 64]
    r.key_grads[...] = jnp.zeros_like(r.key_grads)
    r.value_grads[...] = jnp.zeros_like(r.value_grads)


def attend_back(h, r):
    column = lax.broadcasted_iota(jnp.int32, (512, 256), 1)
    column = 32 * (column // 16) + 16 * h.s + column % 16
    visible = column >= lax.broadcasted_iota(jnp.int32, (512, 256), 0)
    for t in range(4):
        part = slice(256 * t, 256 * t + 256)
        query, grad = r.queries[part], r.grads[part]
        logs = jnp.transpose(r.logs[part])[0:1]
        delta = row_of(grad, r.sorted_out[16 * t : 16 * t + 16].reshape(256, 64))
        query_grad = jnp.zeros((256, 64), F32)
        for u in range(t + 1):
            chunk = slice(512 * u, 512 * u + 512)
            keys = r.keys[chunk]
            scores = dot_nt(keys, query)
            if u == t:
                scores = jnp.where(visible, scores, NEG_LARGE)
            probs = jnp.exp(scores - logs)
            probs_grad = dot_nt(r.values[chunk], grad)
            scores_grad = (probs * (probs_grad - delta)).astype(BF16)
            blocks = slice(16 * u, 16 * u + 16)
            r.value_grads[blocks] += dot(probs.astype(BF16), grad).reshape(16, 32, 64)
            r.key_grads[blocks] += dot(scores_grad, query).reshape(16, 32, 64)
            query_grad = query_grad + dot_tn(scores_grad, keys)
        r.query_grads[16 * t : 16 * t + 16] = (query_grad * 0.125).astype(BF16).reshape(16, 16, 64)
    for c in range(CTX):
        for m in range(2):
            for b in range(2):
                block = 32 * m + r.order[m, 2 * c + b]
                r.message[c, 64 * m + 32 * b : 64 * m + 32 * b + 32, :] = jnp.concatenate(
                    [r.key_grads[block], r.value_grads[block]], axis=1).astype(BF16)
                r.message[c, 128 + 16 * b : 144 + 16 * b, 64 * m : 64 * m + 64] = r.query_grads[block]


def attend_back_last(r):
    kv = r.kept16[...].reshape(SEQ, 128)
    query, grad = r.kept_q16[...] * 0.125, r.grad16[...]
    scores = dot_nt(kv[:, :64], query)
    scores = jnp.where(r.own_positions[...] >= r.positions[...], scores, NEG_LARGE)
    probs = jnp.exp(scores - jnp.transpose(r.logs16[...])[0:1])
    probs_grad = dot_nt(kv[:, 64:], grad)
    scores_grad = (probs * (probs_grad - row_of(grad, r.out16[...]))).astype(BF16)
    both = jnp.concatenate([dot(scores_grad, query), dot(probs.astype(BF16), grad)], axis=1)
    r.kv16_grad[...] = both.astype(BF16).reshape(2, CTX, ROWS, 128)
    r.q16_grad[...] = (dot_tn(scores_grad, kv[:, :64]) * 0.125).astype(BF16)


def tail_ins(at, kept, saved, a_full, x, above, norms):
    return dict(
        **attend_ins(kept, at), sorted_out=(saved.sorted_out, VMEM), logs=(saved.logs, VMEM), logs16=(saved.logs16, VMEM),
        out16=(saved.attended16, VMEM), grad_in=(above.context_grad_in.reshape(32, 16, 128), VMEM), grad16=(above.context16_grad, VMEM),
        a_full=(a_full, ANY), x=(x, VMEM), mid_in=(above.mid_grad, VMEM), norms=(norms, VMEM),
        norm2_in=(above.norm2_g, VMEM))


def tail_outs():
    return dict(in_grad=(spec((ROWS, D)), VMEM))


def tail_scratch():
    return dict(
        keys=VMEM((SEQ, 64), BF16), values=VMEM((SEQ, 64), BF16), queries=VMEM((1024, 64), BF16),
        grads=VMEM((1024, 64), BF16), query_grads=VMEM((64, 16, 64), BF16), key_grads=VMEM((64, 32, 64), F32),
        value_grads=VMEM((64, 32, 64), F32), message=VMEM((CTX, 160, 128), BF16),
        kv16_grad=VMEM((2, CTX, ROWS, 128), BF16), q16_grad=VMEM((ROWS, 64), BF16),
        message_in=VMEM((2, 4, 2, 160, 128), BF16), core16=VMEM((CTX, ROWS, 128), BF16),
        sum16=VMEM((CTX, ROWS, 128), BF16), own16=VMEM((CTX, ROWS, 128), BF16), qkv_grads=VMEM((512, 384), BF16),
        qkv_vm=VMEM(TILES, BF16), a_vm=VMEM((512, D), BF16), main_part=VMEM((4, 4, SHARD, 16, 384), BF16),
        side_part=VMEM((4, 4, SHARD, 16, 256), BF16), to_norm1=scatter_scratch())


def start_tail(h, r, after_last=lambda: None):
    attend_back_last(r)
    cross = h.sem()
    h.send(r.kv16_grad.at[1 - h.s], r.core16, h.sibling(), cross)
    after_last()
    attend_back(h, r)
    arrive = h.sem()
    to_core = h.c // 8
    e, j = lax.rem(h.c // 4, 2), lax.rem(h.c, 4)
    messages = Messages(h, r.message)
    messages.add([
        (r.message.at[c], r.message_in.at[e, j, h.s], (to_core, c, h.y), (h.c == c) & (h.s == to_core), arrive)
        for c in range(CTX)])
    messages.done()
    wait_bytes(r.core16, cross)
    r.sum16[...] = (r.kv16_grad[h.s].astype(F32) + r.core16[...].astype(F32)).astype(BF16)
    leave16, arrive16 = h.sem(), h.sem()
    for step in range(1, CTX):
        to = lax.rem(h.c + step, CTX)
        h.send(r.sum16.at[to], r.own16.at[step], (h.s, to, h.y), arrive16, leave16)
    return arrive, leave16, arrive16


def run_tail(h, r, layer, x, waits, loads, last, main_ready, side_ready, arrived, beside, in_ready):
    arrive, leave16, arrive16 = waits
    for copy in loads:
        copy.wait()
    weights = whole(r.qkv_vm)
    wait_bytes(r.message_in, arrive)
    arrived()
    for j in range(4):
        for e in range(2):
            both = r.message_in[e, j, 0, :128].astype(F32) + r.message_in[e, j, 1, :128].astype(F32)
            r.qkv_grads[128 * j : 128 * j + 128, 128 + 128 * e : 256 + 128 * e] = both.astype(BF16)
        for m in range(2):
            for b in range(2):
                for core in range(2):
                    lanes = slice(64 * m, 64 * m + 64)
                    piece = jnp.concatenate(
                        [r.message_in[e, j, core, 128 + 16 * b : 144 + 16 * b, lanes] for e in range(2)], axis=1)
                    at = 128 * j + 64 * m + 32 * b + 16 * core
                    r.qkv_grads[at : at + 16, :128] = piece
    sums = Scatter8(h, r.to_norm1)
    for step in (2, 1, 3, 0):
        sums.put(step, dot_nt(r.qkv_grads[block_rows(h, step)], weights[:, :384]))
    sums.relay((2, 1, 3))
    wait_bytes(r.own16.at[pl.ds(1, CTX - 1)], arrive16)
    wait_bytes(r.own16.at[pl.ds(1, CTX - 1)], leave16)
    kv16 = r.sum16[h.c].astype(F32)
    for step in range(1, CTX):
        kv16 = kv16 + r.own16[step].astype(F32)
    grads16 = jnp.concatenate([r.q16_grad[...], kv16.astype(BF16)], axis=1)
    own = dot_nt(grads16, weights[:, 384:576])
    place(dot_tn(r.a_vm[...], r.qkv_grads[...]), r.main_part, last.at[:, :, pl.ds(0, 384)])
    main_ready()
    own_grad = dot_tn(r.a_vm[h.rows(h.y, h.s)], grads16)
    beside()
    gain_rows, normed_grad = [], []
    for half in range(PARTS):
        rows = half_rows(half)
        normed_grad.append(own[rows] + sums.result(half))
        back, gains = norm_back(normed_grad[half], x[rows], r.norms[layer, 0:1])
        gain_rows.append(gains)
        in_grad = (r.mid_in[rows] + back).astype(BF16)
        r.in_grad[rows] = in_grad
        in_ready(half, in_grad)
    gain_rows, normed_grad = jnp.concatenate(gain_rows, axis=0), jnp.concatenate(normed_grad, axis=0)

    def finish():
        sums_of_rows = columns(0, gain_rows, normed_grad) + r.norm2_in[...].reshape(D, 64).astype(F32)
        side = jnp.concatenate([own_grad, sums_of_rows], axis=1)
        place(side, r.side_part, last.at[:, :, pl.ds(384, 256)])
        side_ready()

    return finish


def send_out(h, r, out, layer, arrive, arrive_last):
    group = 2 * h.y + h.s
    for i in range(8):
        tile = 8 * group + i
        to = tile // 17
        h.send_or_keep(
            out.at[i], r.out_sum.at[lax.rem(tile, 17)], (layer, h.c, to), (h.s == layer) & (to == h.y), arrive)
    h.send_or_keep(
        out.at[pl.ds(8, 4)], r.last_in.at[group], (layer, h.c, SHARD - 1), (h.s == layer) & (h.y == SHARD - 1),
        arrive_last)


def back_kernel(at, kept, saved, x, above, norms, first, attended16, mid_all, mid_last):
    def body(r):
        h = Here(r.sems)
        tail_loads = load_tiles(h, r.up_all, r.up_last, r.qkv_vm, SHARD)
        tail_loads.append(h.local(r.a_full, r.a_vm))
        out_loads = [h.local(r.hidden1, r.hidden_low), h.local(r.down_tiles.at[1], r.down_grad)]
        loads = load_layer(h, r, 0, 0)
        loads += [h.local(r.b_full, r.b_vm), h.local(r.pre, r.pre_vm), h.local(r.context, r.context_vm)]
        h.barrier()
        sort_grads(r)
        arrive_out, arrive_last = h.sem(), h.sem()
        x, z = h.c // 4, lax.rem(h.c, 4)
        ups = [
            Reduce16(h, None, (None, (r.up_mine_a, r.up_mine_b)[i], r.ups_second.at[i]), i == 0) for i in range(2)]
        main = Reduce16(h, r.main_part, r.main_sums, False)
        side = Reduce16(h, r.side_part, r.side_sums, True)
        up0 = Reduce16(h, r.up_grad, (r.up0_in, r.up0_mine, None), True)
        rows16 = Rows16(h, r, 1)
        first_rows = FirstRows(h, r)
        h.ready()
        for each in ups:
            each.send_on()
        rows16.start()
        send_out(h, r, r.out1_g, 1, arrive_out, arrive_last)
        out_sums = Scatter8(h, r.to_down)
        for copy in out_loads:
            copy.wait()
        for step in (2, 1, 3, 0):
            out_sums.put(step, dot(r.hidden_low[block_rows(h, step)], r.down_grad[...].reshape(WINDOW, D)))
        waits = start_tail(h, r, lambda: out_sums.relay((2, 1, 3)))

        def settle(core):
            @pl.when(h.s == core)
            def _():
                @pl.when(h.y < SHARD - 1)
                def _():
                    wait_bytes(r.out_sum, arrive_out)

                @pl.when(h.y == SHARD - 1)
                def _():
                    wait_bytes(r.out_sum.at[pl.ds(0, 13)], arrive_out)
                    wait_bytes(r.last_in, arrive_last)
                    r.out_sum[13:] = added([r.last_in[g] for g in range(8)])

        arrive_up = h.sem()
        spreads = [Spread16(h, parts, i == 0, 1) for i, parts in enumerate((r.up_low, r.up_high))]

        def arrived():
            for half in range(PARTS):
                rows = half_rows(half)
                r.out[rows] = (r.residual1[rows] + out_sums.result(half)).astype(BF16)
            for i in range(2):
                r.up1_piece[2 * i : 2 * i + 2] = ups[i].result()
            send_piece(h, r.up1_piece, r.up_in, 1, arrive_up)
            settle(1)
            rows16.start_out()

        def beside_sums():
            rows16.middle()

            @pl.when(h.s == 1)
            def _():
                wait_bytes(r.up_in, arrive_up)
                rows = joined_up([r.up_in[g] for g in range(8)])
                for i, parts in enumerate((r.up_low, r.up_high)):
                    parts[x, z] = rows[:, 2176 * i : 2176 * i + 2176]

            for each in spreads:
                each.start()

        gather = Gather8(h, r.m_full)
        finish = run_tail(
            h, r, 1, r.x[...].astype(F32), waits, tail_loads, r.qkv_g_last, main.start, side.start,
            arrived, beside_sums, lambda half, value: gather.start(value, half))
        finish()
        rows16.spread()
        for copy in loads:
            copy.wait()
        sums = Scatter8(h, r.to_norm2)
        for step in ORDER:
            if step:
                gather.relay(step)
            gather.wait(step)
            rows = block_rows(h, step)
            u = r.pre_vm[rows]
            back_block(h, r, rows, sums, step, u, gelu(u).astype(BF16))
            if step == 0:
                for each in spreads:
                    each.middle()
            if step == 1:
                rows16.spread_on()
        sums.relay((1, 3, 2))
        def down_ready(rows, first):
            first_rows.load(rows, first)
            main.middle()
            side.middle()

        def up_ready():
            up0.start()
            first_rows.start()

        def beside():
            r.qkv1_piece[:, :, :384] = main.result()
            r.qkv1_piece[:, :, 384:] = side.result()

        def near_end():
            send_out(h, r, r.out_g, 0, arrive_out, arrive_last)
            up0.add()
            first_rows.add()
            rows16.finish()
            for each in spreads:
                each.finish()
            h.save_on(1, r.up_low, r.up_low_all)
            h.save_on(1, r.up_high, r.up_high_all)

        finish_back(
            h, r, sums, 0, r.residual[...], r.in_grad[...].astype(F32), r.context_vm, down_ready, up_ready, beside, near_end)

        settle(0)
        h.finish()

    ins = dict(
        **tail_ins(at, kept, saved, kept.a_full, x, above, norms), pre=(kept.pre, ANY), b_full=(kept.b_full, ANY),
        context=(kept.context, ANY), residual=(kept.residual, VMEM), attended16=(attended16, VMEM),
        out_w=(first.out_w, ANY), down_w=(first.down_w, ANY), up_all=(mid_all, ANY), up_last=(mid_last, ANY),
        up_mine_a=(above.up_mine_a, VMEM), up_mine_b=(above.up_mine_b, VMEM), out1_g=(above.out_g, VMEM),
        mine_a=(above.next_a, VMEM), mine_b=(above.next_b, VMEM), mine_beside=(above.next_beside, VMEM),
        hidden1=(above.hidden_out, ANY), residual1=(above.residual, VMEM),
        down_tiles=(first.down_w.reshape(2, 40, 16, D), ANY))
    piece, half = (spec((SHARD, 16, WINDOW)), VMEM), (spec((4, 4, 16, 2176)), ANY)
    outs = dict(
        **tail_outs(), **back_outs(), out=(spec((ROWS, D)), VMEM), qkv_g_last=piece, qkv1_piece=piece, up0_mine=(spec((4, SHARD, 16, WINDOW)), VMEM),
        up_low_all=half, up_high_all=half, **rows_outs(), **rows_results(),
        **first_rows_outs(), out_sum=(spec((17, 16, D)), VMEM))
    scratch = dict(
        out_vm=VMEM((192, D), BF16), up_vm=VMEM(TILES, BF16), down_vm=VMEM((WINDOW, D), BF16),
        pre_vm=VMEM((512, WINDOW), F32), to_down=scatter_scratch(), context_vm=VMEM((512, 128), BF16), out_g=VMEM((12, 16, D), BF16),
        ups_second=VMEM((2, 3, 2, 16, WINDOW), BF16), **first_rows_scratch(),
        up0_in=VMEM((3, 4, SHARD, 16, WINDOW), BF16), up_low=VMEM((4, 4, 16, 2176), BF16),
        up_high=VMEM((4, 4, 16, 2176), BF16), main_sums=reduce_scratch(SHARD, 384), side_sums=reduce_scratch(SHARD, 256),
        up1_piece=VMEM((SHARD, 16, WINDOW), BF16), up_in=VMEM((8, 16, WINDOW), BF16), last_in=VMEM((8, 4, 16, D), BF16), **tail_scratch(), **back_scratch(),
        **rows_scratch(), sems=pltpu.SemaphoreType.DMA((200,)))
    return call("back", body, ins, outs, scratch, collective_id=4)


class Plane16:
    def __init__(self, h, x_first, core=None):
        self.h, self.x_first = h, x_first
        self.on = None if core is None else h.s == core
        self.x, self.z = h.c // 4, lax.rem(h.c, 4)
        self.first, self.second = h.sem(), h.sem()

    def when(self, act):
        act() if self.on is None else pl.when(self.on)(act)

    def chip(self, x, z):
        return (self.h.s, 4 * lax.rem(x, 4) + lax.rem(z, 4), self.h.y)

    def along(self, axis_x):
        return [self.chip(self.x + j, self.z) if axis_x else self.chip(self.x, self.z + j) for j in (1, 2, 3)]

    def send(self, pairs, targets, arrive, spare):
        leave = self.h.sem()
        copies = [
            pltpu.make_async_remote_copy(
                src_ref=src, dst_ref=dst, send_sem=leave, recv_sem=arrive, device_id=to, device_id_type=MESH)
            for (src, dst), to in zip(pairs, targets)]

        def start():
            for i in (0, 2, 1):
                copies[i].start()

        self.when(start)
        self.h.sent.append(types.SimpleNamespace(wait_send=lambda: self.when(lambda: wait_bytes(spare, leave))))


class Reduce16(Plane16):
    def __init__(self, h, part, bufs, x_first, core=None):
        super().__init__(h, x_first, core)
        self.part = part
        self.first_in, self.mine, self.second_in = bufs

    def start(self):
        pairs = []
        for j in (1, 2, 3):
            src = self.part.at[lax.rem(self.x + j, 4)] if self.x_first else self.part.at[:, lax.rem(self.z + j, 4)]
            pairs.append((src, self.first_in.at[j - 1]))
        self.send(pairs, self.along(self.x_first), self.first, self.first_in)

    def add(self):
        def add():
            wait_bytes(self.first_in, self.first)
            for k in range(4):
                own = self.part[self.x, k] if self.x_first else self.part[k, self.z]
                self.mine[k] = added([own] + [self.first_in[j, k] for j in range(3)])

        self.when(add)

    def send_on(self):
        at = self.z if self.x_first else self.x
        pairs = [(self.mine.at[lax.rem(at + j, 4)], self.second_in.at[j - 1]) for j in (1, 2, 3)]
        self.send(pairs, self.along(not self.x_first), self.second, self.second_in)

    def middle(self):
        self.add()
        self.send_on()

    def result(self):
        wait_bytes(self.second_in, self.second)
        return added([self.mine[self.z if self.x_first else self.x]] + [self.second_in[j] for j in range(3)])


def reduce_scratch(units, width):
    return [VMEM((3, 4, units, 16, width), BF16), VMEM((4, units, 16, width), BF16), VMEM((3, units, 16, width), BF16)]


class Spread16(Plane16):
    def __init__(self, h, parts, x_first, core=None):
        super().__init__(h, x_first, core)
        self.parts = parts

    def start(self):
        own = self.parts.at[self.x, self.z]
        self.send([(own, own)] * 3, self.along(self.x_first), self.first, self.parts.at[0, pl.ds(0, 3)])

    def middle(self):
        self.when(lambda: wait_bytes(self.parts.at[0, pl.ds(0, 3)], self.first))
        line = self.parts.at[:, self.z] if self.x_first else self.parts.at[self.x]
        self.send([(line, line)] * 3, self.along(not self.x_first), self.second, self.parts.at[pl.ds(0, 3)])

    def finish(self):
        self.when(lambda: wait_bytes(self.parts.at[pl.ds(0, 3)], self.second))


class FirstRows:
    def __init__(self, h, r):
        self.h, self.r = h, r
        self.sums = [
            Reduce16(h, r.rows_a, (r.rows_in.at[0], r.next_a, None), True),
            Reduce16(h, r.rows_b, (r.rows_in.at[1], r.next_b, None), False)]

    def load(self, down, first):
        r = self.r
        for c in range(CTX):
            for i, parts in enumerate((r.rows_a, r.rows_b)):
                parts[c // 4, c % 4, 0] = down[first + 2 * c + i]
        for i in range(2):
            r.next_beside[i] = down[first + 32 + i]

    def start(self):
        for each in self.sums:
            each.start()

    def add(self):
        for each in self.sums:
            each.add()


def first_rows_outs():
    mine = (spec((4, 1, 16, D)), VMEM)
    return dict(next_a=mine, next_b=mine, next_beside=(spec((2, 16, D)), VMEM))


def first_rows_scratch():
    part = VMEM((4, 4, 1, 16, D), BF16)
    return dict(rows_a=part, rows_b=part, rows_in=VMEM((2, 3, 4, 1, 16, D), BF16))


class Rows16:
    def __init__(self, h, r, core):
        self.h, self.r, self.core = h, r, core
        self.sums = [
            Reduce16(h, None, (None, r.mine_a, r.rows_second.at[0]), True),
            Reduce16(h, None, (None, r.mine_b, r.rows_second.at[1]), False),
            Reduce16(h, r.rows_c, r.rows_sums_c, True, core)]
        self.spreads = [
            Spread16(h, r.rows_all.at[0], True), Spread16(h, r.rows_all.at[1], False), Spread16(h, r.rows_out, False, core)]
        self.arrive = h.sem()
        self.arrive_each = [h.sem() for _ in range(3)]
        self.cross = [h.sem() for _ in range(2)]

    def on(self, i):
        return self.h.s == self.core if i == 2 else None

    def when(self, i, act, also=None):
        conditions = [c for c in (self.on(i), also) if c is not None]
        if not conditions:
            return act()
        return pl.when(functools.reduce(jnp.logical_and, conditions))(act)

    def start(self):
        for i in range(2):
            self.sums[i].send_on()
            self.send_tile(self.r.mine_beside.at[i], i)

    def start_out(self):
        h, r = self.h, self.r

        @pl.when(h.s == self.core)
        def _():
            for c in range(CTX):
                r.rows_c[c // 4, c % 4, 0] = r.out_sum[c]

        self.sums[2].start()
        self.send_tile(r.out_sum.at[16], 2)

    def send_tile(self, src, i):
        h = self.h
        dst, leave = self.r.tile_in.at[h.c], h.sem()
        copy = pltpu.make_async_remote_copy(
            src_ref=src, dst_ref=dst, send_sem=leave, recv_sem=self.arrive, device_id=(h.s, 5 * i, h.y),
            device_id_type=MESH)
        kept = pltpu.make_async_copy(src, dst, self.arrive)
        self.when(i, copy.start, h.c != 5 * i)
        self.when(i, kept.start, h.c == 5 * i)
        h.sent.append(types.SimpleNamespace(
            wait_send=functools.partial(self.when, i, copy.wait_send, h.c != 5 * i)))

    def middle(self):
        self.sums[2].middle()

    def spread(self):
        h, r = self.h, self.r
        x, z = h.c // 4, lax.rem(h.c, 4)
        r.rows_all[0, x, z] = self.sums[0].result()
        r.rows_all[1, x, z] = self.sums[1].result()

        def out():
            r.rows_out[x, z] = self.sums[2].result()

        self.when(2, out)
        for each in self.spreads:
            each.start()
        for i in range(3):
            leave = h.sem()
            copies = [
                pltpu.make_async_remote_copy(
                    src_ref=r.tiles.at[i], dst_ref=r.tiles.at[i], send_sem=leave, recv_sem=self.arrive_each[i],
                    device_id=(h.s, lax.rem(h.c + step, CTX), h.y), device_id_type=MESH)
                for step in range(1, CTX)]

            def start(i=i, copies=copies):
                wait_bytes(r.tile_in, self.arrive)
                r.tiles[i] = added([r.tile_in[c] for c in range(CTX)])
                for copy in copies:
                    copy.start()

            self.when(i, start, h.c == 5 * i)
            h.sent.append(types.SimpleNamespace(
                wait_send=functools.partial(
                    self.when, i, functools.partial(wait_bytes, r.tile_in.at[pl.ds(0, 15)], leave), h.c == 5 * i)))

    def spread_on(self):
        for each in self.spreads:
            each.middle()

    def finish(self):
        h, r = self.h, self.r
        for each in self.spreads:
            each.finish()
        for i in range(3):
            self.when(i, functools.partial(wait_bytes, r.tiles.at[i], self.arrive_each[i]), h.c != 5 * i)
        copies = [
            pltpu.make_async_remote_copy(
                src_ref=src, dst_ref=dst, send_sem=h.sem(), recv_sem=sem, device_id=h.sibling(), device_id_type=MESH)
            for src, dst, sem in (
                (r.rows_all, r.rows_other, self.cross[0]),
                (r.tiles.at[pl.ds(0, 2)], r.tiles_other, self.cross[1]))]

        @pl.when(h.s != self.core)
        def _():
            for copy in copies:
                copy.start()

        h.save_on(self.core, r.rows_all, r.rows_own)
        h.save_on(self.core, r.rows_out, r.rows_out_all)

        @pl.when(h.s != self.core)
        def _():
            for copy in copies:
                copy.wait_send()

        @pl.when(h.s == self.core)
        def _():
            wait_bytes(r.rows_other, self.cross[0])
            wait_bytes(r.tiles_other, self.cross[1])

        h.save_on(self.core, r.rows_other, r.rows_cross)


def rows_outs():
    return dict(tiles=(spec((3, 16, D)), VMEM), tiles_other=(spec((2, 16, D)), VMEM))


def rows_scratch():
    part = VMEM((4, 4, 1, 16, D), BF16)
    return dict(
        rows_c=part, rows_sums_c=reduce_scratch(1, D), rows_second=VMEM((2, 3, 1, 16, D), BF16),
        tile_in=VMEM((CTX, 16, D), BF16), rows_all=VMEM((2, 4, 4, 1, 16, D), BF16), rows_out=part,
        rows_other=VMEM((2, 4, 4, 1, 16, D), BF16))


def rows_results():
    whole_rows = (spec((2, 4, 4, 1, 16, D)), ANY)
    return dict(rows_own=whole_rows, rows_cross=whole_rows, rows_out_all=(spec((4, 4, 1, 16, D)), ANY))


def send_piece(h, piece, dst, layer, arrive):
    leave = h.sem()
    for step in (1, 3, 2, 0):
        shard = h.shard(step)
        src, to = piece.at[shard], dst.at[2 * h.y + h.s]
        copy = pltpu.make_async_remote_copy(
            src_ref=src, dst_ref=to, send_sem=leave, recv_sem=arrive, device_id=(layer, h.c, shard),
            device_id_type=MESH)
        if step:
            copy.start()
        else:
            pl.when(h.s != layer)(copy.start)
            pl.when(h.s == layer)(pltpu.make_async_copy(src, to, arrive).start)

    def wait_send():
        pl.when(h.s != layer)(lambda: wait_bytes(dst.at[pl.ds(0, 4)], leave))
        pl.when(h.s == layer)(lambda: wait_bytes(dst.at[pl.ds(0, 3)], leave))

    h.sent.append(types.SimpleNamespace(wait_send=wait_send))


def joined_up(windows):
    parts = []
    for g in range(8):
        main = windows[g][:, :512]
        if g % 4:
            main = jnp.concatenate([main[:, :128] + windows[g - 1][:, 512:], main[:, 128:]], axis=1)
        parts.append(main)
        if g % 4 == 3:
            parts.append(windows[g][:, 512:])
    return jnp.concatenate(parts, axis=1)


def joined_qkv(blocks, own):
    queries = [blocks[g][:, :128] for g in range(8)] + [own[:, :64]]
    keys = [blocks[g][:, a : a + 64] for g in range(8) for a in (128, 256)] + [own[:, 64:128]]
    values = [blocks[g][:, a : a + 64] for g in range(8) for a in (192, 320)] + [own[:, 128:192]]
    return jnp.concatenate(queries + keys + values + [own[:, 192:]], axis=1)


def added(blocks):
    total = blocks[0].astype(F32)
    for block in blocks[1:]:
        total = total + block.astype(F32)
    return total.astype(BF16)


def last_kernel(at, kept, saved, hidden, above, turn_up_last, norms):
    def body(r):
        h = Here(r.sems)
        x, z = h.c // 4, lax.rem(h.c, 4)
        group = 2 * h.y + h.s
        loads = [h.local(r.qkv_w, r.qkv_vm), h.local(r.a_full, r.a_vm)]
        h.barrier()
        sort_grads(r)
        h.ready()
        up0 = Reduce16(h, None, (None, r.up0_mine, r.up0_in), True)
        up0.send_on()
        main = Reduce16(h, r.main_part, r.main_sums, True)
        side = Reduce16(h, r.side_part, r.side_sums, False)
        arrive_wide = h.sem()
        send_piece(h, r.qkv1_piece, r.wide_in, 1, arrive_wide)
        rows16 = Rows16(h, r, 0)
        rows16.start()
        rows16.start_out()
        arrive_last, arrive_late = h.sem(), h.sem()
        for i in range(SHARD):
            chip = 4 * i + h.y
            r.last_message[i, 0] = r.up_last[i]
            r.last_message[i, 1] = r.up1_last[i]
            r.last_message[i, 2] = r.qkv1_last[i]
            h.send_or_keep(r.last_message.at[i], r.last_in.at[h.c], (h.s, chip, h.y), chip == h.c, arrive_last)
        waits = start_tail(h, r)
        wide = [Spread16(h, parts, i == 0) for i, parts in enumerate((r.wide_low, r.wide_high))]

        def spread_wide():
            wait_bytes(r.wide_in, arrive_wide)
            blocks = [r.wide_in[g] for g in range(8)]

            @pl.when(h.s == 0)
            def _():
                rows = joined_up(blocks)
                r.wide_low[x, z] = rows[:, :2176]
                r.wide_high[x, z] = rows[:, 2176:]

            @pl.when(h.s == 1)
            def _():
                rows = joined_qkv(blocks, added([block[:, 384:] for block in blocks]))
                r.wide_low[x, z] = rows[:, :2176]
                r.wide_high[x, z] = jnp.concatenate([rows[:, 2176:], jnp.zeros((16, 1024), BF16)], axis=1)

            for each in wide:
                each.start()

        def arrived():
            rows16.middle()
            r.up0_piece[...] = up0.result()
            send_piece(h, r.up0_piece, r.wide_in, 0, arrive_wide)

        def beside():
            rows16.spread()
            spread_wide()

        finish = run_tail(
            h, r, 0, r.x[h.s].astype(F32), waits, loads, r.qkv_last, main.start, side.start, arrived, beside,
            lambda half, value: None)
        finish()
        for i in range(SHARD):
            chip = 4 * i + h.y
            h.send_or_keep(r.qkv_last.at[i], r.late_in.at[h.c], (h.s, chip, h.y), chip == h.c, arrive_late)
        main.middle()
        side.middle()
        for each in wide:
            each.middle()
        rows16.spread_on()
        arrive_rest = h.sem()
        reduces = z == h.y

        @pl.when(reduces)
        def _():
            wait_bytes(r.last_in, arrive_last)
            wait_bytes(r.late_in, arrive_late)
            early = added([r.last_in[c] for c in range(CTX)])
            r.rest_message[0, 0] = early[0]
            r.rest_message[0, 1] = added([r.late_in[c] for c in range(CTX)])
            r.rest_message[1] = early[1:]

        rest = []
        for layer in range(2):
            leave = h.sem()
            src, dst = r.rest_message.at[layer], r.rest.at[z, h.s]
            copy = pltpu.make_async_remote_copy(
                src_ref=src, dst_ref=dst, send_sem=leave, recv_sem=arrive_rest, device_id=(layer, h.c, x),
                device_id_type=MESH)
            kept = pltpu.make_async_copy(src, dst, arrive_rest)
            is_self = (h.s == layer) & (x == h.y)
            pl.when(reduces & is_self)(kept.start)
            away = reduces & jnp.logical_not(is_self)
            pl.when(away)(copy.start)
            rest.append((away, copy))
        r.qkv_piece[:, :, :384] = main.result()
        r.qkv_piece[:, :, 384:] = side.result()
        arrive_qkv = h.sem()
        send_piece(h, r.qkv_piece, r.qkv_in, 0, arrive_qkv)
        owner = x == h.y
        across = [h.sem() for _ in range(4)]
        along = [h.sem() for _ in range(3)]
        line = r.rest.at[z]
        lines = []
        for j in range(1, 4):
            lines.append(pltpu.make_async_remote_copy(
                src_ref=line, dst_ref=line, send_sem=across[j], recv_sem=across[0],
                device_id=(h.s, 4 * lax.rem(x + j, 4) + z, h.y), device_id_type=MESH))

        @pl.when(owner)
        def _():
            wait_bytes(line, arrive_rest)
            for copy in lines:
                copy.start()

        spreads = [Spread16(h, parts, i == 0, 0) for i, parts in enumerate((r.qkv_low, r.qkv_high))]

        @pl.when(h.s == 0)
        def _():
            wait_bytes(r.qkv_in, arrive_qkv)
            blocks = [r.qkv_in[g] for g in range(8)]
            rows = joined_qkv(blocks, added([block[:, 384:] for block in blocks]))
            r.qkv_low[x, z] = rows[:, :1664]
            r.qkv_high[x, z] = rows[:, 1664:]

        for each in spreads:
            each.start()
        for each in wide:
            each.finish()
        h.save(r.wide_low, r.wide_low_all)
        h.save(r.wide_high, r.wide_high_all)

        @pl.when(jnp.logical_not(owner))
        def _():
            wait_bytes(line, across[0])

        for j in range(1, 4):
            h.send(line, line, (h.s, 4 * x + lax.rem(z + j, 4), h.y), along[j - 1])
        for each in spreads:
            each.middle()
        rows16.finish()
        for sem in along:
            wait_bytes(line, sem)
        r.up_rest[...] = joined_up([r.rest[g // 2, g % 2, 0] for g in range(8)])
        blocks = [r.rest[g // 2, g % 2, 1] for g in range(8)]
        r.qkv_rest[...] = joined_qkv(blocks, added([block[:, 384:] for block in blocks]))
        for each in spreads:
            each.finish()
        h.save_on(0, r.qkv_low, r.qkv_low_all)
        h.save_on(0, r.qkv_high, r.qkv_high_all)

        @pl.when(owner)
        def _():
            for copy in lines:
                copy.wait_send()

        for away, copy in rest:
            pl.when(away)(copy.wait_send)
        h.finish()

    ins = dict(
        **tail_ins(at, kept, saved, kept.a_full, hidden, above, norms), qkv_w=(kept.qkv_w, ANY), up0_mine=(above.up0_mine, VMEM),
        qkv1_piece=(above.qkv1_piece, VMEM), up_last=(above.up_g_last, VMEM), qkv1_last=(above.qkv_g_last, VMEM),
        up1_last=(turn_up_last, VMEM), mine_a=(above.next_a, VMEM), mine_b=(above.next_b, VMEM), mine_beside=(above.next_beside, VMEM),
        out_sum=(above.out_sum, VMEM))
    up_half, qkv_half = (spec((4, 4, 16, 2176)), ANY), (spec((4, 4, 16, 1664)), ANY)
    outs = dict(
        **tail_outs(), wide_low_all=up_half, wide_high_all=up_half, qkv_low_all=qkv_half, qkv_high_all=qkv_half,
        up_rest=(spec((16, FF)), VMEM), qkv_rest=(spec((16, 3328)), VMEM), **rows_outs(), **rows_results())
    piece, eight = VMEM((SHARD, 16, WINDOW), BF16), VMEM((8, 16, WINDOW), BF16)
    scratch = dict(
        **tail_scratch(),
        main_sums=reduce_scratch(SHARD, 384), side_sums=reduce_scratch(SHARD, 256), **rows_scratch(), wide_low=VMEM((4, 4, 16, 2176), BF16), wide_high=VMEM((4, 4, 16, 2176), BF16),
        qkv_low=VMEM((4, 4, 16, 1664), BF16), qkv_high=VMEM((4, 4, 16, 1664), BF16), qkv_piece=piece, qkv_last=piece, last_message=VMEM((SHARD, 3, 16, WINDOW), BF16),
        last_in=VMEM((CTX, 3, 16, WINDOW), BF16), late_in=VMEM((CTX, 16, WINDOW), BF16), wide_in=eight, qkv_in=eight, up0_piece=piece,
        up0_in=VMEM((3, SHARD, 16, WINDOW), BF16),
        rest_message=VMEM((2, 2, 16, WINDOW), BF16), rest=VMEM((4, 2, 2, 16, WINDOW), BF16),
        sems=pltpu.SemaphoreType.DMA((124,)))
    return call("last", body, ins, outs, scratch, collective_id=5)


def join_kernel(back, last):
    def body(
        _, up_low, up_high, wide_low, wide_high, qkv_low, qkv_high, own0, cross0, out0, own1, cross1, out1, up_rest, qkv_rest,
        tiles0, tiles_other0, tiles1, tiles_other1, up_ref, qkv_ref, norm_ref, down_ref, out_ref):
        def store(rows, up_parts, qkv_parts):
            for at, block in up_parts:
                up_ref[:rows, at : at + block.shape[1]] = block.astype(F32)
            for at, block in qkv_parts:
                block = block.astype(F32)
                if at + block.shape[1] == 3328:
                    norm_ref[:rows] = block[:, -128:]
                    block = block[:, :-64]
                qkv_ref[:rows, at : at + block.shape[1]] = block

        def rows_from(halves, out, tiles):
            @pl.when(pl.program_id(0) < 4)
            def _():
                for c in range(4):
                    for i in range(2):
                        for half in range(2):
                            at = 32 * c + 16 * i
                            down_ref[half, at : at + 16] = halves[half][i, 0, c, 0].astype(F32)
                    out_ref[16 * c : 16 * c + 16] = out[0, c, 0].astype(F32)

            @pl.when(pl.program_id(0) == 4)
            def _():
                for half in range(2):
                    down_ref[half, :32] = tiles[half][:2].reshape(32, D).astype(F32)
                out_ref[:16] = tiles[2].astype(F32)

        first = lax.axis_index(SECTION) == 0
        pl.when(first)(lambda: rows_from((own0, cross0), out0, (tiles0, tiles_other0, tiles0[2])))
        pl.when(jnp.logical_not(first))(
            lambda: rows_from((cross1, own1), out1, (tiles_other1, tiles1, tiles1[2])))
        low, high = (ref[0].reshape(64, 2176) for ref in (wide_low, wide_high))

        @pl.when((pl.program_id(0) < 4) & first)
        def _():
            parts = [ref[0].reshape(64, 1664) for ref in (qkv_low, qkv_high)]
            store(64, ((0, low), (2176, high)), ((0, parts[0]), (1664, parts[1])))

        @pl.when((pl.program_id(0) < 4) & jnp.logical_not(first))
        def _():
            parts = [ref[0].reshape(64, 2176) for ref in (up_low, up_high)]
            store(64, ((0, parts[0]), (2176, parts[1])), ((0, low), (2176, high[:, :1152])))

        @pl.when(pl.program_id(0) == 4)
        def _():
            store(16, ((0, up_rest[...]),), ((0, qkv_rest[...]),))

    def place(i, section, core):
        return jnp.where((core < 0) | (section[0] == core), jnp.minimum(i, 3), 0)

    def line(width, core):
        return pl.BlockSpec((1, 4, 16, width), lambda i, section: (place(i, section, core), 0, 0, 0))

    def tile_line(core, *lead):
        zeros = (0,) * len(lead)
        return pl.BlockSpec(
            (*lead, 1, 4, 1, 16, D), lambda i, section: (*zeros, place(i, section, core), 0, 0, 0, 0))

    def tiles_of(count):
        return pl.BlockSpec((count, 16, D), lambda i, section: (0, 0, 0))

    def rows(width, count=64):
        return pl.BlockSpec((count, width), lambda i, section: (i, 0))

    def all_of(width):
        return pl.BlockSpec((16, width), lambda i, section: (0, 0))

    return pl.pallas_call(
        body,
        out_shape=(
            spec((SLICE, FF), F32), spec((SLICE, 3 * D), F32), spec((SLICE, 128), F32), spec((2, 544, D), F32),
            spec((SLICE, D), F32)),
        grid_spec=pltpu.PrefetchScalarGridSpec(
            num_scalar_prefetch=1,
            grid=(5,),
            in_specs=[
                line(2176, 1), line(2176, 1), line(2176, -1), line(2176, -1), line(1664, 0), line(1664, 0),
                tile_line(0, 2), tile_line(0, 2), tile_line(0), tile_line(1, 2), tile_line(1, 2), tile_line(1),
                all_of(FF), all_of(3328), *[tiles_of(3), tiles_of(2)] * 2],
            out_specs=(
                rows(FF), rows(3 * D), rows(128), pl.BlockSpec((2, 128, D), lambda i, section: (0, i, 0)), rows(D))),
        name="join",
    )(lax.axis_index(SECTION).astype(jnp.int32).reshape(1), back.up_low_all, back.up_high_all, last.wide_low_all, last.wide_high_all, last.qkv_low_all, last.qkv_high_all, last.rows_own,
      last.rows_cross, last.rows_out_all, back.rows_own, back.rows_cross, back.rows_out_all, last.up_rest, last.qkv_rest,
      last.tiles, last.tiles_other, back.tiles, back.tiles_other)


def token_positions(block_order):
    offsets = jnp.arange(32, dtype=jnp.int32)
    groups = jnp.arange(2, dtype=jnp.int32)[:, None, None] * GROUP
    return (groups + block_order[:, :, None] * 32 + offsets).reshape(2, GROUP)


def swapped(section, first, second):
    own = jnp.where(section == 0, first, second)
    other = lax.ppermute(jnp.where(section == 0, second, first), SECTION, [(0, 1), (1, 0)])
    return jnp.where(section == 0, own, other), jnp.where(section == 0, other, own)


def gathered(x):
    return lax.all_gather(x, CONTEXT)


def shards(hidden_in, cotangent, block_order, qkv_weight, out_weight, up_weight, down_weight, norm_gains, norm_biases):
    section, ctx = lax.axis_index(SECTION), lax.axis_index(CONTEXT)
    params = jnp.concatenate([norm_gains[0], norm_biases[0]], axis=0).astype(F32)
    params = jnp.pad(params, ((0, 4), (0, 0)))
    grid = token_positions(block_order)
    own_positions = lax.dynamic_slice(grid, (section, ctx * ROWS), (1, ROWS))
    positions = grid.reshape(1, SEQ)
    slots = jnp.arange(32, dtype=jnp.int32)
    slot = jnp.sum(jnp.where(block_order[:, None, :] == slots[None, :, None], slots[None, None, :], 0), axis=2)
    group, odd = jnp.arange(2, dtype=jnp.int32)[:, None], slot % 2
    chip = slot // 2
    places = jnp.stack([10 * chip + 4 * group + 2 * odd, 10 * chip + 8 + odd, 2 * chip + odd])
    at = (block_order, places, positions, own_positions.reshape(ROWS, 1))
    at_back = (block_order, places, positions.reshape(SEQ, 1), own_positions)
    hidden = hidden_in[0]
    spread = spread_kernel(params, qkv_weight, up_weight)
    norms = spread.norms
    mid_all = gathered(spread.mid_piece)
    first = first_kernel(hidden, norms, spread.side_piece, spread.side_last, out_weight, down_weight)
    up_piece, first.q16 = lax.optimization_barrier((spread.side_piece[SHARD:], first.q16))
    up_all = gathered(up_piece)
    middle = middle_kernel(at, hidden, norms, first, mid_all, spread.mid_last)
    turn = turn_kernel(at, middle, middle.y, norms, first, up_all, spread.side_last[SHARD:], cotangent[0])
    back = back_kernel(
        at_back, middle, turn, middle.y, turn, norms, first, middle.attended16, mid_all, spread.mid_last)
    last = last_kernel(at_back, first, middle, hidden, back, turn.up_g_last, norms)
    up, qkv, norm_sums, down, out = join_kernel(back, last)
    norm_sums = norm_sums[:, 64:68].T
    activations = jnp.stack(swapped(section, middle.y, back.out))
    input_grads = jnp.stack(swapped(section, last.in_grad, back.in_grad))
    return (
        activations[None, None],
        input_grads[None, None],
        qkv[None],
        out[None],
        up[None],
        down.reshape(D, D)[None],
        norm_sums[None, 0::2],
        norm_sums[None, 1::2],
    )


def solution(mesh):
    tokens = P(LINE, None, CONTEXT, None)
    rows = P(SECTION, LINE, None)
    norms = P(SECTION, None, LINE)
    layers = P(SECTION, LINE, None, CONTEXT, None)
    return jax.shard_map(
        shards,
        mesh=mesh,
        in_specs=(tokens, tokens, P(), rows, rows, rows, rows, norms, norms),
        out_specs=(layers, layers, rows, rows, rows, rows, norms, norms),
        check_vma=False,
    )
```

```python
import functools
import types

import jax
import jax.numpy as jnp
from jax import lax
from jax.experimental import pallas as pl
from jax.experimental.pallas import tpu as pltpu
from jax.sharding import PartitionSpec as P

D = 1088
HEADS = 17
HEAD_DIM = 64
FF = 4352
SHARD = 4
CTX = 16
ROWS = 64
GROUP = 1024
SEQ = 2048
WINDOW = 640
SLICE = D // SHARD
EPSILON = 1e-05
NEG_LARGE = -1e30
BF16 = jnp.bfloat16
F32 = jnp.float32
MESH = pl.DeviceIdType.MESH
VMEM = pltpu.VMEM
ANY = pl.ANY
VMEM_BYTES = 58 * 2**20
SECTION, CONTEXT, LINE = "section", "ctx", "shard"
TILES = (68, 16, WINDOW)


def spec(shape, dtype=BF16):
    return jax.ShapeDtypeStruct(shape, dtype)


def call(name, body, ins, outs, scratch, collective_id=None):
    def kernel(*refs):
        refs, found = list(refs), {}
        for key, value in [*ins.items(), *outs.items(), *scratch.items()]:
            if isinstance(value, list):
                found[key], refs = refs[: len(value)], refs[len(value) :]
            else:
                found[key] = refs.pop(0)
        body(types.SimpleNamespace(**found))

    extra = {} if collective_id is None else dict(collective_id=collective_id, has_side_effects=True)
    shapes, given = [], []
    for value in scratch.values():
        shapes += value if isinstance(value, list) else [value]
    for value in ins.values():
        given += value if isinstance(value, list) else [value]
    results = pl.pallas_call(
        kernel,
        out_shape=tuple(value[0] for value in outs.values()),
        in_specs=[pl.BlockSpec(memory_space=space) for _, space in given],
        out_specs=tuple(pl.BlockSpec(memory_space=value[1]) for value in outs.values()),
        scratch_shapes=shapes,
        compiler_params=pltpu.CompilerParams(vmem_limit_bytes=VMEM_BYTES, **extra),
        name=name,
    )(*(array for array, _ in given))
    return types.SimpleNamespace(**dict(zip(outs, results)))


def dot(a, b):
    return jnp.dot(a, b, preferred_element_type=F32)


def dot_nt(a, b):
    return lax.dot_general(a, b, (((1,), (1,)), ((), ())), preferred_element_type=F32)


def dot_tn(a, b):
    return lax.dot_general(a, b, (((0,), (0,)), ((), ())), preferred_element_type=F32)


def norm_parts(values):
    center = values - jnp.mean(values, axis=-1, keepdims=True)
    rate = lax.rsqrt(jnp.mean(center * center, axis=-1, keepdims=True) + EPSILON)
    return center * rate, rate


def layer_norm(values, gain, bias):
    return norm_parts(values)[0] * gain + bias


def gelu(u):
    return 0.5 * u * (1.0 + jnp.tanh(0.7978845608028654 * (u + 0.044715 * u * u * u)))


class Here:
    def __init__(self, sems):
        self.s = lax.axis_index(SECTION)
        self.c = lax.axis_index(CONTEXT)
        self.y = lax.axis_index(LINE)
        self.sems, self.used, self.sent = sems, 0, []

    def sem(self):
        self.used += 1
        return self.sems.at[self.used - 1]

    def shard(self, step):
        return lax.rem(self.y + step, SHARD)

    def rows(self, shard, core):
        return pl.ds(pl.multiple_of((shard * 2 + core) * ROWS, ROWS), ROWS)

    def barrier(self, whole=True):
        sem = pltpu.get_barrier_semaphore()
        peers = []
        for step in range(SHARD):
            for core in range(2):
                if step or core:
                    peers.append((lax.rem(self.s + core, 2), self.c, self.shard(step)))
        for step in range(1, CTX if whole else 1):
            for core in range(2):
                peers.append((core, lax.rem(self.c + step, CTX), self.y))
        for to in peers:
            pl.semaphore_signal(sem, inc=1, device_id=to, device_id_type=MESH)
        self.awaited = len(peers)

    def ready(self):
        pl.semaphore_wait(pltpu.get_barrier_semaphore(), self.awaited)

    def save_on(self, core, src, dst):
        copy = pltpu.make_async_copy(src, dst, self.sem())
        pl.when(self.s == core)(copy.start)
        self.sent.append(types.SimpleNamespace(wait_send=lambda: pl.when(self.s == core)(copy.wait)))

    def local(self, src, dst):
        copy = pltpu.make_async_copy(src, dst, self.sem())
        copy.start()
        return copy

    def save(self, src, dst):
        copy = self.local(src, dst)
        self.sent.append(types.SimpleNamespace(wait_send=copy.wait))

    def wait_later(self, ref, sem):
        self.sent.append(types.SimpleNamespace(wait_send=lambda: wait_bytes(ref, sem)))

    def send(self, src, dst, to, arrive, leave=None):
        copy = pltpu.make_async_remote_copy(
            src_ref=src, dst_ref=dst, send_sem=self.sem() if leave is None else leave,
            recv_sem=arrive, device_id=to, device_id_type=MESH)
        copy.start()
        if leave is None:
            self.sent.append(copy)
        return copy

    def send_or_keep(self, src, dst, to, is_self, arrive):
        leave = self.sem()
        copy = pltpu.make_async_remote_copy(
            src_ref=src, dst_ref=dst, send_sem=leave, recv_sem=arrive, device_id=to, device_id_type=MESH)
        kept = pltpu.make_async_copy(src, dst, arrive)
        pl.when(jnp.logical_not(is_self))(copy.start)
        pl.when(is_self)(kept.start)

        def wait_send():
            pl.when(jnp.logical_not(is_self))(copy.wait_send)

        self.sent.append(types.SimpleNamespace(wait_send=wait_send))

    def sibling(self):
        return (1 - self.s, self.c, self.y)

    def finish(self):
        for copy in self.sent:
            copy.wait_send()
        self.sent = []


def wait_bytes(ref, sem):
    pltpu.make_async_copy(ref, ref, sem).wait()


PARTS = 2
HALF = ROWS // PARTS


def half_rows(half):
    return slice(HALF * half, HALF * half + HALF)


class Messages:
    def __init__(self, h, arrived):
        self.h, self.arrived, self.leave = h, arrived, h.sem()

    def add(self, sends):
        for src, dst, to, here, arrive in sends:
            copy = pltpu.make_async_remote_copy(
                src_ref=src, dst_ref=dst, send_sem=self.leave, recv_sem=arrive, device_id=to, device_id_type=MESH)
            pl.when(jnp.logical_not(here))(copy.start)
            pl.when(here)(pltpu.make_async_copy(src, dst, arrive).start)

    def done(self):
        h = self.h

        def wait_send():
            pl.when(h.c // 8 != h.s)(lambda: wait_bytes(self.arrived, self.leave))
            pl.when(h.c // 8 == h.s)(lambda: wait_bytes(self.arrived.at[pl.ds(0, 15)], self.leave))

        h.sent.append(types.SimpleNamespace(wait_send=wait_send))


class Gather8:
    def __init__(self, here, full):
        self.here, self.full = here, full
        self.own = [[here.sem() for _ in range(PARTS)] for _ in range(SHARD)]
        self.other = [[here.sem() for _ in range(PARTS)] for _ in range(SHARD)]
        self.leave = here.sem()
        here.wait_later(full.at[pl.ds(0, 7 * ROWS)], self.leave)

    def rows(self, shard, core, half):
        return self.full.at[pl.ds(pl.multiple_of((shard * 2 + core) * ROWS + half * HALF, HALF), HALF)]

    def start(self, value, half):
        h = self.here
        mine = self.rows(h.y, h.s, half)
        mine[...] = value
        h.send(mine, mine, h.sibling(), self.other[0][half], self.leave)
        for step in (1, 3, 2):
            h.send(mine, mine, (h.s, h.c, h.shard(step)), self.own[SHARD - step][half], self.leave)

    def relay(self, step):
        h = self.here
        for half in range(PARTS):
            part = self.rows(h.shard(step), h.s, half)
            wait_bytes(part, self.own[step][half])
            h.send(part, part, h.sibling(), self.other[step][half], self.leave)

    def wait(self, step):
        h = self.here
        for half in range(PARTS):
            wait_bytes(self.rows(h.shard(step), 1 - h.s, half), self.other[step][half])


class Scatter8:
    def __init__(self, here, bufs):
        self.here = here
        self.to_core, self.mine, self.from_core, self.to_shard, self.from_shard = bufs
        self.core = [[here.sem() for _ in range(PARTS)] for _ in range(SHARD)]
        self.shard = [[here.sem() for _ in range(PARTS)] for _ in range(SHARD)]
        self.leave = [here.sem(), here.sem()]
        here.wait_later(self.from_core, self.leave[0])
        here.wait_later(self.from_shard.at[pl.ds(0, 3)], self.leave[1])

    def part(self, ref, step, half):
        return ref.at[step, pl.ds(half * HALF, HALF)]

    def put(self, step, block):
        h = self.here
        low, high = block[:ROWS], block[ROWS:]
        self.to_core[step] = jnp.where(h.s == 0, high, low).astype(BF16)
        self.mine[step] = jnp.where(h.s == 0, low, high)
        for half in range(PARTS):
            h.send(
                self.part(self.to_core, step, half), self.part(self.from_core, step, half), h.sibling(),
                self.core[step][half], self.leave[0])

    def relay(self, steps):
        h = self.here
        for half in range(PARTS):
            for step in steps:
                part = self.part(self.from_core, step, half)
                wait_bytes(part, self.core[step][half])
                total = self.mine[step, half_rows(half)] + part[...].astype(F32)
                out = self.part(self.to_shard, step, half)
                out[...] = total.astype(BF16)
                h.send(
                    out, self.part(self.from_shard, step, half), (h.s, h.c, h.shard(step)), self.shard[step][half],
                    self.leave[1])

    def result(self, half):
        part = self.part(self.from_core, 0, half)
        wait_bytes(part, self.core[0][half])
        total = self.mine[0, half_rows(half)] + part[...].astype(F32)
        for step in (1, 3, 2):
            part = self.part(self.from_shard, step, half)
            wait_bytes(part, self.shard[step][half])
            total = total + part[...].astype(F32)
        return total


def scatter_scratch():
    quarter = (SHARD, ROWS, D)
    return [VMEM(quarter, BF16), VMEM(quarter, F32), VMEM(quarter, BF16), VMEM(quarter, BF16), VMEM(quarter, BF16)]


ORDER = (0, 1, 3, 2)


def window_offset(group):
    return 32 * lax.rem(group, 4)


def everyone(h):
    for step in (1, 3, 2, 0):
        for other in range(2):
            yield step, other, (lax.rem(h.s + other, 2), h.c, h.shard(step))


def packed_qkv(rows, g):
    keys = rows[:, D + 128 * g : D + 128 * g + 128]
    values = rows[:, 2 * D + 128 * g : 2 * D + 128 * g + 128]
    return jnp.concatenate([
        rows[:, 128 * g : 128 * g + 128], keys[:, :64], values[:, :64], keys[:, 64:], values[:, 64:],
        rows[:, D - 64 : D], rows[:, 2 * D - 64 : 2 * D], rows[:, 3 * D - 64 : 3 * D], jnp.zeros_like(keys[:, :64])],
        axis=1)


def window(g):
    return slice(128 * (17 * g // 4), 128 * (17 * g // 4) + WINDOW)


def spread_kernel(gains, biases, w_qkv, w_up):
    def body(r):
        h = Here(r.sems)
        own = pl.ds(pl.multiple_of(h.c * 16, 16), 16)
        loads = [
            h.local(ref.at[0, rows], dst.at[pl.ds(16 * i, 16)])
            for ref, dst in ((r.w_up, r.up_rows), (r.w_qkv, r.qkv_rows)) for i, rows in enumerate((own, pl.ds(256, 16)))]
        h.barrier(whole=False)
        h.ready()
        arrive, arrive_mid, arrive_up = h.sem(), h.sem(), h.sem()
        mine = r.params_in.at[h.s * SHARD + h.y]
        zeros = jnp.zeros((4, SLICE), F32)
        mine[...] = jnp.concatenate([r.gains[0].astype(F32), r.biases[0].astype(F32), zeros], axis=0)
        for step, other, to in everyone(h):
            if step or other:
                h.send(mine, mine, to, arrive)
        for copy in loads:
            copy.wait()

        @pl.when(h.s == 0)
        def _():
            for g in range(8):
                r.mid[g] = r.up_rows[:, window(g)].reshape(2, 16, WINDOW)
                r.up[g] = packed_qkv(r.qkv_rows[...], g).reshape(2, 16, WINDOW)

        @pl.when(h.s == 1)
        def _():
            for g in range(8):
                r.mid[g] = packed_qkv(r.qkv_rows[...], g).reshape(2, 16, WINDOW)
                r.up[g] = r.up_rows[:, window(g)].reshape(2, 16, WINDOW)

        for step, other, to in everyone(h):
            g = 2 * to[2] + to[0]
            slot = h.s * SHARD + h.y
            for sem, source, targets in (
                    (arrive_up, r.up, (r.side_piece, r.side_last)), (arrive_mid, r.mid, (r.mid_piece, r.mid_last))):
                for half in range(2):
                    src, dst = source.at[g, half], targets[half].at[slot]
                    if step or other:
                        h.send(src, dst, to, sem)
                    else:
                        pltpu.make_async_copy(src, dst, sem).start()
        wait_bytes(r.params_in.at[pl.ds(0, 7)], arrive)
        for layer in range(2):
            r.norms[layer] = jnp.concatenate([r.params_in[layer * SHARD + i] for i in range(SHARD)], axis=1)
        wait_bytes(r.mid, arrive_mid)
        wait_bytes(r.up, arrive_up)
        h.finish()

    ins = dict(gains=(gains, VMEM), biases=(biases, VMEM), w_qkv=(w_qkv, ANY), w_up=(w_up, ANY))
    outs = dict(
        norms=(spec((2, 8, D), F32), VMEM), mid_piece=(spec((8, 16, WINDOW)), VMEM),
        mid_last=(spec((8, 16, WINDOW)), VMEM), side_piece=(spec((8, 16, WINDOW)), VMEM),
        side_last=(spec((8, 16, WINDOW)), VMEM))
    scratch = dict(
        params_in=VMEM((8, 8, SLICE), F32), up_rows=VMEM((32, FF), BF16), qkv_rows=VMEM((32, 3 * D), BF16),
        mid=VMEM((8, 2, 16, WINDOW), BF16), up=VMEM((8, 2, 16, WINDOW), BF16), sems=pltpu.SemaphoreType.DMA((42,)))
    return call("spread", body, ins, outs, scratch, collective_id=0)


def load_tiles(h, gathered, last, dst, first=0):
    sem = h.sem()
    for i in range(SHARD):
        pltpu.make_async_copy(gathered.at[:, first + i], dst.at[pl.ds(17 * i, 16)], sem).start()
        pltpu.make_async_copy(last.at[first + i], dst.at[17 * i + 16], sem).start()
    return [types.SimpleNamespace(wait=lambda: wait_bytes(dst, sem))]


def place(value, parts, last):
    tiles = value.astype(BF16).reshape(68, 16, value.shape[1])
    for i in range(SHARD):
        for c in range(CTX):
            parts[c // 4, c % 4, i] = tiles[17 * i + c]
        last[i] = tiles[17 * i + 16]


def whole(ref):
    return ref[...].reshape(D, WINDOW)


class FirstWeights:
    def __init__(self, h, r):
        self.h, self.r = h, r
        self.arrive = [h.sem() for _ in range(3)]
        self.spreads = [Spread16(h, parts, i == 0) for i, parts in enumerate((r.qkv_low, r.qkv_high))]

    def load(self):
        h, r = self.h, self.r
        self.loads = [h.local(r.w_down.at[0], r.down_rows), h.local(r.w_out.at[0], r.out_rows)]

    def send_qkv(self):
        r = self.r
        for i, (each, parts) in enumerate(zip(self.spreads, (r.qkv_low, r.qkv_high))):
            parts[each.x, each.z] = r.side_piece[2 * i : 2 * i + 2]
            each.start()

    def send_qkv_on(self):
        for each in self.spreads:
            each.middle()

    def send_rest(self):
        h, r = self.h, self.r
        for copy in self.loads:
            copy.wait()
        for other in range(2):
            core = lax.rem(h.s + other, 2)
            at = pl.multiple_of(window_offset(h.y * 2 + core), 32)
            src = r.down_rows.at[pl.ds(pl.multiple_of(544 * core, 16), 544)]
            dst = r.down_vm.at[h.s, pl.ds(at, 544)]
            if other:
                h.send(src, dst, h.sibling(), self.arrive[1])
            else:
                pltpu.make_async_copy(src, dst, self.arrive[1]).start()
        self.tiles = []
        for i in range(17):
            tile = h.y * 17 + i
            group = jnp.minimum(tile // 8, 7)
            core, shard = lax.rem(group, 2), group // 2
            src = r.out_rows.at[pl.ds(16 * i, 16)]
            dst = r.out_vm.at[h.s, pl.ds(pl.multiple_of(lax.rem(tile, 8) * 16, 16), 16)]
            copy = pltpu.make_async_remote_copy(
                src_ref=src, dst_ref=dst, send_sem=h.sem(), recv_sem=self.arrive[2],
                device_id=(core, h.c, shard), device_id_type=MESH)
            same = pltpu.make_async_copy(src, dst, self.arrive[2])
            is_self = (core == h.s) & (shard == h.y)
            pl.when((tile < 64) & is_self)(same.start)
            away = (tile < 64) & jnp.logical_not(is_self)
            pl.when(away)(copy.start)
            self.tiles.append((away, copy))
        src, dst = r.out_rows.at[pl.ds(SLICE - 64, 64)], r.out_vm.at[h.s, pl.ds(128, 64)]
        same = pltpu.make_async_copy(src, dst, self.arrive[2])
        self.last = []
        for step, other, to in everyone(h):
            if step or other:
                self.last.append(pltpu.make_async_remote_copy(
                    src_ref=src, dst_ref=dst, send_sem=h.sem(), recv_sem=self.arrive[2], device_id=to,
                    device_id_type=MESH))

        @pl.when(h.y == SHARD - 1)
        def _():
            same.start()
            for copy in self.last:
                copy.start()

    def wait_qkv(self):
        r = self.r
        for each in self.spreads:
            each.finish()
        for i in range(SHARD):
            for c in range(CTX):
                parts = (r.qkv_low, r.qkv_high)[i // 2]
                r.qkv_vm[17 * i + c] = parts[c // 4, c % 4, i % 2]
            r.qkv_vm[17 * i + 16] = r.side_last[i]

    def finish(self):
        r, h = self.r, self.h
        wait_bytes(r.down_vm.at[:, pl.ds(0, 544)], self.arrive[1])
        h.save(r.down_vm, r.down_w)
        wait_bytes(r.out_vm, self.arrive[2])
        h.save(r.out_vm, r.out_w)

        for away, copy in self.tiles:
            pl.when(away)(copy.wait_send)

        @pl.when(h.y == SHARD - 1)
        def _():
            for copy in self.last:
                copy.wait_send()


def head_outs():
    return dict(
        a_full=(spec((512, D)), ANY), message_in=(spec((CTX, 160, 128)), VMEM),
        kv16_in=(spec((2, CTX, ROWS, 128)), VMEM), q16=(spec((ROWS, HEAD_DIM)), VMEM))


def head_scratch():
    return dict(message=VMEM((2, 4, 2, 160, 128), BF16), qkv_vm=VMEM(TILES, BF16), a_vm=VMEM((512, D), BF16))


def run_head(h, r, gather, after=None):
    arrive = h.sem()
    own16 = dot(r.a_vm[h.rows(h.y, h.s)], r.qkv_vm[:, :, 384:].reshape(D, 256)).astype(BF16)
    r.q16[...] = own16[:, :64]
    r.kv16_in[h.s, h.c] = own16[:, 64:192]
    own_kv = r.kv16_in.at[h.s, h.c]
    leave16, arrive16, cross16 = h.sem(), h.sem(), h.sem()
    for step in range(1, CTX):
        h.send(own_kv, own_kv, (h.s, lax.rem(h.c + step, CTX), h.y), arrive16, leave16)
    messages = Messages(h, r.message_in)
    for step in ORDER:
        if step:
            gather.relay(step)
        gather.wait(step)
        sends = []
        shard = h.shard(step)
        block = r.a_vm[pl.ds(pl.multiple_of(shard * 128, 128), 128)]
        out = dot(block, r.qkv_vm[:, :, :384].reshape(D, 384)).astype(BF16)
        for e in range(2):
            for core in range(2):
                r.message[e, shard, core, :128] = out[:, 128 + 128 * e : 256 + 128 * e]
                for b in range(2):
                    at = 32 * b + 16 * core
                    lanes = slice(64 * e, 64 * e + 64)
                    packed = jnp.concatenate([out[at : at + 16, lanes], out[64 + at : 80 + at, lanes]], axis=1)
                    r.message[e, shard, core, 128 + 16 * b : 144 + 16 * b] = packed
                chip = 8 * h.s + 4 * e + shard
                sends.append((
                    r.message.at[e, shard, core], r.message_in.at[h.c], (core, chip, h.y),
                    (chip == h.c) & (h.s == core), arrive))
        messages.add(sends)
    messages.done()
    h.save(r.a_vm, r.a_full)
    if after is not None:
        after()
    wait_bytes(r.kv16_in.at[h.s, pl.ds(0, CTX - 1)], arrive16)
    cross = r.kv16_in.at[h.s]
    h.send(cross, cross, h.sibling(), cross16)
    wait_bytes(r.kv16_in.at[h.s, pl.ds(0, CTX - 1)], leave16)
    wait_bytes(r.kv16_in.at[1 - h.s], cross16)
    wait_bytes(r.message_in, arrive)


def first_kernel(hidden, norms, side_piece, side_last, w_out, w_down):
    def body(r):
        h = Here(r.sems)
        weights = FirstWeights(h, r)
        weights.load()
        r.down_vm[...] = jnp.zeros_like(r.down_vm)
        h.barrier()
        x = r.hidden[h.s].astype(F32)
        a_value = layer_norm(x, r.norms[0, 0:1], r.norms[0, 2:3]).astype(BF16)
        h.ready()
        weights.send_qkv()
        gather = Gather8(h, r.a_vm)
        for half in range(PARTS):
            gather.start(a_value[half_rows(half)], half)
        weights.send_qkv_on()
        weights.wait_qkv()
        h.save(r.qkv_vm, r.qkv_w)
        run_head(h, r, gather, weights.send_rest)
        weights.finish()
        h.finish()

    ins = dict(hidden=(hidden, VMEM), norms=(norms, VMEM), side_piece=(side_piece, VMEM), side_last=(side_last, VMEM),
        w_out=(w_out, ANY), w_down=(w_down, ANY))
    outs = dict(
        **head_outs(), qkv_w=(spec(TILES), ANY), out_w=(spec((2, 192, D)), ANY), down_w=(spec((2, WINDOW, D)), ANY))
    scratch = dict(
        **head_scratch(), qkv_low=VMEM((4, 4, 2, 16, WINDOW), BF16), qkv_high=VMEM((4, 4, 2, 16, WINDOW), BF16),
        down_rows=VMEM((D, D), BF16), out_rows=VMEM((SLICE, D), BF16), down_vm=VMEM((2, WINDOW, D), BF16),
        out_vm=VMEM((2, 192, D), BF16), sems=pltpu.SemaphoreType.DMA((65,)))
    return call("first", body, ins, outs, scratch, collective_id=1)


def sort_rows(r):
    for m in range(2):
        for p in range(32):
            at = 32 * m + p
            tile = r.places[0, m, p]
            for i in range(2):
                rows = r.kept[tile + i]
                r.keys[32 * at + 16 * i : 32 * at + 16 * i + 16] = rows[:, :64]
                r.values[32 * at + 16 * i : 32 * at + 16 * i + 16] = rows[:, 64:]
            query = r.kept[r.places[1, m, p]]
            r.queries[16 * at : 16 * at + 16] = query[:, 64 * m : 64 * m + 64] * 0.125


def attend(h, r):
    row = lax.broadcasted_iota(jnp.int32, (256, 512), 0)
    row = 32 * (row // 16) + 16 * h.s + row % 16
    visible = row >= lax.broadcasted_iota(jnp.int32, (256, 512), 1)
    for t in range(4):
        query = r.queries[256 * t : 256 * t + 256]
        parts = [dot_nt(query, r.keys[512 * u : 512 * u + 512]) for u in range(t + 1)]
        parts[t] = jnp.where(visible, parts[t], NEG_LARGE)
        top = parts[0]
        for p in parts[1:]:
            top = jnp.maximum(top, p)
        top = jnp.max(top, axis=-1, keepdims=True)
        parts = [jnp.exp(p - top) for p in parts]
        total = parts[0]
        for p in parts[1:]:
            total = total + p
        total = jnp.sum(total, axis=-1, keepdims=True)
        out = dot(parts[0].astype(BF16), r.values[:512])
        for u in range(1, t + 1):
            out = out + dot(parts[u].astype(BF16), r.values[512 * u : 512 * u + 512])
        r.sorted_out[16 * t : 16 * t + 16] = (out / total).astype(BF16).reshape(16, 16, 64)
        r.logs[256 * t : 256 * t + 256] = jnp.broadcast_to(top + jnp.log(total), (256, 128))
    for c in range(CTX):
        for m in range(2):
            for b in range(2):
                rows = r.sorted_out[32 * m + r.order[m, 2 * c + b]]
                r.attended[c, 16 * b : 16 * b + 16, 64 * m : 64 * m + 64] = rows


def attend_last(r):
    kv = r.kept16[...].reshape(SEQ, 128)
    scores = dot_nt(r.kept_q16[...] * 0.125, kv[:, :64])
    scores = jnp.where(r.own_positions[...] >= r.positions[...], scores, NEG_LARGE)
    top = jnp.max(scores, axis=-1, keepdims=True)
    scores = jnp.exp(scores - top)
    total = jnp.sum(scores, axis=-1, keepdims=True)
    out = dot(scores.astype(BF16), kv[:, 64:])
    r.attended16[...] = (out / total).astype(BF16)
    r.logs16[...] = jnp.broadcast_to(top + jnp.log(total), (ROWS, 128))


def attend_ins(kept, at):
    order, places, positions, own_positions = at
    return dict(
        order=(order, pltpu.SMEM), places=(places, pltpu.SMEM), positions=(positions, VMEM),
        own_positions=(own_positions, VMEM), kept=(kept.message_in.reshape(160, 16, 128), VMEM), kept16=(kept.kv16_in, VMEM),
        kept_q16=(kept.q16, VMEM))


def attend_outs():
    return dict(
        attended16=(spec((ROWS, 64)), VMEM), sorted_out=(spec((64, 16, 64)), VMEM), logs=(spec((1024, 128), F32), VMEM),
        logs16=(spec((ROWS, 128), F32), VMEM))


def attend_scratch():
    return dict(
        keys=VMEM((SEQ, 64), BF16), values=VMEM((SEQ, 64), BF16), queries=VMEM((1024, 64), BF16),
        attended=VMEM((CTX, 32, 128), BF16))


def middle_scratch():
    return dict(
        context_in=VMEM((2, 4, 2, 32, 128), BF16), out_vm=VMEM((192, D), BF16), up_vm=VMEM(TILES, BF16),
        down_vm=VMEM((WINDOW, D), BF16), to_out=scatter_scratch(), to_down=scatter_scratch())


def load_layer(h, r, layer, first):
    loads = [h.local(r.out_w.at[layer], r.out_vm), h.local(r.down_w.at[layer], r.down_vm)]
    return loads + load_tiles(h, r.up_all, r.up_last, r.up_vm, first)


def gather_context(h, r):
    arrive = h.sem()
    to_core = h.c // 8
    e, j = lax.rem(h.c // 4, 2), lax.rem(h.c, 4)
    messages = Messages(h, r.attended)
    messages.add([
        (r.attended.at[c], r.context_in.at[e, j, h.s], (to_core, c, h.y), (h.c == c) & (h.s == to_core), arrive)
        for c in range(CTX)])
    messages.done()
    return arrive


def unpack_context(r, store):
    for j in range(4):
        for m in range(2):
            for b in range(2):
                for core in range(2):
                    lanes = slice(64 * m, 64 * m + 64)
                    piece = jnp.concatenate(
                        [r.context_in[e, j, core, 16 * b : 16 * b + 16, lanes] for e in range(2)], axis=1)
                    at = 128 * j + 64 * m + 32 * b + 16 * core
                    store[at : at + 16] = piece


def block_rows(h, step):
    return pl.ds(pl.multiple_of(h.shard(step) * 128, 128), 128)


def run_out(h, r, x, ready):
    sums = Scatter8(h, r.to_out)
    for step in (2, 1, 3, 0):
        sums.put(step, dot(r.context[block_rows(h, step)], r.out_vm[:128]))
    sums.relay((2, 1, 3))
    own = x + dot(r.attended16[...], r.out_vm[128:])
    for half in range(PARTS):
        residual = own[half_rows(half)] + sums.result(half)
        r.residual[half_rows(half)] = residual
        ready(half, residual)


def middle_kernel(at, x, norms, first, mid_all, mid_last):
    def body(r):
        h = Here(r.sems)
        loads = load_layer(h, r, 0, 0)
        head_loads = load_tiles(h, r.up_all, r.up_last, r.qkv_vm, SHARD)
        h.barrier()
        sort_rows(r)
        attend(h, r)
        h.ready()
        arrive = gather_context(h, r)
        attend_last(r)
        for copy in loads:
            copy.wait()
        wait_bytes(r.context_in, arrive)
        unpack_context(r, r.context)
        gather = Gather8(h, r.b_vm)

        def ready(half, residual):
            gather.start(layer_norm(residual, r.norms[0, 1:2], r.norms[0, 3:4]).astype(BF16), half)

        run_out(h, r, r.x[h.s].astype(F32), ready)
        sums = Scatter8(h, r.to_down)
        for step in ORDER:
            if step:
                gather.relay(step)
            gather.wait(step)
            rows = block_rows(h, step)
            u = dot(r.b_vm[rows], whole(r.up_vm))
            r.pre_vm[rows] = u
            sums.put(step, dot(gelu(u).astype(BF16), r.down_vm[...]))
        sums.relay((1, 3, 2))
        h.save(r.b_vm, r.b_full)
        h.save(r.pre_vm, r.pre)
        for copy in head_loads:
            copy.wait()
        gather = Gather8(h, r.a_vm)
        for half in range(PARTS):
            y = (r.residual[half_rows(half)] + sums.result(half)).astype(BF16)
            r.y[half_rows(half)] = y
            gather.start(layer_norm(y.astype(F32), r.norms[1, 0:1], r.norms[1, 2:3]).astype(BF16), half)
        run_head(h, r, gather)
        h.finish()

    ins = dict(
        **attend_ins(first, at), x=(x, VMEM), norms=(norms, VMEM), out_w=(first.out_w, ANY),
        down_w=(first.down_w, ANY), up_all=(mid_all, ANY), up_last=(mid_last, ANY))
    outs = dict(
        **attend_outs(), context=(spec((512, 128)), VMEM), residual=(spec((ROWS, D), F32), VMEM), b_full=(spec((512, D)), ANY),
        pre=(spec((512, WINDOW), F32), ANY), y=(spec((ROWS, D)), VMEM), **head_outs())
    scratch = dict(
        **attend_scratch(), **middle_scratch(), **head_scratch(), b_vm=VMEM((512, D), BF16), pre_vm=VMEM((512, WINDOW), F32),
        sems=pltpu.SemaphoreType.DMA((85,)))
    return call("middle", body, ins, outs, scratch, collective_id=2)


def gelu_slope(u):
    t = jnp.tanh(0.7978845608028654 * (u + 0.044715 * u * u * u))
    return 0.5 * (1.0 + t) + 0.5 * u * (1.0 - t * t) * 0.7978845608028654 * (1.0 + 0.134145 * u * u)


def norm_back(grad, values, gain):
    normed, rate = norm_parts(values)
    scaled = grad * gain
    mean = jnp.mean(scaled, axis=-1, keepdims=True)
    along = jnp.mean(scaled * normed, axis=-1, keepdims=True)
    back = rate * (scaled - mean - normed * along)
    return back, grad * normed


def columns(at, gain_rows, bias_rows):
    lane = lax.broadcasted_iota(jnp.int32, (ROWS, 64), 1)

    def into(rows, column):
        return dot_tn(rows.astype(BF16), (lane == column).astype(BF16))

    return into(gain_rows, at) + into(bias_rows, at + 1)


def back_outs():
    return dict(
        mid_grad=(spec((ROWS, D), F32), VMEM), context_grad_in=(spec((CTX, 32, 128)), VMEM),
        context16_grad=(spec((ROWS, HEAD_DIM)), VMEM),
        up_g_last=(spec((SHARD, 16, WINDOW)), VMEM), norm2_g=(spec((68, 16, 64)), VMEM))


def back_scratch():
    return dict(
        m_full=VMEM((512, D), BF16), z_full=VMEM((512, D), BF16), hidden_low=VMEM((512, WINDOW), BF16),
        pre_grad=VMEM((512, WINDOW), BF16), context_message=VMEM((2, 4, 2, 32, 128), BF16), up_grad=VMEM((4, 4, SHARD, 16, WINDOW), BF16),
        down_grad=VMEM((40, 16, D), BF16), b_vm=VMEM((512, D), BF16), to_norm2=scatter_scratch())


def back_block(h, r, rows, sums, step, u, g):
    r.hidden_low[rows] = g
    hidden_grad = dot_nt(r.m_full[rows], r.down_vm[...])
    pre_grad = (hidden_grad * gelu_slope(u)).astype(BF16)
    r.pre_grad[rows] = pre_grad
    sums.put(step, dot_nt(pre_grad, whole(r.up_vm)))


def finish_back(h, r, sums, layer, residual, out_grad, context, down_ready, up_ready, beside, near_end=None):
    r.down_grad[...] = dot_tn(r.hidden_low[...], r.m_full[...]).astype(BF16).reshape(40, 16, D)
    down_ready(r.down_grad, 2 * lax.rem(h.y * 2 + h.s, 4))
    place(dot_tn(r.b_vm[...], r.pre_grad[...]), r.up_grad, r.up_g_last)
    up_ready()
    gather = Gather8(h, r.z_full)
    gain_rows, normed_grad = [], []
    for half in range(PARTS):
        rows = half_rows(half)
        normed_grad.append(sums.result(half))
        back, gains = norm_back(normed_grad[half], residual[rows], r.norms[layer, 1:2])
        gain_rows.append(gains)
        mid_grad = out_grad[rows] + back
        r.mid_grad[rows] = mid_grad
        gather.start(mid_grad.astype(BF16), half)
    gain_rows, normed_grad = jnp.concatenate(gain_rows, axis=0), jnp.concatenate(normed_grad, axis=0)
    z = r.z_full[h.rows(h.y, h.s)]
    r.norm2_g[...] = columns(2, gain_rows, normed_grad).astype(BF16).reshape(68, 16, 64)
    beside()
    arrive = h.sem()
    r.context16_grad[...] = dot_nt(z, r.out_vm[128:]).astype(BF16)
    messages = Messages(h, r.context_grad_in)
    for step in ORDER:
        if step:
            gather.relay(step)
        gather.wait(step)
        sends = []
        shard = h.shard(step)
        out = dot_nt(r.z_full[block_rows(h, step)], r.out_vm[:128]).astype(BF16)
        for e in range(2):
            for core in range(2):
                lanes = slice(64 * e, 64 * e + 64)
                for b in range(2):
                    at = 32 * b + 16 * core
                    r.context_message[e, shard, core, 16 * b : 16 * b + 16] = jnp.concatenate(
                        [out[at : at + 16, lanes], out[64 + at : 80 + at, lanes]], axis=1)
                chip = 8 * h.s + 4 * e + shard
                sends.append((
                    r.context_message.at[e, shard, core], r.context_grad_in.at[h.c], (core, chip, h.y),
                    (chip == h.c) & (h.s == core), arrive))
        messages.add(sends)
    messages.done()
    r.out_g[:8] = dot_tn(context[...], r.z_full[...]).astype(BF16).reshape(8, 16, D)
    r.out_g[8:] = dot_tn(r.attended16[...], z).astype(BF16).reshape(4, 16, D)
    if near_end is not None:
        near_end()
    wait_bytes(r.context_grad_in, arrive)


def turn_kernel(at, kept, x, norms, first, up_all, up_last, cotangent):
    def body(r):
        h = Here(r.sems)
        loads = load_layer(h, r, 1, SHARD)
        h.barrier()
        sort_rows(r)
        h.ready()
        out_grad = r.cotangent[h.s]
        gather_m = Gather8(h, r.m_full)
        for half in range(PARTS):
            gather_m.start(out_grad[half_rows(half)], half)
        attend(h, r)
        arrive = gather_context(h, r)
        attend_last(r)
        for step in (1, 3, 2):
            gather_m.relay(step)
        for copy in loads:
            copy.wait()
        wait_bytes(r.context_in, arrive)
        unpack_context(r, r.context)
        gather = Gather8(h, r.b_vm)

        def ready(half, residual):
            gather.start(layer_norm(residual, r.norms[1, 1:2], r.norms[1, 3:4]).astype(BF16), half)

        run_out(h, r, r.x[...].astype(F32), ready)
        back_sums = Scatter8(h, r.to_norm2)
        for step in ORDER:
            if step:
                gather.relay(step)
            gather_m.wait(step)
            gather.wait(step)
            rows = block_rows(h, step)
            u = dot(r.b_vm[rows], whole(r.up_vm))
            g = gelu(u).astype(BF16)
            back_block(h, r, rows, back_sums, step, u, g)
        back_sums.relay((1, 3, 2))
        h.save(r.hidden_low, r.hidden_out)

        ups = [
            Reduce16(h, r.up_grad.at[:, :, pl.ds(2 * i, 2)], (r.ups_in.at[i], (r.up_mine_a, r.up_mine_b)[i], None), i == 0)
            for i in range(2)]
        first_rows = FirstRows(h, r)

        def up_ready():
            for each in ups:
                each.start()
            first_rows.start()

        def near_end():
            for each in ups:
                each.add()
            first_rows.add()

        finish_back(
            h, r, back_sums, 1, r.residual[...], out_grad.astype(F32), r.context, first_rows.load,
            up_ready, lambda: None, near_end)
        h.finish()

    ins = dict(
        **attend_ins(kept, at), x=(x, VMEM), norms=(norms, VMEM), out_w=(first.out_w, ANY),
        down_w=(first.down_w, ANY), up_all=(up_all, ANY), up_last=(up_last, ANY),
        cotangent=(cotangent, VMEM))
    outs = dict(
        **attend_outs(), hidden_out=(spec((512, WINDOW)), ANY), residual=(spec((ROWS, D), F32), VMEM), **first_rows_outs(),
        up_mine_a=(spec((4, 2, 16, WINDOW)), VMEM), up_mine_b=(spec((4, 2, 16, WINDOW)), VMEM), out_g=(spec((12, 16, D)), VMEM), **back_outs())
    scratch = dict(
        **attend_scratch(), context=VMEM((512, 128), BF16), **middle_scratch(),
        **first_rows_scratch(), ups_in=VMEM((2, 3, 4, 2, 16, WINDOW), BF16), **back_scratch(), sems=pltpu.SemaphoreType.DMA((107,)))
    return call("turn", body, ins, outs, scratch, collective_id=3)


def row_of(grads, outs):
    product = grads.astype(F32) * outs.astype(F32)
    return lax.dot_general(
        jnp.ones((8, 64), F32), product, (((1,), (1,)), ((), ())), precision=lax.Precision.HIGHEST,
        preferred_element_type=F32)[0:1]


def sort_grads(r):
    sort_rows(r)
    for m in range(2):
        for p in range(32):
            at = 32 * m + p
            r.grads[16 * at : 16 * at + 16] = r.grad_in[r.places[2, m, p]][:, 64 * m : 64 * m + 64]
    r.key_grads[...] = jnp.zeros_like(r.key_grads)
    r.value_grads[...] = jnp.zeros_like(r.value_grads)


def attend_back(h, r):
    column = lax.broadcasted_iota(jnp.int32, (512, 256), 1)
    column = 32 * (column // 16) + 16 * h.s + column % 16
    visible = column >= lax.broadcasted_iota(jnp.int32, (512, 256), 0)
    for t in range(4):
        part = slice(256 * t, 256 * t + 256)
        query, grad = r.queries[part], r.grads[part]
        logs = jnp.transpose(r.logs[part])[0:1]
        delta = row_of(grad, r.sorted_out[16 * t : 16 * t + 16].reshape(256, 64))
        query_grad = jnp.zeros((256, 64), F32)
        for u in range(t + 1):
            chunk = slice(512 * u, 512 * u + 512)
            keys = r.keys[chunk]
            scores = dot_nt(keys, query)
            if u == t:
                scores = jnp.where(visible, scores, NEG_LARGE)
            probs = jnp.exp(scores - logs)
            probs_grad = dot_nt(r.values[chunk], grad)
            scores_grad = (probs * (probs_grad - delta)).astype(BF16)
            blocks = slice(16 * u, 16 * u + 16)
            r.value_grads[blocks] += dot(probs.astype(BF16), grad).reshape(16, 32, 64)
            r.key_grads[blocks] += dot(scores_grad, query).reshape(16, 32, 64)
            query_grad = query_grad + dot_tn(scores_grad, keys)
        r.query_grads[16 * t : 16 * t + 16] = (query_grad * 0.125).astype(BF16).reshape(16, 16, 64)
    for c in range(CTX):
        for m in range(2):
            for b in range(2):
                block = 32 * m + r.order[m, 2 * c + b]
                r.message[c, 64 * m + 32 * b : 64 * m + 32 * b + 32, :] = jnp.concatenate(
                    [r.key_grads[block], r.value_grads[block]], axis=1).astype(BF16)
                r.message[c, 128 + 16 * b : 144 + 16 * b, 64 * m : 64 * m + 64] = r.query_grads[block]


def attend_back_last(r):
    kv = r.kept16[...].reshape(SEQ, 128)
    query, grad = r.kept_q16[...] * 0.125, r.grad16[...]
    scores = dot_nt(kv[:, :64], query)
    scores = jnp.where(r.own_positions[...] >= r.positions[...], scores, NEG_LARGE)
    probs = jnp.exp(scores - jnp.transpose(r.logs16[...])[0:1])
    probs_grad = dot_nt(kv[:, 64:], grad)
    scores_grad = (probs * (probs_grad - row_of(grad, r.out16[...]))).astype(BF16)
    both = jnp.concatenate([dot(scores_grad, query), dot(probs.astype(BF16), grad)], axis=1)
    r.kv16_grad[...] = both.astype(BF16).reshape(2, CTX, ROWS, 128)
    r.q16_grad[...] = (dot_tn(scores_grad, kv[:, :64]) * 0.125).astype(BF16)


def tail_ins(at, kept, saved, a_full, x, above, norms):
    return dict(
        **attend_ins(kept, at), sorted_out=(saved.sorted_out, VMEM), logs=(saved.logs, VMEM), logs16=(saved.logs16, VMEM),
        out16=(saved.attended16, VMEM), grad_in=(above.context_grad_in.reshape(32, 16, 128), VMEM), grad16=(above.context16_grad, VMEM),
        a_full=(a_full, ANY), x=(x, VMEM), mid_in=(above.mid_grad, VMEM), norms=(norms, VMEM),
        norm2_in=(above.norm2_g, VMEM))


def tail_outs():
    return dict(in_grad=(spec((ROWS, D)), VMEM))


def tail_scratch():
    return dict(
        keys=VMEM((SEQ, 64), BF16), values=VMEM((SEQ, 64), BF16), queries=VMEM((1024, 64), BF16),
        grads=VMEM((1024, 64), BF16), query_grads=VMEM((64, 16, 64), BF16), key_grads=VMEM((64, 32, 64), F32),
        value_grads=VMEM((64, 32, 64), F32), message=VMEM((CTX, 160, 128), BF16),
        kv16_grad=VMEM((2, CTX, ROWS, 128), BF16), q16_grad=VMEM((ROWS, 64), BF16),
        message_in=VMEM((2, 4, 2, 160, 128), BF16), core16=VMEM((CTX, ROWS, 128), BF16),
        sum16=VMEM((CTX, ROWS, 128), BF16), own16=VMEM((CTX, ROWS, 128), BF16), qkv_grads=VMEM((512, 384), BF16),
        qkv_vm=VMEM(TILES, BF16), a_vm=VMEM((512, D), BF16), main_part=VMEM((4, 4, SHARD, 16, 384), BF16),
        side_part=VMEM((4, 4, SHARD, 16, 256), BF16), to_norm1=scatter_scratch())


def start_tail(h, r, after_last=lambda: None):
    attend_back_last(r)
    cross = h.sem()
    h.send(r.kv16_grad.at[1 - h.s], r.core16, h.sibling(), cross)
    after_last()
    attend_back(h, r)
    arrive = h.sem()
    to_core = h.c // 8
    e, j = lax.rem(h.c // 4, 2), lax.rem(h.c, 4)
    messages = Messages(h, r.message)
    messages.add([
        (r.message.at[c], r.message_in.at[e, j, h.s], (to_core, c, h.y), (h.c == c) & (h.s == to_core), arrive)
        for c in range(CTX)])
    messages.done()
    wait_bytes(r.core16, cross)
    r.sum16[...] = (r.kv16_grad[h.s].astype(F32) + r.core16[...].astype(F32)).astype(BF16)
    leave16, arrive16 = h.sem(), h.sem()
    for step in range(1, CTX):
        to = lax.rem(h.c + step, CTX)
        h.send(r.sum16.at[to], r.own16.at[step], (h.s, to, h.y), arrive16, leave16)
    return arrive, leave16, arrive16


def run_tail(h, r, layer, x, waits, loads, last, main_ready, side_ready, arrived, beside, in_ready):
    arrive, leave16, arrive16 = waits
    for copy in loads:
        copy.wait()
    weights = whole(r.qkv_vm)
    wait_bytes(r.message_in, arrive)
    arrived()
    for j in range(4):
        for e in range(2):
            both = r.message_in[e, j, 0, :128].astype(F32) + r.message_in[e, j, 1, :128].astype(F32)
            r.qkv_grads[128 * j : 128 * j + 128, 128 + 128 * e : 256 + 128 * e] = both.astype(BF16)
        for m in range(2):
            for b in range(2):
                for core in range(2):
                    lanes = slice(64 * m, 64 * m + 64)
                    piece = jnp.concatenate(
                        [r.message_in[e, j, core, 128 + 16 * b : 144 + 16 * b, lanes] for e in range(2)], axis=1)
                    at = 128 * j + 64 * m + 32 * b + 16 * core
                    r.qkv_grads[at : at + 16, :128] = piece
    sums = Scatter8(h, r.to_norm1)
    for step in (2, 1, 3, 0):
        sums.put(step, dot_nt(r.qkv_grads[block_rows(h, step)], weights[:, :384]))
    sums.relay((2, 1, 3))
    wait_bytes(r.own16.at[pl.ds(1, CTX - 1)], arrive16)
    wait_bytes(r.own16.at[pl.ds(1, CTX - 1)], leave16)
    kv16 = r.sum16[h.c].astype(F32)
    for step in range(1, CTX):
        kv16 = kv16 + r.own16[step].astype(F32)
    grads16 = jnp.concatenate([r.q16_grad[...], kv16.astype(BF16)], axis=1)
    own = dot_nt(grads16, weights[:, 384:576])
    place(dot_tn(r.a_vm[...], r.qkv_grads[...]), r.main_part, last.at[:, :, pl.ds(0, 384)])
    main_ready()
    own_grad = dot_tn(r.a_vm[h.rows(h.y, h.s)], grads16)
    beside()
    gain_rows, normed_grad = [], []
    for half in range(PARTS):
        rows = half_rows(half)
        normed_grad.append(own[rows] + sums.result(half))
        back, gains = norm_back(normed_grad[half], x[rows], r.norms[layer, 0:1])
        gain_rows.append(gains)
        in_grad = (r.mid_in[rows] + back).astype(BF16)
        r.in_grad[rows] = in_grad
        in_ready(half, in_grad)
    gain_rows, normed_grad = jnp.concatenate(gain_rows, axis=0), jnp.concatenate(normed_grad, axis=0)

    def finish():
        sums_of_rows = columns(0, gain_rows, normed_grad) + r.norm2_in[...].reshape(D, 64).astype(F32)
        side = jnp.concatenate([own_grad, sums_of_rows], axis=1)
        place(side, r.side_part, last.at[:, :, pl.ds(384, 256)])
        side_ready()

    return finish


def send_out(h, r, out, layer, arrive, arrive_last):
    group = 2 * h.y + h.s
    for i in range(8):
        tile = 8 * group + i
        to = tile // 17
        h.send_or_keep(
            out.at[i], r.out_sum.at[lax.rem(tile, 17)], (1 - layer, h.c, to), (h.s != layer) & (to == h.y), arrive)
    h.send_or_keep(
        out.at[pl.ds(8, 4)], r.last_in.at[group], (1 - layer, h.c, SHARD - 1), (h.s != layer) & (h.y == SHARD - 1),
        arrive_last)


def back_kernel(at, kept, saved, x, above, norms, first, attended16, mid_all, mid_last):
    def body(r):
        h = Here(r.sems)
        tail_loads = load_tiles(h, r.up_all, r.up_last, r.qkv_vm, SHARD)
        tail_loads.append(h.local(r.a_full, r.a_vm))
        out_loads = [h.local(r.hidden1, r.hidden_low), h.local(r.down_tiles.at[1], r.down_grad)]
        loads = load_layer(h, r, 0, 0)
        loads += [h.local(r.b_full, r.b_vm), h.local(r.pre, r.pre_vm), h.local(r.context, r.context_vm)]
        h.barrier()
        sort_grads(r)
        arrive_out, arrive_last = h.sem(), h.sem()
        x, z = h.c // 4, lax.rem(h.c, 4)
        ups = [
            Reduce16(h, None, (None, (r.up_mine_a, r.up_mine_b)[i], r.ups_second.at[i]), i == 0) for i in range(2)]
        main = Reduce16(h, r.main_part, r.main_sums, False)
        side = Reduce16(h, r.side_part, r.side_sums, True)
        up0 = Reduce16(h, r.up_grad, (r.up0_in, r.up0_mine, None), True)
        rows16 = Rows16(h, r, 1)
        first_rows = FirstRows(h, r)
        h.ready()
        for each in ups:
            each.send_on()
        rows16.start()
        send_out(h, r, r.out1_g, 1, arrive_out, arrive_last)
        out_sums = Scatter8(h, r.to_down)
        for copy in out_loads:
            copy.wait()
        for step in (2, 1, 3, 0):
            out_sums.put(step, dot(r.hidden_low[block_rows(h, step)], r.down_grad[...].reshape(WINDOW, D)))
        waits = start_tail(h, r, lambda: out_sums.relay((2, 1, 3)))

        def settle(core):
            @pl.when(h.s == core)
            def _():
                @pl.when(h.y < SHARD - 1)
                def _():
                    wait_bytes(r.out_sum, arrive_out)

                @pl.when(h.y == SHARD - 1)
                def _():
                    wait_bytes(r.out_sum.at[pl.ds(0, 13)], arrive_out)
                    wait_bytes(r.last_in, arrive_last)
                    r.out_sum[13:] = added([r.last_in[g] for g in range(8)])

        arrive_up = h.sem()
        spreads = [Spread16(h, parts, i == 0, 1) for i, parts in enumerate((r.up_low, r.up_high))]

        def arrived():
            for half in range(PARTS):
                rows = half_rows(half)
                r.out[rows] = (r.residual1[rows] + out_sums.result(half)).astype(BF16)
            for i in range(2):
                r.up1_piece[2 * i : 2 * i + 2] = ups[i].result()
            send_piece(h, r.up1_piece, r.up_in, 1, arrive_up)
            settle(0)
            rows16.start_out()

        def beside_sums():
            rows16.middle()

            @pl.when(h.s == 1)
            def _():
                wait_bytes(r.up_in, arrive_up)
                rows = joined_up([r.up_in[g] for g in range(8)])
                for i, parts in enumerate((r.up_low, r.up_high)):
                    parts[x, z] = rows[:, 2176 * i : 2176 * i + 2176]

            for each in spreads:
                each.start()

        gather = Gather8(h, r.m_full)
        finish = run_tail(
            h, r, 1, r.x[...].astype(F32), waits, tail_loads, r.qkv_g_last, main.start, side.start,
            arrived, beside_sums, lambda half, value: gather.start(value, half))
        finish()
        rows16.spread()
        for copy in loads:
            copy.wait()
        sums = Scatter8(h, r.to_norm2)
        for step in ORDER:
            if step:
                gather.relay(step)
            gather.wait(step)
            rows = block_rows(h, step)
            u = r.pre_vm[rows]
            back_block(h, r, rows, sums, step, u, gelu(u).astype(BF16))
            if step == 0:
                for each in spreads:
                    each.middle()
            if step == 1:
                rows16.spread_on()
        sums.relay((1, 3, 2))
        def down_ready(rows, first):
            first_rows.load(rows, first)
            main.middle()
            side.middle()

        def up_ready():
            up0.start()
            first_rows.start()

        def beside():
            r.qkv1_piece[:, :, :384] = main.result()
            r.qkv1_piece[:, :, 384:] = side.result()

        def near_end():
            send_out(h, r, r.out_g, 0, arrive_out, arrive_last)
            up0.add()
            first_rows.add()
            rows16.finish()
            for each in spreads:
                each.finish()
            h.save_on(1, r.up_low, r.up_low_all)
            h.save_on(1, r.up_high, r.up_high_all)

        finish_back(
            h, r, sums, 0, r.residual[...], r.in_grad[...].astype(F32), r.context_vm, down_ready, up_ready, beside, near_end)

        settle(1)
        h.finish()

    ins = dict(
        **tail_ins(at, kept, saved, kept.a_full, x, above, norms), pre=(kept.pre, ANY), b_full=(kept.b_full, ANY),
        context=(kept.context, ANY), residual=(kept.residual, VMEM), attended16=(attended16, VMEM),
        out_w=(first.out_w, ANY), down_w=(first.down_w, ANY), up_all=(mid_all, ANY), up_last=(mid_last, ANY),
        up_mine_a=(above.up_mine_a, VMEM), up_mine_b=(above.up_mine_b, VMEM), out1_g=(above.out_g, VMEM),
        mine_a=(above.next_a, VMEM), mine_b=(above.next_b, VMEM), mine_beside=(above.next_beside, VMEM),
        hidden1=(above.hidden_out, ANY), residual1=(above.residual, VMEM),
        down_tiles=(first.down_w.reshape(2, 40, 16, D), ANY))
    piece, half = (spec((SHARD, 16, WINDOW)), VMEM), (spec((4, 4, 16, 2176)), ANY)
    outs = dict(
        **tail_outs(), **back_outs(), out=(spec((ROWS, D)), VMEM), qkv_g_last=piece, qkv1_piece=piece, up0_mine=(spec((4, SHARD, 16, WINDOW)), VMEM),
        up_low_all=half, up_high_all=half, **rows_outs(), **rows_results(),
        **first_rows_outs(), out_sum=(spec((17, 16, D)), VMEM))
    scratch = dict(
        out_vm=VMEM((192, D), BF16), up_vm=VMEM(TILES, BF16), down_vm=VMEM((WINDOW, D), BF16),
        pre_vm=VMEM((512, WINDOW), F32), to_down=scatter_scratch(), context_vm=VMEM((512, 128), BF16), out_g=VMEM((12, 16, D), BF16),
        ups_second=VMEM((2, 3, 2, 16, WINDOW), BF16), **first_rows_scratch(),
        up0_in=VMEM((3, 4, SHARD, 16, WINDOW), BF16), up_low=VMEM((4, 4, 16, 2176), BF16),
        up_high=VMEM((4, 4, 16, 2176), BF16), main_sums=reduce_scratch(SHARD, 384), side_sums=reduce_scratch(SHARD, 256),
        up1_piece=VMEM((SHARD, 16, WINDOW), BF16), up_in=VMEM((8, 16, WINDOW), BF16), last_in=VMEM((8, 4, 16, D), BF16), **tail_scratch(), **back_scratch(),
        **rows_scratch(), sems=pltpu.SemaphoreType.DMA((202,)))
    return call("back", body, ins, outs, scratch, collective_id=4)


class Plane16:
    def __init__(self, h, x_first, core=None):
        self.h, self.x_first = h, x_first
        self.on = None if core is None else h.s == core
        self.x, self.z = h.c // 4, lax.rem(h.c, 4)
        self.first, self.second = h.sem(), h.sem()

    def when(self, act):
        act() if self.on is None else pl.when(self.on)(act)

    def chip(self, x, z):
        return (self.h.s, 4 * lax.rem(x, 4) + lax.rem(z, 4), self.h.y)

    def along(self, axis_x):
        return [self.chip(self.x + j, self.z) if axis_x else self.chip(self.x, self.z + j) for j in (1, 2, 3)]

    def send(self, pairs, targets, arrive, spare):
        leave = self.h.sem()
        copies = [
            pltpu.make_async_remote_copy(
                src_ref=src, dst_ref=dst, send_sem=leave, recv_sem=arrive, device_id=to, device_id_type=MESH)
            for (src, dst), to in zip(pairs, targets)]

        def start():
            for i in (0, 2, 1):
                copies[i].start()

        self.when(start)
        self.h.sent.append(types.SimpleNamespace(wait_send=lambda: self.when(lambda: wait_bytes(spare, leave))))


class Reduce16(Plane16):
    def __init__(self, h, part, bufs, x_first, core=None):
        super().__init__(h, x_first, core)
        self.part = part
        self.first_in, self.mine, self.second_in = bufs

    def start(self):
        pairs = []
        for j in (1, 2, 3):
            src = self.part.at[lax.rem(self.x + j, 4)] if self.x_first else self.part.at[:, lax.rem(self.z + j, 4)]
            pairs.append((src, self.first_in.at[j - 1]))
        self.send(pairs, self.along(self.x_first), self.first, self.first_in)

    def add(self):
        def add():
            wait_bytes(self.first_in, self.first)
            for k in range(4):
                own = self.part[self.x, k] if self.x_first else self.part[k, self.z]
                self.mine[k] = added([own] + [self.first_in[j, k] for j in range(3)])

        self.when(add)

    def send_on(self):
        at = self.z if self.x_first else self.x
        pairs = [(self.mine.at[lax.rem(at + j, 4)], self.second_in.at[j - 1]) for j in (1, 2, 3)]
        self.send(pairs, self.along(not self.x_first), self.second, self.second_in)

    def middle(self):
        self.add()
        self.send_on()

    def result(self):
        wait_bytes(self.second_in, self.second)
        return added([self.mine[self.z if self.x_first else self.x]] + [self.second_in[j] for j in range(3)])


def reduce_scratch(units, width):
    return [VMEM((3, 4, units, 16, width), BF16), VMEM((4, units, 16, width), BF16), VMEM((3, units, 16, width), BF16)]


class Spread16(Plane16):
    def __init__(self, h, parts, x_first, core=None):
        super().__init__(h, x_first, core)
        self.parts = parts

    def start(self):
        own = self.parts.at[self.x, self.z]
        self.send([(own, own)] * 3, self.along(self.x_first), self.first, self.parts.at[0, pl.ds(0, 3)])

    def middle(self):
        self.when(lambda: wait_bytes(self.parts.at[0, pl.ds(0, 3)], self.first))
        line = self.parts.at[:, self.z] if self.x_first else self.parts.at[self.x]
        self.send([(line, line)] * 3, self.along(not self.x_first), self.second, self.parts.at[pl.ds(0, 3)])

    def finish(self):
        self.when(lambda: wait_bytes(self.parts.at[pl.ds(0, 3)], self.second))


class FirstRows:
    def __init__(self, h, r):
        self.h, self.r = h, r
        self.sums = [
            Reduce16(h, r.rows_a, (r.rows_in.at[0], r.next_a, None), True),
            Reduce16(h, r.rows_b, (r.rows_in.at[1], r.next_b, None), False)]

    def load(self, down, first):
        r = self.r
        for c in range(CTX):
            for i, parts in enumerate((r.rows_a, r.rows_b)):
                parts[c // 4, c % 4, 0] = down[first + 2 * c + i]
        for i in range(2):
            r.next_beside[i] = down[first + 32 + i]

    def start(self):
        for each in self.sums:
            each.start()

    def add(self):
        for each in self.sums:
            each.add()


def first_rows_outs():
    mine = (spec((4, 1, 16, D)), VMEM)
    return dict(next_a=mine, next_b=mine, next_beside=(spec((2, 16, D)), VMEM))


def first_rows_scratch():
    part = VMEM((4, 4, 1, 16, D), BF16)
    return dict(rows_a=part, rows_b=part, rows_in=VMEM((2, 3, 4, 1, 16, D), BF16))


class Rows16:
    def __init__(self, h, r, core):
        self.h, self.r, self.core = h, r, core
        self.sums = [
            Reduce16(h, None, (None, r.mine_a, r.rows_second.at[0]), True),
            Reduce16(h, None, (None, r.mine_b, r.rows_second.at[1]), False),
            Reduce16(h, r.rows_c, r.rows_sums_c, True, 1 - core)]
        self.spreads = [
            Spread16(h, r.rows_all.at[0], True), Spread16(h, r.rows_all.at[1], False), Spread16(h, r.rows_out, False, 1 - core)]
        self.arrive = h.sem()
        self.arrive_each = [h.sem() for _ in range(3)]
        self.cross = [h.sem() for _ in range(3)]

    def on(self, i):
        return self.h.s != self.core if i == 2 else None

    def when(self, i, act, also=None):
        conditions = [c for c in (self.on(i), also) if c is not None]
        if not conditions:
            return act()
        return pl.when(functools.reduce(jnp.logical_and, conditions))(act)

    def start(self):
        for i in range(2):
            self.sums[i].send_on()
            self.send_tile(self.r.mine_beside.at[i], i)

    def start_out(self):
        h, r = self.h, self.r

        @pl.when(h.s != self.core)
        def _():
            for c in range(CTX):
                r.rows_c[c // 4, c % 4, 0] = r.out_sum[c]

        self.sums[2].start()
        self.send_tile(r.out_sum.at[16], 2)

    def send_tile(self, src, i):
        h = self.h
        dst, leave = self.r.tile_in.at[h.c], h.sem()
        copy = pltpu.make_async_remote_copy(
            src_ref=src, dst_ref=dst, send_sem=leave, recv_sem=self.arrive, device_id=(h.s, 5 * i, h.y),
            device_id_type=MESH)
        kept = pltpu.make_async_copy(src, dst, self.arrive)
        self.when(i, copy.start, h.c != 5 * i)
        self.when(i, kept.start, h.c == 5 * i)
        h.sent.append(types.SimpleNamespace(
            wait_send=functools.partial(self.when, i, copy.wait_send, h.c != 5 * i)))

    def middle(self):
        self.sums[2].middle()

    def spread(self):
        h, r = self.h, self.r
        x, z = h.c // 4, lax.rem(h.c, 4)
        r.rows_all[0, x, z] = self.sums[0].result()
        r.rows_all[1, x, z] = self.sums[1].result()

        def out():
            r.rows_out[x, z] = self.sums[2].result()

        self.when(2, out)
        for each in self.spreads:
            each.start()
        for i in range(3):
            leave = h.sem()
            copies = [
                pltpu.make_async_remote_copy(
                    src_ref=r.tiles.at[i], dst_ref=r.tiles.at[i], send_sem=leave, recv_sem=self.arrive_each[i],
                    device_id=(h.s, lax.rem(h.c + step, CTX), h.y), device_id_type=MESH)
                for step in range(1, CTX)]

            def start(i=i, copies=copies):
                wait_bytes(r.tile_in, self.arrive)
                r.tiles[i] = added([r.tile_in[c] for c in range(CTX)])
                for copy in copies:
                    copy.start()

            self.when(i, start, h.c == 5 * i)
            h.sent.append(types.SimpleNamespace(
                wait_send=functools.partial(
                    self.when, i, functools.partial(wait_bytes, r.tile_in.at[pl.ds(0, 15)], leave), h.c == 5 * i)))

    def spread_on(self):
        for each in self.spreads:
            each.middle()

    def finish(self):
        h, r = self.h, self.r
        for each in self.spreads:
            each.finish()
        for i in range(3):
            self.when(i, functools.partial(wait_bytes, r.tiles.at[i], self.arrive_each[i]), h.c != 5 * i)
        copies = [
            pltpu.make_async_remote_copy(
                src_ref=src, dst_ref=dst, send_sem=h.sem(), recv_sem=sem, device_id=h.sibling(), device_id_type=MESH)
            for src, dst, sem in (
                (r.rows_all, r.rows_other, self.cross[0]),
                (r.tiles, r.tiles_other, self.cross[1]), (r.rows_out, r.rows_out, self.cross[2]))]

        @pl.when(h.s != self.core)
        def _():
            for copy in copies:
                copy.start()

        h.save_on(self.core, r.rows_all, r.rows_own)

        @pl.when(h.s != self.core)
        def _():
            for copy in copies:
                copy.wait_send()

        @pl.when(h.s == self.core)
        def _():
            wait_bytes(r.rows_other, self.cross[0])
            wait_bytes(r.tiles_other, self.cross[1])
            wait_bytes(r.rows_out, self.cross[2])

        h.save_on(self.core, r.rows_other, r.rows_cross)
        h.save_on(self.core, r.rows_out, r.rows_out_all)


def rows_outs():
    return dict(tiles=(spec((3, 16, D)), VMEM), tiles_other=(spec((3, 16, D)), VMEM))


def rows_scratch():
    part = VMEM((4, 4, 1, 16, D), BF16)
    return dict(
        rows_c=part, rows_sums_c=reduce_scratch(1, D), rows_second=VMEM((2, 3, 1, 16, D), BF16),
        tile_in=VMEM((CTX, 16, D), BF16), rows_all=VMEM((2, 4, 4, 1, 16, D), BF16), rows_out=part,
        rows_other=VMEM((2, 4, 4, 1, 16, D), BF16))


def rows_results():
    whole_rows = (spec((2, 4, 4, 1, 16, D)), ANY)
    return dict(rows_own=whole_rows, rows_cross=whole_rows, rows_out_all=(spec((4, 4, 1, 16, D)), ANY))


def send_piece(h, piece, dst, layer, arrive):
    leave = h.sem()
    for step in (1, 3, 2, 0):
        shard = h.shard(step)
        src, to = piece.at[shard], dst.at[2 * h.y + h.s]
        copy = pltpu.make_async_remote_copy(
            src_ref=src, dst_ref=to, send_sem=leave, recv_sem=arrive, device_id=(layer, h.c, shard),
            device_id_type=MESH)
        if step:
            copy.start()
        else:
            pl.when(h.s != layer)(copy.start)
            pl.when(h.s == layer)(pltpu.make_async_copy(src, to, arrive).start)

    def wait_send():
        pl.when(h.s != layer)(lambda: wait_bytes(dst.at[pl.ds(0, 4)], leave))
        pl.when(h.s == layer)(lambda: wait_bytes(dst.at[pl.ds(0, 3)], leave))

    h.sent.append(types.SimpleNamespace(wait_send=wait_send))


def joined_up(windows):
    parts = []
    for g in range(8):
        main = windows[g][:, :512]
        if g % 4:
            main = jnp.concatenate([main[:, :128] + windows[g - 1][:, 512:], main[:, 128:]], axis=1)
        parts.append(main)
        if g % 4 == 3:
            parts.append(windows[g][:, 512:])
    return jnp.concatenate(parts, axis=1)


def joined_qkv(blocks, own):
    queries = [blocks[g][:, :128] for g in range(8)] + [own[:, :64]]
    keys = [blocks[g][:, a : a + 64] for g in range(8) for a in (128, 256)] + [own[:, 64:128]]
    values = [blocks[g][:, a : a + 64] for g in range(8) for a in (192, 320)] + [own[:, 128:192]]
    return jnp.concatenate(queries + keys + values + [own[:, 192:]], axis=1)


def added(blocks):
    total = blocks[0].astype(F32)
    for block in blocks[1:]:
        total = total + block.astype(F32)
    return total.astype(BF16)


def last_kernel(at, kept, saved, hidden, above, turn_up_last, norms):
    def body(r):
        h = Here(r.sems)
        x, z = h.c // 4, lax.rem(h.c, 4)
        group = 2 * h.y + h.s
        loads = [h.local(r.qkv_w, r.qkv_vm), h.local(r.a_full, r.a_vm)]
        h.barrier()
        sort_grads(r)
        h.ready()
        up0 = Reduce16(h, None, (None, r.up0_mine, r.up0_in), True)
        up0.send_on()
        main = Reduce16(h, r.main_part, r.main_sums, True)
        side = Reduce16(h, r.side_part, r.side_sums, False)
        arrive_wide = h.sem()
        send_piece(h, r.qkv1_piece, r.wide_in, 1, arrive_wide)
        rows16 = Rows16(h, r, 0)
        rows16.start()
        rows16.start_out()
        arrive_last, arrive_late = h.sem(), h.sem()
        for i in range(SHARD):
            chip = 4 * i + h.y
            r.last_message[i, 0] = r.up_last[i]
            r.last_message[i, 1] = r.up1_last[i]
            r.last_message[i, 2] = r.qkv1_last[i]
            h.send_or_keep(r.last_message.at[i], r.last_in.at[h.c], (h.s, chip, h.y), chip == h.c, arrive_last)
        early, late = [
            [Spread16(h, parts, i == 0, core) for i, parts in enumerate((r.wide_low, r.wide_high))] for core in (1, 0)]

        def spread_early():
            @pl.when(h.s == 1)
            def _():
                wait_bytes(r.wide_in, arrive_wide)
                blocks = [r.wide_in[g] for g in range(8)]
                rows = joined_qkv(blocks, added([block[:, 384:] for block in blocks]))
                r.wide_low[x, z] = rows[:, :2176]
                r.wide_high[x, z] = jnp.concatenate([rows[:, 2176:], jnp.zeros((16, 1024), BF16)], axis=1)

            for each in early:
                each.start()

        def spread_late():
            @pl.when(h.s == 0)
            def _():
                wait_bytes(r.wide_in, arrive_wide)
                rows = joined_up([r.wide_in[g] for g in range(8)])
                r.wide_low[x, z] = rows[:, :2176]
                r.wide_high[x, z] = rows[:, 2176:]

            for each in late:
                each.start()

        waits = start_tail(h, r, spread_early)

        def arrived():
            for each in early:
                each.middle()
            rows16.middle()
            r.up0_piece[...] = up0.result()
            send_piece(h, r.up0_piece, r.wide_in, 0, arrive_wide)

        def beside():
            rows16.spread()
            spread_late()

        finish = run_tail(
            h, r, 0, r.x[h.s].astype(F32), waits, loads, r.qkv_last, main.start, side.start, arrived, beside,
            lambda half, value: None)
        finish()
        for i in range(SHARD):
            chip = 4 * i + h.y
            h.send_or_keep(r.qkv_last.at[i], r.late_in.at[h.c], (h.s, chip, h.y), chip == h.c, arrive_late)
        main.middle()
        side.middle()
        for each in late:
            each.middle()
        rows16.spread_on()
        arrive_rest = h.sem()
        reduces = z == h.y

        @pl.when(reduces)
        def _():
            wait_bytes(r.last_in, arrive_last)
            wait_bytes(r.late_in, arrive_late)
            early = added([r.last_in[c] for c in range(CTX)])
            r.rest_message[0, 0] = early[0]
            r.rest_message[0, 1] = added([r.late_in[c] for c in range(CTX)])
            r.rest_message[1] = early[1:]

        rest = []
        for layer in range(2):
            leave = h.sem()
            src, dst = r.rest_message.at[layer], r.rest.at[z, h.s]
            copy = pltpu.make_async_remote_copy(
                src_ref=src, dst_ref=dst, send_sem=leave, recv_sem=arrive_rest, device_id=(layer, h.c, x),
                device_id_type=MESH)
            kept = pltpu.make_async_copy(src, dst, arrive_rest)
            is_self = (h.s == layer) & (x == h.y)
            pl.when(reduces & is_self)(kept.start)
            away = reduces & jnp.logical_not(is_self)
            pl.when(away)(copy.start)
            rest.append((away, copy))
        r.qkv_piece[:, :, :384] = main.result()
        r.qkv_piece[:, :, 384:] = side.result()
        arrive_qkv = h.sem()
        send_piece(h, r.qkv_piece, r.qkv_in, 0, arrive_qkv)
        owner = x == h.y
        across = [h.sem() for _ in range(4)]
        along = [h.sem() for _ in range(3)]
        line = r.rest.at[z]
        lines = []
        for j in range(1, 4):
            lines.append(pltpu.make_async_remote_copy(
                src_ref=line, dst_ref=line, send_sem=across[j], recv_sem=across[0],
                device_id=(h.s, 4 * lax.rem(x + j, 4) + z, h.y), device_id_type=MESH))

        @pl.when(owner)
        def _():
            wait_bytes(line, arrive_rest)
            for copy in lines:
                copy.start()

        spreads = [Spread16(h, parts, i == 0, 0) for i, parts in enumerate((r.qkv_low, r.qkv_high))]

        @pl.when(h.s == 0)
        def _():
            wait_bytes(r.qkv_in, arrive_qkv)
            blocks = [r.qkv_in[g] for g in range(8)]
            rows = joined_qkv(blocks, added([block[:, 384:] for block in blocks]))
            r.qkv_low[x, z] = rows[:, :1664]
            r.qkv_high[x, z] = rows[:, 1664:]

        for each in spreads:
            each.start()
        for each in early + late:
            each.finish()
        h.save(r.wide_low, r.wide_low_all)
        h.save(r.wide_high, r.wide_high_all)

        @pl.when(jnp.logical_not(owner))
        def _():
            wait_bytes(line, across[0])

        for j in range(1, 4):
            h.send(line, line, (h.s, 4 * x + lax.rem(z + j, 4), h.y), along[j - 1])
        for each in spreads:
            each.middle()
        rows16.finish()
        for sem in along:
            wait_bytes(line, sem)
        r.up_rest[...] = joined_up([r.rest[g // 2, g % 2, 0] for g in range(8)])
        blocks = [r.rest[g // 2, g % 2, 1] for g in range(8)]
        r.qkv_rest[...] = joined_qkv(blocks, added([block[:, 384:] for block in blocks]))
        for each in spreads:
            each.finish()
        h.save_on(0, r.qkv_low, r.qkv_low_all)
        h.save_on(0, r.qkv_high, r.qkv_high_all)

        @pl.when(owner)
        def _():
            for copy in lines:
                copy.wait_send()

        for away, copy in rest:
            pl.when(away)(copy.wait_send)
        h.finish()

    ins = dict(
        **tail_ins(at, kept, saved, kept.a_full, hidden, above, norms), qkv_w=(kept.qkv_w, ANY), up0_mine=(above.up0_mine, VMEM),
        qkv1_piece=(above.qkv1_piece, VMEM), up_last=(above.up_g_last, VMEM), qkv1_last=(above.qkv_g_last, VMEM),
        up1_last=(turn_up_last, VMEM), mine_a=(above.next_a, VMEM), mine_b=(above.next_b, VMEM), mine_beside=(above.next_beside, VMEM),
        out_sum=(above.out_sum, VMEM))
    up_half, qkv_half = (spec((4, 4, 16, 2176)), ANY), (spec((4, 4, 16, 1664)), ANY)
    outs = dict(
        **tail_outs(), wide_low_all=up_half, wide_high_all=up_half, qkv_low_all=qkv_half, qkv_high_all=qkv_half,
        up_rest=(spec((16, FF)), VMEM), qkv_rest=(spec((16, 3328)), VMEM), **rows_outs(), **rows_results())
    piece, eight = VMEM((SHARD, 16, WINDOW), BF16), VMEM((8, 16, WINDOW), BF16)
    scratch = dict(
        **tail_scratch(),
        main_sums=reduce_scratch(SHARD, 384), side_sums=reduce_scratch(SHARD, 256), **rows_scratch(), wide_low=VMEM((4, 4, 16, 2176), BF16), wide_high=VMEM((4, 4, 16, 2176), BF16),
        qkv_low=VMEM((4, 4, 16, 1664), BF16), qkv_high=VMEM((4, 4, 16, 1664), BF16), qkv_piece=piece, qkv_last=piece, last_message=VMEM((SHARD, 3, 16, WINDOW), BF16),
        last_in=VMEM((CTX, 3, 16, WINDOW), BF16), late_in=VMEM((CTX, 16, WINDOW), BF16), wide_in=eight, qkv_in=eight, up0_piece=piece,
        up0_in=VMEM((3, SHARD, 16, WINDOW), BF16),
        rest_message=VMEM((2, 2, 16, WINDOW), BF16), rest=VMEM((4, 2, 2, 16, WINDOW), BF16),
        sems=pltpu.SemaphoreType.DMA((134,)))
    return call("last", body, ins, outs, scratch, collective_id=5)


def join_kernel(back, last):
    def body(
        _, up_low, up_high, wide_low, wide_high, qkv_low, qkv_high, own0, cross0, out0, own1, cross1, out1, up_rest, qkv_rest,
        tiles0, tiles_other0, tiles1, tiles_other1, up_ref, qkv_ref, gain_ref, bias_ref, down_ref, out_ref):
        def store_norms(rows, sums):
            for i in range(5):

                @pl.when(pl.program_id(0) == i)
                def _():
                    for k in range(2):
                        part = slice(64 * i, 64 * i + min(rows, SLICE - 64 * i))
                        count = part.stop - part.start
                        gain_ref[0, k : k + 1, part] = sums[64 + 2 * k : 65 + 2 * k, :count]
                        bias_ref[0, k : k + 1, part] = sums[65 + 2 * k : 66 + 2 * k, :count]

        def store(rows, up_parts, qkv_parts):
            for at, block in up_parts:
                up_ref[:rows, at : at + block.shape[1]] = block.astype(F32)
            for at, block in qkv_parts:
                block = block.astype(F32)
                if at + block.shape[1] == 3328:
                    store_norms(rows, jnp.transpose(block[:, -128:]))
                    block = block[:, :-64]
                qkv_ref[:rows, at : at + block.shape[1]] = block

        def rows_from(halves, out, tiles):
            @pl.when(pl.program_id(0) < 4)
            def _():
                for c in range(4):
                    for i in range(2):
                        for half in range(2):
                            at = 32 * c + 16 * i
                            down_ref[half, at : at + 16] = halves[half][i, 0, c, 0].astype(F32)
                    out_ref[16 * c : 16 * c + 16] = out[0, c, 0].astype(F32)

            @pl.when(pl.program_id(0) == 4)
            def _():
                for half in range(2):
                    down_ref[half, :32] = tiles[half][:2].reshape(32, D).astype(F32)
                out_ref[:16] = tiles[2].astype(F32)

        first = lax.axis_index(SECTION) == 0
        pl.when(first)(lambda: rows_from((own0, cross0), out0, (tiles0, tiles_other0, tiles_other0[2])))
        pl.when(jnp.logical_not(first))(
            lambda: rows_from((cross1, own1), out1, (tiles_other1, tiles1, tiles_other1[2])))
        low, high = (ref[0].reshape(64, 2176) for ref in (wide_low, wide_high))

        @pl.when((pl.program_id(0) < 4) & first)
        def _():
            parts = [ref[0].reshape(64, 1664) for ref in (qkv_low, qkv_high)]
            store(64, ((0, low), (2176, high)), ((0, parts[0]), (1664, parts[1])))

        @pl.when((pl.program_id(0) < 4) & jnp.logical_not(first))
        def _():
            parts = [ref[0].reshape(64, 2176) for ref in (up_low, up_high)]
            store(64, ((0, parts[0]), (2176, parts[1])), ((0, low), (2176, high[:, :1152])))

        @pl.when(pl.program_id(0) == 4)
        def _():
            store(16, ((0, up_rest[...]),), ((0, qkv_rest[...]),))

    def place(i, section, core):
        return jnp.where((core < 0) | (section[0] == core), jnp.minimum(i, 3), 0)

    def line(width, core):
        return pl.BlockSpec((1, 4, 16, width), lambda i, section: (place(i, section, core), 0, 0, 0))

    def tile_line(core, *lead):
        zeros = (0,) * len(lead)
        return pl.BlockSpec(
            (*lead, 1, 4, 1, 16, D), lambda i, section: (*zeros, place(i, section, core), 0, 0, 0, 0))

    def tiles_of(count):
        return pl.BlockSpec((count, 16, D), lambda i, section: (0, 0, 0))

    def rows(width, count=64):
        return pl.BlockSpec((count, width), lambda i, section: (i, 0))

    def all_of(width):
        return pl.BlockSpec((16, width), lambda i, section: (0, 0))

    norms = pl.BlockSpec((1, 2, SLICE), lambda i, section: (0, 0, 0))
    return pl.pallas_call(
        body,
        out_shape=(
            spec((SLICE, FF), F32), spec((SLICE, 3 * D), F32), spec((1, 2, SLICE), F32), spec((1, 2, SLICE), F32),
            spec((2, 544, D), F32),
            spec((SLICE, D), F32)),
        grid_spec=pltpu.PrefetchScalarGridSpec(
            num_scalar_prefetch=1,
            grid=(5,),
            in_specs=[
                line(2176, 1), line(2176, 1), line(2176, -1), line(2176, -1), line(1664, 0), line(1664, 0),
                tile_line(0, 2), tile_line(0, 2), tile_line(0), tile_line(1, 2), tile_line(1, 2), tile_line(1),
                all_of(FF), all_of(3328), *[tiles_of(3)] * 4],
            out_specs=(
                rows(FF), rows(3 * D), norms, norms, pl.BlockSpec((2, 128, D), lambda i, section: (0, i, 0)), rows(D))),
        name="join",
    )(lax.axis_index(SECTION).astype(jnp.int32).reshape(1), back.up_low_all, back.up_high_all, last.wide_low_all, last.wide_high_all, last.qkv_low_all, last.qkv_high_all, last.rows_own,
      last.rows_cross, last.rows_out_all, back.rows_own, back.rows_cross, back.rows_out_all, last.up_rest, last.qkv_rest,
      last.tiles, last.tiles_other, back.tiles, back.tiles_other)


def token_positions(block_order):
    offsets = jnp.arange(32, dtype=jnp.int32)
    groups = jnp.arange(2, dtype=jnp.int32)[:, None, None] * GROUP
    return (groups + block_order[:, :, None] * 32 + offsets).reshape(2, GROUP)


def swapped(section, first, second):
    own = jnp.where(section == 0, first, second)
    other = lax.ppermute(jnp.where(section == 0, second, first), SECTION, [(0, 1), (1, 0)])
    return jnp.where(section == 0, own, other), jnp.where(section == 0, other, own)


def gathered(x):
    return lax.all_gather(x, CONTEXT)


def shards(hidden_in, cotangent, block_order, qkv_weight, out_weight, up_weight, down_weight, norm_gains, norm_biases):
    section, ctx = lax.axis_index(SECTION), lax.axis_index(CONTEXT)
    grid = token_positions(block_order)
    own_positions = lax.dynamic_slice(grid, (section, ctx * ROWS), (1, ROWS))
    positions = grid.reshape(1, SEQ)
    slots = jnp.arange(32, dtype=jnp.int32)
    slot = jnp.sum(jnp.where(block_order[:, None, :] == slots[None, :, None], slots[None, None, :], 0), axis=2)
    group, odd = jnp.arange(2, dtype=jnp.int32)[:, None], slot % 2
    chip = slot // 2
    places = jnp.stack([10 * chip + 4 * group + 2 * odd, 10 * chip + 8 + odd, 2 * chip + odd])
    at = (block_order, places, positions, own_positions.reshape(ROWS, 1))
    at_back = (block_order, places, positions.reshape(SEQ, 1), own_positions)
    hidden = hidden_in[0]
    spread = spread_kernel(norm_gains, norm_biases, qkv_weight, up_weight)
    norms = spread.norms
    mid_all = gathered(spread.mid_piece)
    first = first_kernel(hidden, norms, spread.side_piece, spread.side_last, out_weight, down_weight)
    up_piece, first.q16 = lax.optimization_barrier((spread.side_piece, first.q16))
    up_all = gathered(up_piece)
    middle = middle_kernel(at, hidden, norms, first, mid_all, spread.mid_last)
    turn = turn_kernel(at, middle, middle.y, norms, first, up_all, spread.side_last, cotangent[0])
    back = back_kernel(
        at_back, middle, turn, middle.y, turn, norms, first, middle.attended16, mid_all, spread.mid_last)
    last = last_kernel(at_back, first, middle, hidden, back, turn.up_g_last, norms)
    up, qkv, gain, bias, down, out = join_kernel(back, last)
    activations = jnp.stack(swapped(section, middle.y, back.out))
    input_grads = jnp.stack(swapped(section, last.in_grad, back.in_grad))
    return (
        activations[None, None],
        input_grads[None, None],
        qkv[None],
        out[None],
        up[None],
        down.reshape(D, D)[None],
        gain,
        bias,
    )


def solution(mesh):
    tokens = P(LINE, None, CONTEXT, None)
    rows = P(SECTION, LINE, None)
    norms = P(SECTION, None, LINE)
    layers = P(SECTION, LINE, None, CONTEXT, None)
    return jax.shard_map(
        shards,
        mesh=mesh,
        in_specs=(tokens, tokens, P(), rows, rows, rows, rows, norms, norms),
        out_specs=(layers, layers, rows, rows, rows, rows, norms, norms),
        check_vma=False,
    )
```

```python
import functools
import types

import jax
import jax.numpy as jnp
from jax import lax
from jax.experimental import pallas as pl
from jax.experimental.pallas import tpu as pltpu
from jax.sharding import PartitionSpec as P

D = 1088
HEADS = 17
HEAD_DIM = 64
FF = 4352
SHARD = 4
CTX = 16
ROWS = 64
GROUP = 1024
SEQ = 2048
WINDOW = 640
SLICE = D // SHARD
EPSILON = 1e-05
NEG_LARGE = -1e30
BF16 = jnp.bfloat16
F32 = jnp.float32
MESH = pl.DeviceIdType.MESH
VMEM = pltpu.VMEM
ANY = pl.ANY
VMEM_BYTES = 58 * 2**20
SECTION, CONTEXT, LINE = "section", "ctx", "shard"
TILES = (68, 16, WINDOW)


def spec(shape, dtype=BF16):
    return jax.ShapeDtypeStruct(shape, dtype)


def call(name, body, ins, outs, scratch, collective_id=None):
    def kernel(*refs):
        refs, found = list(refs), {}
        for key, value in [*ins.items(), *outs.items(), *scratch.items()]:
            if isinstance(value, list):
                found[key], refs = refs[: len(value)], refs[len(value) :]
            else:
                found[key] = refs.pop(0)
        body(types.SimpleNamespace(**found))

    extra = {} if collective_id is None else dict(collective_id=collective_id, has_side_effects=True)
    shapes, given = [], []
    for value in scratch.values():
        shapes += value if isinstance(value, list) else [value]
    for value in ins.values():
        given += value if isinstance(value, list) else [value]
    results = pl.pallas_call(
        kernel,
        out_shape=tuple(value[0] for value in outs.values()),
        in_specs=[pl.BlockSpec(memory_space=space) for _, space in given],
        out_specs=tuple(pl.BlockSpec(memory_space=value[1]) for value in outs.values()),
        scratch_shapes=shapes,
        compiler_params=pltpu.CompilerParams(vmem_limit_bytes=VMEM_BYTES, **extra),
        name=name,
    )(*(array for array, _ in given))
    return types.SimpleNamespace(**dict(zip(outs, results)))


def dot(a, b):
    return jnp.dot(a, b, preferred_element_type=F32)


def dot_nt(a, b):
    return lax.dot_general(a, b, (((1,), (1,)), ((), ())), preferred_element_type=F32)


def dot_tn(a, b):
    return lax.dot_general(a, b, (((0,), (0,)), ((), ())), preferred_element_type=F32)


def norm_parts(values):
    center = values - jnp.mean(values, axis=-1, keepdims=True)
    rate = lax.rsqrt(jnp.mean(center * center, axis=-1, keepdims=True) + EPSILON)
    return center * rate, rate


def layer_norm(values, gain, bias):
    return norm_parts(values)[0] * gain + bias


def gelu(u):
    return 0.5 * u * (1.0 + jnp.tanh(0.7978845608028654 * (u + 0.044715 * u * u * u)))


class Here:
    def __init__(self, sems):
        self.s = lax.axis_index(SECTION)
        self.c = lax.axis_index(CONTEXT)
        self.y = lax.axis_index(LINE)
        self.sems, self.used, self.sent = sems, 0, []

    def sem(self):
        self.used += 1
        return self.sems.at[self.used - 1]

    def shard(self, step):
        return lax.rem(self.y + step, SHARD)

    def rows(self, shard, core):
        return pl.ds(pl.multiple_of((shard * 2 + core) * ROWS, ROWS), ROWS)

    def barrier(self, whole=True):
        sem = pltpu.get_barrier_semaphore()
        peers = []
        for step in range(SHARD):
            for core in range(2):
                if step or core:
                    peers.append((lax.rem(self.s + core, 2), self.c, self.shard(step)))
        for step in range(1, CTX if whole else 1):
            for core in range(2):
                peers.append((core, lax.rem(self.c + step, CTX), self.y))
        for to in peers:
            pl.semaphore_signal(sem, inc=1, device_id=to, device_id_type=MESH)
        self.awaited = len(peers)

    def ready(self):
        pl.semaphore_wait(pltpu.get_barrier_semaphore(), self.awaited)

    def save_on(self, core, src, dst):
        copy = pltpu.make_async_copy(src, dst, self.sem())
        pl.when(self.s == core)(copy.start)
        self.sent.append(types.SimpleNamespace(wait_send=lambda: pl.when(self.s == core)(copy.wait)))

    def local(self, src, dst):
        copy = pltpu.make_async_copy(src, dst, self.sem())
        copy.start()
        return copy

    def save(self, src, dst):
        copy = self.local(src, dst)
        self.sent.append(types.SimpleNamespace(wait_send=copy.wait))

    def wait_later(self, ref, sem):
        self.sent.append(types.SimpleNamespace(wait_send=lambda: wait_bytes(ref, sem)))

    def send(self, src, dst, to, arrive, leave=None):
        copy = pltpu.make_async_remote_copy(
            src_ref=src, dst_ref=dst, send_sem=self.sem() if leave is None else leave,
            recv_sem=arrive, device_id=to, device_id_type=MESH)
        copy.start()
        if leave is None:
            self.sent.append(copy)
        return copy

    def send_or_keep(self, src, dst, to, is_self, arrive):
        leave = self.sem()
        copy = pltpu.make_async_remote_copy(
            src_ref=src, dst_ref=dst, send_sem=leave, recv_sem=arrive, device_id=to, device_id_type=MESH)
        kept = pltpu.make_async_copy(src, dst, arrive)
        pl.when(jnp.logical_not(is_self))(copy.start)
        pl.when(is_self)(kept.start)

        def wait_send():
            pl.when(jnp.logical_not(is_self))(copy.wait_send)

        self.sent.append(types.SimpleNamespace(wait_send=wait_send))

    def sibling(self):
        return (1 - self.s, self.c, self.y)

    def finish(self):
        for copy in self.sent:
            copy.wait_send()
        self.sent = []


def wait_bytes(ref, sem):
    pltpu.make_async_copy(ref, ref, sem).wait()


PARTS = 2
HALF = ROWS // PARTS


def half_rows(half):
    return slice(HALF * half, HALF * half + HALF)


class Messages:
    def __init__(self, h, arrived):
        self.h, self.arrived, self.leave = h, arrived, h.sem()

    def add(self, sends):
        for src, dst, to, here, arrive in sends:
            copy = pltpu.make_async_remote_copy(
                src_ref=src, dst_ref=dst, send_sem=self.leave, recv_sem=arrive, device_id=to, device_id_type=MESH)
            pl.when(jnp.logical_not(here))(copy.start)
            pl.when(here)(pltpu.make_async_copy(src, dst, arrive).start)

    def done(self):
        h = self.h

        def wait_send():
            pl.when(h.c // 8 != h.s)(lambda: wait_bytes(self.arrived, self.leave))
            pl.when(h.c // 8 == h.s)(lambda: wait_bytes(self.arrived.at[pl.ds(0, 15)], self.leave))

        h.sent.append(types.SimpleNamespace(wait_send=wait_send))


class Gather8:
    def __init__(self, here, full):
        self.here, self.full = here, full
        self.own = [[here.sem() for _ in range(PARTS)] for _ in range(SHARD)]
        self.other = [[here.sem() for _ in range(PARTS)] for _ in range(SHARD)]
        self.leave = here.sem()
        here.wait_later(full.at[pl.ds(0, 7 * ROWS)], self.leave)

    def rows(self, shard, core, half):
        return self.full.at[pl.ds(pl.multiple_of((shard * 2 + core) * ROWS + half * HALF, HALF), HALF)]

    def start(self, value, half):
        h = self.here
        mine = self.rows(h.y, h.s, half)
        mine[...] = value
        h.send(mine, mine, h.sibling(), self.other[0][half], self.leave)
        for step in (1, 3, 2):
            h.send(mine, mine, (h.s, h.c, h.shard(step)), self.own[SHARD - step][half], self.leave)

    def relay(self, step):
        h = self.here
        for half in range(PARTS):
            part = self.rows(h.shard(step), h.s, half)
            wait_bytes(part, self.own[step][half])
            h.send(part, part, h.sibling(), self.other[step][half], self.leave)

    def wait(self, step):
        h = self.here
        for half in range(PARTS):
            wait_bytes(self.rows(h.shard(step), 1 - h.s, half), self.other[step][half])


class Scatter8:
    def __init__(self, here, bufs):
        self.here = here
        self.to_core, self.mine, self.from_core, self.to_shard, self.from_shard = bufs
        self.core = [[here.sem() for _ in range(PARTS)] for _ in range(SHARD)]
        self.shard = [[here.sem() for _ in range(PARTS)] for _ in range(SHARD)]
        self.leave = [here.sem(), here.sem()]
        here.wait_later(self.from_core, self.leave[0])
        here.wait_later(self.from_shard.at[pl.ds(0, 3)], self.leave[1])

    def part(self, ref, step, half):
        return ref.at[step, pl.ds(half * HALF, HALF)]

    def put(self, step, block):
        h = self.here
        low, high = block[:ROWS], block[ROWS:]
        self.to_core[step] = jnp.where(h.s == 0, high, low).astype(BF16)
        self.mine[step] = jnp.where(h.s == 0, low, high)
        for half in range(PARTS):
            h.send(
                self.part(self.to_core, step, half), self.part(self.from_core, step, half), h.sibling(),
                self.core[step][half], self.leave[0])

    def relay(self, steps):
        h = self.here
        for half in range(PARTS):
            for step in steps:
                part = self.part(self.from_core, step, half)
                wait_bytes(part, self.core[step][half])
                total = self.mine[step, half_rows(half)] + part[...].astype(F32)
                out = self.part(self.to_shard, step, half)
                out[...] = total.astype(BF16)
                h.send(
                    out, self.part(self.from_shard, step, half), (h.s, h.c, h.shard(step)), self.shard[step][half],
                    self.leave[1])

    def result(self, half):
        part = self.part(self.from_core, 0, half)
        wait_bytes(part, self.core[0][half])
        total = self.mine[0, half_rows(half)] + part[...].astype(F32)
        for step in (1, 3, 2):
            part = self.part(self.from_shard, step, half)
            wait_bytes(part, self.shard[step][half])
            total = total + part[...].astype(F32)
        return total


def scatter_scratch():
    quarter = (SHARD, ROWS, D)
    return [VMEM(quarter, BF16), VMEM(quarter, F32), VMEM(quarter, BF16), VMEM(quarter, BF16), VMEM(quarter, BF16)]


ORDER = (0, 1, 3, 2)


def window_offset(group):
    return 32 * lax.rem(group, 4)


def everyone(h):
    for step in (1, 3, 2, 0):
        for other in range(2):
            yield step, other, (lax.rem(h.s + other, 2), h.c, h.shard(step))


def packed_qkv(rows, g):
    keys = rows[:, D + 128 * g : D + 128 * g + 128]
    values = rows[:, 2 * D + 128 * g : 2 * D + 128 * g + 128]
    return jnp.concatenate([
        rows[:, 128 * g : 128 * g + 128], keys[:, :64], values[:, :64], keys[:, 64:], values[:, 64:],
        rows[:, D - 64 : D], rows[:, 2 * D - 64 : 2 * D], rows[:, 3 * D - 64 : 3 * D], jnp.zeros_like(keys[:, :64])],
        axis=1)


def window(g):
    return slice(128 * (17 * g // 4), 128 * (17 * g // 4) + WINDOW)


def spread_kernel(gains, biases, w_qkv, w_up):
    def body(r):
        h = Here(r.sems)
        own = pl.ds(pl.multiple_of(h.c * 16, 16), 16)
        loads = [
            h.local(ref.at[0, rows], dst.at[pl.ds(16 * i, 16)])
            for ref, dst in ((r.w_up, r.up_rows), (r.w_qkv, r.qkv_rows)) for i, rows in enumerate((own, pl.ds(256, 16)))]
        h.barrier(whole=False)
        arrive, arrive_mid, arrive_up = h.sem(), h.sem(), h.sem()
        mine = r.params_in.at[h.s * SHARD + h.y]
        zeros = jnp.zeros((4, SLICE), F32)
        mine[...] = jnp.concatenate([r.gains[0].astype(F32), r.biases[0].astype(F32), zeros], axis=0)
        for copy in loads:
            copy.wait()

        @pl.when(h.s == 0)
        def _():
            for g in range(8):
                r.mid[g] = r.up_rows[:, window(g)].reshape(2, 16, WINDOW)
                r.up[g] = packed_qkv(r.qkv_rows[...], g).reshape(2, 16, WINDOW)

        @pl.when(h.s == 1)
        def _():
            for g in range(8):
                r.mid[g] = packed_qkv(r.qkv_rows[...], g).reshape(2, 16, WINDOW)
                r.up[g] = r.up_rows[:, window(g)].reshape(2, 16, WINDOW)

        h.ready()
        for step, other, to in everyone(h):
            if step or other:
                h.send(mine, mine, to, arrive)
        for step, other, to in everyone(h):
            g = 2 * to[2] + to[0]
            slot = h.s * SHARD + h.y
            for sem, source, targets in (
                    (arrive_up, r.up, (r.side_piece, r.side_last)), (arrive_mid, r.mid, (r.mid_piece, r.mid_last))):
                for half in range(2):
                    src, dst = source.at[g, half], targets[half].at[slot]
                    if step or other:
                        h.send(src, dst, to, sem)
                    else:
                        pltpu.make_async_copy(src, dst, sem).start()
        wait_bytes(r.params_in.at[pl.ds(0, 7)], arrive)
        for layer in range(2):
            r.norms[layer] = jnp.concatenate([r.params_in[layer * SHARD + i] for i in range(SHARD)], axis=1)
        wait_bytes(r.mid, arrive_mid)
        wait_bytes(r.up, arrive_up)
        h.finish()

    ins = dict(gains=(gains, VMEM), biases=(biases, VMEM), w_qkv=(w_qkv, ANY), w_up=(w_up, ANY))
    outs = dict(
        norms=(spec((2, 8, D), F32), VMEM), mid_piece=(spec((8, 16, WINDOW)), VMEM),
        mid_last=(spec((8, 16, WINDOW)), VMEM), side_piece=(spec((8, 16, WINDOW)), VMEM),
        side_last=(spec((8, 16, WINDOW)), VMEM))
    scratch = dict(
        params_in=VMEM((8, 8, SLICE), F32), up_rows=VMEM((32, FF), BF16), qkv_rows=VMEM((32, 3 * D), BF16),
        mid=VMEM((8, 2, 16, WINDOW), BF16), up=VMEM((8, 2, 16, WINDOW), BF16), sems=pltpu.SemaphoreType.DMA((42,)))
    return call("spread", body, ins, outs, scratch, collective_id=0)


def load_tiles(h, gathered, last, dst, first=0):
    sem = h.sem()
    for i in range(SHARD):
        pltpu.make_async_copy(gathered.at[:, first + i], dst.at[pl.ds(17 * i, 16)], sem).start()
        pltpu.make_async_copy(last.at[first + i], dst.at[17 * i + 16], sem).start()
    return [types.SimpleNamespace(wait=lambda: wait_bytes(dst, sem))]


def place(value, parts, last):
    tiles = value.astype(BF16).reshape(68, 16, value.shape[1])
    for i in range(SHARD):
        for c in range(CTX):
            parts[c // 4, c % 4, i] = tiles[17 * i + c]
        last[i] = tiles[17 * i + 16]


def whole(ref):
    return ref[...].reshape(D, WINDOW)


class FirstWeights:
    def __init__(self, h, r):
        self.h, self.r = h, r
        self.arrive = [h.sem() for _ in range(3)]
        self.spreads = [Spread16(h, parts, i == 0) for i, parts in enumerate((r.qkv_low, r.qkv_high))]

    def load(self):
        h, r = self.h, self.r
        self.loads = [h.local(r.w_down.at[0], r.down_rows), h.local(r.w_out.at[0], r.out_rows)]

    def send_qkv(self):
        r = self.r
        for i, (each, parts) in enumerate(zip(self.spreads, (r.qkv_low, r.qkv_high))):
            parts[each.x, each.z] = r.side_piece[2 * i : 2 * i + 2]
            each.start()

    def send_qkv_on(self):
        for each in self.spreads:
            each.middle()

    def send_rest(self):
        h, r = self.h, self.r
        for copy in self.loads:
            copy.wait()
        for other in range(2):
            core = lax.rem(h.s + other, 2)
            at = pl.multiple_of(window_offset(h.y * 2 + core), 32)
            src = r.down_rows.at[pl.ds(pl.multiple_of(544 * core, 16), 544)]
            dst = r.down_vm.at[h.s, pl.ds(at, 544)]
            if other:
                h.send(src, dst, h.sibling(), self.arrive[1])
            else:
                pltpu.make_async_copy(src, dst, self.arrive[1]).start()
        self.tiles = []
        for i in range(17):
            tile = h.y * 17 + i
            group = jnp.minimum(tile // 8, 7)
            core, shard = lax.rem(group, 2), group // 2
            src = r.out_rows.at[pl.ds(16 * i, 16)]
            dst = r.out_vm.at[h.s, pl.ds(pl.multiple_of(lax.rem(tile, 8) * 16, 16), 16)]
            copy = pltpu.make_async_remote_copy(
                src_ref=src, dst_ref=dst, send_sem=h.sem(), recv_sem=self.arrive[2],
                device_id=(core, h.c, shard), device_id_type=MESH)
            same = pltpu.make_async_copy(src, dst, self.arrive[2])
            is_self = (core == h.s) & (shard == h.y)
            pl.when((tile < 64) & is_self)(same.start)
            away = (tile < 64) & jnp.logical_not(is_self)
            pl.when(away)(copy.start)
            self.tiles.append((away, copy))
        src, dst = r.out_rows.at[pl.ds(SLICE - 64, 64)], r.out_vm.at[h.s, pl.ds(128, 64)]
        same = pltpu.make_async_copy(src, dst, self.arrive[2])
        self.last = []
        for step, other, to in everyone(h):
            if step or other:
                self.last.append(pltpu.make_async_remote_copy(
                    src_ref=src, dst_ref=dst, send_sem=h.sem(), recv_sem=self.arrive[2], device_id=to,
                    device_id_type=MESH))

        @pl.when(h.y == SHARD - 1)
        def _():
            same.start()
            for copy in self.last:
                copy.start()

    def wait_qkv(self):
        r = self.r
        for each in self.spreads:
            each.finish()
        for i in range(SHARD):
            for c in range(CTX):
                parts = (r.qkv_low, r.qkv_high)[i // 2]
                r.qkv_vm[17 * i + c] = parts[c // 4, c % 4, i % 2]
            r.qkv_vm[17 * i + 16] = r.side_last[i]

    def finish(self):
        r, h = self.r, self.h
        wait_bytes(r.down_vm.at[:, pl.ds(0, 544)], self.arrive[1])
        h.save(r.down_vm, r.down_w)
        wait_bytes(r.out_vm, self.arrive[2])
        h.save(r.out_vm, r.out_w)

        for away, copy in self.tiles:
            pl.when(away)(copy.wait_send)

        @pl.when(h.y == SHARD - 1)
        def _():
            for copy in self.last:
                copy.wait_send()


def head_outs():
    return dict(
        a_full=(spec((512, D)), ANY), message_in=(spec((CTX, 160, 128)), VMEM),
        kv16_in=(spec((2, CTX, ROWS, 128)), VMEM), q16=(spec((ROWS, HEAD_DIM)), VMEM))


def head_scratch():
    return dict(message=VMEM((2, 4, 2, 160, 128), BF16), qkv_vm=VMEM(TILES, BF16), a_vm=VMEM((512, D), BF16))


def run_head(h, r, gather, after=None):
    arrive = h.sem()
    own16 = dot(r.a_vm[h.rows(h.y, h.s)], r.qkv_vm[:, :, 384:].reshape(D, 256)).astype(BF16)
    r.q16[...] = own16[:, :64]
    r.kv16_in[h.s, h.c] = own16[:, 64:192]
    own_kv = r.kv16_in.at[h.s, h.c]
    leave16, arrive16, cross16 = h.sem(), h.sem(), h.sem()
    for step in range(1, CTX):
        h.send(own_kv, own_kv, (h.s, lax.rem(h.c + step, CTX), h.y), arrive16, leave16)
    messages = Messages(h, r.message_in)
    for step in ORDER:
        if step:
            gather.relay(step)
        gather.wait(step)
        sends = []
        shard = h.shard(step)
        block = r.a_vm[pl.ds(pl.multiple_of(shard * 128, 128), 128)]
        out = dot(block, r.qkv_vm[:, :, :384].reshape(D, 384)).astype(BF16)
        for e in range(2):
            for core in range(2):
                r.message[e, shard, core, :128] = out[:, 128 + 128 * e : 256 + 128 * e]
                for b in range(2):
                    at = 32 * b + 16 * core
                    lanes = slice(64 * e, 64 * e + 64)
                    packed = jnp.concatenate([out[at : at + 16, lanes], out[64 + at : 80 + at, lanes]], axis=1)
                    r.message[e, shard, core, 128 + 16 * b : 144 + 16 * b] = packed
                chip = 8 * h.s + 4 * e + shard
                sends.append((
                    r.message.at[e, shard, core], r.message_in.at[h.c], (core, chip, h.y),
                    (chip == h.c) & (h.s == core), arrive))
        messages.add(sends)
    messages.done()
    h.save(r.a_vm, r.a_full)
    if after is not None:
        after()
    wait_bytes(r.kv16_in.at[h.s, pl.ds(0, CTX - 1)], arrive16)
    cross = r.kv16_in.at[h.s]
    h.send(cross, cross, h.sibling(), cross16)
    wait_bytes(r.kv16_in.at[h.s, pl.ds(0, CTX - 1)], leave16)
    wait_bytes(r.kv16_in.at[1 - h.s], cross16)
    wait_bytes(r.message_in, arrive)


def first_kernel(hidden, norms, side_piece, side_last, w_out, w_down):
    def body(r):
        h = Here(r.sems)
        weights = FirstWeights(h, r)
        weights.load()
        r.down_vm[...] = jnp.zeros_like(r.down_vm)
        h.barrier()
        x = r.hidden[h.s].astype(F32)
        a_value = layer_norm(x, r.norms[0, 0:1], r.norms[0, 2:3]).astype(BF16)
        h.ready()
        weights.send_qkv()
        gather = Gather8(h, r.a_vm)
        for half in range(PARTS):
            gather.start(a_value[half_rows(half)], half)
        weights.send_qkv_on()
        weights.wait_qkv()
        h.save(r.qkv_vm, r.qkv_w)
        run_head(h, r, gather, weights.send_rest)
        weights.finish()
        h.finish()

    ins = dict(hidden=(hidden, VMEM), norms=(norms, VMEM), side_piece=(side_piece, VMEM), side_last=(side_last, VMEM),
        w_out=(w_out, ANY), w_down=(w_down, ANY))
    outs = dict(
        **head_outs(), qkv_w=(spec(TILES), ANY), out_w=(spec((2, 192, D)), ANY), down_w=(spec((2, WINDOW, D)), ANY))
    scratch = dict(
        **head_scratch(), qkv_low=VMEM((4, 4, 2, 16, WINDOW), BF16), qkv_high=VMEM((4, 4, 2, 16, WINDOW), BF16),
        down_rows=VMEM((D, D), BF16), out_rows=VMEM((SLICE, D), BF16), down_vm=VMEM((2, WINDOW, D), BF16),
        out_vm=VMEM((2, 192, D), BF16), sems=pltpu.SemaphoreType.DMA((65,)))
    return call("first", body, ins, outs, scratch, collective_id=1)


def sort_rows(r):
    for m in range(2):
        for p in range(32):
            at = 32 * m + p
            tile = r.places[0, m, p]
            for i in range(2):
                rows = r.kept[tile + i]
                r.keys[32 * at + 16 * i : 32 * at + 16 * i + 16] = rows[:, :64]
                r.values[32 * at + 16 * i : 32 * at + 16 * i + 16] = rows[:, 64:]
            query = r.kept[r.places[1, m, p]]
            r.queries[16 * at : 16 * at + 16] = query[:, 64 * m : 64 * m + 64] * 0.125


def attend(h, r):
    row = lax.broadcasted_iota(jnp.int32, (256, 512), 0)
    row = 32 * (row // 16) + 16 * h.s + row % 16
    visible = row >= lax.broadcasted_iota(jnp.int32, (256, 512), 1)
    for t in range(4):
        query = r.queries[256 * t : 256 * t + 256]
        parts = [dot_nt(query, r.keys[512 * u : 512 * u + 512]) for u in range(t + 1)]
        parts[t] = jnp.where(visible, parts[t], NEG_LARGE)
        top = parts[0]
        for p in parts[1:]:
            top = jnp.maximum(top, p)
        top = jnp.max(top, axis=-1, keepdims=True)
        parts = [jnp.exp(p - top) for p in parts]
        total = parts[0]
        for p in parts[1:]:
            total = total + p
        total = jnp.sum(total, axis=-1, keepdims=True)
        out = dot(parts[0].astype(BF16), r.values[:512])
        for u in range(1, t + 1):
            out = out + dot(parts[u].astype(BF16), r.values[512 * u : 512 * u + 512])
        r.sorted_out[16 * t : 16 * t + 16] = (out / total).astype(BF16).reshape(16, 16, 64)
        logs = jnp.transpose(jnp.broadcast_to(top + jnp.log(total), (256, 128)))
        r.logs[:, 256 * t : 256 * t + 256] = logs[:8]
    for c in range(CTX):
        for m in range(2):
            for b in range(2):
                rows = r.sorted_out[32 * m + r.order[m, 2 * c + b]]
                r.attended[c, 16 * b : 16 * b + 16, 64 * m : 64 * m + 64] = rows


def attend_last(r):
    kv = r.kept16[...].reshape(SEQ, 128)
    scores = dot_nt(r.kept_q16[...] * 0.125, kv[:, :64])
    scores = jnp.where(r.own_positions[...] >= r.positions[...], scores, NEG_LARGE)
    top = jnp.max(scores, axis=-1, keepdims=True)
    scores = jnp.exp(scores - top)
    total = jnp.sum(scores, axis=-1, keepdims=True)
    out = dot(scores.astype(BF16), kv[:, 64:])
    r.attended16[...] = (out / total).astype(BF16)
    r.logs16[...] = jnp.broadcast_to(top + jnp.log(total), (ROWS, 128))


def attend_ins(kept, at):
    order, places, positions, own_positions = at
    return dict(
        order=(order, pltpu.SMEM), places=(places, pltpu.SMEM), positions=(positions, VMEM),
        own_positions=(own_positions, VMEM), kept=(kept.message_in.reshape(160, 16, 128), VMEM), kept16=(kept.kv16_in, VMEM),
        kept_q16=(kept.q16, VMEM))


def attend_outs():
    return dict(
        attended16=(spec((ROWS, 64)), VMEM), sorted_out=(spec((64, 16, 64)), VMEM), logs=(spec((8, 1024), F32), VMEM),
        logs16=(spec((ROWS, 128), F32), VMEM))


def attend_scratch():
    return dict(
        keys=VMEM((SEQ, 64), BF16), values=VMEM((SEQ, 64), BF16), queries=VMEM((1024, 64), BF16),
        attended=VMEM((CTX, 32, 128), BF16))


def middle_scratch():
    return dict(
        context_in=VMEM((2, 4, 2, 32, 128), BF16), out_vm=VMEM((192, D), BF16), up_vm=VMEM(TILES, BF16),
        down_vm=VMEM((WINDOW, D), BF16), to_out=scatter_scratch(), to_down=scatter_scratch())


def load_layer(h, r, layer, first):
    loads = [h.local(r.out_w.at[layer], r.out_vm), h.local(r.down_w.at[layer], r.down_vm)]
    return loads + load_tiles(h, r.up_all, r.up_last, r.up_vm, first)


def gather_context(h, r):
    arrive = h.sem()
    to_core = h.c // 8
    e, j = lax.rem(h.c // 4, 2), lax.rem(h.c, 4)
    messages = Messages(h, r.attended)
    messages.add([
        (r.attended.at[c], r.context_in.at[e, j, h.s], (to_core, c, h.y), (h.c == c) & (h.s == to_core), arrive)
        for c in range(CTX)])
    messages.done()
    return arrive


def unpack_context(r, store):
    for j in range(4):
        for m in range(2):
            for b in range(2):
                for core in range(2):
                    lanes = slice(64 * m, 64 * m + 64)
                    piece = jnp.concatenate(
                        [r.context_in[e, j, core, 16 * b : 16 * b + 16, lanes] for e in range(2)], axis=1)
                    at = 128 * j + 64 * m + 32 * b + 16 * core
                    store[at : at + 16] = piece


def block_rows(h, step):
    return pl.ds(pl.multiple_of(h.shard(step) * 128, 128), 128)


def run_out(h, r, x, ready):
    sums = Scatter8(h, r.to_out)
    for step in (2, 1, 3, 0):
        sums.put(step, dot(r.context[block_rows(h, step)], r.out_vm[:128]))
    sums.relay((2, 1, 3))
    own = x + dot(r.attended16[...], r.out_vm[128:])
    for half in range(PARTS):
        residual = own[half_rows(half)] + sums.result(half)
        r.residual[half_rows(half)] = residual
        ready(half, residual)


def middle_kernel(at, x, norms, first, mid_all, mid_last):
    def body(r):
        h = Here(r.sems)
        loads = load_layer(h, r, 0, 0)
        head_loads = load_tiles(h, r.up_all, r.up_last, r.qkv_vm, SHARD)
        h.barrier()
        sort_rows(r)
        attend(h, r)
        h.ready()
        arrive = gather_context(h, r)
        attend_last(r)
        for copy in loads:
            copy.wait()
        wait_bytes(r.context_in, arrive)
        unpack_context(r, r.context)
        gather = Gather8(h, r.b_vm)

        def ready(half, residual):
            gather.start(layer_norm(residual, r.norms[0, 1:2], r.norms[0, 3:4]).astype(BF16), half)

        run_out(h, r, r.x[h.s].astype(F32), ready)
        sums = Scatter8(h, r.to_down)
        for step in ORDER:
            if step:
                gather.relay(step)
            gather.wait(step)
            rows = block_rows(h, step)
            u = dot(r.b_vm[rows], whole(r.up_vm))
            r.pre_vm[rows] = u
            sums.put(step, dot(gelu(u).astype(BF16), r.down_vm[...]))
        sums.relay((1, 3, 2))
        h.save(r.b_vm, r.b_full)
        h.save(r.pre_vm, r.pre)
        for copy in head_loads:
            copy.wait()
        gather = Gather8(h, r.a_vm)
        for half in range(PARTS):
            y = (r.residual[half_rows(half)] + sums.result(half)).astype(BF16)
            r.y[half_rows(half)] = y
            gather.start(layer_norm(y.astype(F32), r.norms[1, 0:1], r.norms[1, 2:3]).astype(BF16), half)
        run_head(h, r, gather)
        h.finish()

    ins = dict(
        **attend_ins(first, at), x=(x, VMEM), norms=(norms, VMEM), out_w=(first.out_w, ANY),
        down_w=(first.down_w, ANY), up_all=(mid_all, ANY), up_last=(mid_last, ANY))
    outs = dict(
        **attend_outs(), context=(spec((512, 128)), VMEM), residual=(spec((ROWS, D), F32), VMEM), b_full=(spec((512, D)), ANY),
        pre=(spec((512, WINDOW), F32), ANY), y=(spec((ROWS, D)), VMEM), **head_outs())
    scratch = dict(
        **attend_scratch(), **middle_scratch(), **head_scratch(), b_vm=VMEM((512, D), BF16), pre_vm=VMEM((512, WINDOW), F32),
        sems=pltpu.SemaphoreType.DMA((85,)))
    return call("middle", body, ins, outs, scratch, collective_id=2)


def gelu_slope(u):
    t = jnp.tanh(0.7978845608028654 * (u + 0.044715 * u * u * u))
    return 0.5 * (1.0 + t) + 0.5 * u * (1.0 - t * t) * 0.7978845608028654 * (1.0 + 0.134145 * u * u)


def norm_back(grad, values, gain):
    normed, rate = norm_parts(values)
    scaled = grad * gain
    mean = jnp.mean(scaled, axis=-1, keepdims=True)
    along = jnp.mean(scaled * normed, axis=-1, keepdims=True)
    back = rate * (scaled - mean - normed * along)
    return back, grad * normed


def columns(at, gain_rows, bias_rows):
    lane = lax.broadcasted_iota(jnp.int32, (ROWS, 64), 1)

    def into(rows, column):
        return dot_tn(rows.astype(BF16), (lane == column).astype(BF16))

    return into(gain_rows, at) + into(bias_rows, at + 1)


def back_outs():
    return dict(
        mid_grad=(spec((ROWS, D), F32), VMEM), context_grad_in=(spec((CTX, 32, 128)), VMEM),
        context16_grad=(spec((ROWS, HEAD_DIM)), VMEM),
        up_g_last=(spec((SHARD, 16, WINDOW)), VMEM), norm2_g=(spec((68, 16, 64)), VMEM))


def back_scratch():
    return dict(
        m_full=VMEM((512, D), BF16), z_full=VMEM((512, D), BF16), hidden_low=VMEM((512, WINDOW), BF16),
        pre_grad=VMEM((512, WINDOW), BF16), context_message=VMEM((2, 4, 2, 32, 128), BF16), up_grad=VMEM((4, 4, SHARD, 16, WINDOW), BF16),
        down_grad=VMEM((40, 16, D), BF16), b_vm=VMEM((512, D), BF16), to_norm2=scatter_scratch())


def back_block(h, r, rows, sums, step, u, g):
    r.hidden_low[rows] = g
    hidden_grad = dot_nt(r.m_full[rows], r.down_vm[...])
    pre_grad = (hidden_grad * gelu_slope(u)).astype(BF16)
    r.pre_grad[rows] = pre_grad
    sums.put(step, dot_nt(pre_grad, whole(r.up_vm)))


def finish_back(h, r, sums, layer, residual, out_grad, context, down_ready, up_ready, beside, near_end=None):
    r.down_grad[...] = dot_tn(r.hidden_low[...], r.m_full[...]).astype(BF16).reshape(40, 16, D)
    down_ready(r.down_grad, 2 * lax.rem(h.y * 2 + h.s, 4))
    place(dot_tn(r.b_vm[...], r.pre_grad[...]), r.up_grad, r.up_g_last)
    up_ready()
    gather = Gather8(h, r.z_full)
    gain_rows, normed_grad = [], []
    for half in range(PARTS):
        rows = half_rows(half)
        normed_grad.append(sums.result(half))
        back, gains = norm_back(normed_grad[half], residual[rows], r.norms[layer, 1:2])
        gain_rows.append(gains)
        mid_grad = out_grad[rows] + back
        r.mid_grad[rows] = mid_grad
        gather.start(mid_grad.astype(BF16), half)
    gain_rows, normed_grad = jnp.concatenate(gain_rows, axis=0), jnp.concatenate(normed_grad, axis=0)
    z = r.z_full[h.rows(h.y, h.s)]
    r.norm2_g[...] = columns(2, gain_rows, normed_grad).astype(BF16).reshape(68, 16, 64)
    beside()
    arrive = h.sem()
    r.context16_grad[...] = dot_nt(z, r.out_vm[128:]).astype(BF16)
    messages = Messages(h, r.context_grad_in)
    for step in ORDER:
        if step:
            gather.relay(step)
        gather.wait(step)
        sends = []
        shard = h.shard(step)
        out = dot_nt(r.z_full[block_rows(h, step)], r.out_vm[:128]).astype(BF16)
        for e in range(2):
            for core in range(2):
                lanes = slice(64 * e, 64 * e + 64)
                for b in range(2):
                    at = 32 * b + 16 * core
                    r.context_message[e, shard, core, 16 * b : 16 * b + 16] = jnp.concatenate(
                        [out[at : at + 16, lanes], out[64 + at : 80 + at, lanes]], axis=1)
                chip = 8 * h.s + 4 * e + shard
                sends.append((
                    r.context_message.at[e, shard, core], r.context_grad_in.at[h.c], (core, chip, h.y),
                    (chip == h.c) & (h.s == core), arrive))
        messages.add(sends)
    messages.done()
    r.out_g[:8] = dot_tn(context[...], r.z_full[...]).astype(BF16).reshape(8, 16, D)
    r.out_g[8:] = dot_tn(r.attended16[...], z).astype(BF16).reshape(4, 16, D)
    if near_end is not None:
        near_end()
    wait_bytes(r.context_grad_in, arrive)


def turn_kernel(at, kept, x, norms, first, up_all, up_last, cotangent):
    def body(r):
        h = Here(r.sems)
        loads = load_layer(h, r, 1, SHARD)
        h.barrier()
        sort_rows(r)
        h.ready()
        out_grad = r.cotangent[h.s]
        gather_m = Gather8(h, r.m_full)
        for half in range(PARTS):
            gather_m.start(out_grad[half_rows(half)], half)
        attend(h, r)
        arrive = gather_context(h, r)
        attend_last(r)
        for step in (1, 3, 2):
            gather_m.relay(step)
        for copy in loads:
            copy.wait()
        wait_bytes(r.context_in, arrive)
        unpack_context(r, r.context)
        gather = Gather8(h, r.b_vm)

        def ready(half, residual):
            gather.start(layer_norm(residual, r.norms[1, 1:2], r.norms[1, 3:4]).astype(BF16), half)

        run_out(h, r, r.x[...].astype(F32), ready)
        back_sums = Scatter8(h, r.to_norm2)
        for step in ORDER:
            if step:
                gather.relay(step)
            gather_m.wait(step)
            gather.wait(step)
            rows = block_rows(h, step)
            u = dot(r.b_vm[rows], whole(r.up_vm))
            g = gelu(u).astype(BF16)
            back_block(h, r, rows, back_sums, step, u, g)
        back_sums.relay((1, 3, 2))
        h.save(r.hidden_low, r.hidden_out)

        ups = [
            Reduce16(h, r.up_grad.at[:, :, pl.ds(2 * i, 2)], (r.ups_in.at[i], (r.up_mine_a, r.up_mine_b)[i], None), i == 0)
            for i in range(2)]
        first_rows = FirstRows(h, r)

        def up_ready():
            for each in ups:
                each.start()
            first_rows.start()

        def near_end():
            for each in ups:
                each.add()
            first_rows.add()

        finish_back(
            h, r, back_sums, 1, r.residual[...], out_grad.astype(F32), r.context, first_rows.load,
            up_ready, lambda: None, near_end)
        h.finish()

    ins = dict(
        **attend_ins(kept, at), x=(x, VMEM), norms=(norms, VMEM), out_w=(first.out_w, ANY),
        down_w=(first.down_w, ANY), up_all=(up_all, ANY), up_last=(up_last, ANY),
        cotangent=(cotangent, VMEM))
    outs = dict(
        **attend_outs(), hidden_out=(spec((512, WINDOW)), ANY), residual=(spec((ROWS, D), F32), VMEM), **first_rows_outs(),
        up_mine_a=(spec((4, 2, 16, WINDOW)), VMEM), up_mine_b=(spec((4, 2, 16, WINDOW)), VMEM), out_g=(spec((12, 16, D)), VMEM), **back_outs())
    scratch = dict(
        **attend_scratch(), context=VMEM((512, 128), BF16), **middle_scratch(),
        **first_rows_scratch(), ups_in=VMEM((2, 3, 4, 2, 16, WINDOW), BF16), **back_scratch(), sems=pltpu.SemaphoreType.DMA((107,)))
    return call("turn", body, ins, outs, scratch, collective_id=3)


def row_of(grads, outs):
    product = grads.astype(F32) * outs.astype(F32)
    return lax.dot_general(
        jnp.ones((8, 64), F32), product, (((1,), (1,)), ((), ())), precision=lax.Precision.HIGHEST,
        preferred_element_type=F32)[0:1]


def sort_grads(r):
    sort_rows(r)
    for m in range(2):
        for p in range(32):
            at = 32 * m + p
            r.grads[16 * at : 16 * at + 16] = r.grad_in[r.places[2, m, p]][:, 64 * m : 64 * m + 64]
    r.key_grads[...] = jnp.zeros_like(r.key_grads)
    r.value_grads[...] = jnp.zeros_like(r.value_grads)


def attend_back(h, r):
    column = lax.broadcasted_iota(jnp.int32, (512, 256), 1)
    column = 32 * (column // 16) + 16 * h.s + column % 16
    visible = column >= lax.broadcasted_iota(jnp.int32, (512, 256), 0)
    for t in range(4):
        part = slice(256 * t, 256 * t + 256)
        query, grad = r.queries[part], r.grads[part]
        logs = r.logs[0:1, part]
        delta = row_of(grad, r.sorted_out[16 * t : 16 * t + 16].reshape(256, 64))
        query_grad = jnp.zeros((256, 64), F32)
        for u in range(t + 1):
            chunk = slice(512 * u, 512 * u + 512)
            keys = r.keys[chunk]
            scores = dot_nt(keys, query)
            if u == t:
                scores = jnp.where(visible, scores, NEG_LARGE)
            probs = jnp.exp(scores - logs)
            probs_grad = dot_nt(r.values[chunk], grad)
            scores_grad = (probs * (probs_grad - delta)).astype(BF16)
            blocks = slice(16 * u, 16 * u + 16)
            r.value_grads[blocks] += dot(probs.astype(BF16), grad).reshape(16, 32, 64)
            r.key_grads[blocks] += dot(scores_grad, query).reshape(16, 32, 64)
            query_grad = query_grad + dot_tn(scores_grad, keys)
        r.query_grads[16 * t : 16 * t + 16] = (query_grad * 0.125).astype(BF16).reshape(16, 16, 64)
    for c in range(CTX):
        for m in range(2):
            for b in range(2):
                block = 32 * m + r.order[m, 2 * c + b]
                r.message[c, 64 * m + 32 * b : 64 * m + 32 * b + 32, :] = jnp.concatenate(
                    [r.key_grads[block], r.value_grads[block]], axis=1).astype(BF16)
                r.message[c, 128 + 16 * b : 144 + 16 * b, 64 * m : 64 * m + 64] = r.query_grads[block]


def attend_back_last(r):
    kv = r.kept16[...].reshape(SEQ, 128)
    query, grad = r.kept_q16[...] * 0.125, r.grad16[...]
    scores = dot_nt(kv[:, :64], query)
    scores = jnp.where(r.own_positions[...] >= r.positions[...], scores, NEG_LARGE)
    probs = jnp.exp(scores - jnp.transpose(r.logs16[...])[0:1])
    probs_grad = dot_nt(kv[:, 64:], grad)
    scores_grad = (probs * (probs_grad - row_of(grad, r.out16[...]))).astype(BF16)
    both = jnp.concatenate([dot(scores_grad, query), dot(probs.astype(BF16), grad)], axis=1)
    r.kv16_grad[...] = both.astype(BF16).reshape(2, CTX, ROWS, 128)
    r.q16_grad[...] = (dot_tn(scores_grad, kv[:, :64]) * 0.125).astype(BF16)


def tail_ins(at, kept, saved, a_full, x, above, norms):
    return dict(
        **attend_ins(kept, at), sorted_out=(saved.sorted_out, VMEM), logs=(saved.logs, VMEM), logs16=(saved.logs16, VMEM),
        out16=(saved.attended16, VMEM), grad_in=(above.context_grad_in.reshape(32, 16, 128), VMEM), grad16=(above.context16_grad, VMEM),
        a_full=(a_full, ANY), x=(x, VMEM), mid_in=(above.mid_grad, VMEM), norms=(norms, VMEM),
        norm2_in=(above.norm2_g, VMEM))


def tail_outs():
    return dict(in_grad=(spec((ROWS, D)), VMEM))


def tail_scratch():
    return dict(
        keys=VMEM((SEQ, 64), BF16), values=VMEM((SEQ, 64), BF16), queries=VMEM((1024, 64), BF16),
        grads=VMEM((1024, 64), BF16), query_grads=VMEM((64, 16, 64), BF16), key_grads=VMEM((64, 32, 64), F32),
        value_grads=VMEM((64, 32, 64), F32), message=VMEM((CTX, 160, 128), BF16),
        kv16_grad=VMEM((2, CTX, ROWS, 128), BF16), q16_grad=VMEM((ROWS, 64), BF16),
        message_in=VMEM((2, 4, 2, 160, 128), BF16), core16=VMEM((CTX, ROWS, 128), BF16),
        sum16=VMEM((CTX, ROWS, 128), BF16), own16=VMEM((CTX, ROWS, 128), BF16), qkv_grads=VMEM((512, 384), BF16),
        qkv_vm=VMEM(TILES, BF16), a_vm=VMEM((512, D), BF16), main_part=VMEM((4, 4, SHARD, 16, 384), BF16),
        side_part=VMEM((4, 4, SHARD, 16, 256), BF16), to_norm1=scatter_scratch())


def start_tail(h, r, after_last=lambda: None):
    attend_back_last(r)
    cross = h.sem()
    h.send(r.kv16_grad.at[1 - h.s], r.core16, h.sibling(), cross)
    after_last()
    attend_back(h, r)
    arrive = h.sem()
    to_core = h.c // 8
    e, j = lax.rem(h.c // 4, 2), lax.rem(h.c, 4)
    messages = Messages(h, r.message)
    messages.add([
        (r.message.at[c], r.message_in.at[e, j, h.s], (to_core, c, h.y), (h.c == c) & (h.s == to_core), arrive)
        for c in range(CTX)])
    messages.done()
    wait_bytes(r.core16, cross)
    r.sum16[...] = (r.kv16_grad[h.s].astype(F32) + r.core16[...].astype(F32)).astype(BF16)
    leave16, arrive16 = h.sem(), h.sem()
    for step in range(1, CTX):
        to = lax.rem(h.c + step, CTX)
        h.send(r.sum16.at[to], r.own16.at[step], (h.s, to, h.y), arrive16, leave16)
    return arrive, leave16, arrive16


def run_tail(h, r, layer, x, waits, loads, last, main_ready, side_ready, arrived, beside, in_ready):
    arrive, leave16, arrive16 = waits
    for copy in loads:
        copy.wait()
    weights = whole(r.qkv_vm)
    wait_bytes(r.message_in, arrive)
    arrived()
    for j in range(4):
        for e in range(2):
            both = r.message_in[e, j, 0, :128].astype(F32) + r.message_in[e, j, 1, :128].astype(F32)
            r.qkv_grads[128 * j : 128 * j + 128, 128 + 128 * e : 256 + 128 * e] = both.astype(BF16)
        for m in range(2):
            for b in range(2):
                for core in range(2):
                    lanes = slice(64 * m, 64 * m + 64)
                    piece = jnp.concatenate(
                        [r.message_in[e, j, core, 128 + 16 * b : 144 + 16 * b, lanes] for e in range(2)], axis=1)
                    at = 128 * j + 64 * m + 32 * b + 16 * core
                    r.qkv_grads[at : at + 16, :128] = piece
    sums = Scatter8(h, r.to_norm1)
    for step in (2, 1, 3, 0):
        sums.put(step, dot_nt(r.qkv_grads[block_rows(h, step)], weights[:, :384]))
    sums.relay((2, 1, 3))
    wait_bytes(r.own16.at[pl.ds(1, CTX - 1)], arrive16)
    wait_bytes(r.own16.at[pl.ds(1, CTX - 1)], leave16)
    kv16 = r.sum16[h.c].astype(F32)
    for step in range(1, CTX):
        kv16 = kv16 + r.own16[step].astype(F32)
    grads16 = jnp.concatenate([r.q16_grad[...], kv16.astype(BF16)], axis=1)
    own = dot_nt(grads16, weights[:, 384:576])
    place(dot_tn(r.a_vm[...], r.qkv_grads[...]), r.main_part, last.at[:, :, pl.ds(0, 384)])
    main_ready()
    own_grad = dot_tn(r.a_vm[h.rows(h.y, h.s)], grads16)
    beside()
    gain_rows, normed_grad = [], []
    for half in range(PARTS):
        rows = half_rows(half)
        normed_grad.append(own[rows] + sums.result(half))
        back, gains = norm_back(normed_grad[half], x[rows], r.norms[layer, 0:1])
        gain_rows.append(gains)
        in_grad = (r.mid_in[rows] + back).astype(BF16)
        r.in_grad[rows] = in_grad
        in_ready(half, in_grad)
    gain_rows, normed_grad = jnp.concatenate(gain_rows, axis=0), jnp.concatenate(normed_grad, axis=0)

    def finish():
        sums_of_rows = columns(0, gain_rows, normed_grad) + r.norm2_in[...].reshape(D, 64).astype(F32)
        side = jnp.concatenate([own_grad, sums_of_rows], axis=1)
        place(side, r.side_part, last.at[:, :, pl.ds(384, 256)])
        side_ready()

    return finish


def send_out(h, r, out, layer, arrive, arrive_last):
    group = 2 * h.y + h.s
    for i in range(8):
        tile = 8 * group + i
        to = tile // 17
        h.send_or_keep(
            out.at[i], r.out_sum.at[lax.rem(tile, 17)], (1 - layer, h.c, to), (h.s != layer) & (to == h.y), arrive)
    h.send_or_keep(
        out.at[pl.ds(8, 4)], r.last_in.at[group], (1 - layer, h.c, SHARD - 1), (h.s != layer) & (h.y == SHARD - 1),
        arrive_last)


def back_kernel(at, kept, saved, x, above, norms, first, attended16, mid_all, mid_last):
    def body(r):
        h = Here(r.sems)
        tail_loads = load_tiles(h, r.up_all, r.up_last, r.qkv_vm, SHARD)
        tail_loads.append(h.local(r.a_full, r.a_vm))
        out_loads = [h.local(r.hidden1, r.hidden_low), h.local(r.down_tiles.at[1], r.down_grad)]
        loads = load_layer(h, r, 0, 0)
        loads += [h.local(r.b_full, r.b_vm), h.local(r.pre, r.pre_vm), h.local(r.context, r.context_vm)]
        h.barrier()
        sort_grads(r)
        arrive_out, arrive_last = h.sem(), h.sem()
        x, z = h.c // 4, lax.rem(h.c, 4)
        ups = [
            Reduce16(h, None, (None, (r.up_mine_a, r.up_mine_b)[i], r.ups_second.at[i]), i == 0) for i in range(2)]
        main = Reduce16(h, r.main_part, r.main_sums, False)
        side = Reduce16(h, r.side_part, r.side_sums, True)
        up0 = Reduce16(h, r.up_grad, (r.up0_in, r.up0_mine, None), True)
        rows16 = Rows16(h, r, 1)
        first_rows = FirstRows(h, r)
        h.ready()
        for each in ups:
            each.send_on()
        rows16.start()
        send_out(h, r, r.out1_g, 1, arrive_out, arrive_last)
        out_sums = Scatter8(h, r.to_down)
        for copy in out_loads:
            copy.wait()
        for step in (2, 1, 3, 0):
            out_sums.put(step, dot(r.hidden_low[block_rows(h, step)], r.down_grad[...].reshape(WINDOW, D)))
        waits = start_tail(h, r, lambda: out_sums.relay((2, 1, 3)))

        def settle(core):
            @pl.when(h.s == core)
            def _():
                @pl.when(h.y < SHARD - 1)
                def _():
                    wait_bytes(r.out_sum, arrive_out)

                @pl.when(h.y == SHARD - 1)
                def _():
                    wait_bytes(r.out_sum.at[pl.ds(0, 13)], arrive_out)
                    wait_bytes(r.last_in, arrive_last)
                    r.out_sum[13:] = added([r.last_in[g] for g in range(8)])

        arrive_up = h.sem()
        spreads = [Spread16(h, parts, i == 0, 1) for i, parts in enumerate((r.up_low, r.up_high))]

        def arrived():
            for half in range(PARTS):
                rows = half_rows(half)
                r.out[rows] = (r.residual1[rows] + out_sums.result(half)).astype(BF16)
            for i in range(2):
                r.up1_piece[2 * i : 2 * i + 2] = ups[i].result()
            send_piece(h, r.up1_piece, r.up_in, 1, arrive_up)
            settle(0)
            rows16.start_out()

        def beside_sums():
            rows16.middle()

            @pl.when(h.s == 1)
            def _():
                wait_bytes(r.up_in, arrive_up)
                rows = joined_up([r.up_in[g] for g in range(8)])
                for i, parts in enumerate((r.up_low, r.up_high)):
                    parts[x, z] = rows[:, 2176 * i : 2176 * i + 2176]

            for each in spreads:
                each.start()

        gather = Gather8(h, r.m_full)
        finish = run_tail(
            h, r, 1, r.x[...].astype(F32), waits, tail_loads, r.qkv_g_last, main.start, side.start,
            arrived, beside_sums, lambda half, value: gather.start(value, half))
        finish()
        rows16.spread()
        for copy in loads:
            copy.wait()
        sums = Scatter8(h, r.to_norm2)
        for step in ORDER:
            if step:
                gather.relay(step)
            gather.wait(step)
            rows = block_rows(h, step)
            u = r.pre_vm[rows]
            back_block(h, r, rows, sums, step, u, gelu(u).astype(BF16))
            if step == 0:
                for each in spreads:
                    each.middle()
            if step == 1:
                rows16.spread_on()
        sums.relay((1, 3, 2))
        def down_ready(rows, first):
            first_rows.load(rows, first)
            main.middle()
            side.middle()

        def up_ready():
            up0.start()
            first_rows.start()

        def beside():
            r.qkv1_piece[:, :, :384] = main.result()
            r.qkv1_piece[:, :, 384:] = side.result()

        def near_end():
            send_out(h, r, r.out_g, 0, arrive_out, arrive_last)
            up0.add()
            first_rows.add()
            rows16.finish()
            for each in spreads:
                each.finish()
            h.save_on(1, r.up_low, r.up_low_all)
            h.save_on(1, r.up_high, r.up_high_all)

        finish_back(
            h, r, sums, 0, r.residual[...], r.in_grad[...].astype(F32), r.context_vm, down_ready, up_ready, beside, near_end)

        settle(1)
        h.finish()

    ins = dict(
        **tail_ins(at, kept, saved, kept.a_full, x, above, norms), pre=(kept.pre, ANY), b_full=(kept.b_full, ANY),
        context=(kept.context, ANY), residual=(kept.residual, VMEM), attended16=(attended16, VMEM),
        out_w=(first.out_w, ANY), down_w=(first.down_w, ANY), up_all=(mid_all, ANY), up_last=(mid_last, ANY),
        up_mine_a=(above.up_mine_a, VMEM), up_mine_b=(above.up_mine_b, VMEM), out1_g=(above.out_g, VMEM),
        mine_a=(above.next_a, VMEM), mine_b=(above.next_b, VMEM), mine_beside=(above.next_beside, VMEM),
        hidden1=(above.hidden_out, ANY), residual1=(above.residual, VMEM),
        down_tiles=(first.down_w.reshape(2, 40, 16, D), ANY))
    piece, half = (spec((SHARD, 16, WINDOW)), VMEM), (spec((4, 4, 16, 2176)), ANY)
    outs = dict(
        **tail_outs(), **back_outs(), out=(spec((ROWS, D)), VMEM), qkv_g_last=piece, qkv1_piece=piece, up0_mine=(spec((4, SHARD, 16, WINDOW)), VMEM),
        up_low_all=half, up_high_all=half, **rows_outs(), **rows_results(),
        **first_rows_outs(), out_sum=(spec((17, 16, D)), VMEM))
    scratch = dict(
        out_vm=VMEM((192, D), BF16), up_vm=VMEM(TILES, BF16), down_vm=VMEM((WINDOW, D), BF16),
        pre_vm=VMEM((512, WINDOW), F32), to_down=scatter_scratch(), context_vm=VMEM((512, 128), BF16), out_g=VMEM((12, 16, D), BF16),
        ups_second=VMEM((2, 3, 2, 16, WINDOW), BF16), **first_rows_scratch(),
        up0_in=VMEM((3, 4, SHARD, 16, WINDOW), BF16), up_low=VMEM((4, 4, 16, 2176), BF16),
        up_high=VMEM((4, 4, 16, 2176), BF16), main_sums=reduce_scratch(SHARD, 384), side_sums=reduce_scratch(SHARD, 256),
        up1_piece=VMEM((SHARD, 16, WINDOW), BF16), up_in=VMEM((8, 16, WINDOW), BF16), last_in=VMEM((8, 4, 16, D), BF16), **tail_scratch(), **back_scratch(),
        **rows_scratch(), sems=pltpu.SemaphoreType.DMA((202,)))
    return call("back", body, ins, outs, scratch, collective_id=4)


class Plane16:
    def __init__(self, h, x_first, core=None):
        self.h, self.x_first = h, x_first
        self.on = None if core is None else h.s == core
        self.x, self.z = h.c // 4, lax.rem(h.c, 4)
        self.first, self.second = h.sem(), h.sem()

    def when(self, act):
        act() if self.on is None else pl.when(self.on)(act)

    def chip(self, x, z):
        return (self.h.s, 4 * lax.rem(x, 4) + lax.rem(z, 4), self.h.y)

    def along(self, axis_x):
        return [self.chip(self.x + j, self.z) if axis_x else self.chip(self.x, self.z + j) for j in (1, 2, 3)]

    def send(self, pairs, targets, arrive, spare):
        leave = self.h.sem()
        copies = [
            pltpu.make_async_remote_copy(
                src_ref=src, dst_ref=dst, send_sem=leave, recv_sem=arrive, device_id=to, device_id_type=MESH)
            for (src, dst), to in zip(pairs, targets)]

        def start():
            for i in (0, 2, 1):
                copies[i].start()

        self.when(start)
        self.h.sent.append(types.SimpleNamespace(wait_send=lambda: self.when(lambda: wait_bytes(spare, leave))))


class Reduce16(Plane16):
    def __init__(self, h, part, bufs, x_first, core=None):
        super().__init__(h, x_first, core)
        self.part = part
        self.first_in, self.mine, self.second_in = bufs

    def start(self):
        pairs = []
        for j in (1, 2, 3):
            src = self.part.at[lax.rem(self.x + j, 4)] if self.x_first else self.part.at[:, lax.rem(self.z + j, 4)]
            pairs.append((src, self.first_in.at[j - 1]))
        self.send(pairs, self.along(self.x_first), self.first, self.first_in)

    def add(self):
        def add():
            wait_bytes(self.first_in, self.first)
            for k in range(4):
                own = self.part[self.x, k] if self.x_first else self.part[k, self.z]
                self.mine[k] = added([own] + [self.first_in[j, k] for j in range(3)])

        self.when(add)

    def send_on(self):
        at = self.z if self.x_first else self.x
        pairs = [(self.mine.at[lax.rem(at + j, 4)], self.second_in.at[j - 1]) for j in (1, 2, 3)]
        self.send(pairs, self.along(not self.x_first), self.second, self.second_in)

    def middle(self):
        self.add()
        self.send_on()

    def result(self):
        wait_bytes(self.second_in, self.second)
        return added([self.mine[self.z if self.x_first else self.x]] + [self.second_in[j] for j in range(3)])


def reduce_scratch(units, width):
    return [VMEM((3, 4, units, 16, width), BF16), VMEM((4, units, 16, width), BF16), VMEM((3, units, 16, width), BF16)]


class Spread16(Plane16):
    def __init__(self, h, parts, x_first, core=None):
        super().__init__(h, x_first, core)
        self.parts = parts

    def start(self):
        own = self.parts.at[self.x, self.z]
        self.send([(own, own)] * 3, self.along(self.x_first), self.first, self.parts.at[0, pl.ds(0, 3)])

    def middle(self):
        self.when(lambda: wait_bytes(self.parts.at[0, pl.ds(0, 3)], self.first))
        line = self.parts.at[:, self.z] if self.x_first else self.parts.at[self.x]
        self.send([(line, line)] * 3, self.along(not self.x_first), self.second, self.parts.at[pl.ds(0, 3)])

    def finish(self):
        self.when(lambda: wait_bytes(self.parts.at[pl.ds(0, 3)], self.second))


class FirstRows:
    def __init__(self, h, r):
        self.h, self.r = h, r
        self.sums = [
            Reduce16(h, r.rows_a, (r.rows_in.at[0], r.next_a, None), True),
            Reduce16(h, r.rows_b, (r.rows_in.at[1], r.next_b, None), False)]

    def load(self, down, first):
        r = self.r
        for c in range(CTX):
            for i, parts in enumerate((r.rows_a, r.rows_b)):
                parts[c // 4, c % 4, 0] = down[first + 2 * c + i]
        for i in range(2):
            r.next_beside[i] = down[first + 32 + i]

    def start(self):
        for each in self.sums:
            each.start()

    def add(self):
        for each in self.sums:
            each.add()


def first_rows_outs():
    mine = (spec((4, 1, 16, D)), VMEM)
    return dict(next_a=mine, next_b=mine, next_beside=(spec((2, 16, D)), VMEM))


def first_rows_scratch():
    part = VMEM((4, 4, 1, 16, D), BF16)
    return dict(rows_a=part, rows_b=part, rows_in=VMEM((2, 3, 4, 1, 16, D), BF16))


class Rows16:
    def __init__(self, h, r, core):
        self.h, self.r, self.core = h, r, core
        self.sums = [
            Reduce16(h, None, (None, r.mine_a, r.rows_second.at[0]), True),
            Reduce16(h, None, (None, r.mine_b, r.rows_second.at[1]), False),
            Reduce16(h, r.rows_c, r.rows_sums_c, True, 1 - core)]
        self.spreads = [
            Spread16(h, r.rows_all.at[0], True), Spread16(h, r.rows_all.at[1], False), Spread16(h, r.rows_out, False, 1 - core)]
        self.arrive = h.sem()
        self.arrive_each = [h.sem() for _ in range(3)]
        self.cross = [h.sem() for _ in range(3)]

    def on(self, i):
        return self.h.s != self.core if i == 2 else None

    def when(self, i, act, also=None):
        conditions = [c for c in (self.on(i), also) if c is not None]
        if not conditions:
            return act()
        return pl.when(functools.reduce(jnp.logical_and, conditions))(act)

    def start(self):
        for i in range(2):
            self.sums[i].send_on()
            self.send_tile(self.r.mine_beside.at[i], i)

    def start_out(self):
        h, r = self.h, self.r

        @pl.when(h.s != self.core)
        def _():
            for c in range(CTX):
                r.rows_c[c // 4, c % 4, 0] = r.out_sum[c]

        self.sums[2].start()
        self.send_tile(r.out_sum.at[16], 2)

    def send_tile(self, src, i):
        h = self.h
        dst, leave = self.r.tile_in.at[h.c], h.sem()
        copy = pltpu.make_async_remote_copy(
            src_ref=src, dst_ref=dst, send_sem=leave, recv_sem=self.arrive, device_id=(h.s, 5 * i, h.y),
            device_id_type=MESH)
        kept = pltpu.make_async_copy(src, dst, self.arrive)
        self.when(i, copy.start, h.c != 5 * i)
        self.when(i, kept.start, h.c == 5 * i)
        h.sent.append(types.SimpleNamespace(
            wait_send=functools.partial(self.when, i, copy.wait_send, h.c != 5 * i)))

    def middle(self):
        self.sums[2].middle()

    def spread(self):
        h, r = self.h, self.r
        x, z = h.c // 4, lax.rem(h.c, 4)
        r.rows_all[0, x, z] = self.sums[0].result()
        r.rows_all[1, x, z] = self.sums[1].result()

        def out():
            r.rows_out[x, z] = self.sums[2].result()

        self.when(2, out)
        for each in self.spreads:
            each.start()
        for i in range(3):
            leave = h.sem()
            copies = [
                pltpu.make_async_remote_copy(
                    src_ref=r.tiles.at[i], dst_ref=r.tiles.at[i], send_sem=leave, recv_sem=self.arrive_each[i],
                    device_id=(h.s, lax.rem(h.c + step, CTX), h.y), device_id_type=MESH)
                for step in range(1, CTX)]

            def start(i=i, copies=copies):
                wait_bytes(r.tile_in, self.arrive)
                r.tiles[i] = added([r.tile_in[c] for c in range(CTX)])
                for copy in copies:
                    copy.start()

            self.when(i, start, h.c == 5 * i)
            h.sent.append(types.SimpleNamespace(
                wait_send=functools.partial(
                    self.when, i, functools.partial(wait_bytes, r.tile_in.at[pl.ds(0, 15)], leave), h.c == 5 * i)))

    def spread_on(self):
        for each in self.spreads:
            each.middle()

    def finish(self):
        h, r = self.h, self.r
        for each in self.spreads:
            each.finish()
        for i in range(3):
            self.when(i, functools.partial(wait_bytes, r.tiles.at[i], self.arrive_each[i]), h.c != 5 * i)
        copies = [
            pltpu.make_async_remote_copy(
                src_ref=src, dst_ref=dst, send_sem=h.sem(), recv_sem=sem, device_id=h.sibling(), device_id_type=MESH)
            for src, dst, sem in (
                (r.rows_all, r.rows_other, self.cross[0]),
                (r.tiles, r.tiles_other, self.cross[1]), (r.rows_out, r.rows_out, self.cross[2]))]

        @pl.when(h.s != self.core)
        def _():
            for copy in copies:
                copy.start()

        h.save_on(self.core, r.rows_all, r.rows_own)

        @pl.when(h.s != self.core)
        def _():
            for copy in copies:
                copy.wait_send()

        @pl.when(h.s == self.core)
        def _():
            wait_bytes(r.rows_other, self.cross[0])
            wait_bytes(r.tiles_other, self.cross[1])
            wait_bytes(r.rows_out, self.cross[2])

        h.save_on(self.core, r.rows_other, r.rows_cross)
        h.save_on(self.core, r.rows_out, r.rows_out_all)


def rows_outs():
    return dict(tiles=(spec((3, 16, D)), VMEM), tiles_other=(spec((3, 16, D)), VMEM))


def rows_scratch():
    part = VMEM((4, 4, 1, 16, D), BF16)
    return dict(
        rows_c=part, rows_sums_c=reduce_scratch(1, D), rows_second=VMEM((2, 3, 1, 16, D), BF16),
        tile_in=VMEM((CTX, 16, D), BF16), rows_all=VMEM((2, 4, 4, 1, 16, D), BF16), rows_out=part,
        rows_other=VMEM((2, 4, 4, 1, 16, D), BF16))


def rows_results():
    whole_rows = (spec((2, 4, 4, 1, 16, D)), ANY)
    return dict(rows_own=whole_rows, rows_cross=whole_rows, rows_out_all=(spec((4, 4, 1, 16, D)), ANY))


def send_piece(h, piece, dst, layer, arrive):
    leave = h.sem()
    for step in (1, 3, 2, 0):
        shard = h.shard(step)
        src, to = piece.at[shard], dst.at[2 * h.y + h.s]
        copy = pltpu.make_async_remote_copy(
            src_ref=src, dst_ref=to, send_sem=leave, recv_sem=arrive, device_id=(layer, h.c, shard),
            device_id_type=MESH)
        if step:
            copy.start()
        else:
            pl.when(h.s != layer)(copy.start)
            pl.when(h.s == layer)(pltpu.make_async_copy(src, to, arrive).start)

    def wait_send():
        pl.when(h.s != layer)(lambda: wait_bytes(dst.at[pl.ds(0, 4)], leave))
        pl.when(h.s == layer)(lambda: wait_bytes(dst.at[pl.ds(0, 3)], leave))

    h.sent.append(types.SimpleNamespace(wait_send=wait_send))


def joined_up(windows):
    parts = []
    for g in range(8):
        main = windows[g][:, :512]
        if g % 4:
            main = jnp.concatenate([main[:, :128] + windows[g - 1][:, 512:], main[:, 128:]], axis=1)
        parts.append(main)
        if g % 4 == 3:
            parts.append(windows[g][:, 512:])
    return jnp.concatenate(parts, axis=1)


def joined_qkv(blocks, own):
    queries = [blocks[g][:, :128] for g in range(8)] + [own[:, :64]]
    keys = [blocks[g][:, a : a + 64] for g in range(8) for a in (128, 256)] + [own[:, 64:128]]
    values = [blocks[g][:, a : a + 64] for g in range(8) for a in (192, 320)] + [own[:, 128:192]]
    return jnp.concatenate(queries + keys + values + [own[:, 192:]], axis=1)


def added(blocks):
    total = blocks[0].astype(F32)
    for block in blocks[1:]:
        total = total + block.astype(F32)
    return total.astype(BF16)


def last_kernel(at, kept, saved, hidden, above, turn_up_last, norms):
    def body(r):
        h = Here(r.sems)
        x, z = h.c // 4, lax.rem(h.c, 4)
        group = 2 * h.y + h.s
        loads = [h.local(r.qkv_w, r.qkv_vm), h.local(r.a_full, r.a_vm)]
        h.barrier()
        sort_grads(r)
        h.ready()
        up0 = Reduce16(h, None, (None, r.up0_mine, r.up0_in), True)
        up0.send_on()
        main = Reduce16(h, r.main_part, r.main_sums, True)
        side = Reduce16(h, r.side_part, r.side_sums, False)
        arrive_wide = h.sem()
        send_piece(h, r.qkv1_piece, r.wide_in, 1, arrive_wide)
        rows16 = Rows16(h, r, 0)
        rows16.start()
        rows16.start_out()
        arrive_last, arrive_late = h.sem(), h.sem()
        for i in range(SHARD):
            chip = 4 * i + h.y
            r.last_message[i, 0] = r.up_last[i]
            r.last_message[i, 1] = r.up1_last[i]
            r.last_message[i, 2] = r.qkv1_last[i]
            h.send_or_keep(r.last_message.at[i], r.last_in.at[h.c], (h.s, chip, h.y), chip == h.c, arrive_last)
        early, late = [
            [Spread16(h, parts, i == 0, core) for i, parts in enumerate((r.wide_low, r.wide_high))] for core in (1, 0)]

        def spread_early():
            @pl.when(h.s == 1)
            def _():
                wait_bytes(r.wide_in, arrive_wide)
                blocks = [r.wide_in[g] for g in range(8)]
                rows = joined_qkv(blocks, added([block[:, 384:] for block in blocks]))
                r.wide_low[x, z] = rows[:, :2176]
                r.wide_high[x, z] = jnp.concatenate([rows[:, 2176:], jnp.zeros((16, 1024), BF16)], axis=1)

            for each in early:
                each.start()

        def spread_late():
            @pl.when(h.s == 0)
            def _():
                wait_bytes(r.wide_in, arrive_wide)
                rows = joined_up([r.wide_in[g] for g in range(8)])
                r.wide_low[x, z] = rows[:, :2176]
                r.wide_high[x, z] = rows[:, 2176:]

            for each in late:
                each.start()

        waits = start_tail(h, r, spread_early)

        def arrived():
            for each in early:
                each.middle()
            rows16.middle()
            r.up0_piece[...] = up0.result()
            send_piece(h, r.up0_piece, r.wide_in, 0, arrive_wide)

        def beside():
            rows16.spread()
            spread_late()

        finish = run_tail(
            h, r, 0, r.x[h.s].astype(F32), waits, loads, r.qkv_last, main.start, side.start, arrived, beside,
            lambda half, value: None)
        finish()
        for i in range(SHARD):
            chip = 4 * i + h.y
            h.send_or_keep(r.qkv_last.at[i], r.late_in.at[h.c], (h.s, chip, h.y), chip == h.c, arrive_late)
        main.middle()
        side.middle()
        for each in late:
            each.middle()
        rows16.spread_on()
        arrive_rest = h.sem()
        reduces = z == h.y

        @pl.when(reduces)
        def _():
            wait_bytes(r.last_in, arrive_last)
            wait_bytes(r.late_in, arrive_late)
            early = added([r.last_in[c] for c in range(CTX)])
            r.rest_message[0, 0] = early[0]
            r.rest_message[0, 1] = added([r.late_in[c] for c in range(CTX)])
            r.rest_message[1] = early[1:]

        rest = []
        for layer in range(2):
            leave = h.sem()
            src, dst = r.rest_message.at[layer], r.rest.at[z, h.s]
            copy = pltpu.make_async_remote_copy(
                src_ref=src, dst_ref=dst, send_sem=leave, recv_sem=arrive_rest, device_id=(layer, h.c, x),
                device_id_type=MESH)
            kept = pltpu.make_async_copy(src, dst, arrive_rest)
            is_self = (h.s == layer) & (x == h.y)
            pl.when(reduces & is_self)(kept.start)
            away = reduces & jnp.logical_not(is_self)
            pl.when(away)(copy.start)
            rest.append((away, copy))
        r.qkv_piece[:, :, :384] = main.result()
        r.qkv_piece[:, :, 384:] = side.result()
        arrive_qkv = h.sem()
        send_piece(h, r.qkv_piece, r.qkv_in, 0, arrive_qkv)
        owner = x == h.y
        across = [h.sem() for _ in range(4)]
        along = [h.sem() for _ in range(3)]
        line = r.rest.at[z]
        lines = []
        for j in range(1, 4):
            lines.append(pltpu.make_async_remote_copy(
                src_ref=line, dst_ref=line, send_sem=across[j], recv_sem=across[0],
                device_id=(h.s, 4 * lax.rem(x + j, 4) + z, h.y), device_id_type=MESH))

        @pl.when(owner)
        def _():
            wait_bytes(line, arrive_rest)
            for copy in lines:
                copy.start()

        spreads = [Spread16(h, parts, i == 0, 0) for i, parts in enumerate((r.qkv_low, r.qkv_high))]

        @pl.when(h.s == 0)
        def _():
            wait_bytes(r.qkv_in, arrive_qkv)
            blocks = [r.qkv_in[g] for g in range(8)]
            rows = joined_qkv(blocks, added([block[:, 384:] for block in blocks]))
            r.qkv_low[x, z] = rows[:, :1664]
            r.qkv_high[x, z] = rows[:, 1664:]

        for each in spreads:
            each.start()
        for each in early + late:
            each.finish()
        h.save(r.wide_low, r.wide_low_all)
        h.save(r.wide_high, r.wide_high_all)

        @pl.when(jnp.logical_not(owner))
        def _():
            wait_bytes(line, across[0])

        for j in range(1, 4):
            h.send(line, line, (h.s, 4 * x + lax.rem(z + j, 4), h.y), along[j - 1])
        for each in spreads:
            each.middle()
        rows16.finish()
        for sem in along:
            wait_bytes(line, sem)
        r.up_rest[...] = joined_up([r.rest[g // 2, g % 2, 0] for g in range(8)])
        blocks = [r.rest[g // 2, g % 2, 1] for g in range(8)]
        r.qkv_rest[...] = joined_qkv(blocks, added([block[:, 384:] for block in blocks]))
        for each in spreads:
            each.finish()
        h.save_on(0, r.qkv_low, r.qkv_low_all)
        h.save_on(0, r.qkv_high, r.qkv_high_all)

        @pl.when(owner)
        def _():
            for copy in lines:
                copy.wait_send()

        for away, copy in rest:
            pl.when(away)(copy.wait_send)
        h.finish()

    ins = dict(
        **tail_ins(at, kept, saved, kept.a_full, hidden, above, norms), qkv_w=(kept.qkv_w, ANY), up0_mine=(above.up0_mine, VMEM),
        qkv1_piece=(above.qkv1_piece, VMEM), up_last=(above.up_g_last, VMEM), qkv1_last=(above.qkv_g_last, VMEM),
        up1_last=(turn_up_last, VMEM), mine_a=(above.next_a, VMEM), mine_b=(above.next_b, VMEM), mine_beside=(above.next_beside, VMEM),
        out_sum=(above.out_sum, VMEM))
    up_half, qkv_half = (spec((4, 4, 16, 2176)), ANY), (spec((4, 4, 16, 1664)), ANY)
    outs = dict(
        **tail_outs(), wide_low_all=up_half, wide_high_all=up_half, qkv_low_all=qkv_half, qkv_high_all=qkv_half,
        up_rest=(spec((16, FF)), VMEM), qkv_rest=(spec((16, 3328)), VMEM), **rows_outs(), **rows_results())
    piece, eight = VMEM((SHARD, 16, WINDOW), BF16), VMEM((8, 16, WINDOW), BF16)
    scratch = dict(
        **tail_scratch(),
        main_sums=reduce_scratch(SHARD, 384), side_sums=reduce_scratch(SHARD, 256), **rows_scratch(), wide_low=VMEM((4, 4, 16, 2176), BF16), wide_high=VMEM((4, 4, 16, 2176), BF16),
        qkv_low=VMEM((4, 4, 16, 1664), BF16), qkv_high=VMEM((4, 4, 16, 1664), BF16), qkv_piece=piece, qkv_last=piece, last_message=VMEM((SHARD, 3, 16, WINDOW), BF16),
        last_in=VMEM((CTX, 3, 16, WINDOW), BF16), late_in=VMEM((CTX, 16, WINDOW), BF16), wide_in=eight, qkv_in=eight, up0_piece=piece,
        up0_in=VMEM((3, SHARD, 16, WINDOW), BF16),
        rest_message=VMEM((2, 2, 16, WINDOW), BF16), rest=VMEM((4, 2, 2, 16, WINDOW), BF16),
        sems=pltpu.SemaphoreType.DMA((134,)))
    return call("last", body, ins, outs, scratch, collective_id=5)


def join_kernel(back, last):
    def body(
        _, up_low, up_high, wide_low, wide_high, qkv_low, qkv_high, own0, cross0, out0, own1, cross1, out1, up_rest, qkv_rest,
        tiles0, tiles_other0, tiles1, tiles_other1, up_ref, qkv_ref, gain_ref, bias_ref, down_ref, out_ref):
        def store_norms(rows, sums):
            for i in range(5):

                @pl.when(pl.program_id(0) == i)
                def _():
                    for k in range(2):
                        part = slice(64 * i, 64 * i + min(rows, SLICE - 64 * i))
                        count = part.stop - part.start
                        gain_ref[0, k : k + 1, part] = sums[64 + 2 * k : 65 + 2 * k, :count]
                        bias_ref[0, k : k + 1, part] = sums[65 + 2 * k : 66 + 2 * k, :count]

        def store(rows, up_parts, qkv_parts):
            for at, block in up_parts:
                up_ref[:rows, at : at + block.shape[1]] = block.astype(F32)
            for at, block in qkv_parts:
                block = block.astype(F32)
                if at + block.shape[1] == 3328:
                    store_norms(rows, jnp.transpose(block[:, -128:]))
                    block = block[:, :-64]
                qkv_ref[:rows, at : at + block.shape[1]] = block

        def rows_from(halves, out, tiles):
            @pl.when(pl.program_id(0) < 4)
            def _():
                for c in range(4):
                    for i in range(2):
                        for half in range(2):
                            at = 32 * c + 16 * i
                            down_ref[half, at : at + 16] = halves[half][i, 0, c, 0].astype(F32)
                    out_ref[16 * c : 16 * c + 16] = out[0, c, 0].astype(F32)

            @pl.when(pl.program_id(0) == 4)
            def _():
                for half in range(2):
                    down_ref[half, :32] = tiles[half][:2].reshape(32, D).astype(F32)
                out_ref[:16] = tiles[2].astype(F32)

        first = lax.axis_index(SECTION) == 0
        pl.when(first)(lambda: rows_from((own0, cross0), out0, (tiles0, tiles_other0, tiles_other0[2])))
        pl.when(jnp.logical_not(first))(
            lambda: rows_from((cross1, own1), out1, (tiles_other1, tiles1, tiles_other1[2])))
        low, high = (ref[0].reshape(64, 2176) for ref in (wide_low, wide_high))

        @pl.when((pl.program_id(0) < 4) & first)
        def _():
            parts = [ref[0].reshape(64, 1664) for ref in (qkv_low, qkv_high)]
            store(64, ((0, low), (2176, high)), ((0, parts[0]), (1664, parts[1])))

        @pl.when((pl.program_id(0) < 4) & jnp.logical_not(first))
        def _():
            parts = [ref[0].reshape(64, 2176) for ref in (up_low, up_high)]
            store(64, ((0, parts[0]), (2176, parts[1])), ((0, low), (2176, high[:, :1152])))

        @pl.when(pl.program_id(0) == 4)
        def _():
            store(16, ((0, up_rest[...]),), ((0, qkv_rest[...]),))

    def place(i, section, core):
        return jnp.where((core < 0) | (section[0] == core), jnp.minimum(i, 3), 0)

    def line(width, core):
        return pl.BlockSpec((1, 4, 16, width), lambda i, section: (place(i, section, core), 0, 0, 0))

    def tile_line(core, *lead):
        zeros = (0,) * len(lead)
        return pl.BlockSpec(
            (*lead, 1, 4, 1, 16, D), lambda i, section: (*zeros, place(i, section, core), 0, 0, 0, 0))

    def tiles_of(count):
        return pl.BlockSpec((count, 16, D), lambda i, section: (0, 0, 0))

    def rows(width, count=64):
        return pl.BlockSpec((count, width), lambda i, section: (i, 0))

    def all_of(width):
        return pl.BlockSpec((16, width), lambda i, section: (0, 0))

    norms = pl.BlockSpec((1, 2, SLICE), lambda i, section: (0, 0, 0))
    return pl.pallas_call(
        body,
        out_shape=(
            spec((SLICE, FF), F32), spec((SLICE, 3 * D), F32), spec((1, 2, SLICE), F32), spec((1, 2, SLICE), F32),
            spec((2, 544, D), F32),
            spec((SLICE, D), F32)),
        grid_spec=pltpu.PrefetchScalarGridSpec(
            num_scalar_prefetch=1,
            grid=(5,),
            in_specs=[
                line(2176, 1), line(2176, 1), line(2176, -1), line(2176, -1), line(1664, 0), line(1664, 0),
                tile_line(0, 2), tile_line(0, 2), tile_line(0), tile_line(1, 2), tile_line(1, 2), tile_line(1),
                all_of(FF), all_of(3328), *[tiles_of(3)] * 4],
            out_specs=(
                rows(FF), rows(3 * D), norms, norms, pl.BlockSpec((2, 128, D), lambda i, section: (0, i, 0)), rows(D))),
        name="join",
    )(lax.axis_index(SECTION).astype(jnp.int32).reshape(1), back.up_low_all, back.up_high_all, last.wide_low_all, last.wide_high_all, last.qkv_low_all, last.qkv_high_all, last.rows_own,
      last.rows_cross, last.rows_out_all, back.rows_own, back.rows_cross, back.rows_out_all, last.up_rest, last.qkv_rest,
      last.tiles, last.tiles_other, back.tiles, back.tiles_other)


def token_positions(block_order):
    offsets = jnp.arange(32, dtype=jnp.int32)
    groups = jnp.arange(2, dtype=jnp.int32)[:, None, None] * GROUP
    return (groups + block_order[:, :, None] * 32 + offsets).reshape(2, GROUP)


def swapped(section, first, second):
    own = jnp.where(section == 0, first, second)
    other = lax.ppermute(jnp.where(section == 0, second, first), SECTION, [(0, 1), (1, 0)])
    return jnp.where(section == 0, own, other), jnp.where(section == 0, other, own)


def gathered(x):
    return lax.all_gather(x, CONTEXT)


def shards(hidden_in, cotangent, block_order, qkv_weight, out_weight, up_weight, down_weight, norm_gains, norm_biases):
    section, ctx = lax.axis_index(SECTION), lax.axis_index(CONTEXT)
    grid = token_positions(block_order)
    own_positions = lax.dynamic_slice(grid, (section, ctx * ROWS), (1, ROWS))
    positions = grid.reshape(1, SEQ)
    slots = jnp.arange(32, dtype=jnp.int32)
    slot = jnp.sum(jnp.where(block_order[:, None, :] == slots[None, :, None], slots[None, None, :], 0), axis=2)
    group, odd = jnp.arange(2, dtype=jnp.int32)[:, None], slot % 2
    chip = slot // 2
    places = jnp.stack([10 * chip + 4 * group + 2 * odd, 10 * chip + 8 + odd, 2 * chip + odd])
    at = (block_order, places, positions, own_positions.reshape(ROWS, 1))
    at_back = (block_order, places, positions.reshape(SEQ, 1), own_positions)
    hidden = hidden_in[0]
    spread = spread_kernel(norm_gains, norm_biases, qkv_weight, up_weight)
    norms = spread.norms
    mid_all = gathered(spread.mid_piece)
    first = first_kernel(hidden, norms, spread.side_piece, spread.side_last, out_weight, down_weight)
    up_piece, first.q16 = lax.optimization_barrier((spread.side_piece, first.q16))
    up_all = gathered(up_piece)
    middle = middle_kernel(at, hidden, norms, first, mid_all, spread.mid_last)
    turn = turn_kernel(at, middle, middle.y, norms, first, up_all, spread.side_last, cotangent[0])
    back = back_kernel(
        at_back, middle, turn, middle.y, turn, norms, first, middle.attended16, mid_all, spread.mid_last)
    last = last_kernel(at_back, first, middle, hidden, back, turn.up_g_last, norms)
    up, qkv, gain, bias, down, out = join_kernel(back, last)
    activations = jnp.stack(swapped(section, middle.y, back.out))
    input_grads = jnp.stack(swapped(section, last.in_grad, back.in_grad))
    return (
        activations[None, None],
        input_grads[None, None],
        qkv[None],
        out[None],
        up[None],
        down.reshape(D, D)[None],
        gain,
        bias,
    )


def solution(mesh):
    tokens = P(LINE, None, CONTEXT, None)
    rows = P(SECTION, LINE, None)
    norms = P(SECTION, None, LINE)
    layers = P(SECTION, LINE, None, CONTEXT, None)
    return jax.shard_map(
        shards,
        mesh=mesh,
        in_specs=(tokens, tokens, P(), rows, rows, rows, rows, norms, norms),
        out_specs=(layers, layers, rows, rows, rows, rows, norms, norms),
        check_vma=False,
    )
```
